32 devices in a mesh: fsdp: 8 (over z, y), tp: 4 (over x, core).
Axes of the slice: x: 2, y: 2, z: 4, core: 2. Of those that a mesh axis runs over, the one named last changes fastest.
Arguments:
- inputs: float32 [16, 2048, 1280], P('fsdp', 'tp'), may hold values from -6 to 6
- cotangent: float32 [16, 2048, 1280], P('fsdp', 'tp'), may hold values from -6 to 6
- w_qkv: bfloat16 [2, 3, 1280, 1280], P(None, None, 'fsdp', 'tp'), may hold values from -0.15625 to 0.15625
- w_out: bfloat16 [2, 1280, 1280], P(None, 'tp', 'fsdp'), may hold values from -2 to 2
- w_up: bfloat16 [2, 1280, 1280], P(None, 'fsdp', 'tp'), may hold values from -0.15625 to 0.15625
- w_down: bfloat16 [2, 1280, 1280], P(None, 'tp', 'fsdp'), may hold values from -0.15625 to 0.15625
- norm_gain: float32 [2, 2, 1280], replicated, may hold values from 0.1 to 1.9
- query_scale: float32 [2, 80], replicated, may hold values from -1 to 1
- prefix_len: int32 [16], P('fsdp'), may hold values from 204 to 1024
Outputs:
- outputs: float32 [16, 2048, 1280], P('fsdp', 'tp')
- input_grad: float32 [16, 2048, 1280], P('fsdp', 'tp')
- w_qkv_grad: float32 [2, 3, 1280, 1280], P(None, None, 'fsdp', 'tp')
- w_out_grad: float32 [2, 1280, 1280], P(None, 'tp', 'fsdp')
- w_up_grad: float32 [2, 1280, 1280], P(None, 'fsdp', 'tp')
- w_down_grad: float32 [2, 1280, 1280], P(None, 'tp', 'fsdp')
- attn_gain_grad: float32 [2, 1280], replicated
- mlp_gain_grad: float32 [2, 1280], replicated
- scale_grad: float32 [2, 80], replicated
The draws below stay inside these ranges and needn't reach their ends.
All inputs are finite; a program needn't handle non-finite values.
Results may differ from the reference program's by a relative error of at most 0.04.
Values may be sent and summed in bfloat16 or wider, within the bound.
A program may use at most 384 MiB of HBM per device.

```python
import math
import jax
import jax.numpy as jnp
from jax import lax

D = 1280
HEADS = 16
DH = 80
FF = 1280
LAYERS = 2
LEN = 2048
SEQS = 16


def touch_ends(array, stream_key, low, largest):
    shape = array.shape
    index_at = [jax.random.randint(jax.random.fold_in(stream_key, axis), (), 0, shape[axis]) for axis in range(len(shape))]
    array = array.at[tuple(index_at)].set(low)
    longest = shape.index(max(shape))
    index_at[longest] = (index_at[longest] + 1) % shape[longest]
    return array.at[tuple(index_at)].set(largest)


def shard_levels(stream_key, dims, cuts, low, largest):
    loudness = 1.0
    for axis_at, shards_of in cuts:
        draws = jax.random.uniform(jax.random.fold_in(jax.random.fold_in(stream_key, 6), axis_at), (shards_of,), jnp.float32, low / len(cuts), largest / len(cuts))
        loudness = loudness * jnp.repeat(jnp.exp(draws), dims[axis_at] // shards_of).reshape((-1,) + (1,) * (len(dims) - 1 - axis_at))
    return loudness


def normal_values(stream_key, shape, width, most, cuts=(), held_as=jnp.bfloat16):
    array = width * jax.random.normal(stream_key, shape, jnp.float32)
    if cuts:
        array = array * shard_levels(stream_key, shape, cuts, -0.22, 0.18)
    return jnp.clip(array, -most, most).astype(held_as)


def setup_inputs(seed: int = 0) -> dict:
    keys = jax.random.split(jax.random.key(seed), 10)
    inputs = normal_values(keys[0], (SEQS, LEN, D), 1.0, 6.0, ((0, 8), (1, 4)), jnp.float32)
    cotangent = normal_values(keys[1], (SEQS, LEN, D), 1.0, 6.0, ((0, 8), (1, 4)), jnp.float32)
    w_qkv = normal_values(keys[2], (LAYERS, 3, D, D), D ** -0.5, 0.15625, ((2, 8), (3, 4)))
    w_out = normal_values(keys[3], (LAYERS, D, D), (max(4, D * 16 // LEN)) ** -0.5, 2.0, ((1, 4), (2, 8)))
    w_up = normal_values(keys[4], (LAYERS, D, FF), D ** -0.5, 0.15625, ((1, 8), (2, 4)))
    w_down = normal_values(keys[5], (LAYERS, FF, D), FF ** -0.5, 0.15625, ((1, 4), (2, 8)))
    norm_gain = jnp.clip(1.0 + 0.18 * jax.random.normal(keys[6], (LAYERS, 2, D), jnp.float32), 0.1, 1.9)
    query_scale = jnp.clip(jax.random.uniform(keys[7], (LAYERS, DH), jnp.float32, -1.0, 1.0), -1.0, 1.0)
    prefix_len = touch_ends(jax.random.randint(keys[8], (SEQS,), LEN // 10, LEN // 2 + 1), jax.random.fold_in(keys[8], 1), LEN // 10, (LEN // 2 + 1) - 1).astype(jnp.int32)
    return dict(inputs=inputs, cotangent=cotangent, w_qkv=w_qkv, w_out=w_out, w_up=w_up, w_down=w_down, norm_gain=norm_gain, query_scale=query_scale, prefix_len=prefix_len)


EPSILON = 1e-06
SOFT_ONE = 1.442695041
MASKED = -1e+30
HIGH = lax.Precision.HIGHEST

@jax.custom_vjp
def low(v):
    return lax.optimization_barrier(v.astype(jnp.bfloat16)).astype(jnp.float32)

@jax.custom_vjp
def low_back(v):
    return v

def low_keep(v):
    return (low(v), None)

def low_pass(kept, grad):
    return (grad,)

def back_keep(v):
    return (v, None)

def back_low(kept, grad):
    return (low(grad),)
low.defvjp(low_keep, low_pass)
low_back.defvjp(back_keep, back_low)

def rms_apply(x_rows, gain_row):
    normed = x_rows * lax.rsqrt(lax.optimization_barrier(jnp.mean(x_rows * x_rows, axis=-1, keepdims=True)) + EPSILON)
    return normed * gain_row

def one_layer(x_rows, prefix, qkv_mat, out_mat, up_mat, down_mat, gains, scale_row):
    length = x_rows.shape[0]
    block = min(512, length)
    nblocks = length // block
    h_attn = low(rms_apply(x_rows, gains[0]))
    projected = jnp.einsum('rd,cde->cre', h_attn, qkv_mat, precision=HIGH)
    factor = jax.nn.softplus(scale_row) * (SOFT_ONE / math.sqrt(DH))
    head_shape = (length, HEADS, DH)
    queries = low(low_back(projected[0]).reshape(head_shape) * factor)
    key_vals = low(low_back(projected[1])).reshape(head_shape)
    value_vals = low(low_back(projected[2])).reshape(head_shape)

    def one_block(element):
        query_block, row_start = element
        scores = low_back(jnp.einsum('qhd,khd->hqk', query_block, key_vals, precision=HIGH))
        row_ids = row_start + lax.broadcasted_iota(jnp.int32, (block, length), 0)
        col_ids = lax.broadcasted_iota(jnp.int32, (block, length), 1)
        allowed = (col_ids <= row_ids) | (col_ids < prefix)
        scores = jnp.where(allowed[None], scores, MASKED)
        softmaxed = low(jax.nn.softmax(scores, axis=-1))
        return jnp.einsum('hqk,khd->qhd', softmaxed, value_vals, precision=HIGH)
    block_starts = jnp.arange(nblocks, dtype=jnp.int32) * block
    attended = lax.map(jax.checkpoint(one_block), (queries.reshape(nblocks, block, HEADS, DH), block_starts))
    attended = low(low_back(attended.reshape(length, D)))
    middle = x_rows + low_back(jnp.dot(attended, out_mat, precision=HIGH))
    h_mlp = low(rms_apply(middle, gains[1]))
    hidden = low(jax.nn.silu(low_back(jnp.dot(h_mlp, up_mat, precision=HIGH))))
    return middle + low_back(jnp.dot(hidden, down_mat, precision=HIGH))

def reference(inputs, cotangent, w_qkv, w_out, w_up, w_down, norm_gain, query_scale, prefix_len):
    params = (w_qkv.astype(jnp.float32), w_out.astype(jnp.float32), w_up.astype(jnp.float32), w_down.astype(jnp.float32), norm_gain.astype(jnp.float32), query_scale.astype(jnp.float32))

    def one_sequence(totals, element):
        x_rows, grad_rows, prefix = element

        def forward(start_rows, qkv_all, out_all, up_all, down_all, gain_all, scale_all):
            current = start_rows
            for layer_id in range(LAYERS):
                current = one_layer(current, prefix, qkv_all[layer_id], out_all[layer_id], up_all[layer_id], down_all[layer_id], gain_all[layer_id], scale_all[layer_id])
            return current
        result, pullback = jax.vjp(forward, x_rows, *params)
        grad_list = pullback(grad_rows)
        totals = tuple((old + new for old, new in zip(totals, grad_list[1:])))
        return (totals, (result, grad_list[0]))
    initial = tuple((jnp.zeros_like(entry) for entry in params))
    totals, (results, grads_in) = lax.scan(one_sequence, initial, (inputs.astype(jnp.float32), cotangent.astype(jnp.float32), prefix_len))
    gain_total = totals[4]
    return (results, grads_in, totals[0], totals[1], totals[2], totals[3], gain_total[:, 0], gain_total[:, 1], totals[5])
```

```python
import functools, math
import jax
import jax.numpy as jnp
from jax import lax
from jax.experimental import pallas as pl
from jax.experimental.pallas import tpu as pltpu
from jax.sharding import PartitionSpec as P

MASKED = -1e30
F32, BF16 = jnp.float32, jnp.bfloat16
EPSILON = 1e-06
SOFT_ONE = 1.442695041
LOG2E = math.log2(math.e)
VMEM_LIMIT = 60 * 2**20

def dot(a, b, dims=((1,), (0,))):
    return lax.dot_general(a, b, (dims, ((), ())), preferred_element_type=F32)

def key_range(row_start, rows, prefix, block):
    full = jnp.maximum(row_start + 1, prefix) // block
    stop = (jnp.maximum(row_start + rows, prefix) + block - 1) // block
    return full, stop

def forward_kernel(prefix_ref, q_ref, k_ref, v_ref, o_ref, lse_ref, key_rows, value_ext, *, pair, dh, bq, bk):
    length = q_ref.shape[1]
    prefix = prefix_ref[0]
    ext = value_ext.shape[1]
    for h in range(pair):
        key_rows[h] = k_ref[h * dh:(h + 1) * dh, :].T
        value_ext[h, :dh] = v_ref[h * dh:(h + 1) * dh, :]
        value_ext[h, dh:] = jnp.ones((ext - dh, length), BF16)

    def one_query(qi, carry):
        start = pl.multiple_of(qi * bq, bq)
        here = pl.ds(start, bq)
        queries = [q_ref[h * dh:(h + 1) * dh, here] for h in range(pair)]
        full, stop = key_range(start, bq, prefix, bk)

        def step(masked, ki, state):
            first = pl.multiple_of(ki * bk, bk)
            if masked:
                rows = first + lax.broadcasted_iota(jnp.int32, (bk, bq), 0)
                cols = start + lax.broadcasted_iota(jnp.int32, (bk, bq), 1)
                allowed = rows <= jnp.maximum(cols, prefix - 1)
            scores = [dot(key_rows[h, pl.ds(first, bk)], queries[h]) for h in range(pair)]
            fresh = []
            for h in range(pair):
                top, total = state[h]
                s = scores[h]
                if masked:
                    s = jnp.where(allowed, s, MASKED)
                new_top = jnp.maximum(top, jnp.max(s, axis=0, keepdims=True))
                p = jnp.exp2(s - new_top).astype(BF16)
                total = total * jnp.exp2(top - new_top) + dot(value_ext[h, :, pl.ds(first, bk)], p)
                fresh.append((new_top, total))
            return tuple(fresh)

        state = tuple((jnp.full((1, bq), MASKED, F32), jnp.zeros((ext, bq), F32)) for _ in range(pair))
        state = lax.fori_loop(0, full, functools.partial(step, False), state)
        state = lax.fori_loop(full, stop, functools.partial(step, True), state)
        for h in range(pair):
            top, total = state[h]
            norm = total[dh:dh + 1]
            o_ref[h * dh:(h + 1) * dh, here] = (total[:dh] / norm).astype(BF16)
            lse_ref[h, :, here] = top + jnp.log2(norm)
        return carry

    lax.fori_loop(0, length // bq, one_query, 0)

def attention_forward(q, k, v, prefix, dh, pair=2, bq=512, bk=512):
    width, length = q.shape
    heads = width // dh
    pair = min(pair, heads); bq = min(bq, length); bk = min(bk, length)
    ext = dh + 16
    spec = pl.BlockSpec((pair * dh, length), lambda i, p: (i, 0))
    return pl.pallas_call(
        functools.partial(forward_kernel, pair=pair, dh=dh, bq=bq, bk=bk),
        grid_spec=pltpu.PrefetchScalarGridSpec(
            num_scalar_prefetch=1, grid=(heads // pair,),
            in_specs=[spec, spec, spec],
            out_specs=[spec, pl.BlockSpec((pair, 1, length), lambda i, p: (i, 0, 0))],
            scratch_shapes=[pltpu.VMEM((pair, length, dh), BF16), pltpu.VMEM((pair, ext, length), BF16)],
        ),
        out_shape=[jax.ShapeDtypeStruct((width, length), BF16), jax.ShapeDtypeStruct((heads, 1, length), F32)],
        compiler_params=pltpu.CompilerParams(vmem_limit_bytes=VMEM_LIMIT),
        cost_estimate=pl.CostEstimate(flops=2 * 2 * 256 * length * length * heads * 2 // 3, bytes_accessed=8 * width * length, transcendentals=0),
        name="attention_forward",
    )(prefix, q, k, v)

def split3(x):
    a = x.astype(BF16)
    r = x - a.astype(F32)
    b = r.astype(BF16)
    c = (r - b.astype(F32)).astype(BF16)
    return a, b, c

def backward_kernel(prefix_ref, q_ref, k_ref, v_ref, o_ref, g_ref, lse_ref, scale_ref, dq_ref, dk_ref, dv_ref, fg_ref,
                    key_rows, key_ext, value_ext, query_ext, grad_ext, dk_acc, dv_acc, *, pair, dh, bq, bk):
    length = q_ref.shape[1]
    prefix = prefix_ref[0]
    ext = key_ext.shape[1]
    pad = ext - dh
    ones = (lax.broadcasted_iota(jnp.int32, (pad, length), 0) < 3).astype(F32).astype(BF16)
    fg_zero = pl.program_id(0) == 0
    @pl.when(fg_zero)
    def _():
        fg_ref[...] = jnp.zeros_like(fg_ref)
    for h in range(pair):
        rows = slice(h * dh, (h + 1) * dh)
        q, k, v, g = q_ref[rows, :], k_ref[rows, :], v_ref[rows, :], g_ref[rows, :]
        key_rows[h] = k.T
        key_ext[h, :dh] = k
        key_ext[h, dh:] = ones
        value_ext[h, :dh] = v
        value_ext[h, dh:] = ones
        delta = jnp.sum(o_ref[rows, :].astype(F32) * g.astype(F32), axis=0, keepdims=True)
        def stack(base, row):
            parts = split3(-row)
            idx = lax.broadcasted_iota(jnp.int32, (pad, length), 0)
            tail = jnp.where(idx == 0, parts[0].astype(F32), jnp.where(idx == 1, parts[1].astype(F32), jnp.where(idx == 2, parts[2].astype(F32), 0.0)))
            return jnp.concatenate([base, tail.astype(BF16)], axis=0).T
        query_ext[h] = stack(q, lse_ref[h])
        grad_ext[h] = stack(g, delta)
        dk_acc[h] = jnp.zeros((dh, length), F32)
        dv_acc[h] = jnp.zeros((dh, length), F32)

    def one_query(qi, carry):
        start = pl.multiple_of(qi * bq, bq)
        here = pl.ds(start, bq)
        full, stop = key_range(start, bq, prefix, bk)

        def step(masked, ki, state):
            first = pl.multiple_of(ki * bk, bk)
            there = pl.ds(first, bk)
            if masked:
                rows = start + lax.broadcasted_iota(jnp.int32, (bq, bk), 0)
                cols = first + lax.broadcasted_iota(jnp.int32, (bq, bk), 1)
                allowed = cols <= jnp.maximum(rows, prefix - 1)
            fresh = []
            s = [dot(query_ext[h, here], key_ext[h, :, there]) for h in range(pair)]
            gp = [dot(grad_ext[h, here], value_ext[h, :, there]) for h in range(pair)]
            for h in range(pair):
                x = jnp.where(allowed, s[h], MASKED) if masked else s[h]
                p = jnp.exp2(x)
                ds = (p * gp[h]).astype(BF16)
                rows = slice(h * dh, (h + 1) * dh)
                dv_acc[h, :, there] += dot(g_ref[rows, here], p.astype(BF16))
                dk_acc[h, :, there] += dot(q_ref[rows, here], ds)
                fresh.append(state[h] + dot(ds, key_rows[h, there]))
            return tuple(fresh)

        state = tuple(jnp.zeros((bq, dh), F32) for _ in range(pair))
        state = lax.fori_loop(0, full, functools.partial(step, False), state)
        state = lax.fori_loop(full, stop, functools.partial(step, True), state)
        for h in range(pair):
            rows = slice(h * dh, (h + 1) * dh)
            dq = state[h].T
            prod = dq * q_ref[rows, here].astype(F32)
            part = prod[:, :128]
            for c in range(1, bq // 128):
                part = part + prod[:, c * 128:(c + 1) * 128]
            fg_ref[...] += part
            dq_ref[rows, here] = (dq * scale_ref[...]).astype(BF16)
        return carry

    lax.fori_loop(0, length // bq, one_query, 0)
    for h in range(pair):
        rows = slice(h * dh, (h + 1) * dh)
        dk_ref[rows, :] = (dk_acc[h] * math.log(2.0)).astype(BF16)
        dv_ref[rows, :] = dv_acc[h].astype(BF16)

def attention_backward(q, k, v, o, g, lse, factor, prefix, dh, pair=2, bq=512, bk=512):
    width, length = q.shape
    heads = width // dh
    pair = min(pair, heads); bq = min(bq, length); bk = min(bk, length)
    ext = dh + 16
    spec = pl.BlockSpec((pair * dh, length), lambda i, p: (i, 0))
    wide = jax.ShapeDtypeStruct((width, length), BF16)
    return pl.pallas_call(
        functools.partial(backward_kernel, pair=pair, dh=dh, bq=bq, bk=bk),
        grid_spec=pltpu.PrefetchScalarGridSpec(
            num_scalar_prefetch=1, grid=(heads // pair,),
            in_specs=[spec] * 5 + [pl.BlockSpec((pair, 1, length), lambda i, p: (i, 0, 0)), pl.BlockSpec((dh, 1), lambda i, p: (0, 0))],
            out_specs=[spec] * 3 + [pl.BlockSpec((dh, 128), lambda i, p: (0, 0))],
            scratch_shapes=[
                pltpu.VMEM((pair, length, dh), BF16),
                pltpu.VMEM((pair, ext, length), BF16),
                pltpu.VMEM((pair, ext, length), BF16),
                pltpu.VMEM((pair, length, ext), BF16),
                pltpu.VMEM((pair, length, ext), BF16),
                pltpu.VMEM((pair, dh, length), F32),
                pltpu.VMEM((pair, dh, length), F32)],
        ),
        out_shape=[wide] * 3 + [jax.ShapeDtypeStruct((dh, 128), F32)],
        compiler_params=pltpu.CompilerParams(vmem_limit_bytes=VMEM_LIMIT),
        cost_estimate=pl.CostEstimate(flops=5 * 2 * 256 * length * length * heads * 2 // 3, bytes_accessed=16 * width * length, transcendentals=0),
        name="attention_backward",
    )(prefix, q, k, v, o, g, lse, factor.reshape(dh, 1))


def rms(x):
    inv = lax.rsqrt(jnp.mean(x * x, axis=-1, keepdims=True) + EPSILON)
    return x * inv, inv


def rms_back(normed, inv, gain, grad):
    scaled = grad * gain
    out = inv * (scaled - normed * jnp.mean(scaled * normed, axis=-1, keepdims=True))
    return out, jnp.sum(grad * normed, axis=0)


def ein(spec, *args):
    return jnp.einsum(spec, *args, preferred_element_type=F32)


class Plan:
    def __init__(self, seqs, tp):
        self.seqs, self.tp, self.ring = seqs, tp, tp // seqs
        self.same_member = [[s * self.ring + r for s in range(seqs)] for r in range(self.ring)]
        self.same_seq = [[s * self.ring + r for r in range(self.ring)] for s in range(seqs)]

    def swap(self, blocks):
        return lax.all_to_all(
            blocks, "tp", 0, 0, tiled=True, axis_index_groups=self.same_member
        )

    def whole(self, rows):
        got = lax.all_gather(rows, "tp", axis=1, axis_index_groups=self.same_seq)
        return got.reshape(-1, rows.shape[-1])

    def share(self, full, positions):
        cut = full.reshape(self.seqs, self.ring, positions, full.shape[-1])
        return lax.psum_scatter(
            cut, "tp", scatter_dimension=1, axis_index_groups=self.same_seq
        )


def gather_heads(plan, shards):
    rows = lax.all_gather(shards, "fsdp", axis=1, tiled=True)
    return lax.all_gather(rows, "tp", axis_index_groups=plan.same_member)


def gather_full(plan, shards):
    part = gather_heads(plan, shards)
    every = lax.all_gather(part, "tp", axis_index_groups=plan.same_seq)
    r, s, m, d, w = every.shape
    return every.transpose(2, 3, 0, 1, 4).reshape(m, d, r * s * w)


def scatter_heads(plan, grads):
    mine = lax.psum_scatter(
        grads.astype(BF16), "tp", scatter_dimension=0, axis_index_groups=plan.same_member
    )
    return lax.psum_scatter(mine, "fsdp", scatter_dimension=1, tiled=True).astype(F32)


def scatter_full(plan, grads):
    m, d, cols = grads.shape
    cut = grads.astype(BF16).reshape(m, d, plan.ring, plan.seqs, -1).transpose(2, 3, 0, 1, 4)
    mine = lax.psum_scatter(cut, "tp", scatter_dimension=0, axis_index_groups=plan.same_seq)
    return scatter_heads(plan, mine)


def layer_forward(plan, x, prefix, qkv, out_t, up, down_t, gains, factor, positions):
    dh = factor.shape[0]
    normed, inv = rms(x)
    low = (normed * gains[0]).astype(BF16)
    h = plan.whole(low.reshape(plan.seqs, positions, -1))
    seqs, _, d, w = qkv.shape
    raw = [ein("sdc,td->sct", qkv[:, c], h).reshape(seqs * w, -1) for c in range(3)]
    scale = jnp.tile(factor * LOG2E, seqs * w // dh)[:, None]
    q, k, v = (raw[0] * scale).astype(BF16), raw[1].astype(BF16), raw[2].astype(BF16)
    att, lse = attention_forward(q, k, v, prefix, dh)
    part = ein("sct,sdc->td", att.reshape(seqs, w, -1), out_t).astype(BF16)
    middle = x + plan.share(part, positions).reshape(x.shape).astype(F32)
    normed_m, inv_m = rms(middle)
    h_m = (normed_m * gains[1]).astype(BF16)
    pre = ein("td,df->tf", h_m, up)
    hidden = jax.nn.silu(pre).astype(BF16)
    result = middle + ein("tf,df->td", hidden, down_t)
    return result, (x, inv, h, q, k, v, att, lse, middle, inv_m, h_m, pre, hidden)


def layer_backward(plan, g, saved, prefix, qkv, out_t, up, down_t, gains, factor, positions):
    x, inv, h, q, k, v, att, lse, middle, inv_m, h_m, pre, hidden = saved
    dh = factor.shape[0]
    seqs, _, d, w = qkv.shape
    length = h.shape[0]
    g_low = g.astype(BF16)
    down_grad = ein("td,tf->df", g_low, hidden)
    g_hidden = ein("td,df->tf", g_low, down_t)
    sig = jax.nn.sigmoid(pre)
    g_pre = (g_hidden * sig * (1.0 + pre * (1.0 - sig))).astype(BF16)
    up_grad = ein("td,tf->df", h_m, g_pre)
    g_hm = ein("tf,df->td", g_pre, up)
    back_m, gain_m = rms_back(middle * inv_m, inv_m, gains[1], g_hm)
    g_mid = g + back_m
    g_all = plan.whole(g_mid.astype(BF16).reshape(plan.seqs, positions, -1))
    att3 = att.reshape(seqs, w, length)
    out_grad = ein("td,sct->sdc", g_all, att3)
    g_att = ein("td,sdc->sct", g_all, out_t).astype(BF16).reshape(seqs * w, length)
    dq, dk, dv, fg = attention_backward(q, k, v, att, g_att, lse, factor, prefix, dh)
    factor_grad = jnp.sum(fg, axis=1) / (factor * LOG2E)
    parts = [a.reshape(seqs, w, length) for a in (dq, dk, dv)]
    qkv_grad = jnp.stack([ein("td,sct->sdc", h, a) for a in parts], axis=1)
    g_ha = sum(ein("sct,sdc->td", a, qkv[:, c]) for c, a in enumerate(parts)).astype(BF16)
    g_ha = plan.share(g_ha, positions).reshape(x.shape).astype(F32)
    back_a, gain_a = rms_back(x * inv, inv, gains[0], g_ha)
    return g_mid + back_a, (qkv_grad, out_grad, up_grad, down_grad, gain_a, gain_m, factor_grad)


def body(inputs, cotangent, w_qkv, w_out, w_up, w_down, norm_gain, query_scale, prefix_len):
    seqs, positions, d = inputs.shape
    tp = lax.axis_size("tp")
    plan = Plan(seqs, tp)
    layers = w_qkv.shape[0]
    dh = query_scale.shape[1]
    unit = SOFT_ONE / math.sqrt(dh)
    factors = jax.nn.softplus(query_scale) * unit
    mine = lax.axis_index("tp") // plan.ring
    prefix = lax.dynamic_slice_in_dim(prefix_len, mine, 1)
    out_shard, down_shard = jnp.swapaxes(w_out, 1, 2), jnp.swapaxes(w_down, 1, 2)

    weights = []
    for l in range(layers):
        qkv = gather_heads(plan, w_qkv[l])
        out_t = gather_heads(plan, out_shard[l][None])[:, 0]
        up, down_t = gather_full(plan, jnp.stack([w_up[l], down_shard[l]]))
        weights.append((qkv, out_t, up, down_t))

    x = plan.swap(inputs.astype(BF16)).astype(F32).reshape(seqs * positions, d)
    g = plan.swap(cotangent.astype(BF16)).astype(F32).reshape(seqs * positions, d)
    kept = []
    for l in range(layers):
        x, saved = layer_forward(plan, x, prefix, *weights[l], norm_gain[l], factors[l], positions)
        kept.append(saved)
    outputs = plan.swap(x.astype(BF16).reshape(seqs, positions, d)).astype(F32)
    grads = [None] * layers
    for l in reversed(range(layers)):
        g, (qkv_g, out_g, up_g, down_g, gain_a, gain_m, f_g) = layer_backward(
            plan, g, kept[l], prefix, *weights[l], norm_gain[l], factors[l], positions
        )
        qkv_g = scatter_heads(plan, qkv_g)
        out_g = scatter_heads(plan, out_g[:, None])[0].T
        up_g, down_g = scatter_full(plan, jnp.stack([up_g, down_g]))
        grads[l] = (qkv_g, out_g, up_g, down_g.T, gain_a, gain_m, f_g)
    input_grad = plan.swap(g.astype(BF16).reshape(seqs, positions, d)).astype(F32)
    qkv_g, out_g, up_g, down_g, gain_a, gain_m, f_g = (jnp.stack(a) for a in zip(*grads))
    scale_g = f_g * jax.nn.sigmoid(query_scale) * unit
    gain_a, gain_m, scale_g = lax.psum((gain_a, gain_m, scale_g), ("fsdp", "tp"))
    return outputs, input_grad, qkv_g, out_g, up_g, down_g, gain_a, gain_m, scale_g


def solution(mesh):
    placed = (
        P("fsdp", "tp", None),
        P("fsdp", "tp", None),
        P(None, None, "fsdp", "tp"),
        P(None, "tp", "fsdp"),
        P(None, "fsdp", "tp"),
        P(None, "tp", "fsdp"),
        P(),
        P(),
        P("fsdp"),
    )
    return jax.shard_map(
        body,
        mesh=mesh,
        in_specs=placed,
        out_specs=placed[:6] + (P(), P(), P()),
        check_vma=False,
    )
```

```python
import functools, math
import jax
import jax.numpy as jnp
from jax import lax
from jax.experimental import pallas as pl
from jax.experimental.pallas import tpu as pltpu
from jax.sharding import PartitionSpec as P

MASKED = -1e30
F32, BF16 = jnp.float32, jnp.bfloat16
EPSILON = 1e-06
SOFT_ONE = 1.442695041
LOG2E = math.log2(math.e)
MESH = pl.DeviceIdType.MESH
HINT = 1
VMEM_LIMIT = 60 * 2**20

def dot(a, b, dims=((1,), (0,))):
    return lax.dot_general(a, b, (dims, ((), ())), preferred_element_type=F32)

def key_range(row_start, rows, prefix, block):
    full = jnp.maximum(row_start + 1, prefix) // block
    stop = (jnp.maximum(row_start + rows, prefix) + block - 1) // block
    return full, stop

def forward_kernel(prefix_ref, order_ref, q_ref, k_ref, v_ref, o_ref, lse_ref, key_rows, value_ext, *, pair, dh, bq, bk):
    length = q_ref.shape[1]
    prefix = prefix_ref[0]
    ext = value_ext.shape[1]
    for h in range(pair):
        key_rows[h] = k_ref[h * dh:(h + 1) * dh, :].T
        value_ext[h, :dh] = v_ref[h * dh:(h + 1) * dh, :]
        value_ext[h, dh:] = jnp.ones((ext - dh, length), BF16)

    def one_query(qi, carry):
        start = qi * bq
        here = pl.ds(pl.multiple_of(order_ref[qi] * bq, bq), bq)
        queries = [q_ref[h * dh:(h + 1) * dh, here] for h in range(pair)]
        full, stop = key_range(start, bq, prefix, bk)

        def step(masked, ki, state):
            first = ki * bk
            there = pl.ds(pl.multiple_of(order_ref[ki] * bk, bk), bk)
            if masked:
                rows = first + lax.broadcasted_iota(jnp.int32, (bk, bq), 0)
                cols = start + lax.broadcasted_iota(jnp.int32, (bk, bq), 1)
                allowed = rows <= jnp.maximum(cols, prefix - 1)
            scores = [dot(key_rows[h, there], queries[h]) for h in range(pair)]
            fresh = []
            for h in range(pair):
                top, total = state[h]
                s = scores[h]
                if masked:
                    s = jnp.where(allowed, s, MASKED)
                new_top = jnp.maximum(top, jnp.max(s, axis=0, keepdims=True))
                p = jnp.exp2(s - new_top).astype(BF16)
                total = total * jnp.exp2(top - new_top) + dot(value_ext[h, :, there], p)
                fresh.append((new_top, total))
            return tuple(fresh)

        state = tuple((jnp.full((1, bq), MASKED, F32), jnp.zeros((ext, bq), F32)) for _ in range(pair))
        state = lax.fori_loop(0, full, functools.partial(step, False), state)
        state = lax.fori_loop(full, stop, functools.partial(step, True), state)
        for h in range(pair):
            top, total = state[h]
            norm = total[dh:dh + 1]
            o_ref[h * dh:(h + 1) * dh, here] = (total[:dh] / norm).astype(BF16)
            lse_ref[h, :, here] = top + jnp.log2(norm)
        return carry

    lax.fori_loop(0, length // bq, one_query, 0)

def attention_forward(q, k, v, prefix, order, dh, pair=4):
    width, length = q.shape
    heads = width // dh
    pair = min(pair, heads)
    bq = bk = length // order.shape[0]
    ext = dh + 16
    spec = pl.BlockSpec((pair * dh, length), lambda i, p, o: (i, 0))
    return pl.pallas_call(
        functools.partial(forward_kernel, pair=pair, dh=dh, bq=bq, bk=bk),
        grid_spec=pltpu.PrefetchScalarGridSpec(
            num_scalar_prefetch=2, grid=(heads // pair,),
            in_specs=[spec, spec, spec],
            out_specs=[spec, pl.BlockSpec((pair, 1, length), lambda i, p, o: (i, 0, 0))],
            scratch_shapes=[pltpu.VMEM((pair, length, dh), BF16), pltpu.VMEM((pair, ext, length), BF16)],
        ),
        out_shape=[jax.ShapeDtypeStruct((width, length), BF16), jax.ShapeDtypeStruct((heads, 1, length), F32)],
        compiler_params=pltpu.CompilerParams(vmem_limit_bytes=VMEM_LIMIT),
        cost_estimate=pl.CostEstimate(flops=int(HINT * 600 * length * length * heads), bytes_accessed=int(HINT * 8 * width * length), transcendentals=0),
        name="attention_forward",
    )(prefix, order, q, k, v)

def split3(x):
    a = x.astype(BF16)
    r = x - a.astype(F32)
    b = r.astype(BF16)
    c = (r - b.astype(F32)).astype(BF16)
    return a, b, c

def backward_kernel(prefix_ref, order_ref, q_ref, k_ref, v_ref, o_ref, g_ref, lse_ref, scale_ref, dq_ref, dk_ref, dv_ref, fg_ref,
                    key_rows, key_ext, value_ext, query_ext, grad_ext, dk_acc, dv_acc, *, pair, dh, bq, bk):
    length = q_ref.shape[1]
    prefix = prefix_ref[0]
    ext = key_ext.shape[1]
    pad = ext - dh
    ones = (lax.broadcasted_iota(jnp.int32, (pad, length), 0) < 3).astype(F32).astype(BF16)
    fg_zero = pl.program_id(0) == 0
    @pl.when(fg_zero)
    def _():
        fg_ref[...] = jnp.zeros_like(fg_ref)
    for h in range(pair):
        rows = slice(h * dh, (h + 1) * dh)
        q, k, v, g = q_ref[rows, :], k_ref[rows, :], v_ref[rows, :], g_ref[rows, :]
        key_rows[h] = k.T
        key_ext[h, :dh] = k
        key_ext[h, dh:] = ones
        value_ext[h, :dh] = v
        value_ext[h, dh:] = ones
        delta = jnp.sum(o_ref[rows, :].astype(F32) * g.astype(F32), axis=0, keepdims=True)
        def stack(base, row):
            parts = split3(-row)
            idx = lax.broadcasted_iota(jnp.int32, (pad, length), 0)
            tail = jnp.where(idx == 0, parts[0].astype(F32), jnp.where(idx == 1, parts[1].astype(F32), jnp.where(idx == 2, parts[2].astype(F32), 0.0)))
            return jnp.concatenate([base, tail.astype(BF16)], axis=0).T
        query_ext[h] = stack(q, lse_ref[h])
        grad_ext[h] = stack(g, delta)
        dk_acc[h] = jnp.zeros((dh, length), F32)
        dv_acc[h] = jnp.zeros((dh, length), F32)

    def one_query(qi, carry):
        start = qi * bq
        here = pl.ds(pl.multiple_of(order_ref[qi] * bq, bq), bq)
        full, stop = key_range(start, bq, prefix, bk)

        def step(masked, ki, state):
            first = ki * bk
            there = pl.ds(pl.multiple_of(order_ref[ki] * bk, bk), bk)
            if masked:
                rows = start + lax.broadcasted_iota(jnp.int32, (bq, bk), 0)
                cols = first + lax.broadcasted_iota(jnp.int32, (bq, bk), 1)
                allowed = cols <= jnp.maximum(rows, prefix - 1)
            fresh = []
            s = [dot(query_ext[h, here], key_ext[h, :, there]) for h in range(pair)]
            gp = [dot(grad_ext[h, here], value_ext[h, :, there]) for h in range(pair)]
            for h in range(pair):
                x = jnp.where(allowed, s[h], MASKED) if masked else s[h]
                p = jnp.exp2(x)
                ds = (p * gp[h]).astype(BF16)
                rows = slice(h * dh, (h + 1) * dh)
                dv_acc[h, :, there] += dot(g_ref[rows, here], p.astype(BF16))
                dk_acc[h, :, there] += dot(q_ref[rows, here], ds)
                fresh.append(state[h] + dot(ds, key_rows[h, there]))
            return tuple(fresh)

        state = tuple(jnp.zeros((bq, dh), F32) for _ in range(pair))
        state = lax.fori_loop(0, full, functools.partial(step, False), state)
        state = lax.fori_loop(full, stop, functools.partial(step, True), state)
        for h in range(pair):
            rows = slice(h * dh, (h + 1) * dh)
            dq = state[h].T
            prod = dq * q_ref[rows, here].astype(F32)
            part = prod[:, :128]
            for c in range(1, bq // 128):
                part = part + prod[:, c * 128:(c + 1) * 128]
            fg_ref[...] += part
            dq_ref[rows, here] = (dq * scale_ref[...]).astype(BF16)
        return carry

    lax.fori_loop(0, length // bq, one_query, 0)
    for h in range(pair):
        rows = slice(h * dh, (h + 1) * dh)
        dk_ref[rows, :] = (dk_acc[h] * math.log(2.0)).astype(BF16)
        dv_ref[rows, :] = dv_acc[h].astype(BF16)

def attention_backward(q, k, v, o, g, lse, factor, prefix, order, dh, base=0, width=None, pair=2):
    full, length = q.shape
    width = width or full
    heads = width // dh
    pair = min(pair, heads)
    bq = bk = length // order.shape[0]
    ext = dh + 16
    spec = pl.BlockSpec((pair * dh, length), lambda i, p, o: (i, 0))
    skip = base // (pair * dh)
    source = pl.BlockSpec((pair * dh, length), lambda i, p, o: (i + skip, 0))
    wide = jax.ShapeDtypeStruct((width, length), BF16)
    return pl.pallas_call(
        functools.partial(backward_kernel, pair=pair, dh=dh, bq=bq, bk=bk),
        grid_spec=pltpu.PrefetchScalarGridSpec(
            num_scalar_prefetch=2, grid=(heads // pair,),
            in_specs=[source] * 5 + [pl.BlockSpec((pair, 1, length), lambda i, p, o: (i + skip, 0, 0)), pl.BlockSpec((dh, 1), lambda i, p, o: (0, 0))],
            out_specs=[spec] * 3 + [pl.BlockSpec((dh, 128), lambda i, p, o: (0, 0))],
            scratch_shapes=[
                pltpu.VMEM((pair, length, dh), BF16),
                pltpu.VMEM((pair, ext, length), BF16),
                pltpu.VMEM((pair, ext, length), BF16),
                pltpu.VMEM((pair, length, ext), BF16),
                pltpu.VMEM((pair, length, ext), BF16),
                pltpu.VMEM((pair, dh, length), F32),
                pltpu.VMEM((pair, dh, length), F32)],
        ),
        out_shape=[wide] * 3 + [jax.ShapeDtypeStruct((dh, 128), F32)],
        compiler_params=pltpu.CompilerParams(vmem_limit_bytes=VMEM_LIMIT),
        cost_estimate=pl.CostEstimate(flops=int(HINT * 1600 * length * length * heads), bytes_accessed=int(HINT * 16 * width * length), transcendentals=0),
        name="attention_backward",
    )(prefix, order, q, k, v, o, g, lse, factor.reshape(dh, 1))


def rms(x):
    inv = lax.rsqrt(jnp.mean(x * x, axis=-1, keepdims=True) + EPSILON)
    return x * inv, inv


def rms_back(normed, inv, gain, grad):
    scaled = grad * gain
    out = inv * (scaled - normed * jnp.mean(scaled * normed, axis=-1, keepdims=True))
    return out, jnp.sum(grad * normed, axis=0)


def ein(spec, *args):
    return jnp.einsum(spec, *args, preferred_element_type=F32)


def gather_kernel(pieces, pairs, outer, ring, shard_ref, block_ref, *refs):
    outs = [refs[2 * m:2 * m + 2] for m in range(pairs)]
    got_ref = refs[2 * pairs]
    send, recv, local = refs[2 * pairs + 1:]
    f, t = lax.axis_index("fsdp"), lax.axis_index("tp")
    zz, yy = f // 2, f % 2
    across = {"tp": lax.rem(t + ring, 2 * ring)}
    beside = {"fsdp": zz * 2 + 1 - yy}
    along = [{"fsdp": lax.rem(zz + k, outer) * 2 + yy} for k in range(1, outer)]
    peers = along + [across, beside]
    barrier = pltpu.get_barrier_semaphore()
    for peer in peers:
        pl.semaphore_signal(barrier, inc=1, device_id=peer, device_id_type=MESH)
    pl.semaphore_wait(barrier, len(peers))
    used = [0]

    def copy(src, dst, peer):
        slot = used[0]
        used[0] += 1
        return pltpu.make_async_remote_copy(
            src_ref=src, dst_ref=dst, send_sem=send.at[slot], recv_sem=recv.at[slot],
            device_id=peer, device_id_type=MESH,
        )

    count = len(pieces)
    chunks = 4
    step = block_ref.shape[0] // chunks
    blocks = [
        copy(block_ref.at[pl.ds(i * step, step)], got_ref.at[pl.ds(i * step, step)], across)
        for i in range(chunks)
    ]
    own, first, second, third = [], [], [], []
    for i, (m, low, rows, route) in enumerate(pieces):
        part = pl.ds(low, rows)
        w = [out.at[:, :, part] for out in outs[m]]
        src = shard_ref.at[m, part]
        own.append(pltpu.make_async_copy(src, w[0].at[zz, yy], local.at[i]))
        first.append([copy(src, w[0].at[zz, yy], peer) for peer in along])
        if route:
            second.append([copy(w[0].at[:, yy], w[0].at[:, yy], beside)])
            third.append([copy(w[0], w[1], across)])
        else:
            second.append([copy(w[0].at[:, yy], w[1].at[:, yy], across)])
            third.append([copy(w[s].at[:, yy], w[s].at[:, yy], beside) for s in range(2)])

    def begin(i):
        own[i].start()
        for c in first[i]:
            c.start()

    ahead = 3
    for i in range(min(ahead, count)):
        begin(i)
    started = 0
    for b in blocks[:2]:
        b.start()
    started = 2
    for i in range(count + 2):
        if i < count:
            own[i].wait()
            for c in first[i]:
                c.wait_recv()
            for c in second[i]:
                c.start()
            if i + ahead < count:
                begin(i + ahead)
            if started < chunks:
                blocks[started].start()
                started += 1
        if 0 <= i - 1 < count:
            for c in second[i - 1]:
                c.wait_recv()
            for c in third[i - 1]:
                c.start()
        if 0 <= i - 2 < count:
            for c in third[i - 2]:
                c.wait_recv()
    for b in blocks[started:]:
        b.start()
    for i in range(count):
        for c in first[i] + second[i] + third[i]:
            c.wait_send()
    for b in blocks:
        b.wait()


def pieces_of(pairs, rows):
    half = rows // 32 * 16
    return tuple(
        (m, low, size, m_part) for m in range(pairs) for m_part, (low, size) in enumerate(((0, half), (half, rows - half)))
    )


def gather_call(shards, block, pieces, fsdp, ring):
    pairs, rows, w = shards.shape
    outer = fsdp // 2
    slots = 4 + len(pieces) * (outer + 2)
    any_spec = pl.BlockSpec(memory_space=pl.ANY)
    got = pl.pallas_call(
        functools.partial(gather_kernel, pieces, pairs, outer, ring),
        out_shape=[jax.ShapeDtypeStruct((outer, 2, rows, w), BF16)] * (2 * pairs)
        + [jax.ShapeDtypeStruct(block.shape, block.dtype)],
        in_specs=[any_spec] * 2,
        out_specs=[any_spec] * (2 * pairs + 1),
        scratch_shapes=[
            pltpu.SemaphoreType.DMA((slots,)),
            pltpu.SemaphoreType.DMA((slots,)),
            pltpu.SemaphoreType.DMA((len(pieces),)),
        ],
        compiler_params=pltpu.CompilerParams(collective_id=0, has_side_effects=True),
        name="gather_weights",
    )(shards, block)
    return [a.reshape(outer * 2 * rows, w) for a in got[:-1]], got[-1]


class Plan:
    def __init__(self, seqs, tp, fsdp, rows):
        self.seqs, self.tp, self.ring, self.fsdp = seqs, tp, tp // seqs, fsdp
        self.same_member = [[s * self.ring + r for s in range(seqs)] for r in range(self.ring)]
        self.same_seq = [[s * self.ring + r for r in range(self.ring)] for s in range(seqs)]
        self.fast = seqs == 2 and self.ring == 2 and fsdp % 2 == 0 and rows % 32 == 0
        t = lax.axis_index("tp")
        self.seq, self.member = t // self.ring, lax.rem(t, self.ring)

    def across(self, a):
        n = self.tp
        return lax.ppermute(a, "tp", [(t, (t + self.ring) % n) for t in range(n)])

    def core(self, a):
        return lax.ppermute(a, "tp", [(t, t ^ 1) for t in range(self.tp)])

    def pick(self, blocks, index):
        return lax.dynamic_index_in_dim(blocks, index, 0, keepdims=False)

    def order(self, own, other):
        first = self.seq == 0
        return jnp.concatenate([jnp.where(first, own, other), jnp.where(first, other, own)])

    def swap(self, blocks):
        if self.seqs == 2:
            other = self.across(self.pick(blocks, 1 - self.seq).astype(BF16))
            return self.order(self.pick(blocks, self.seq), other.astype(F32))
        got = lax.all_to_all(
            blocks.astype(BF16), "tp", 0, 0, tiled=True, axis_index_groups=self.same_member
        )
        return got.reshape(-1, got.shape[-1]).astype(F32)

    def unswap(self, rows):
        blocks = rows.reshape(self.seqs, -1, rows.shape[-1])
        return self.swap(blocks).reshape(blocks.shape)

    def whole(self, rows):
        if self.fast:
            return jnp.concatenate([rows, self.core(rows)])
        cut = rows.reshape(self.seqs, -1, rows.shape[-1])
        got = lax.all_gather(cut, "tp", axis=1, axis_index_groups=self.same_seq)
        return got.reshape(-1, rows.shape[-1])

    def share(self, full):
        if self.fast:
            own = full.shape[0] // 2
            return full[:own].astype(F32) + self.core(full[own:].astype(BF16)).astype(F32)
        cut = full.astype(BF16).reshape(self.seqs, self.ring, -1, full.shape[-1])
        got = lax.psum_scatter(cut, "tp", scatter_dimension=1, axis_index_groups=self.same_seq)
        return got.reshape(-1, full.shape[-1]).astype(F32)

    def blocks(self, length):
        if self.fast:
            j = jnp.arange(self.tp, dtype=jnp.int32)
            apart = (j % self.ring != self.member).astype(jnp.int32)
            return apart * self.seqs + j // self.ring
        return jnp.arange(max(1, length // 512), dtype=jnp.int32)

    def gather_heads(self, shards):
        rows = lax.all_gather(shards, "fsdp", axis=1, tiled=True)
        if self.fast:
            return jnp.stack([rows, self.across(rows)])
        return lax.all_gather(rows, "tp", axis_index_groups=self.same_member)

    def join(self, every):
        r, s, m, d, w = every.shape
        return every.transpose(2, 3, 0, 1, 4).reshape(m, d, r * s * w)

    def gather_full(self, shards):
        part = self.gather_heads(shards)
        if self.fast:
            return self.join(jnp.stack([part, self.core(part)]))
        return self.join(lax.all_gather(part, "tp", axis_index_groups=self.same_seq))

    def scatter_heads(self, grads):
        if self.fast:
            other = self.across(grads[1].astype(BF16))
            mine = (grads[0].astype(F32) + other.astype(F32)).astype(BF16)
        else:
            mine = lax.psum_scatter(
                grads.astype(BF16), "tp", scatter_dimension=0, axis_index_groups=self.same_member
            )
        return lax.psum_scatter(mine, "fsdp", scatter_dimension=1, tiled=True).astype(F32)

    def scatter_full(self, grads):
        m, d, cols = grads.shape
        if self.fast:
            half = cols // 2
            other = self.core(grads[:, :, half:].astype(BF16))
            mine = grads[:, :, :half].astype(F32) + other.astype(F32)
            mine = mine.astype(BF16).reshape(m, d, self.seqs, -1).transpose(2, 0, 1, 3)
        else:
            cut = grads.astype(BF16).reshape(m, d, self.ring, self.seqs, -1).transpose(2, 3, 0, 1, 4)
            mine = lax.psum_scatter(cut, "tp", scatter_dimension=0, axis_index_groups=self.same_seq)
        return self.scatter_heads(mine)


def layer_forward(plan, x, prefix, order, qkv, out_t, up, down_t, gains, factor):
    dh = factor.shape[0]
    normed, inv = rms(x)
    h = plan.whole((normed * gains[0]).astype(BF16))
    seqs, d, w = out_t.shape
    raw = [ein("sdc,td->sct", qkv[c], h).reshape(seqs * w, -1) for c in range(3)]
    scale = jnp.tile(factor * LOG2E, seqs * w // dh)[:, None]
    q, k, v = (raw[0] * scale).astype(BF16), raw[1].astype(BF16), raw[2].astype(BF16)
    att, lse = attention_forward(q, k, v, prefix, order, dh)
    middle = x + plan.share(ein("sct,sdc->td", att.reshape(seqs, w, -1), out_t))
    normed_m, inv_m = rms(middle)
    h_m = (normed_m * gains[1]).astype(BF16)
    pre = ein("td,df->tf", h_m, up)
    hidden = jax.nn.silu(pre).astype(BF16)
    result = middle + ein("tf,df->td", hidden, down_t)
    return result, (x, inv, h, q, k, v, att, lse, middle, inv_m, h_m, pre, hidden)


def layer_backward(plan, g, saved, prefix, order, qkv, out_t, up, down_t, gains, factor):
    x, inv, h, q, k, v, att, lse, middle, inv_m, h_m, pre, hidden = saved
    dh = factor.shape[0]
    seqs, d, w = out_t.shape
    length = h.shape[0]
    g_low = g.astype(BF16)
    down_grad = ein("td,tf->df", g_low, hidden)
    g_hidden = ein("td,df->tf", g_low, down_t)
    sig = jax.nn.sigmoid(pre)
    g_pre = (g_hidden * sig * (1.0 + pre * (1.0 - sig))).astype(BF16)
    up_grad = ein("td,tf->df", h_m, g_pre)
    mlp_grads = plan.scatter_full(jnp.stack([up_grad, down_grad]))
    g_hm = ein("tf,df->td", g_pre, up)
    back_m, gain_m = rms_back(middle * inv_m, inv_m, gains[1], g_hm)
    g_mid = g + back_m
    g_all = plan.whole(g_mid.astype(BF16))
    att3 = att.reshape(seqs, w, length)
    out_grad = plan.scatter_heads(ein("td,sct->sdc", g_all, att3)[:, None])[0]
    g_att = ein("td,sdc->sct", g_all, out_t).astype(BF16).reshape(seqs * w, length)
    dq, dk, dv, fg = attention_backward(q, k, v, att, g_att, lse, factor, prefix, order, dh)
    factor_grad = jnp.sum(fg, axis=1) / (factor * LOG2E)
    parts = [a.reshape(seqs, w, length) for a in (dq, dk, dv)]
    qkv_grad = plan.scatter_heads(jnp.stack([ein("td,sct->sdc", h, a) for a in parts], axis=1))
    g_ha = plan.share(sum(ein("sct,sdc->td", a, b) for a, b in zip(parts, qkv)))
    back_a, gain_a = rms_back(x * inv, inv, gains[0], g_ha)
    return g_mid + back_a, (qkv_grad, out_grad.T, mlp_grads[0], mlp_grads[1].T, gain_a, gain_m, factor_grad)


TN, NT, TT = ((0,), (0,)), ((1,), (1,)), ((0,), (1,))
ONE = pl.Buffered(1)


def cost(flops, nbytes):
    return pl.CostEstimate(flops=int(flops * HINT), bytes_accessed=int(nbytes * HINT), transcendentals=0)


def params():
    return pltpu.CompilerParams(vmem_limit_bytes=VMEM_LIMIT)


def fixed(shape):
    return pl.BlockSpec(shape, lambda *a: (0,) * len(shape), pipeline_mode=ONE)


def shape_of(shape, dtype=BF16):
    return jax.ShapeDtypeStruct(shape, dtype)


def inverse_rms(x):
    return lax.rsqrt(jnp.mean(x * x, axis=-1, keepdims=True) + EPSILON)


def eight(x):
    return jnp.sum(x.reshape(-1, 8, x.shape[-1]), axis=0)


def join_lanes(dst, refs, low, high):
    width = high - low
    for i, ref in enumerate(refs):
        dst[:, i * width:(i + 1) * width] = ref[:, low:high]


def project_kernel(w, h_ref, qk0, qk1, vo0, vo1, scale_ref, *refs):
    q_ref, k_ref, v_ref = refs[-3:]
    h = h_ref[...]
    for s, (qk, vo) in enumerate(((qk0, vo0), (qk1, vo1))):
        rows = slice(s * w, (s + 1) * w)
        both = dot(qk[...], h, TT)
        q_ref[rows] = (both[:w] * scale_ref[rows]).astype(BF16)
        k_ref[rows] = both[w:].astype(BF16)
        v_ref[rows] = dot(vo[:, :w], h, TT).astype(BF16)


def project(h, qk, vo, scale, base, bufs=None):
    rows, d = h.shape
    w = qk[0].shape[1] // 2
    bt = 512
    steps = rows // bt
    out = pl.BlockSpec((2 * w, bt), lambda i: (0, i + base * steps))
    whole = fixed((d, 2 * w))
    extra = [] if bufs is None else list(bufs)
    return pl.pallas_call(
        functools.partial(project_kernel, w),
        grid=(steps,),
        in_specs=[pl.BlockSpec((bt, d), lambda i: (i, 0))] + [whole] * 4 + [fixed((2 * w, 1))]
        + [pl.BlockSpec(memory_space=pl.ANY)] * len(extra),
        out_specs=[out] * 3,
        out_shape=[shape_of((2 * w, 2 * rows))] * 3,
        input_output_aliases={6 + i: i for i in range(len(extra))},
        compiler_params=params(),
        cost_estimate=cost(2 * rows * d * 6 * w, 4 * rows * d),
        name="project",
    )(h, *qk, *vo, scale, *extra)


def out_kernel(w, att_ref, vo0, vo1, part_ref, mat):
    @pl.when(pl.program_id(0) == 0)
    def _():
        join_lanes(mat, (vo0, vo1), w, 2 * w)

    part_ref[...] = dot(att_ref[...], mat[...], TT).astype(BF16)


def out_project(att, vo, base):
    d, w2 = vo[0].shape
    rows = att.shape[1] // 2
    bt = 512
    steps = rows // bt
    return pl.pallas_call(
        functools.partial(out_kernel, w2 // 2),
        grid=(steps,),
        in_specs=[pl.BlockSpec((w2, bt), lambda i: (0, i + base * steps)), fixed((d, w2)), fixed((d, w2))],
        out_specs=pl.BlockSpec((bt, d), lambda i: (i, 0)),
        out_shape=shape_of((rows, d)),
        scratch_shapes=[pltpu.VMEM((d, w2), BF16)],
        compiler_params=params(),
        cost_estimate=cost(2 * rows * d * w2, 4 * rows * d),
        name="out_project",
    )(att, *vo)


def middle_kernel(w, x_ref, att_ref, got_ref, gm_ref, ga_ref, vo0, vo1, un0, un1, un2, un3,
                  mid_ref, pre_ref, res_ref, h_ref, out_mat, up_mat, down_mat):
    @pl.when(pl.program_id(0) == 0)
    def _():
        join_lanes(out_mat, (vo0, vo1), w, 2 * w)
        join_lanes(up_mat, (un0, un1, un2, un3), 0, w)
        join_lanes(down_mat, (un0, un1, un2, un3), w, 2 * w)

    mid = x_ref[...] + got_ref[...].astype(F32) + dot(att_ref[...], out_mat[...], TT)
    mid_ref[...] = mid
    h_m = (mid * inverse_rms(mid) * gm_ref[...]).astype(BF16)
    pre = dot(h_m, up_mat[...])
    pre_ref[...] = pre
    hidden = (pre / (1.0 + jnp.exp(-pre))).astype(BF16)
    res = mid + dot(hidden, down_mat[...], NT)
    res_ref[...] = res
    h_ref[...] = (res * inverse_rms(res) * ga_ref[...]).astype(BF16)


def middle_call(x, att, got, gain_m, gain_a, vo, un):
    rows, d = x.shape
    w2 = vo[0].shape[1]
    ff = 2 * w2
    bt = 256
    row = pl.BlockSpec((bt, d), lambda i: (i, 0))
    wide = pl.BlockSpec((bt, ff), lambda i: (i, 0))
    return pl.pallas_call(
        functools.partial(middle_kernel, w2 // 2),
        grid=(rows // bt,),
        in_specs=[row, pl.BlockSpec((w2, bt), lambda i: (0, i)), row] + [fixed((1, d))] * 2 + [fixed((d, w2))] * 6,
        out_specs=[row, wide, row, row],
        out_shape=[shape_of((rows, d), F32), shape_of((rows, ff), F32), shape_of((rows, d), F32), shape_of((rows, d))],
        scratch_shapes=[pltpu.VMEM((d, w2), BF16), pltpu.VMEM((d, ff), BF16), pltpu.VMEM((d, ff), BF16)],
        compiler_params=params(),
        cost_estimate=cost(2 * rows * d * (w2 + 2 * ff), 30 * rows * d),
        name="middle",
    )(x, att, got, gain_m, gain_a, *vo, *un)


def mlp_back_kernel(w, g_ref, mid_ref, pre_ref, gm_ref, un0, un1, un2, un3,
                    g_mid_ref, low_ref, gain_ref, o0, o1, o2, o3,
                    up_mat, down_mat, g_all, hid_all, hm_all, gpre_all):
    i = pl.program_id(0)
    bt = g_ref.shape[0]

    @pl.when(i == 0)
    def _():
        join_lanes(up_mat, (un0, un1, un2, un3), 0, w)
        join_lanes(down_mat, (un0, un1, un2, un3), w, 2 * w)
        gain_ref[...] = jnp.zeros_like(gain_ref)

    here = pl.ds(pl.multiple_of(i * bt, bt), bt)
    g = g_ref[...]
    g_low = g.astype(BF16)
    g_all[here] = g_low
    pre = pre_ref[...]
    sig = 1.0 / (1.0 + jnp.exp(-pre))
    hid_all[here] = (pre * sig).astype(BF16)
    g_hidden = dot(g_low, down_mat[...])
    g_pre = (g_hidden * sig * (1.0 + pre * (1.0 - sig))).astype(BF16)
    gpre_all[here] = g_pre
    mid = mid_ref[...]
    inv = inverse_rms(mid)
    normed = mid * inv
    gain = gm_ref[...]
    hm_all[here] = (normed * gain).astype(BF16)
    g_hm = dot(g_pre, up_mat[...], NT)
    gain_ref[...] += eight(g_hm * normed)
    scaled = g_hm * gain
    g_mid = g + inv * (scaled - normed * jnp.mean(scaled * normed, axis=-1, keepdims=True))
    g_mid_ref[...] = g_mid
    low_ref[...] = g_mid.astype(BF16)

    @pl.when(i == pl.num_programs(0) - 1)
    def _():
        d = up_mat.shape[0]
        step = 256

        def chunk(c, carry):
            cols = pl.ds(pl.multiple_of(c * step, step), step)
            up = dot(hm_all[:, cols], gpre_all[...], TN).astype(BF16)
            down = dot(g_all[:, cols], hid_all[...], TN).astype(BF16)
            for b, out in enumerate((o0, o1, o2, o3)):
                out[cols, 0:w] = up[:, b * w:(b + 1) * w]
                out[cols, w:2 * w] = down[:, b * w:(b + 1) * w]
            return carry

        lax.fori_loop(0, d // step, chunk, 0)


def mlp_back(g, mid, pre, gain, un):
    rows, d = g.shape
    ff = pre.shape[1]
    w2 = un[0].shape[1]
    bt = 256
    row = pl.BlockSpec((bt, d), lambda i: (i, 0))
    wide = pl.BlockSpec((bt, ff), lambda i: (i, 0))
    return pl.pallas_call(
        functools.partial(mlp_back_kernel, w2 // 2),
        grid=(rows // bt,),
        in_specs=[row, row, wide, fixed((1, d))] + [fixed((d, w2))] * 4,
        out_specs=[row, row, fixed((8, d))] + [fixed((d, w2))] * 4,
        out_shape=[shape_of((rows, d), F32), shape_of((rows, d)), shape_of((8, d), F32)] + [shape_of((d, w2))] * 4,
        scratch_shapes=[pltpu.VMEM((d, ff), BF16)] * 2
        + [pltpu.VMEM((rows, d), BF16), pltpu.VMEM((rows, ff), BF16), pltpu.VMEM((rows, d), BF16), pltpu.VMEM((rows, ff), BF16)],
        compiler_params=params(),
        cost_estimate=cost(8 * rows * d * ff, 30 * rows * d),
        name="mlp_back",
    )(g, mid, pre, gain, *un)


def grad_att_kernel(w, g_ref, vo0, vo1, *refs):
    out_ref, mat = refs[-2:]

    @pl.when(pl.program_id(0) == 0)
    def _():
        join_lanes(mat, (vo0, vo1), w, 2 * w)

    out_ref[...] = dot(mat[...], g_ref[...], TT).astype(BF16)


def grad_att(g, vo, base, buf=None):
    rows, d = g.shape
    w2 = vo[0].shape[1]
    bt = 512
    steps = rows // bt
    extra = [] if buf is None else [buf]
    return pl.pallas_call(
        functools.partial(grad_att_kernel, w2 // 2),
        grid=(steps,),
        in_specs=[pl.BlockSpec((bt, d), lambda i: (i, 0)), fixed((d, w2)), fixed((d, w2))]
        + [pl.BlockSpec(memory_space=pl.ANY)] * len(extra),
        out_specs=pl.BlockSpec((w2, bt), lambda i: (0, i + base * steps)),
        out_shape=shape_of((w2, 2 * rows)),
        scratch_shapes=[pltpu.VMEM((d, w2), BF16)],
        input_output_aliases={3: 0} if extra else {},
        compiler_params=params(),
        cost_estimate=cost(2 * rows * d * w2, 4 * rows * d),
        name="grad_att",
    )(g, *vo, *extra)


def out_grad_kernel(w, own_ref, other_ref, att_ref, o0, o1):
    half = own_ref.shape[0]
    att = att_ref[...]
    grad = dot(own_ref[...], att[:, :half], TT) + dot(other_ref[...], att[:, half:], TT)
    grad = grad.astype(BF16)
    o0[...] = grad[:, :w]
    o1[...] = grad[:, w:]


def out_grad_call(own, other, att):
    rows, d = own.shape
    w2 = att.shape[0]
    bd = 256
    col = pl.BlockSpec((rows, bd), lambda i: (0, i))
    out = pl.BlockSpec((bd, w2 // 2), lambda i: (i, 0))
    return pl.pallas_call(
        functools.partial(out_grad_kernel, w2 // 2),
        grid=(d // bd,),
        in_specs=[col, col, fixed(att.shape)],
        out_specs=[out] * 2,
        out_shape=[shape_of((d, w2 // 2))] * 2,
        compiler_params=params(),
        cost_estimate=cost(4 * rows * d * w2, 8 * rows * d),
        name="out_grad",
    )(own, other, att)


def weight_grad_kernel(w, own_ref, other_ref, dq_ref, dk_ref, dv_ref, out, stacked):
    half = own_ref.shape[0]

    @pl.when(pl.program_id(0) == 0)
    def _():
        for j, ref in enumerate((dq_ref, dk_ref, dv_ref)):
            stacked[j * w:(j + 1) * w, :] = ref[...]

    grad = dot(own_ref[...], stacked[:, :half], TT) + dot(other_ref[...], stacked[:, half:], TT)
    out[:, :3 * w] = grad.astype(BF16)
    out[:, 3 * w:] = jnp.zeros((out.shape[0], out.shape[1] - 3 * w), BF16)


def weight_grad(own, other, dq, dk, dv, width):
    rows, d = own.shape
    w = dq.shape[0]
    bd = 256
    col = pl.BlockSpec((rows, bd), lambda i: (0, i))
    return pl.pallas_call(
        functools.partial(weight_grad_kernel, w),
        grid=(d // bd,),
        in_specs=[col, col] + [fixed(dq.shape)] * 3,
        out_specs=pl.BlockSpec((bd, width), lambda i: (i, 0)),
        out_shape=shape_of((d, width)),
        scratch_shapes=[pltpu.VMEM((3 * w, 2 * rows), BF16)],
        compiler_params=params(),
        cost_estimate=cost(12 * rows * d * w, 12 * rows * d),
        name="weight_grad",
    )(own, other, dq, dk, dv)


def input_sum(w, grads, qk, vo):
    total = None
    for s in range(2):
        dq, dk, dv = grads[3 * s:3 * s + 3]
        both = jnp.concatenate([dq[...], dk[...]], axis=0)
        part = dot(both, qk[s][...], TT) + dot(dv[...], vo[s][:, :w], TT)
        total = part if total is None else total + part
    return total


def input_other_kernel(w, *refs):
    refs, out_ref = refs[:-1], refs[-1]
    out_ref[...] = input_sum(w, refs[:6], refs[6:8], refs[8:10]).astype(BF16)


def input_other(grads, qk, vo):
    w, length = grads[0].shape
    d, w2 = qk[0].shape
    bt = 512
    steps = length // 2 // bt
    col = pl.BlockSpec((w, bt), lambda i: (0, i + steps))
    return pl.pallas_call(
        functools.partial(input_other_kernel, w),
        grid=(steps,),
        in_specs=[col] * 6 + [fixed((d, w2))] * 4,
        out_specs=pl.BlockSpec((bt, d), lambda i: (i, 0)),
        out_shape=shape_of((length // 2, d)),
        compiler_params=params(),
        cost_estimate=cost(3 * length * d * w2, 4 * length * d),
        name="input_other",
    )(*grads, *qk, *vo)


def input_own_kernel(w, *refs):
    grads, refs = refs[:6], refs[6:]
    got_ref, x_ref, g_ref, gain_ref, qk0, qk1, vo0, vo1, out_ref, sum_ref = refs

    @pl.when(pl.program_id(0) == 0)
    def _():
        sum_ref[...] = jnp.zeros_like(sum_ref)

    g_ha = input_sum(w, grads, (qk0, qk1), (vo0, vo1)) + got_ref[...].astype(F32)
    x = x_ref[...]
    inv = inverse_rms(x)
    normed = x * inv
    sum_ref[...] += eight(g_ha * normed)
    scaled = g_ha * gain_ref[...]
    out_ref[...] = g_ref[...] + inv * (scaled - normed * jnp.mean(scaled * normed, axis=-1, keepdims=True))


def input_own(grads, got, x, g, gain, qk, vo):
    w = grads[0].shape[0]
    rows, d = x.shape
    w2 = 2 * w
    bt = 256
    col = pl.BlockSpec((w, bt), lambda i: (0, i))
    row = pl.BlockSpec((bt, d), lambda i: (i, 0))
    return pl.pallas_call(
        functools.partial(input_own_kernel, w),
        grid=(rows // bt,),
        in_specs=[col] * 6 + [row] * 3 + [fixed((1, d))] + [fixed((d, w2))] * 4,
        out_specs=[row, fixed((8, d))],
        out_shape=[shape_of((rows, d), F32), shape_of((8, d), F32)],
        compiler_params=params(),
        cost_estimate=cost(6 * rows * d * w2, 24 * rows * d),
        name="input_own",
    )(*grads, got, x, g, gain, *qk, *vo)


def total_over_all(plan, a):
    n, f = plan.tp, plan.fsdp
    hop = 1
    while hop < n:
        a = a + lax.ppermute(a, "tp", [(t, t ^ hop) for t in range(n)])
        hop *= 2
    hop = 1
    while hop < f:
        a = a + lax.ppermute(a, "fsdp", [(t, t ^ hop) for t in range(f)])
        hop *= 2
    return a


def add_low(own, got):
    return (own.astype(F32) + got.astype(F32)).astype(BF16)


def scatter_rows(mine):
    return lax.psum_scatter(mine, "fsdp", scatter_dimension=0, tiled=True).astype(F32)


def after(*arrays):
    return lax.optimization_barrier(arrays)


def fast_body(plan, inputs, cotangent, w_qkv, w_out, w_up, w_down, norm_gain, query_scale, prefix_len):
    seqs, positions, d = inputs.shape
    layers, w = w_qkv.shape[0], w_qkv.shape[3]
    dh = query_scale.shape[1]
    unit = SOFT_ONE / math.sqrt(dh)
    factors = jax.nn.softplus(query_scale) * unit
    prefix = lax.dynamic_slice_in_dim(prefix_len, plan.seq, 1)
    order = plan.blocks(positions * plan.tp)
    out_shard, down_shard = jnp.swapaxes(w_out, 1, 2), jnp.swapaxes(w_down, 1, 2)
    pairs = jnp.concatenate(
        [
            jnp.concatenate([w_qkv[:, 0], w_qkv[:, 1]], axis=2)[:, None],
            jnp.concatenate([w_qkv[:, 2], out_shard], axis=2)[:, None],
            jnp.concatenate([w_up, down_shard], axis=2)[:, None],
        ],
        axis=1,
    )

    block = plan.pick(inputs, 1 - plan.seq).astype(BF16)
    got, other = gather_call(pairs[0, :2], block, pieces_of(2, pairs.shape[2]), plan.fsdp, plan.ring)
    qk0, vo0 = got[0:2], got[2:4]

    def along(l, m):
        return lax.all_gather(pairs[l, m], "fsdp", axis=0, tiled=True)

    def both(rows):
        return rows, plan.across(rows)

    def four(pair):
        return (*pair, plan.core(pair[0]), plan.core(pair[1]))

    un0_rows, qk1_rows, vo1_rows, un1_rows = along(0, 2), along(1, 0), along(1, 1), along(1, 2)
    x = plan.order(plan.pick(inputs, plan.seq), other.astype(F32))
    h = (x * inverse_rms(x) * norm_gain[0, 0]).astype(BF16)
    h, un0_rows, qk1_rows, cotangent = after(h, un0_rows, qk1_rows, cotangent)
    un0, qk1 = both(un0_rows), both(qk1_rows)
    cot_block = plan.pick(cotangent, 1 - plan.seq).astype(BF16)
    kept, weights = [], []
    for l in range(layers):
        qk, vo = (qk0, vo0) if l == 0 else (qk1, vo1)
        scale = jnp.tile(factors[l] * LOG2E, 2 * w // dh)[:, None]
        h_other = plan.core(h)
        qkv = project(h, qk, vo, scale, 0)
        q, k, v = project(h_other, qk, vo, scale, 1, qkv)
        att, lse = attention_forward(q, k, v, prefix, order, dh)
        if l == 0:
            att, un0_got, qk1_got, vo1_rows = after(att, un0[1], qk1[1], vo1_rows)
            un, qk1 = four((un0[0], un0_got)), (qk1[0], qk1_got)
            vo1 = both(vo1_rows)
        else:
            att, un1_got, cot_got = after(att, un1[1], cot_got)
            un = four((un1[0], un1_got))
        part = plan.core(out_project(att, vo, 1))
        next_gain = norm_gain[(l + 1) % layers, 0][None]
        mid, pre, res, h_next = middle_call(x, att, part, norm_gain[l, 1][None], next_gain, vo, un)
        kept.append((x, h, h_other, q, k, v, att, lse, mid, pre))
        weights.append((qk, vo, un))
        x, h = res, h_next
        if l == 0:
            h, un1_rows, cot_block = after(h, un1_rows, cot_block)
            un1, cot_got = both(un1_rows), plan.across(cot_block)
    g = plan.order(plan.pick(cotangent, plan.seq), cot_got.astype(F32))
    out_blocks = x.reshape(seqs, positions, d)
    out_send = plan.pick(out_blocks, 1 - plan.seq).astype(BF16)
    g, out_send = after(g, out_send)
    out_got = plan.across(out_send)
    outputs = None
    width = -(-3 * w // 128) * 128
    grads = [None] * layers
    for l in reversed(range(layers)):
        qk, vo, un = weights[l]
        x, h, h_other, q, k, v, att, lse, mid, pre = kept[l]
        g_mid, low, gain_m, u0, u1, u2, u3 = mlp_back(g, mid, pre, norm_gain[l, 1][None], un)
        if outputs is None:
            low, out_got = after(low, out_got)
            outputs = plan.order(plan.pick(out_blocks, plan.seq), out_got.astype(F32)).reshape(out_blocks.shape)
        low_other = plan.core(low)
        g_att = grad_att(low, vo, 0)
        g_att = grad_att(low_other, vo, 1, g_att)
        o0, o1 = out_grad_call(low, low_other, att)
        pad = jnp.zeros((d, width - 3 * w), BF16)
        early = []
        for a, c, o in ((u1, plan.core(u3), o1), (u0, plan.core(u2), o0)):
            early.append(jnp.concatenate([(a.astype(F32) + c.astype(F32)).astype(BF16), o, pad], axis=1))
        g_att, *early = after(g_att, *early)
        early_got = plan.across(early[0])
        dgrads, fgs, pieces = [None] * 6, [], [None] * 2
        for s in (1, 0):
            dq, dk, dv, fg = attention_backward(
                q, k, v, att, g_att, lse, factors[l], prefix, order, dh, s * w, w
            )
            pieces[s] = weight_grad(h, h_other, dq, dk, dv, width)
            if s == 1:
                g_att, pieces[1], early_got = after(g_att, pieces[1], early_got)
                late_got = plan.across(pieces[1])
                mine, g_att = after(add_low(early[1], early_got), g_att)
                early = scatter_rows(mine)
            dgrads[3 * s:3 * s + 3] = [dq, dk, dv]
            fgs.append(fg)
        fg = fgs[0] + fgs[1]
        dgrads[0], pieces[0], late_got = after(dgrads[0], pieces[0], late_got)
        mine, dgrads[0] = after(add_low(pieces[0], late_got), dgrads[0])
        late = scatter_rows(mine)
        part = plan.core(input_other(dgrads, qk, vo))
        g, gain_a = input_own(dgrads, part, x, g_mid, norm_gain[l, 0][None], qk, vo)
        if l > 0:
            g, early = after(g, early)
        factor_grad = jnp.sum(fg, axis=1) / (factors[l] * LOG2E)
        small = jnp.concatenate([jnp.sum(gain_a, axis=0), jnp.sum(gain_m, axis=0), factor_grad])
        grads[l] = (early, late, small)
    input_grad = plan.unswap(g)
    small = jnp.stack([entry[2] for entry in grads])
    small = total_over_all(plan, small)
    early, late = jnp.stack([e[0] for e in grads]), jnp.stack([e[1] for e in grads])
    qkv_g = jnp.stack([late[:, :, c * w:(c + 1) * w] for c in range(3)], axis=1)
    up_g, down_g, out_g = (early[:, :, c * w:(c + 1) * w] for c in range(3))
    scale_g = small[:, 2 * d:] * jax.nn.sigmoid(query_scale) * unit
    return (
        outputs, input_grad, qkv_g, jnp.swapaxes(out_g, 1, 2), up_g, jnp.swapaxes(down_g, 1, 2),
        small[:, :d], small[:, d:2 * d], scale_g,
    )


def body(inputs, cotangent, w_qkv, w_out, w_up, w_down, norm_gain, query_scale, prefix_len):
    seqs, positions, d = inputs.shape
    fsdp, tp = lax.axis_size("fsdp"), lax.axis_size("tp")
    layers = w_qkv.shape[0]
    plan = Plan(seqs, tp, fsdp, w_qkv.shape[2])
    if plan.fast:
        return fast_body(
            plan, inputs, cotangent, w_qkv, w_out, w_up, w_down, norm_gain, query_scale, prefix_len
        )
    dh = query_scale.shape[1]
    unit = SOFT_ONE / math.sqrt(dh)
    factors = jax.nn.softplus(query_scale) * unit
    prefix = lax.dynamic_slice_in_dim(prefix_len, plan.seq, 1)
    order = plan.blocks(positions * tp)
    out_shard, down_shard = jnp.swapaxes(w_out, 1, 2), jnp.swapaxes(w_down, 1, 2)

    weights = []
    for l in range(layers):
        qkv = plan.gather_heads(w_qkv[l])
        out_t = plan.gather_heads(out_shard[l][None])[:, 0]
        up, down_t = plan.gather_full(jnp.stack([w_up[l], down_shard[l]]))
        weights.append(([qkv[:, c] for c in range(3)], out_t, up, down_t))

    x = plan.swap(inputs)
    g = plan.swap(cotangent)
    kept = []
    for l in range(layers):
        x, saved = layer_forward(plan, x, prefix, order, *weights[l], norm_gain[l], factors[l])
        kept.append(saved)
    outputs = plan.unswap(x)
    grads = [None] * layers
    for l in reversed(range(layers)):
        g, grads[l] = layer_backward(
            plan, g, kept[l], prefix, order, *weights[l], norm_gain[l], factors[l]
        )
    input_grad = plan.unswap(g)
    qkv_g, out_g, up_g, down_g, gain_a, gain_m, f_g = (jnp.stack(a) for a in zip(*grads))
    scale_g = f_g * jax.nn.sigmoid(query_scale) * unit
    gain_a, gain_m, scale_g = lax.psum((gain_a, gain_m, scale_g), ("fsdp", "tp"))
    return outputs, input_grad, qkv_g, out_g, up_g, down_g, gain_a, gain_m, scale_g


def solution(mesh):
    placed = (
        P("fsdp", "tp", None),
        P("fsdp", "tp", None),
        P(None, None, "fsdp", "tp"),
        P(None, "tp", "fsdp"),
        P(None, "fsdp", "tp"),
        P(None, "tp", "fsdp"),
        P(),
        P(),
        P("fsdp"),
    )
    return jax.shard_map(
        body,
        mesh=mesh,
        in_specs=placed,
        out_specs=placed[:6] + (P(), P(), P()),
        check_vma=False,
    )
```

```python
import functools, math
import jax
import jax.numpy as jnp
from jax import lax
from jax.experimental import pallas as pl
from jax.experimental.pallas import tpu as pltpu
from jax.sharding import PartitionSpec as P

MASKED = -1e30
F32, BF16 = jnp.float32, jnp.bfloat16
EPSILON = 1e-06
SOFT_ONE = 1.442695041
LOG2E = math.log2(math.e)
MESH = pl.DeviceIdType.MESH
HINT = 1
VMEM_LIMIT = 60 * 2**20

def dot(a, b, dims=((1,), (0,))):
    return lax.dot_general(a, b, (dims, ((), ())), preferred_element_type=F32)

def key_range(row_start, rows, prefix, block):
    full = jnp.maximum(row_start + 1, prefix) // block
    stop = (jnp.maximum(row_start + rows, prefix) + block - 1) // block
    return full, stop

def forward_kernel(prefix_ref, order_ref, q_ref, k_ref, v_ref, o_ref, lse_ref, key_rows, value_ext, *, pair, dh, bq, bk):
    length = q_ref.shape[1]
    prefix = prefix_ref[0]
    ext = value_ext.shape[1]
    for h in range(pair):
        key_rows[h] = k_ref[h * dh:(h + 1) * dh, :].T
        value_ext[h, :dh] = v_ref[h * dh:(h + 1) * dh, :]
        value_ext[h, dh:] = jnp.ones((ext - dh, length), BF16)

    def one_query(qi, carry):
        start = qi * bq
        here = pl.ds(pl.multiple_of(order_ref[qi] * bq, bq), bq)
        queries = [q_ref[h * dh:(h + 1) * dh, here] for h in range(pair)]
        full, stop = key_range(start, bq, prefix, bk)

        def step(masked, ki, state):
            first = ki * bk
            there = pl.ds(pl.multiple_of(order_ref[ki] * bk, bk), bk)
            if masked:
                rows = first + lax.broadcasted_iota(jnp.int32, (bk, bq), 0)
                cols = start + lax.broadcasted_iota(jnp.int32, (bk, bq), 1)
                allowed = rows <= jnp.maximum(cols, prefix - 1)
            scores = [dot(key_rows[h, there], queries[h]) for h in range(pair)]
            fresh = []
            for h in range(pair):
                top, total = state[h]
                s = scores[h]
                if masked:
                    s = jnp.where(allowed, s, MASKED)
                new_top = jnp.maximum(top, jnp.max(s, axis=0, keepdims=True))
                p = jnp.exp2(s - new_top).astype(BF16)
                total = total * jnp.exp2(top - new_top) + dot(value_ext[h, :, there], p)
                fresh.append((new_top, total))
            return tuple(fresh)

        state = tuple((jnp.full((1, bq), MASKED, F32), jnp.zeros((ext, bq), F32)) for _ in range(pair))
        state = lax.fori_loop(0, full, functools.partial(step, False), state)
        state = lax.fori_loop(full, stop, functools.partial(step, True), state)
        for h in range(pair):
            top, total = state[h]
            norm = total[dh:dh + 1]
            o_ref[h * dh:(h + 1) * dh, here] = (total[:dh] / norm).astype(BF16)
            lse_ref[h, :, here] = top + jnp.log2(norm)
        return carry

    lax.fori_loop(0, length // bq, one_query, 0)

def attention_forward(q, k, v, prefix, order, dh, pair=4):
    width, length = q.shape
    heads = width // dh
    pair = min(pair, heads)
    bq = bk = length // order.shape[0]
    ext = dh + 16
    spec = pl.BlockSpec((pair * dh, length), lambda i, p, o: (i, 0))
    return pl.pallas_call(
        functools.partial(forward_kernel, pair=pair, dh=dh, bq=bq, bk=bk),
        grid_spec=pltpu.PrefetchScalarGridSpec(
            num_scalar_prefetch=2, grid=(heads // pair,),
            in_specs=[spec, spec, spec],
            out_specs=[spec, pl.BlockSpec((pair, 1, length), lambda i, p, o: (i, 0, 0))],
            scratch_shapes=[pltpu.VMEM((pair, length, dh), BF16), pltpu.VMEM((pair, ext, length), BF16)],
        ),
        out_shape=[jax.ShapeDtypeStruct((width, length), BF16), jax.ShapeDtypeStruct((heads, 1, length), F32)],
        compiler_params=pltpu.CompilerParams(vmem_limit_bytes=VMEM_LIMIT),
        cost_estimate=pl.CostEstimate(flops=int(HINT * 600 * length * length * heads), bytes_accessed=int(HINT * 8 * width * length), transcendentals=0),
        name="attention_forward",
    )(prefix, order, q, k, v)

def split3(x):
    a = x.astype(BF16)
    r = x - a.astype(F32)
    b = r.astype(BF16)
    c = (r - b.astype(F32)).astype(BF16)
    return a, b, c

def backward_kernel(prefix_ref, order_ref, q_ref, k_ref, v_ref, o_ref, g_ref, lse_ref, scale_ref, dq_ref, dk_ref, dv_ref, fg_ref,
                    key_rows, key_ext, value_ext, query_ext, grad_ext, dk_acc, dv_acc, *, pair, dh, bq, bk):
    length = q_ref.shape[1]
    prefix = prefix_ref[0]
    ext = key_ext.shape[1]
    pad = ext - dh
    ones = (lax.broadcasted_iota(jnp.int32, (pad, length), 0) < 3).astype(F32).astype(BF16)
    fg_zero = pl.program_id(0) == 0
    @pl.when(fg_zero)
    def _():
        fg_ref[...] = jnp.zeros_like(fg_ref)
    for h in range(pair):
        rows = slice(h * dh, (h + 1) * dh)
        q, k, v, g = q_ref[rows, :], k_ref[rows, :], v_ref[rows, :], g_ref[rows, :]
        key_rows[h] = k.T
        key_ext[h, :dh] = k
        key_ext[h, dh:] = ones
        value_ext[h, :dh] = v
        value_ext[h, dh:] = ones
        delta = jnp.sum(o_ref[rows, :].astype(F32) * g.astype(F32), axis=0, keepdims=True)
        def stack(base, row):
            parts = split3(-row)
            idx = lax.broadcasted_iota(jnp.int32, (pad, length), 0)
            tail = jnp.where(idx == 0, parts[0].astype(F32), jnp.where(idx == 1, parts[1].astype(F32), jnp.where(idx == 2, parts[2].astype(F32), 0.0)))
            return jnp.concatenate([base, tail.astype(BF16)], axis=0).T
        query_ext[h] = stack(q, lse_ref[h])
        grad_ext[h] = stack(g, delta)
        dk_acc[h] = jnp.zeros((dh, length), F32)
        dv_acc[h] = jnp.zeros((dh, length), F32)

    def one_query(qi, carry):
        start = qi * bq
        here = pl.ds(pl.multiple_of(order_ref[qi] * bq, bq), bq)
        full, stop = key_range(start, bq, prefix, bk)

        def step(masked, ki, state):
            first = ki * bk
            there = pl.ds(pl.multiple_of(order_ref[ki] * bk, bk), bk)
            if masked:
                rows = start + lax.broadcasted_iota(jnp.int32, (bq, bk), 0)
                cols = first + lax.broadcasted_iota(jnp.int32, (bq, bk), 1)
                allowed = cols <= jnp.maximum(rows, prefix - 1)
            fresh = []
            s = [dot(query_ext[h, here], key_ext[h, :, there]) for h in range(pair)]
            gp = [dot(grad_ext[h, here], value_ext[h, :, there]) for h in range(pair)]
            for h in range(pair):
                x = jnp.where(allowed, s[h], MASKED) if masked else s[h]
                p = jnp.exp2(x)
                ds = (p * gp[h]).astype(BF16)
                rows = slice(h * dh, (h + 1) * dh)
                dv_acc[h, :, there] += dot(g_ref[rows, here], p.astype(BF16))
                dk_acc[h, :, there] += dot(q_ref[rows, here], ds)
                fresh.append(state[h] + dot(ds, key_rows[h, there]))
            return tuple(fresh)

        state = tuple(jnp.zeros((bq, dh), F32) for _ in range(pair))
        state = lax.fori_loop(0, full, functools.partial(step, False), state)
        state = lax.fori_loop(full, stop, functools.partial(step, True), state)
        for h in range(pair):
            rows = slice(h * dh, (h + 1) * dh)
            dq = state[h].T
            prod = dq * q_ref[rows, here].astype(F32)
            part = prod[:, :128]
            for c in range(1, bq // 128):
                part = part + prod[:, c * 128:(c + 1) * 128]
            fg_ref[...] += part
            dq_ref[rows, here] = (dq * scale_ref[...]).astype(BF16)
        return carry

    lax.fori_loop(0, length // bq, one_query, 0)
    for h in range(pair):
        rows = slice(h * dh, (h + 1) * dh)
        dk_ref[rows, :] = (dk_acc[h] * math.log(2.0)).astype(BF16)
        dv_ref[rows, :] = dv_acc[h].astype(BF16)

def attention_backward(q, k, v, o, g, lse, factor, prefix, order, dh, base=0, width=None, pair=2):
    full, length = q.shape
    width = width or full
    heads = width // dh
    pair = min(pair, heads)
    bq = bk = length // order.shape[0]
    ext = dh + 16
    spec = pl.BlockSpec((pair * dh, length), lambda i, p, o: (i, 0))
    skip = base // (pair * dh)
    source = pl.BlockSpec((pair * dh, length), lambda i, p, o: (i + skip, 0))
    wide = jax.ShapeDtypeStruct((width, length), BF16)
    return pl.pallas_call(
        functools.partial(backward_kernel, pair=pair, dh=dh, bq=bq, bk=bk),
        grid_spec=pltpu.PrefetchScalarGridSpec(
            num_scalar_prefetch=2, grid=(heads // pair,),
            in_specs=[source] * 5 + [pl.BlockSpec((pair, 1, length), lambda i, p, o: (i + skip, 0, 0)), pl.BlockSpec((dh, 1), lambda i, p, o: (0, 0))],
            out_specs=[spec] * 3 + [pl.BlockSpec((dh, 128), lambda i, p, o: (0, 0))],
            scratch_shapes=[
                pltpu.VMEM((pair, length, dh), BF16),
                pltpu.VMEM((pair, ext, length), BF16),
                pltpu.VMEM((pair, ext, length), BF16),
                pltpu.VMEM((pair, length, ext), BF16),
                pltpu.VMEM((pair, length, ext), BF16),
                pltpu.VMEM((pair, dh, length), F32),
                pltpu.VMEM((pair, dh, length), F32)],
        ),
        out_shape=[wide] * 3 + [jax.ShapeDtypeStruct((dh, 128), F32)],
        compiler_params=pltpu.CompilerParams(vmem_limit_bytes=VMEM_LIMIT),
        cost_estimate=pl.CostEstimate(flops=int(HINT * 1600 * length * length * heads), bytes_accessed=int(HINT * 16 * width * length), transcendentals=0),
        name="attention_backward",
    )(prefix, order, q, k, v, o, g, lse, factor.reshape(dh, 1))


def rms(x):
    inv = lax.rsqrt(jnp.mean(x * x, axis=-1, keepdims=True) + EPSILON)
    return x * inv, inv


def rms_back(normed, inv, gain, grad):
    scaled = grad * gain
    out = inv * (scaled - normed * jnp.mean(scaled * normed, axis=-1, keepdims=True))
    return out, jnp.sum(grad * normed, axis=0)


def ein(spec, *args):
    return jnp.einsum(spec, *args, preferred_element_type=F32)


def gather_kernel(pieces, pairs, outer, ring, shard_ref, block_ref, *refs):
    outs = [refs[2 * m:2 * m + 2] for m in range(pairs)]
    got_ref = refs[2 * pairs]
    send, recv, local = refs[2 * pairs + 1:]
    f, t = lax.axis_index("fsdp"), lax.axis_index("tp")
    zz, yy = f // 2, f % 2
    across = {"tp": lax.rem(t + ring, 2 * ring)}
    beside = {"fsdp": zz * 2 + 1 - yy}
    along = [{"fsdp": lax.rem(zz + k, outer) * 2 + yy} for k in range(1, outer)]
    peers = along + [across, beside]
    barrier = pltpu.get_barrier_semaphore()
    for peer in peers:
        pl.semaphore_signal(barrier, inc=1, device_id=peer, device_id_type=MESH)
    pl.semaphore_wait(barrier, len(peers))
    used = [0]

    def copy(src, dst, peer):
        slot = used[0]
        used[0] += 1
        return pltpu.make_async_remote_copy(
            src_ref=src, dst_ref=dst, send_sem=send.at[slot], recv_sem=recv.at[slot],
            device_id=peer, device_id_type=MESH,
        )

    count = len(pieces)
    chunks = 4
    step = block_ref.shape[0] // chunks
    blocks = [
        copy(block_ref.at[pl.ds(i * step, step)], got_ref.at[pl.ds(i * step, step)], across)
        for i in range(chunks)
    ]
    own, first, second, third = [], [], [], []
    for i, (m, low, rows, route) in enumerate(pieces):
        part = pl.ds(low, rows)
        w = [out.at[:, :, part] for out in outs[m]]
        src = shard_ref.at[m, part]
        own.append(pltpu.make_async_copy(src, w[0].at[zz, yy], local.at[i]))
        first.append([copy(src, w[0].at[zz, yy], peer) for peer in along])
        if route:
            second.append([copy(w[0].at[:, yy], w[0].at[:, yy], beside)])
            third.append([copy(w[0], w[1], across)])
        else:
            second.append([copy(w[0].at[:, yy], w[1].at[:, yy], across)])
            third.append([copy(w[s].at[:, yy], w[s].at[:, yy], beside) for s in range(2)])

    def begin(i):
        own[i].start()
        for c in first[i]:
            c.start()

    ahead = 3
    for i in range(min(ahead, count)):
        begin(i)
    started = 0
    for b in blocks[:2]:
        b.start()
    started = 2
    for i in range(count + 2):
        if i < count:
            own[i].wait()
            for c in first[i]:
                c.wait_recv()
            for c in second[i]:
                c.start()
            if i + ahead < count:
                begin(i + ahead)
            if started < chunks:
                blocks[started].start()
                started += 1
        if 0 <= i - 1 < count:
            for c in second[i - 1]:
                c.wait_recv()
            for c in third[i - 1]:
                c.start()
        if 0 <= i - 2 < count:
            for c in third[i - 2]:
                c.wait_recv()
    for b in blocks[started:]:
        b.start()
    for i in range(count):
        for c in first[i] + second[i] + third[i]:
            c.wait_send()
    for b in blocks:
        b.wait()


def pieces_of(pairs, rows):
    half = rows // 32 * 16
    return tuple(
        (m, low, size, m_part) for m in range(pairs) for m_part, (low, size) in enumerate(((0, half), (half, rows - half)))
    )


def gather_call(shards, block, pieces, fsdp, ring):
    pairs, rows, w = shards.shape
    outer = fsdp // 2
    slots = 4 + len(pieces) * (outer + 2)
    any_spec = pl.BlockSpec(memory_space=pl.ANY)
    got = pl.pallas_call(
        functools.partial(gather_kernel, pieces, pairs, outer, ring),
        out_shape=[jax.ShapeDtypeStruct((outer, 2, rows, w), BF16)] * (2 * pairs)
        + [jax.ShapeDtypeStruct(block.shape, block.dtype)],
        in_specs=[any_spec] * 2,
        out_specs=[any_spec] * (2 * pairs + 1),
        scratch_shapes=[
            pltpu.SemaphoreType.DMA((slots,)),
            pltpu.SemaphoreType.DMA((slots,)),
            pltpu.SemaphoreType.DMA((len(pieces),)),
        ],
        compiler_params=pltpu.CompilerParams(collective_id=0, has_side_effects=True),
        name="gather_weights",
    )(shards, block)
    return [a.reshape(outer * 2 * rows, w) for a in got[:-1]], got[-1]


class Plan:
    def __init__(self, seqs, tp, fsdp, rows):
        self.seqs, self.tp, self.ring, self.fsdp = seqs, tp, tp // seqs, fsdp
        self.same_member = [[s * self.ring + r for s in range(seqs)] for r in range(self.ring)]
        self.same_seq = [[s * self.ring + r for r in range(self.ring)] for s in range(seqs)]
        self.fast = seqs == 2 and self.ring == 2 and fsdp % 2 == 0 and rows % 32 == 0
        t = lax.axis_index("tp")
        self.seq, self.member = t // self.ring, lax.rem(t, self.ring)

    def across(self, a):
        n = self.tp
        return lax.ppermute(a, "tp", [(t, (t + self.ring) % n) for t in range(n)])

    def core(self, a):
        return lax.ppermute(a, "tp", [(t, t ^ 1) for t in range(self.tp)])

    def pick(self, blocks, index):
        return lax.dynamic_index_in_dim(blocks, index, 0, keepdims=False)

    def order(self, own, other):
        first = self.seq == 0
        return jnp.concatenate([jnp.where(first, own, other), jnp.where(first, other, own)])

    def swap(self, blocks):
        if self.seqs == 2:
            other = self.across(self.pick(blocks, 1 - self.seq).astype(BF16))
            return self.order(self.pick(blocks, self.seq), other.astype(F32))
        got = lax.all_to_all(
            blocks.astype(BF16), "tp", 0, 0, tiled=True, axis_index_groups=self.same_member
        )
        return got.reshape(-1, got.shape[-1]).astype(F32)

    def unswap(self, rows):
        blocks = rows.reshape(self.seqs, -1, rows.shape[-1])
        return self.swap(blocks).reshape(blocks.shape)

    def whole(self, rows):
        if self.fast:
            return jnp.concatenate([rows, self.core(rows)])
        cut = rows.reshape(self.seqs, -1, rows.shape[-1])
        got = lax.all_gather(cut, "tp", axis=1, axis_index_groups=self.same_seq)
        return got.reshape(-1, rows.shape[-1])

    def share(self, full):
        if self.fast:
            own = full.shape[0] // 2
            return full[:own].astype(F32) + self.core(full[own:].astype(BF16)).astype(F32)
        cut = full.astype(BF16).reshape(self.seqs, self.ring, -1, full.shape[-1])
        got = lax.psum_scatter(cut, "tp", scatter_dimension=1, axis_index_groups=self.same_seq)
        return got.reshape(-1, full.shape[-1]).astype(F32)

    def blocks(self, length):
        if self.fast:
            j = jnp.arange(self.tp, dtype=jnp.int32)
            apart = (j % self.ring != self.member).astype(jnp.int32)
            return apart * self.seqs + j // self.ring
        return jnp.arange(max(1, length // 512), dtype=jnp.int32)

    def gather_heads(self, shards):
        rows = lax.all_gather(shards, "fsdp", axis=1, tiled=True)
        if self.fast:
            return jnp.stack([rows, self.across(rows)])
        return lax.all_gather(rows, "tp", axis_index_groups=self.same_member)

    def join(self, every):
        r, s, m, d, w = every.shape
        return every.transpose(2, 3, 0, 1, 4).reshape(m, d, r * s * w)

    def gather_full(self, shards):
        part = self.gather_heads(shards)
        if self.fast:
            return self.join(jnp.stack([part, self.core(part)]))
        return self.join(lax.all_gather(part, "tp", axis_index_groups=self.same_seq))

    def scatter_heads(self, grads):
        if self.fast:
            other = self.across(grads[1].astype(BF16))
            mine = (grads[0].astype(F32) + other.astype(F32)).astype(BF16)
        else:
            mine = lax.psum_scatter(
                grads.astype(BF16), "tp", scatter_dimension=0, axis_index_groups=self.same_member
            )
        return lax.psum_scatter(mine, "fsdp", scatter_dimension=1, tiled=True).astype(F32)

    def scatter_full(self, grads):
        m, d, cols = grads.shape
        if self.fast:
            half = cols // 2
            other = self.core(grads[:, :, half:].astype(BF16))
            mine = grads[:, :, :half].astype(F32) + other.astype(F32)
            mine = mine.astype(BF16).reshape(m, d, self.seqs, -1).transpose(2, 0, 1, 3)
        else:
            cut = grads.astype(BF16).reshape(m, d, self.ring, self.seqs, -1).transpose(2, 3, 0, 1, 4)
            mine = lax.psum_scatter(cut, "tp", scatter_dimension=0, axis_index_groups=self.same_seq)
        return self.scatter_heads(mine)


def layer_forward(plan, x, prefix, order, qkv, out_t, up, down_t, gains, factor):
    dh = factor.shape[0]
    normed, inv = rms(x)
    h = plan.whole((normed * gains[0]).astype(BF16))
    seqs, d, w = out_t.shape
    raw = [ein("sdc,td->sct", qkv[c], h).reshape(seqs * w, -1) for c in range(3)]
    scale = jnp.tile(factor * LOG2E, seqs * w // dh)[:, None]
    q, k, v = (raw[0] * scale).astype(BF16), raw[1].astype(BF16), raw[2].astype(BF16)
    att, lse = attention_forward(q, k, v, prefix, order, dh)
    middle = x + plan.share(ein("sct,sdc->td", att.reshape(seqs, w, -1), out_t))
    normed_m, inv_m = rms(middle)
    h_m = (normed_m * gains[1]).astype(BF16)
    pre = ein("td,df->tf", h_m, up)
    hidden = jax.nn.silu(pre).astype(BF16)
    result = middle + ein("tf,df->td", hidden, down_t)
    return result, (x, inv, h, q, k, v, att, lse, middle, inv_m, h_m, pre, hidden)


def layer_backward(plan, g, saved, prefix, order, qkv, out_t, up, down_t, gains, factor):
    x, inv, h, q, k, v, att, lse, middle, inv_m, h_m, pre, hidden = saved
    dh = factor.shape[0]
    seqs, d, w = out_t.shape
    length = h.shape[0]
    g_low = g.astype(BF16)
    down_grad = ein("td,tf->df", g_low, hidden)
    g_hidden = ein("td,df->tf", g_low, down_t)
    sig = jax.nn.sigmoid(pre)
    g_pre = (g_hidden * sig * (1.0 + pre * (1.0 - sig))).astype(BF16)
    up_grad = ein("td,tf->df", h_m, g_pre)
    mlp_grads = plan.scatter_full(jnp.stack([up_grad, down_grad]))
    g_hm = ein("tf,df->td", g_pre, up)
    back_m, gain_m = rms_back(middle * inv_m, inv_m, gains[1], g_hm)
    g_mid = g + back_m
    g_all = plan.whole(g_mid.astype(BF16))
    att3 = att.reshape(seqs, w, length)
    out_grad = plan.scatter_heads(ein("td,sct->sdc", g_all, att3)[:, None])[0]
    g_att = ein("td,sdc->sct", g_all, out_t).astype(BF16).reshape(seqs * w, length)
    dq, dk, dv, fg = attention_backward(q, k, v, att, g_att, lse, factor, prefix, order, dh)
    factor_grad = jnp.sum(fg, axis=1) / (factor * LOG2E)
    parts = [a.reshape(seqs, w, length) for a in (dq, dk, dv)]
    qkv_grad = plan.scatter_heads(jnp.stack([ein("td,sct->sdc", h, a) for a in parts], axis=1))
    g_ha = plan.share(sum(ein("sct,sdc->td", a, b) for a, b in zip(parts, qkv)))
    back_a, gain_a = rms_back(x * inv, inv, gains[0], g_ha)
    return g_mid + back_a, (qkv_grad, out_grad.T, mlp_grads[0], mlp_grads[1].T, gain_a, gain_m, factor_grad)


TN, NT, TT = ((0,), (0,)), ((1,), (1,)), ((0,), (1,))
ONE = pl.Buffered(1)


def cost(flops, nbytes):
    return pl.CostEstimate(flops=int(flops * HINT), bytes_accessed=int(nbytes * HINT), transcendentals=0)


def params(mib=60):
    return pltpu.CompilerParams(vmem_limit_bytes=mib * 2**20)


def fixed(shape):
    return pl.BlockSpec(shape, lambda *a: (0,) * len(shape), pipeline_mode=ONE)


def shape_of(shape, dtype=BF16):
    return jax.ShapeDtypeStruct(shape, dtype)


def inverse_rms(x):
    return lax.rsqrt(jnp.mean(x * x, axis=-1, keepdims=True) + EPSILON)


def eight(x):
    return jnp.sum(x.reshape(-1, 8, x.shape[-1]), axis=0)


def join_lanes(dst, refs, low, high):
    width = high - low
    for i, ref in enumerate(refs):
        dst[:, i * width:(i + 1) * width] = ref[:, low:high]


def project_kernel(w, h_ref, qk0, qk1, vo0, vo1, scale_ref, *refs):
    q_ref, k_ref, v_ref = refs[-3:]
    h = h_ref[...]
    for s, (qk, vo) in enumerate(((qk0, vo0), (qk1, vo1))):
        rows = slice(s * w, (s + 1) * w)
        both = dot(qk[...], h, TT)
        q_ref[rows] = (both[:w] * scale_ref[rows]).astype(BF16)
        k_ref[rows] = both[w:].astype(BF16)
        v_ref[rows] = dot(vo[:, :w], h, TT).astype(BF16)


def project(h, qk, vo, scale, base, bufs=None):
    rows, d = h.shape
    w = qk[0].shape[1] // 2
    bt = 512
    steps = rows // bt
    out = pl.BlockSpec((2 * w, bt), lambda i: (0, i + base * steps))
    whole = fixed((d, 2 * w))
    extra = [] if bufs is None else list(bufs)
    return pl.pallas_call(
        functools.partial(project_kernel, w),
        grid=(steps,),
        in_specs=[pl.BlockSpec((bt, d), lambda i: (i, 0))] + [whole] * 4 + [fixed((2 * w, 1))]
        + [pl.BlockSpec(memory_space=pl.ANY)] * len(extra),
        out_specs=[out] * 3,
        out_shape=[shape_of((2 * w, 2 * rows))] * 3,
        input_output_aliases={6 + i: i for i in range(len(extra))},
        compiler_params=params(),
        cost_estimate=cost(2 * rows * d * 6 * w, 4 * rows * d),
        name="project",
    )(h, *qk, *vo, scale, *extra)


def out_kernel(w, att_ref, vo0, vo1, part_ref, mat):
    @pl.when(pl.program_id(0) == 0)
    def _():
        join_lanes(mat, (vo0, vo1), w, 2 * w)

    part_ref[...] = dot(att_ref[...], mat[...], TT).astype(BF16)


def out_project(att, vo, base):
    d, w2 = vo[0].shape
    rows = att.shape[1] // 2
    bt = 512
    steps = rows // bt
    return pl.pallas_call(
        functools.partial(out_kernel, w2 // 2),
        grid=(steps,),
        in_specs=[pl.BlockSpec((w2, bt), lambda i: (0, i + base * steps)), fixed((d, w2)), fixed((d, w2))],
        out_specs=pl.BlockSpec((bt, d), lambda i: (i, 0)),
        out_shape=shape_of((rows, d)),
        scratch_shapes=[pltpu.VMEM((d, w2), BF16)],
        compiler_params=params(),
        cost_estimate=cost(2 * rows * d * w2, 4 * rows * d),
        name="out_project",
    )(att, *vo)


def middle_kernel(w, x_ref, att_ref, got_ref, gm_ref, ga_ref, vo0, vo1, un0, un1, un2, un3,
                  mid_ref, pre_ref, res_ref, h_ref, out_mat, up_mat, down_mat):
    @pl.when(pl.program_id(0) == 0)
    def _():
        join_lanes(out_mat, (vo0, vo1), w, 2 * w)
        join_lanes(up_mat, (un0, un1, un2, un3), 0, w)
        join_lanes(down_mat, (un0, un1, un2, un3), w, 2 * w)

    mid = x_ref[...] + got_ref[...].astype(F32) + dot(att_ref[...], out_mat[...], TT)
    mid_ref[...] = mid
    h_m = (mid * inverse_rms(mid) * gm_ref[...]).astype(BF16)
    pre = dot(h_m, up_mat[...])
    pre_ref[...] = pre
    hidden = (pre / (1.0 + jnp.exp(-pre))).astype(BF16)
    res = mid + dot(hidden, down_mat[...], NT)
    res_ref[...] = res
    h_ref[...] = (res * inverse_rms(res) * ga_ref[...]).astype(BF16)


def middle_call(x, att, got, gain_m, gain_a, vo, un):
    rows, d = x.shape
    w2 = vo[0].shape[1]
    ff = 2 * w2
    bt = 256
    row = pl.BlockSpec((bt, d), lambda i: (i, 0))
    wide = pl.BlockSpec((bt, ff), lambda i: (i, 0))
    return pl.pallas_call(
        functools.partial(middle_kernel, w2 // 2),
        grid=(rows // bt,),
        in_specs=[row, pl.BlockSpec((w2, bt), lambda i: (0, i)), row] + [fixed((1, d))] * 2 + [fixed((d, w2))] * 6,
        out_specs=[row, wide, row, row],
        out_shape=[shape_of((rows, d), F32), shape_of((rows, ff), F32), shape_of((rows, d), F32), shape_of((rows, d))],
        scratch_shapes=[pltpu.VMEM((d, w2), BF16), pltpu.VMEM((d, ff), BF16), pltpu.VMEM((d, ff), BF16)],
        compiler_params=params(),
        cost_estimate=cost(2 * rows * d * (w2 + 2 * ff), 30 * rows * d),
        name="middle",
    )(x, att, got, gain_m, gain_a, *vo, *un)


def mlp_back_kernel(w, g_ref, mid_ref, pre_ref, gm_ref, un0, un1, un2, un3,
                    g_mid_ref, low_ref, gain_ref, o0, o1, o2, o3,
                    up_mat, down_mat, g_all, hid_all, hm_all, gpre_all):
    i = pl.program_id(0)
    bt = g_ref.shape[0]

    @pl.when(i == 0)
    def _():
        join_lanes(up_mat, (un0, un1, un2, un3), 0, w)
        join_lanes(down_mat, (un0, un1, un2, un3), w, 2 * w)
        gain_ref[...] = jnp.zeros_like(gain_ref)

    here = pl.ds(pl.multiple_of(i * bt, bt), bt)
    g = g_ref[...]
    g_low = g.astype(BF16)
    g_all[here] = g_low
    pre = pre_ref[...]
    sig = 1.0 / (1.0 + jnp.exp(-pre))
    hid_all[here] = (pre * sig).astype(BF16)
    g_hidden = dot(g_low, down_mat[...])
    g_pre = (g_hidden * sig * (1.0 + pre * (1.0 - sig))).astype(BF16)
    gpre_all[here] = g_pre
    mid = mid_ref[...]
    inv = inverse_rms(mid)
    normed = mid * inv
    gain = gm_ref[...]
    hm_all[here] = (normed * gain).astype(BF16)
    g_hm = dot(g_pre, up_mat[...], NT)
    gain_ref[...] += eight(g_hm * normed)
    scaled = g_hm * gain
    g_mid = g + inv * (scaled - normed * jnp.mean(scaled * normed, axis=-1, keepdims=True))
    g_mid_ref[...] = g_mid
    low_ref[...] = g_mid.astype(BF16)

    @pl.when(i == pl.num_programs(0) - 1)
    def _():
        d = up_mat.shape[0]
        step = 256

        def chunk(c, carry):
            cols = pl.ds(pl.multiple_of(c * step, step), step)
            up = dot(hm_all[:, cols], gpre_all[...], TN).astype(BF16)
            down = dot(g_all[:, cols], hid_all[...], TN).astype(BF16)
            for b, out in enumerate((o0, o1, o2, o3)):
                out[cols, 0:w] = up[:, b * w:(b + 1) * w]
                out[cols, w:2 * w] = down[:, b * w:(b + 1) * w]
            return carry

        lax.fori_loop(0, d // step, chunk, 0)


def mlp_back(g, mid, pre, gain, un):
    rows, d = g.shape
    ff = pre.shape[1]
    w2 = un[0].shape[1]
    bt = 256
    row = pl.BlockSpec((bt, d), lambda i: (i, 0))
    wide = pl.BlockSpec((bt, ff), lambda i: (i, 0))
    return pl.pallas_call(
        functools.partial(mlp_back_kernel, w2 // 2),
        grid=(rows // bt,),
        in_specs=[row, row, wide, fixed((1, d))] + [fixed((d, w2))] * 4,
        out_specs=[row, row, fixed((8, d))] + [fixed((d, w2))] * 4,
        out_shape=[shape_of((rows, d), F32), shape_of((rows, d)), shape_of((8, d), F32)] + [shape_of((d, w2))] * 4,
        scratch_shapes=[pltpu.VMEM((d, ff), BF16)] * 2
        + [pltpu.VMEM((rows, d), BF16), pltpu.VMEM((rows, ff), BF16), pltpu.VMEM((rows, d), BF16), pltpu.VMEM((rows, ff), BF16)],
        compiler_params=params(),
        cost_estimate=cost(8 * rows * d * ff, 30 * rows * d),
        name="mlp_back",
    )(g, mid, pre, gain, *un)


def grad_att_kernel(w, g_ref, vo0, vo1, *refs):
    out_ref, mat = refs[-2:]

    @pl.when(pl.program_id(0) == 0)
    def _():
        join_lanes(mat, (vo0, vo1), w, 2 * w)

    out_ref[...] = dot(mat[...], g_ref[...], TT).astype(BF16)


def grad_att(g, vo, base, buf=None):
    rows, d = g.shape
    w2 = vo[0].shape[1]
    bt = 512
    steps = rows // bt
    extra = [] if buf is None else [buf]
    return pl.pallas_call(
        functools.partial(grad_att_kernel, w2 // 2),
        grid=(steps,),
        in_specs=[pl.BlockSpec((bt, d), lambda i: (i, 0)), fixed((d, w2)), fixed((d, w2))]
        + [pl.BlockSpec(memory_space=pl.ANY)] * len(extra),
        out_specs=pl.BlockSpec((w2, bt), lambda i: (0, i + base * steps)),
        out_shape=shape_of((w2, 2 * rows)),
        scratch_shapes=[pltpu.VMEM((d, w2), BF16)],
        input_output_aliases={3: 0} if extra else {},
        compiler_params=params(),
        cost_estimate=cost(2 * rows * d * w2, 4 * rows * d),
        name="grad_att",
    )(g, *vo, *extra)


def out_grad_kernel(w, own_ref, other_ref, att_ref, u0, u1, got0, got1, o0, o1):
    half = own_ref.shape[0]
    att = att_ref[...]
    grad = dot(own_ref[...], att[:, :half], TT) + dot(other_ref[...], att[:, half:], TT)
    grad = grad.astype(BF16)
    for s, (u, got, out) in enumerate(((u0, got0, o0), (u1, got1, o1))):
        out[:, :2 * w] = (u[...].astype(F32) + got[...].astype(F32)).astype(BF16)
        out[:, 2 * w:3 * w] = grad[:, s * w:(s + 1) * w]
        out[:, 3 * w:] = jnp.zeros((out.shape[0], out.shape[1] - 3 * w), BF16)


def out_grad_call(own, other, att, mlp, got, width):
    rows, d = own.shape
    w2 = att.shape[0]
    bd = 256
    col = pl.BlockSpec((rows, bd), lambda i: (0, i))
    flat = pl.BlockSpec((bd, w2), lambda i: (i, 0))
    out = pl.BlockSpec((bd, width), lambda i: (i, 0))
    return pl.pallas_call(
        functools.partial(out_grad_kernel, w2 // 2),
        grid=(d // bd,),
        in_specs=[col, col, fixed(att.shape)] + [flat] * 4,
        out_specs=[out] * 2,
        out_shape=[shape_of((d, width))] * 2,
        compiler_params=params(),
        cost_estimate=cost(4 * rows * d * w2, 8 * rows * d),
        name="out_grad",
    )(own, other, att, *mlp, *got)


def weight_grad_kernel(w, own_ref, other_ref, dq_ref, dk_ref, dv_ref, *refs):
    out, stacked = refs[-2:]
    half = own_ref.shape[0]

    @pl.when(pl.program_id(0) == 0)
    def _():
        for j, ref in enumerate((dq_ref, dk_ref, dv_ref)):
            stacked[j * w:(j + 1) * w, :] = ref[...]

    grad = dot(own_ref[...], stacked[:, :half], TT) + dot(other_ref[...], stacked[:, half:], TT)
    if len(refs) == 3:
        grad = grad + refs[0][:, :3 * w].astype(F32)
    out[:, :3 * w] = grad.astype(BF16)
    out[:, 3 * w:] = jnp.zeros((out.shape[0], out.shape[1] - 3 * w), BF16)


def weight_grad(own, other, dq, dk, dv, width, got=None):
    rows, d = own.shape
    w = dq.shape[0]
    bd = 256
    col = pl.BlockSpec((rows, bd), lambda i: (0, i))
    flat = pl.BlockSpec((bd, width), lambda i: (i, 0))
    extra = [] if got is None else [got]
    return pl.pallas_call(
        functools.partial(weight_grad_kernel, w),
        grid=(d // bd,),
        in_specs=[col, col] + [fixed(dq.shape)] * 3 + [flat] * len(extra),
        out_specs=flat,
        out_shape=shape_of((d, width)),
        scratch_shapes=[pltpu.VMEM((3 * w, 2 * rows), BF16)],
        compiler_params=params(),
        cost_estimate=cost(12 * rows * d * w, 12 * rows * d),
        name="weight_grad",
    )(own, other, dq, dk, dv, *extra)


def input_sum(w, grads, qk, vo):
    total = None
    for s in range(2):
        dq, dk, dv = grads[3 * s:3 * s + 3]
        both = jnp.concatenate([dq[...], dk[...]], axis=0)
        part = dot(both, qk[s][...], TT) + dot(dv[...], vo[s][:, :w], TT)
        total = part if total is None else total + part
    return total


def input_other_kernel(w, *refs):
    refs, out_ref = refs[:-1], refs[-1]
    out_ref[...] = input_sum(w, refs[:6], refs[6:8], refs[8:10]).astype(BF16)


def input_other(grads, qk, vo):
    w, length = grads[0].shape
    d, w2 = qk[0].shape
    bt = 512
    steps = length // 2 // bt
    col = pl.BlockSpec((w, bt), lambda i: (0, i + steps))
    return pl.pallas_call(
        functools.partial(input_other_kernel, w),
        grid=(steps,),
        in_specs=[col] * 6 + [fixed((d, w2))] * 4,
        out_specs=pl.BlockSpec((bt, d), lambda i: (i, 0)),
        out_shape=shape_of((length // 2, d)),
        compiler_params=params(),
        cost_estimate=cost(3 * length * d * w2, 4 * length * d),
        name="input_other",
    )(*grads, *qk, *vo)


def input_own_kernel(w, *refs):
    grads, refs = refs[:6], refs[6:]
    got_ref, x_ref, g_ref, gain_ref, qk0, qk1, vo0, vo1, out_ref, sum_ref = refs

    @pl.when(pl.program_id(0) == 0)
    def _():
        sum_ref[...] = jnp.zeros_like(sum_ref)

    g_ha = input_sum(w, grads, (qk0, qk1), (vo0, vo1)) + got_ref[...].astype(F32)
    x = x_ref[...]
    inv = inverse_rms(x)
    normed = x * inv
    sum_ref[...] += eight(g_ha * normed)
    scaled = g_ha * gain_ref[...]
    out_ref[...] = g_ref[...] + inv * (scaled - normed * jnp.mean(scaled * normed, axis=-1, keepdims=True))


def input_own(grads, got, x, g, gain, qk, vo):
    w = grads[0].shape[0]
    rows, d = x.shape
    w2 = 2 * w
    bt = 256
    col = pl.BlockSpec((w, bt), lambda i: (0, i))
    row = pl.BlockSpec((bt, d), lambda i: (i, 0))
    return pl.pallas_call(
        functools.partial(input_own_kernel, w),
        grid=(rows // bt,),
        in_specs=[col] * 6 + [row] * 3 + [fixed((1, d))] + [fixed((d, w2))] * 4,
        out_specs=[row, fixed((8, d))],
        out_shape=[shape_of((rows, d), F32), shape_of((8, d), F32)],
        compiler_params=params(),
        cost_estimate=cost(6 * rows * d * w2, 24 * rows * d),
        name="input_own",
    )(*grads, got, x, g, gain, *qk, *vo)


def total_over_all(plan, a):
    n, f = plan.tp, plan.fsdp
    hop = 1
    while hop < n:
        a = a + lax.ppermute(a, "tp", [(t, t ^ hop) for t in range(n)])
        hop *= 2
    hop = 1
    while hop < f:
        a = a + lax.ppermute(a, "fsdp", [(t, t ^ hop) for t in range(f)])
        hop *= 2
    return a


def add_low(own, got):
    return (own.astype(F32) + got.astype(F32)).astype(BF16)


def scatter_rows(mine):
    return lax.psum_scatter(mine, "fsdp", scatter_dimension=0, tiled=True).astype(F32)


def after(*arrays):
    return lax.optimization_barrier(arrays)


def fast_body(plan, inputs, cotangent, w_qkv, w_out, w_up, w_down, norm_gain, query_scale, prefix_len):
    seqs, positions, d = inputs.shape
    layers, w = w_qkv.shape[0], w_qkv.shape[3]
    dh = query_scale.shape[1]
    unit = SOFT_ONE / math.sqrt(dh)
    factors = jax.nn.softplus(query_scale) * unit
    prefix = lax.dynamic_slice_in_dim(prefix_len, plan.seq, 1)
    order = plan.blocks(positions * plan.tp)
    out_shard, down_shard = jnp.swapaxes(w_out, 1, 2), jnp.swapaxes(w_down, 1, 2)
    pairs = jnp.concatenate(
        [
            jnp.concatenate([w_qkv[:, 0], w_qkv[:, 1]], axis=2)[:, None],
            jnp.concatenate([w_qkv[:, 2], out_shard], axis=2)[:, None],
            jnp.concatenate([w_up, down_shard], axis=2)[:, None],
        ],
        axis=1,
    )

    block = plan.pick(inputs, 1 - plan.seq).astype(BF16)
    got, other = gather_call(pairs[0, :2], block, pieces_of(2, pairs.shape[2]), plan.fsdp, plan.ring)
    qk0, vo0 = got[0:2], got[2:4]

    def along(l, m):
        return lax.all_gather(pairs[l, m], "fsdp", axis=0, tiled=True)

    def both(rows):
        return rows, plan.across(rows)

    def four(pair):
        return (*pair, plan.core(pair[0]), plan.core(pair[1]))

    un0_rows, qk1_rows, vo1_rows, un1_rows = along(0, 2), along(1, 0), along(1, 1), along(1, 2)
    x = plan.order(plan.pick(inputs, plan.seq), other.astype(F32))
    h = (x * inverse_rms(x) * norm_gain[0, 0]).astype(BF16)
    h, un0_rows, qk1_rows, cotangent = after(h, un0_rows, qk1_rows, cotangent)
    un0, qk1 = both(un0_rows), both(qk1_rows)
    cot_block = plan.pick(cotangent, 1 - plan.seq).astype(BF16)
    kept, weights = [], []
    for l in range(layers):
        qk, vo = (qk0, vo0) if l == 0 else (qk1, vo1)
        scale = jnp.tile(factors[l] * LOG2E, 2 * w // dh)[:, None]
        h_other = plan.core(h)
        qkv = project(h, qk, vo, scale, 0)
        q, k, v = project(h_other, qk, vo, scale, 1, qkv)
        if l == 1:
            q, un1_rows = after(q, un1_rows)
            un1 = both(un1_rows)
        att, lse = attention_forward(q, k, v, prefix, order, dh)
        if l == 0:
            att, un0_got, qk1_got, vo1_rows = after(att, un0[1], qk1[1], vo1_rows)
            un, qk1 = four((un0[0], un0_got)), (qk1[0], qk1_got)
            vo1 = both(vo1_rows)
        else:
            att, un1_got, cot_got = after(att, un1[1], cot_got)
            un = four((un1[0], un1_got))
        part = plan.core(out_project(att, vo, 1))
        if l == 0:
            part, un1_rows = after(part, un1_rows)
        next_gain = norm_gain[(l + 1) % layers, 0][None]
        mid, pre, res, h_next = middle_call(x, att, part, norm_gain[l, 1][None], next_gain, vo, un)
        if l == 0:
            h_next, vo1_got, cot_block = after(h_next, vo1[1], cot_block)
            vo1 = (vo1[0], vo1_got)
            cot_got = plan.across(cot_block)
        kept.append((x, h, h_other, q, k, v, att, lse, mid, pre))
        weights.append((qk, vo, un))
        x, h = res, h_next
    g = plan.order(plan.pick(cotangent, plan.seq), cot_got.astype(F32))
    out_blocks = x.reshape(seqs, positions, d)
    out_send = plan.pick(out_blocks, 1 - plan.seq).astype(BF16)
    g, out_send = after(g, out_send)
    out_got = plan.across(out_send)
    outputs = None
    width = -(-3 * w // 128) * 128
    grads = [None] * layers
    for l in reversed(range(layers)):
        qk, vo, un = weights[l]
        x, h, h_other, q, k, v, att, lse, mid, pre = kept[l]
        g_mid, low, gain_m, u0, u1, u2, u3 = mlp_back(g, mid, pre, norm_gain[l, 1][None], un)
        if outputs is None:
            low, out_got = after(low, out_got)
            outputs = plan.order(plan.pick(out_blocks, plan.seq), out_got.astype(F32)).reshape(out_blocks.shape)
        low_other = plan.core(low)
        g_att = grad_att(low, vo, 0)
        early = out_grad_call(low, low_other, att, (u0, u1), (plan.core(u2), plan.core(u3)), width)
        early = [early[1], early[0]]
        low_other, *early = after(low_other, *early)
        early_got = plan.across(early[0])
        g_att = grad_att(low_other, vo, 1, g_att)
        dgrads, fgs, pieces = [None] * 6, [], [None] * 2
        for s in (1, 0):
            dq, dk, dv, fg = attention_backward(
                q, k, v, att, g_att, lse, factors[l], prefix, order, dh, s * w, w
            )
            if s == 0 and l + 1 < layers:
                dq, upper = after(dq, grads[l + 1][1])
                grads[l + 1] = (grads[l + 1][0], upper, grads[l + 1][2])
            if s == 1:
                pieces[1] = weight_grad(h, h_other, dq, dk, dv, width)
                g_att, pieces[1], early_got = after(g_att, pieces[1], early_got)
                late_got = plan.across(pieces[1])
                mine, g_att = after(add_low(early[1], early_got), g_att)
                early = scatter_rows(mine)
            dgrads[3 * s:3 * s + 3] = [dq, dk, dv]
            fgs.append(fg)
        fg = fgs[0] + fgs[1]
        part = input_other(dgrads, qk, vo)
        part, dgrads[0], late_got = after(part, dgrads[0], late_got)
        part = plan.core(part)
        mine, dgrads[1] = after(weight_grad(h, h_other, *dgrads[:3], width, late_got), dgrads[1])
        late = scatter_rows(mine)
        g, gain_a = input_own(dgrads, part, x, g_mid, norm_gain[l, 0][None], qk, vo)
        if l > 0:
            g, early = after(g, early)
        factor_grad = jnp.sum(fg, axis=1) / (factors[l] * LOG2E)
        small = jnp.concatenate([jnp.sum(gain_a, axis=0), jnp.sum(gain_m, axis=0), factor_grad])
        grads[l] = (early, late, small)
    input_grad = plan.unswap(g)
    small = jnp.stack([entry[2] for entry in grads])
    small = total_over_all(plan, small)
    early, late = jnp.stack([e[0] for e in grads]), jnp.stack([e[1] for e in grads])
    qkv_g = jnp.stack([late[:, :, c * w:(c + 1) * w] for c in range(3)], axis=1)
    up_g, down_g, out_g = (early[:, :, c * w:(c + 1) * w] for c in range(3))
    scale_g = small[:, 2 * d:] * jax.nn.sigmoid(query_scale) * unit
    return (
        outputs, input_grad, qkv_g, jnp.swapaxes(out_g, 1, 2), up_g, jnp.swapaxes(down_g, 1, 2),
        small[:, :d], small[:, d:2 * d], scale_g,
    )


def body(inputs, cotangent, w_qkv, w_out, w_up, w_down, norm_gain, query_scale, prefix_len):
    seqs, positions, d = inputs.shape
    fsdp, tp = lax.axis_size("fsdp"), lax.axis_size("tp")
    layers = w_qkv.shape[0]
    plan = Plan(seqs, tp, fsdp, w_qkv.shape[2])
    if plan.fast:
        return fast_body(
            plan, inputs, cotangent, w_qkv, w_out, w_up, w_down, norm_gain, query_scale, prefix_len
        )
    dh = query_scale.shape[1]
    unit = SOFT_ONE / math.sqrt(dh)
    factors = jax.nn.softplus(query_scale) * unit
    prefix = lax.dynamic_slice_in_dim(prefix_len, plan.seq, 1)
    order = plan.blocks(positions * tp)
    out_shard, down_shard = jnp.swapaxes(w_out, 1, 2), jnp.swapaxes(w_down, 1, 2)

    weights = []
    for l in range(layers):
        qkv = plan.gather_heads(w_qkv[l])
        out_t = plan.gather_heads(out_shard[l][None])[:, 0]
        up, down_t = plan.gather_full(jnp.stack([w_up[l], down_shard[l]]))
        weights.append(([qkv[:, c] for c in range(3)], out_t, up, down_t))

    x = plan.swap(inputs)
    g = plan.swap(cotangent)
    kept = []
    for l in range(layers):
        x, saved = layer_forward(plan, x, prefix, order, *weights[l], norm_gain[l], factors[l])
        kept.append(saved)
    outputs = plan.unswap(x)
    grads = [None] * layers
    for l in reversed(range(layers)):
        g, grads[l] = layer_backward(
            plan, g, kept[l], prefix, order, *weights[l], norm_gain[l], factors[l]
        )
    input_grad = plan.unswap(g)
    qkv_g, out_g, up_g, down_g, gain_a, gain_m, f_g = (jnp.stack(a) for a in zip(*grads))
    scale_g = f_g * jax.nn.sigmoid(query_scale) * unit
    gain_a, gain_m, scale_g = lax.psum((gain_a, gain_m, scale_g), ("fsdp", "tp"))
    return outputs, input_grad, qkv_g, out_g, up_g, down_g, gain_a, gain_m, scale_g


def solution(mesh):
    placed = (
        P("fsdp", "tp", None),
        P("fsdp", "tp", None),
        P(None, None, "fsdp", "tp"),
        P(None, "tp", "fsdp"),
        P(None, "fsdp", "tp"),
        P(None, "tp", "fsdp"),
        P(),
        P(),
        P("fsdp"),
    )
    return jax.shard_map(
        body,
        mesh=mesh,
        in_specs=placed,
        out_specs=placed[:6] + (P(), P(), P()),
        check_vma=False,
    )
```

```python
import functools, math
import jax
import jax.numpy as jnp
from jax import lax
from jax.experimental import pallas as pl
from jax.experimental.pallas import tpu as pltpu
from jax.sharding import PartitionSpec as P

MASKED = -1e30
F32, BF16 = jnp.float32, jnp.bfloat16
EPSILON = 1e-06
SOFT_ONE = 1.442695041
LOG2E = math.log2(math.e)
MESH = pl.DeviceIdType.MESH
HINT = 1
VMEM_LIMIT = 60 * 2**20

def dot(a, b, dims=((1,), (0,))):
    return lax.dot_general(a, b, (dims, ((), ())), preferred_element_type=F32)

def key_range(row_start, rows, prefix, block):
    full = jnp.maximum(row_start + 1, prefix) // block
    stop = (jnp.maximum(row_start + rows, prefix) + block - 1) // block
    return full, stop

def forward_kernel(prefix_ref, order_ref, q_ref, k_ref, v_ref, o_ref, lse_ref, key_rows, value_ext, *, pair, dh, bq, bk):
    length = q_ref.shape[1]
    prefix = prefix_ref[0]
    ext = value_ext.shape[1]
    bound = 0.0
    for h in range(pair):
        rows = slice(h * dh, (h + 1) * dh)
        q, k = q_ref[rows, :].astype(F32), k_ref[rows, :].astype(F32)
        bound = jnp.maximum(bound, jnp.max(jnp.sum(q * q, axis=0)) * jnp.max(jnp.sum(k * k, axis=0)))
        key_rows[h] = k_ref[rows, :].T
        value_ext[h, :dh] = v_ref[rows, :]
        value_ext[h, dh:] = jnp.ones((ext - dh, length), BF16)

    def one_query(shifted, qi, carry):
        start = qi * bq
        here = pl.ds(pl.multiple_of(order_ref[qi] * bq, bq), bq)
        queries = [q_ref[h * dh:(h + 1) * dh, here] for h in range(pair)]
        full, stop = key_range(start, bq, prefix, bk)

        def step(masked, ki, state):
            first = ki * bk
            there = pl.ds(pl.multiple_of(order_ref[ki] * bk, bk), bk)
            if masked:
                rows = first + lax.broadcasted_iota(jnp.int32, (bk, bq), 0)
                cols = start + lax.broadcasted_iota(jnp.int32, (bk, bq), 1)
                allowed = rows <= jnp.maximum(cols, prefix - 1)
            scores = [dot(key_rows[h, there], queries[h]) for h in range(pair)]
            fresh = []
            for h in range(pair):
                s = jnp.where(allowed, scores[h], MASKED) if masked else scores[h]
                if shifted:
                    top, total = state[h]
                    new_top = jnp.maximum(top, jnp.max(s, axis=0, keepdims=True))
                    p = jnp.exp2(s - new_top).astype(BF16)
                    total = total * jnp.exp2(top - new_top) + dot(value_ext[h, :, there], p)
                    fresh.append((new_top, total))
                else:
                    fresh.append(state[h] + dot(value_ext[h, :, there], jnp.exp2(s).astype(BF16)))
            return tuple(fresh)

        zero = jnp.zeros((ext, bq), F32)
        state = tuple((jnp.full((1, bq), MASKED, F32), zero) if shifted else zero for _ in range(pair))
        state = lax.fori_loop(0, full, functools.partial(step, False), state)
        state = lax.fori_loop(full, stop, functools.partial(step, True), state)
        for h in range(pair):
            top, total = state[h] if shifted else (0.0, state[h])
            norm = total[dh:dh + 1]
            o_ref[h * dh:(h + 1) * dh, here] = (total[:dh] / norm).astype(BF16)
            lse_ref[h, :, here] = top + jnp.log2(norm)
        return carry

    small = bound <= 3600.0

    @pl.when(small)
    def _():
        lax.fori_loop(0, length // bq, functools.partial(one_query, False), 0)

    @pl.when(jnp.logical_not(small))
    def _():
        lax.fori_loop(0, length // bq, functools.partial(one_query, True), 0)


def attention_forward(q, k, v, prefix, order, dh, pair=4):
    width, length = q.shape
    heads = width // dh
    pair = min(pair, heads)
    bq = bk = length // order.shape[0]
    ext = dh + 16
    spec = pl.BlockSpec((pair * dh, length), lambda i, p, o: (i, 0))
    return pl.pallas_call(
        functools.partial(forward_kernel, pair=pair, dh=dh, bq=bq, bk=bk),
        grid_spec=pltpu.PrefetchScalarGridSpec(
            num_scalar_prefetch=2, grid=(heads // pair,),
            in_specs=[spec, spec, spec],
            out_specs=[spec, pl.BlockSpec((pair, 1, length), lambda i, p, o: (i, 0, 0))],
            scratch_shapes=[pltpu.VMEM((pair, length, dh), BF16), pltpu.VMEM((pair, ext, length), BF16)],
        ),
        out_shape=[jax.ShapeDtypeStruct((width, length), BF16), jax.ShapeDtypeStruct((heads, 1, length), F32)],
        compiler_params=pltpu.CompilerParams(vmem_limit_bytes=VMEM_LIMIT),
        cost_estimate=pl.CostEstimate(flops=int(HINT * 600 * length * length * heads), bytes_accessed=int(HINT * 8 * width * length), transcendentals=0),
        name="attention_forward",
    )(prefix, order, q, k, v)

def split3(x):
    a = x.astype(BF16)
    r = x - a.astype(F32)
    b = r.astype(BF16)
    c = (r - b.astype(F32)).astype(BF16)
    return a, b, c

def backward_kernel(prefix_ref, order_ref, q_ref, k_ref, v_ref, o_ref, g_ref, lse_ref, scale_ref, dq_ref, dk_ref, dv_ref, fg_ref,
                    key_ext, value_ext, query_ext, grad_ext, dk_acc, dv_acc, *, pair, dh, bq, bk):
    length = q_ref.shape[1]
    prefix = prefix_ref[0]
    pad = key_ext.shape[1] - dh
    index = lax.broadcasted_iota(jnp.int32, (pad, length), 0)
    ones = (index < 3).astype(F32).astype(BF16)

    @pl.when(pl.program_id(0) == 0)
    def _():
        fg_ref[...] = jnp.zeros_like(fg_ref)

    def tail(row):
        high, mid, low = (part.astype(F32) for part in split3(-row))
        rest = jnp.where(index == 1, mid, jnp.where(index == 2, low, 0.0))
        return jnp.where(index == 0, high, rest).astype(BF16)

    for h in range(pair):
        rows = slice(h * dh, (h + 1) * dh)
        g = g_ref[rows, :]
        key_ext[h, :dh] = k_ref[rows, :]
        key_ext[h, dh:] = ones
        value_ext[h, :dh] = v_ref[rows, :]
        value_ext[h, dh:] = ones
        delta = jnp.sum(o_ref[rows, :].astype(F32) * g.astype(F32), axis=0, keepdims=True)
        query_ext[h, :dh] = q_ref[rows, :]
        query_ext[h, dh:] = tail(lse_ref[h])
        grad_ext[h, :dh] = g
        grad_ext[h, dh:] = tail(delta)
        dk_acc[h] = jnp.zeros((dh, length), F32)
        dv_acc[h] = jnp.zeros((dh, length), F32)

    def one_query(qi, carry):
        start = qi * bq
        here = pl.ds(pl.multiple_of(order_ref[qi] * bq, bq), bq)
        full, stop = key_range(start, bq, prefix, bk)

        def step(masked, ki, state):
            first = ki * bk
            there = pl.ds(pl.multiple_of(order_ref[ki] * bk, bk), bk)
            if masked:
                rows = start + lax.broadcasted_iota(jnp.int32, (bq, bk), 0)
                cols = first + lax.broadcasted_iota(jnp.int32, (bq, bk), 1)
                allowed = cols <= jnp.maximum(rows, prefix - 1)
            fresh = []
            s = [dot(query_ext[h, :, here], key_ext[h, :, there], ((0,), (0,))) for h in range(pair)]
            gp = [dot(grad_ext[h, :, here], value_ext[h, :, there], ((0,), (0,))) for h in range(pair)]
            for h in range(pair):
                x = jnp.where(allowed, s[h], MASKED) if masked else s[h]
                p = jnp.exp2(x)
                ds = (p * gp[h]).astype(BF16)
                rows = slice(h * dh, (h + 1) * dh)
                dv_acc[h, :, there] += dot(g_ref[rows, here], p.astype(BF16))
                dk_acc[h, :, there] += dot(q_ref[rows, here], ds)
                fresh.append(state[h] + dot(ds, k_ref[rows, there], ((1,), (1,))))
            return tuple(fresh)

        state = tuple(jnp.zeros((bq, dh), F32) for _ in range(pair))
        state = lax.fori_loop(0, full, functools.partial(step, False), state)
        state = lax.fori_loop(full, stop, functools.partial(step, True), state)
        for h in range(pair):
            rows = slice(h * dh, (h + 1) * dh)
            dq = state[h].T
            prod = dq * q_ref[rows, here].astype(F32)
            part = prod[:, :128]
            for c in range(1, bq // 128):
                part = part + prod[:, c * 128:(c + 1) * 128]
            fg_ref[...] += part
            dq_ref[rows, here] = (dq * scale_ref[...]).astype(BF16)
        return carry

    lax.fori_loop(0, length // bq, one_query, 0)
    for h in range(pair):
        rows = slice(h * dh, (h + 1) * dh)
        dk_ref[rows, :] = (dk_acc[h] * math.log(2.0)).astype(BF16)
        dv_ref[rows, :] = dv_acc[h].astype(BF16)


def attention_backward(q, k, v, o, g, lse, factor, prefix, order, dh, base=0, width=None, pair=2):
    full, length = q.shape
    width = width or full
    heads = width // dh
    pair = min(pair, heads)
    bq = bk = length // order.shape[0]
    ext = dh + 16
    spec = pl.BlockSpec((pair * dh, length), lambda i, p, o: (i, 0))
    skip = base // (pair * dh)
    source = pl.BlockSpec((pair * dh, length), lambda i, p, o: (i + skip, 0))
    wide = jax.ShapeDtypeStruct((width, length), BF16)
    return pl.pallas_call(
        functools.partial(backward_kernel, pair=pair, dh=dh, bq=bq, bk=bk),
        grid_spec=pltpu.PrefetchScalarGridSpec(
            num_scalar_prefetch=2, grid=(heads // pair,),
            in_specs=[source] * 5 + [pl.BlockSpec((pair, 1, length), lambda i, p, o: (i + skip, 0, 0)), pl.BlockSpec((dh, 1), lambda i, p, o: (0, 0))],
            out_specs=[spec] * 3 + [pl.BlockSpec((dh, 128), lambda i, p, o: (0, 0))],
            scratch_shapes=[
                pltpu.VMEM((pair, ext, length), BF16),
                pltpu.VMEM((pair, ext, length), BF16),
                pltpu.VMEM((pair, ext, length), BF16),
                pltpu.VMEM((pair, ext, length), BF16),
                pltpu.VMEM((pair, dh, length), F32),
                pltpu.VMEM((pair, dh, length), F32)],
        ),
        out_shape=[wide] * 3 + [jax.ShapeDtypeStruct((dh, 128), F32)],
        compiler_params=pltpu.CompilerParams(vmem_limit_bytes=VMEM_LIMIT),
        cost_estimate=pl.CostEstimate(flops=int(HINT * 1600 * length * length * heads), bytes_accessed=int(HINT * 16 * width * length), transcendentals=0),
        name="attention_backward",
    )(prefix, order, q, k, v, o, g, lse, factor.reshape(dh, 1))


def rms(x):
    inv = lax.rsqrt(jnp.mean(x * x, axis=-1, keepdims=True) + EPSILON)
    return x * inv, inv


def rms_back(normed, inv, gain, grad):
    scaled = grad * gain
    out = inv * (scaled - normed * jnp.mean(scaled * normed, axis=-1, keepdims=True))
    return out, jnp.sum(grad * normed, axis=0)


def ein(spec, *args):
    return jnp.einsum(spec, *args, preferred_element_type=F32)


def gather_kernel(pieces, pairs, outer, ring, shard_ref, block_ref, *refs):
    outs = [refs[2 * m:2 * m + 2] for m in range(pairs)]
    got_ref = refs[2 * pairs]
    send, recv, local = refs[2 * pairs + 1:]
    f, t = lax.axis_index("fsdp"), lax.axis_index("tp")
    zz, yy = f // 2, f % 2
    across = {"tp": lax.rem(t + ring, 2 * ring)}
    beside = {"fsdp": zz * 2 + 1 - yy}
    along = [{"fsdp": lax.rem(zz + k, outer) * 2 + yy} for k in range(1, outer)]
    peers = along + [across, beside]
    barrier = pltpu.get_barrier_semaphore()
    for peer in peers:
        pl.semaphore_signal(barrier, inc=1, device_id=peer, device_id_type=MESH)
    pl.semaphore_wait(barrier, len(peers))
    used = [0]

    def copy(src, dst, peer):
        slot = used[0]
        used[0] += 1
        return pltpu.make_async_remote_copy(
            src_ref=src, dst_ref=dst, send_sem=send.at[slot], recv_sem=recv.at[slot],
            device_id=peer, device_id_type=MESH,
        )

    count = len(pieces)
    chunks = 4
    step = block_ref.shape[0] // chunks
    blocks = [
        copy(block_ref.at[pl.ds(i * step, step)], got_ref.at[pl.ds(i * step, step)], across)
        for i in range(chunks)
    ]
    own, first, second, third = [], [], [], []
    for i, (m, low, rows, route) in enumerate(pieces):
        part = pl.ds(low, rows)
        w = [out.at[:, :, part] for out in outs[m]]
        src = shard_ref.at[m, part]
        own.append(pltpu.make_async_copy(src, w[0].at[zz, yy], local.at[i]))
        first.append([copy(src, w[0].at[zz, yy], peer) for peer in along])
        if route:
            second.append([copy(w[0].at[:, yy], w[0].at[:, yy], beside)])
            third.append([copy(w[0], w[1], across)])
        else:
            second.append([copy(w[0].at[:, yy], w[1].at[:, yy], across)])
            third.append([copy(w[s].at[:, yy], w[s].at[:, yy], beside) for s in range(2)])

    def begin(i):
        own[i].start()
        for c in first[i]:
            c.start()

    ahead = 3
    for i in range(min(ahead, count)):
        begin(i)
    started = 0
    for b in blocks[:2]:
        b.start()
    started = 2
    for i in range(count + 2):
        if i < count:
            own[i].wait()
            for c in first[i]:
                c.wait_recv()
            for c in second[i]:
                c.start()
            if i + ahead < count:
                begin(i + ahead)
            if started < chunks:
                blocks[started].start()
                started += 1
        if 0 <= i - 1 < count:
            for c in second[i - 1]:
                c.wait_recv()
            for c in third[i - 1]:
                c.start()
        if 0 <= i - 2 < count:
            for c in third[i - 2]:
                c.wait_recv()
    for b in blocks[started:]:
        b.start()
    for i in range(count):
        for c in first[i] + second[i] + third[i]:
            c.wait_send()
    for b in blocks:
        b.wait()


def pieces_of(pairs, rows):
    half = rows // 32 * 16
    return tuple(
        (m, low, size, m_part) for m in range(pairs) for m_part, (low, size) in enumerate(((0, half), (half, rows - half)))
    )


def gather_call(shards, block, pieces, fsdp, ring):
    pairs, rows, w = shards.shape
    outer = fsdp // 2
    slots = 4 + len(pieces) * (outer + 2)
    any_spec = pl.BlockSpec(memory_space=pl.ANY)
    got = pl.pallas_call(
        functools.partial(gather_kernel, pieces, pairs, outer, ring),
        out_shape=[jax.ShapeDtypeStruct((outer, 2, rows, w), BF16)] * (2 * pairs)
        + [jax.ShapeDtypeStruct(block.shape, block.dtype)],
        in_specs=[any_spec] * 2,
        out_specs=[any_spec] * (2 * pairs + 1),
        scratch_shapes=[
            pltpu.SemaphoreType.DMA((slots,)),
            pltpu.SemaphoreType.DMA((slots,)),
            pltpu.SemaphoreType.DMA((len(pieces),)),
        ],
        compiler_params=pltpu.CompilerParams(collective_id=0, has_side_effects=True),
        name="gather_weights",
    )(shards, block)
    return [a.reshape(outer * 2 * rows, w) for a in got[:-1]], got[-1]


class Plan:
    def __init__(self, seqs, tp, fsdp, rows):
        self.seqs, self.tp, self.ring, self.fsdp = seqs, tp, tp // seqs, fsdp
        self.same_member = [[s * self.ring + r for s in range(seqs)] for r in range(self.ring)]
        self.same_seq = [[s * self.ring + r for r in range(self.ring)] for s in range(seqs)]
        self.fast = seqs == 2 and self.ring == 2 and fsdp % 2 == 0 and rows % 32 == 0
        t = lax.axis_index("tp")
        self.seq, self.member = t // self.ring, lax.rem(t, self.ring)

    def across(self, a):
        n = self.tp
        return lax.ppermute(a, "tp", [(t, (t + self.ring) % n) for t in range(n)])

    def core(self, a):
        return lax.ppermute(a, "tp", [(t, t ^ 1) for t in range(self.tp)])

    def pick(self, blocks, index):
        return lax.dynamic_index_in_dim(blocks, index, 0, keepdims=False)

    def order(self, own, other):
        first = self.seq == 0
        return jnp.concatenate([jnp.where(first, own, other), jnp.where(first, other, own)])

    def swap(self, blocks):
        if self.seqs == 2:
            other = self.across(self.pick(blocks, 1 - self.seq).astype(BF16))
            return self.order(self.pick(blocks, self.seq), other.astype(F32))
        got = lax.all_to_all(
            blocks.astype(BF16), "tp", 0, 0, tiled=True, axis_index_groups=self.same_member
        )
        return got.reshape(-1, got.shape[-1]).astype(F32)

    def unswap(self, rows):
        blocks = rows.reshape(self.seqs, -1, rows.shape[-1])
        return self.swap(blocks).reshape(blocks.shape)

    def whole(self, rows):
        if self.fast:
            return jnp.concatenate([rows, self.core(rows)])
        cut = rows.reshape(self.seqs, -1, rows.shape[-1])
        got = lax.all_gather(cut, "tp", axis=1, axis_index_groups=self.same_seq)
        return got.reshape(-1, rows.shape[-1])

    def share(self, full):
        if self.fast:
            own = full.shape[0] // 2
            return full[:own].astype(F32) + self.core(full[own:].astype(BF16)).astype(F32)
        cut = full.astype(BF16).reshape(self.seqs, self.ring, -1, full.shape[-1])
        got = lax.psum_scatter(cut, "tp", scatter_dimension=1, axis_index_groups=self.same_seq)
        return got.reshape(-1, full.shape[-1]).astype(F32)

    def blocks(self, length):
        if self.fast:
            j = jnp.arange(self.tp, dtype=jnp.int32)
            apart = (j % self.ring != self.member).astype(jnp.int32)
            return apart * self.seqs + j // self.ring
        return jnp.arange(max(1, length // 512), dtype=jnp.int32)

    def gather_heads(self, shards):
        rows = lax.all_gather(shards, "fsdp", axis=1, tiled=True)
        if self.fast:
            return jnp.stack([rows, self.across(rows)])
        return lax.all_gather(rows, "tp", axis_index_groups=self.same_member)

    def join(self, every):
        r, s, m, d, w = every.shape
        return every.transpose(2, 3, 0, 1, 4).reshape(m, d, r * s * w)

    def gather_full(self, shards):
        part = self.gather_heads(shards)
        if self.fast:
            return self.join(jnp.stack([part, self.core(part)]))
        return self.join(lax.all_gather(part, "tp", axis_index_groups=self.same_seq))

    def scatter_heads(self, grads):
        if self.fast:
            other = self.across(grads[1].astype(BF16))
            mine = (grads[0].astype(F32) + other.astype(F32)).astype(BF16)
        else:
            mine = lax.psum_scatter(
                grads.astype(BF16), "tp", scatter_dimension=0, axis_index_groups=self.same_member
            )
        return lax.psum_scatter(mine, "fsdp", scatter_dimension=1, tiled=True).astype(F32)

    def scatter_full(self, grads):
        m, d, cols = grads.shape
        if self.fast:
            half = cols // 2
            other = self.core(grads[:, :, half:].astype(BF16))
            mine = grads[:, :, :half].astype(F32) + other.astype(F32)
            mine = mine.astype(BF16).reshape(m, d, self.seqs, -1).transpose(2, 0, 1, 3)
        else:
            cut = grads.astype(BF16).reshape(m, d, self.ring, self.seqs, -1).transpose(2, 3, 0, 1, 4)
            mine = lax.psum_scatter(cut, "tp", scatter_dimension=0, axis_index_groups=self.same_seq)
        return self.scatter_heads(mine)


def layer_forward(plan, x, prefix, order, qkv, out_t, up, down_t, gains, factor):
    dh = factor.shape[0]
    normed, inv = rms(x)
    h = plan.whole((normed * gains[0]).astype(BF16))
    seqs, d, w = out_t.shape
    raw = [ein("sdc,td->sct", qkv[c], h).reshape(seqs * w, -1) for c in range(3)]
    scale = jnp.tile(factor * LOG2E, seqs * w // dh)[:, None]
    q, k, v = (raw[0] * scale).astype(BF16), raw[1].astype(BF16), raw[2].astype(BF16)
    att, lse = attention_forward(q, k, v, prefix, order, dh)
    middle = x + plan.share(ein("sct,sdc->td", att.reshape(seqs, w, -1), out_t))
    normed_m, inv_m = rms(middle)
    h_m = (normed_m * gains[1]).astype(BF16)
    pre = ein("td,df->tf", h_m, up)
    hidden = jax.nn.silu(pre).astype(BF16)
    result = middle + ein("tf,df->td", hidden, down_t)
    return result, (x, inv, h, q, k, v, att, lse, middle, inv_m, h_m, pre, hidden)


def layer_backward(plan, g, saved, prefix, order, qkv, out_t, up, down_t, gains, factor):
    x, inv, h, q, k, v, att, lse, middle, inv_m, h_m, pre, hidden = saved
    dh = factor.shape[0]
    seqs, d, w = out_t.shape
    length = h.shape[0]
    g_low = g.astype(BF16)
    down_grad = ein("td,tf->df", g_low, hidden)
    g_hidden = ein("td,df->tf", g_low, down_t)
    sig = jax.nn.sigmoid(pre)
    g_pre = (g_hidden * sig * (1.0 + pre * (1.0 - sig))).astype(BF16)
    up_grad = ein("td,tf->df", h_m, g_pre)
    mlp_grads = plan.scatter_full(jnp.stack([up_grad, down_grad]))
    g_hm = ein("tf,df->td", g_pre, up)
    back_m, gain_m = rms_back(middle * inv_m, inv_m, gains[1], g_hm)
    g_mid = g + back_m
    g_all = plan.whole(g_mid.astype(BF16))
    att3 = att.reshape(seqs, w, length)
    out_grad = plan.scatter_heads(ein("td,sct->sdc", g_all, att3)[:, None])[0]
    g_att = ein("td,sdc->sct", g_all, out_t).astype(BF16).reshape(seqs * w, length)
    dq, dk, dv, fg = attention_backward(q, k, v, att, g_att, lse, factor, prefix, order, dh)
    factor_grad = jnp.sum(fg, axis=1) / (factor * LOG2E)
    parts = [a.reshape(seqs, w, length) for a in (dq, dk, dv)]
    qkv_grad = plan.scatter_heads(jnp.stack([ein("td,sct->sdc", h, a) for a in parts], axis=1))
    g_ha = plan.share(sum(ein("sct,sdc->td", a, b) for a, b in zip(parts, qkv)))
    back_a, gain_a = rms_back(x * inv, inv, gains[0], g_ha)
    return g_mid + back_a, (qkv_grad, out_grad.T, mlp_grads[0], mlp_grads[1].T, gain_a, gain_m, factor_grad)


TN, NT, TT = ((0,), (0,)), ((1,), (1,)), ((0,), (1,))
ONE = pl.Buffered(1)


def cost(flops, nbytes):
    return pl.CostEstimate(flops=int(flops * HINT), bytes_accessed=int(nbytes * HINT), transcendentals=0)


def params(mib=60):
    return pltpu.CompilerParams(vmem_limit_bytes=mib * 2**20)


def fixed(shape):
    return pl.BlockSpec(shape, lambda *a: (0,) * len(shape), pipeline_mode=ONE)


def weight(w, lanes=None):
    stack, index = w if isinstance(w, tuple) else (w, None)
    shape = (stack.shape[-2], lanes or stack.shape[-1])
    if index is None:
        return fixed(shape)
    return pl.BlockSpec((None,) + shape, lambda *a: (index, 0, 0), pipeline_mode=ONE)


def plain(weights):
    return [w[0] if isinstance(w, tuple) else w for w in weights]


def shape_of(shape, dtype=BF16):
    return jax.ShapeDtypeStruct(shape, dtype)


def inverse_rms(x):
    return lax.rsqrt(jnp.mean(x * x, axis=-1, keepdims=True) + EPSILON)


def eight(x):
    return jnp.sum(x.reshape(-1, 8, x.shape[-1]), axis=0)


def join_lanes(dst, refs, low, high):
    width = high - low
    for i, ref in enumerate(refs):
        dst[:, i * width:(i + 1) * width] = ref[:, low:high]


def project_kernel(w, h_ref, qk0, qk1, vo0, vo1, scale_ref, *refs):
    q_ref, k_ref, v_ref = refs[-3:]
    h = h_ref[...]
    for s, (qk, vo) in enumerate(((qk0, vo0), (qk1, vo1))):
        rows = slice(s * w, (s + 1) * w)
        both = dot(qk[...], h, TT)
        q_ref[rows] = (both[:w] * scale_ref[rows]).astype(BF16)
        k_ref[rows] = both[w:].astype(BF16)
        v_ref[rows] = dot(vo[:, :w], h, TT).astype(BF16)


def project(h, qk, vo, scale, base, bufs=None):
    rows, d = h.shape
    w = plain(qk)[0].shape[-1] // 2
    bt = 512
    steps = rows // bt
    out = pl.BlockSpec((2 * w, bt), lambda i: (0, i + base * steps))
    extra = [] if bufs is None else list(bufs)
    return pl.pallas_call(
        functools.partial(project_kernel, w),
        grid=(steps,),
        in_specs=[pl.BlockSpec((bt, d), lambda i: (i, 0))] + [weight(a) for a in (*qk, *vo)] + [fixed((2 * w, 1))]
        + [pl.BlockSpec(memory_space=pl.ANY)] * len(extra),
        out_specs=[out] * 3,
        out_shape=[shape_of((2 * w, 2 * rows))] * 3,
        input_output_aliases={6 + i: i for i in range(len(extra))},
        compiler_params=params(),
        cost_estimate=cost(2 * rows * d * 6 * w, 4 * rows * d),
        name="project",
    )(h, *plain(qk), *plain(vo), scale, *extra)


def out_kernel(w, att_ref, vo0, vo1, part_ref, mat):
    @pl.when(pl.program_id(0) == 0)
    def _():
        join_lanes(mat, (vo0, vo1), w, 2 * w)

    part_ref[...] = dot(att_ref[...], mat[...], TT).astype(BF16)


def out_project(att, vo, base):
    d, w2 = plain(vo)[0].shape[-2:]
    rows = att.shape[1] // 2
    bt = 512
    steps = rows // bt
    return pl.pallas_call(
        functools.partial(out_kernel, w2 // 2),
        grid=(steps,),
        in_specs=[pl.BlockSpec((w2, bt), lambda i: (0, i + base * steps))] + [weight(a) for a in vo],
        out_specs=pl.BlockSpec((bt, d), lambda i: (i, 0)),
        out_shape=shape_of((rows, d)),
        scratch_shapes=[pltpu.VMEM((d, w2), BF16)],
        compiler_params=params(),
        cost_estimate=cost(2 * rows * d * w2, 4 * rows * d),
        name="out_project",
    )(att, *plain(vo))


def middle_kernel(w, x_ref, att_ref, got_ref, gm_ref, ga_ref, vo0, vo1, un0, un1, un2, un3,
                  mid_ref, pre_ref, res_ref, h_ref, out_mat, up_mat, down_mat):
    @pl.when(pl.program_id(0) == 0)
    def _():
        join_lanes(out_mat, (vo0, vo1), w, 2 * w)
        join_lanes(up_mat, (un0, un1, un2, un3), 0, w)
        join_lanes(down_mat, (un0, un1, un2, un3), w, 2 * w)

    mid = x_ref[...] + got_ref[...].astype(F32) + dot(att_ref[...], out_mat[...], TT)
    mid_ref[...] = mid
    h_m = (mid * inverse_rms(mid) * gm_ref[...]).astype(BF16)
    pre = dot(h_m, up_mat[...])
    pre_ref[...] = pre
    hidden = (pre / (1.0 + jnp.exp(-pre))).astype(BF16)
    res = mid + dot(hidden, down_mat[...], NT)
    res_ref[...] = res
    h_ref[...] = (res * inverse_rms(res) * ga_ref[...]).astype(BF16)


def middle_call(x, att, got, gain_m, gain_a, vo, un):
    rows, d = x.shape
    w2 = plain(vo)[0].shape[-1]
    ff = 2 * w2
    bt = 256
    row = pl.BlockSpec((bt, d), lambda i: (i, 0))
    wide = pl.BlockSpec((bt, ff), lambda i: (i, 0))
    return pl.pallas_call(
        functools.partial(middle_kernel, w2 // 2),
        grid=(rows // bt,),
        in_specs=[row, pl.BlockSpec((w2, bt), lambda i: (0, i)), row] + [fixed((1, d))] * 2
        + [weight(a) for a in (*vo, *un)],
        out_specs=[row, wide, row, row],
        out_shape=[shape_of((rows, d), F32), shape_of((rows, ff), F32), shape_of((rows, d), F32), shape_of((rows, d))],
        scratch_shapes=[pltpu.VMEM((d, w2), BF16), pltpu.VMEM((d, ff), BF16), pltpu.VMEM((d, ff), BF16)],
        compiler_params=params(),
        cost_estimate=cost(2 * rows * d * (w2 + 2 * ff), 30 * rows * d),
        name="middle",
    )(x, att, got, gain_m, gain_a, *plain(vo), *plain(un))


def mlp_back_kernel(w, sides, steps, index, g_ref, mid_ref, pre_ref, gm_ref, att_any, *refs):
    weights, refs = refs[:6], refs[6:]
    g_mid_ref, gain_ref, g_att_ref, o0, o1 = refs[:5]
    (up_mat, down_mat, out_mat, g_all, hid_all, hm_all, gpre_all, low_own, low_other, blocks, got, vo_side, att,
     load, send, recv) = refs[5:]
    i = pl.program_id(0)
    rows_steps, grad_steps, att_steps, _ = steps
    bt, bd, ba = g_ref.shape[0], o0.shape[0], g_att_ref.shape[1]
    t = lax.axis_index("tp")
    core = {"tp": t + 1 - 2 * lax.rem(t, 2)}
    low_lane = sides[0]

    def loads():
        pairs = [(weights[2 + b], blocks.at[b]) for b in range(4)]
        for s in range(2):
            pairs.append((weights[s], vo_side.at[s]))
        views = []
        for n, ((ref, dst), k) in enumerate(zip(pairs, index[2:] + index[:2])):
            src = ref if k is None else ref.at[k]
            if n >= 4:
                src = src.at[:, pl.ds(low_lane, vo_side.shape[2])]
            views.append(pltpu.make_async_copy(src, dst, load.at[n]))
        views.append(pltpu.make_async_copy(att_any, att, load.at[6]))
        return views

    def push(src, dst, slot):
        return pltpu.make_async_remote_copy(
            src_ref=src, dst_ref=dst, send_sem=send.at[slot], recv_sem=recv.at[slot],
            device_id=core, device_id_type=MESH,
        )

    def push_rows(k):
        part = pl.ds(pl.multiple_of(k * bt, bt), bt)
        return push(low_own.at[part], low_other.at[part], k)

    def push_block(c, s):
        part = pl.ds(pl.multiple_of(c * bd, bd), bd)
        return push(blocks.at[2 + s, part], got.at[s, part], rows_steps + 2 * c + s)

    @pl.when(i == 0)
    def _():
        copies = loads()
        for c in copies:
            c.start()
        barrier = pltpu.get_barrier_semaphore()
        pl.semaphore_signal(barrier, inc=1, device_id=core, device_id_type=MESH)
        gain_ref[...] = jnp.zeros_like(gain_ref)
        for b in range(4):
            copies[b].wait()
            up_mat[:, b * w:(b + 1) * w] = blocks[b, :, 0:w]
            down_mat[:, b * w:(b + 1) * w] = blocks[b, :, w:2 * w]
        pl.semaphore_wait(barrier, 1)

    @pl.when(i < rows_steps)
    def _():
        here = pl.ds(pl.multiple_of(i * bt, bt), bt)
        g = g_ref[...]
        g_low = g.astype(BF16)
        g_all[here] = g_low
        pre = pre_ref[...]
        sig = 1.0 / (1.0 + jnp.exp(-pre))
        hid_all[here] = (pre * sig).astype(BF16)
        g_hidden = dot(g_low, down_mat[...])
        g_pre = (g_hidden * sig * (1.0 + pre * (1.0 - sig))).astype(BF16)
        gpre_all[here] = g_pre
        mid = mid_ref[...]
        inv = inverse_rms(mid)
        normed = mid * inv
        gain = gm_ref[...]
        hm_all[here] = (normed * gain).astype(BF16)
        g_hm = dot(g_pre, up_mat[...], NT)
        gain_ref[...] += eight(g_hm * normed)
        scaled = g_hm * gain
        g_mid = g + inv * (scaled - normed * jnp.mean(scaled * normed, axis=-1, keepdims=True))
        g_mid_ref[...] = g_mid
        low_own[here] = g_mid.astype(BF16)
        push_rows(i).start()

    at = i - rows_steps

    @pl.when((at >= 0) & (at < grad_steps))
    def _():
        cols = pl.ds(pl.multiple_of(at * bd, bd), bd)
        up = dot(hm_all[:, cols], gpre_all[...], TN).astype(BF16)
        down = dot(g_all[:, cols], hid_all[...], TN).astype(BF16)
        for b in range(4):
            blocks[b, cols, 0:w] = up[:, b * w:(b + 1) * w]
            blocks[b, cols, w:2 * w] = down[:, b * w:(b + 1) * w]
        for s in range(2):
            push_block(at, s).start()

    to = at - grad_steps

    @pl.when(to == 0)
    def _():
        copies = loads()
        for s in range(2):
            copies[4 + s].wait()
            out_mat[:, s * w:(s + 1) * w] = vo_side[s, :, sides[1]:sides[1] + w]

    half = att_steps // 2

    @pl.when((to >= 0) & (to < half))
    def _():
        here = pl.ds(pl.multiple_of(to * ba, ba), ba)
        g_att_ref[...] = dot(out_mat[...], low_own[here], TT).astype(BF16)

    @pl.when(to == half)
    def _():
        for k in range(rows_steps):
            push_rows(k).wait()

    @pl.when((to >= half) & (to < att_steps))
    def _():
        here = pl.ds(pl.multiple_of((to - half) * ba, ba), ba)
        g_att_ref[...] = dot(out_mat[...], low_other[here], TT).astype(BF16)

    last = to - att_steps

    @pl.when(last == 0)
    def _():
        loads()[6].wait()

    @pl.when(last >= 0)
    def _():
        cols = pl.ds(pl.multiple_of(last * bd, bd), bd)
        rows = low_own.shape[0]
        grad = dot(low_own[:, cols], att[:, :rows], TT) + dot(low_other[:, cols], att[:, rows:], TT)
        grad = grad.astype(BF16)
        for s, out in enumerate((o0, o1)):
            push_block(last, s).wait()
            out[:, :2 * w] = (blocks[s, cols].astype(F32) + got[s, cols].astype(F32)).astype(BF16)
            out[:, 2 * w:3 * w] = grad[:, s * w:(s + 1) * w]
            out[:, 3 * w:] = jnp.zeros((bd, out.shape[1] - 3 * w), BF16)


def mlp_back(g, mid, pre, gain, att, vo, un, width, call):
    rows, d = g.shape
    ff = pre.shape[1]
    w2 = plain(un)[0].shape[-1]
    w = w2 // 2
    bt, bd, ba = 256, 256, 512
    steps = (rows // bt, d // bd, 2 * rows // ba, d // bd)
    starts = [sum(steps[:n]) for n in range(4)]
    low = w // 128 * 128
    sides = (low, w - low)

    def at(n, make):
        return lambda i: make(jnp.clip(i - starts[n], 0, steps[n] - 1))

    row = pl.BlockSpec((bt, d), at(0, lambda k: (k, 0)))
    wide = pl.BlockSpec((bt, ff), at(0, lambda k: (k, 0)))
    block = pl.BlockSpec((bd, width), at(3, lambda k: (k, 0)))
    any_spec = pl.BlockSpec(memory_space=pl.ANY)
    index = tuple(a[1] if isinstance(a, tuple) else None for a in (*vo, *un))
    slots = steps[0] + 2 * steps[1]
    return pl.pallas_call(
        functools.partial(mlp_back_kernel, w, sides, steps, index),
        grid=(sum(steps),),
        in_specs=[row, row, wide, fixed((1, d))] + [any_spec] * 7,
        out_specs=[row, fixed((8, d)), pl.BlockSpec((w2, ba), at(2, lambda k: (0, k))), block, block],
        out_shape=[shape_of((rows, d), F32), shape_of((8, d), F32), shape_of((w2, 2 * rows))] + [shape_of((d, width))] * 2,
        scratch_shapes=[pltpu.VMEM((d, ff), BF16)] * 2
        + [pltpu.VMEM((d, w2), BF16)]
        + [pltpu.VMEM((rows, d), BF16), pltpu.VMEM((rows, ff), BF16)] * 2
        + [pltpu.VMEM((rows, d), BF16)] * 2
        + [pltpu.VMEM((4, d, w2), BF16), pltpu.VMEM((2, d, w2), BF16), pltpu.VMEM((2, d, w2 - low), BF16)]
        + [pltpu.VMEM(att.shape, BF16)]
        + [pltpu.SemaphoreType.DMA((7,)), pltpu.SemaphoreType.DMA((slots,)), pltpu.SemaphoreType.DMA((slots,))],
        compiler_params=pltpu.CompilerParams(vmem_limit_bytes=62 * 2**20, collective_id=call, has_side_effects=True),
        cost_estimate=cost(8 * rows * d * ff + 8 * rows * d * w2, 40 * rows * d),
        name="mlp_back",
    )(g, mid, pre, gain, att, *plain(vo), *plain(un))


def weight_grad_kernel(w, own_ref, other_ref, dq_ref, dk_ref, dv_ref, *refs):
    out, stacked = refs[-2:]
    half = own_ref.shape[0]

    @pl.when(pl.program_id(0) == 0)
    def _():
        for j, ref in enumerate((dq_ref, dk_ref, dv_ref)):
            stacked[j * w:(j + 1) * w, :] = ref[...]

    grad = dot(own_ref[...], stacked[:, :half], TT) + dot(other_ref[...], stacked[:, half:], TT)
    if len(refs) == 3:
        grad = grad + refs[0][:, :3 * w].astype(F32)
    out[:, :3 * w] = grad.astype(BF16)
    out[:, 3 * w:] = jnp.zeros((out.shape[0], out.shape[1] - 3 * w), BF16)


def weight_grad(own, other, dq, dk, dv, width, got=None):
    rows, d = own.shape
    w = dq.shape[0]
    bd = 256
    col = pl.BlockSpec((rows, bd), lambda i: (0, i))
    flat = pl.BlockSpec((bd, width), lambda i: (i, 0))
    extra = [] if got is None else [got]
    return pl.pallas_call(
        functools.partial(weight_grad_kernel, w),
        grid=(d // bd,),
        in_specs=[col, col] + [fixed(dq.shape)] * 3 + [flat] * len(extra),
        out_specs=flat,
        out_shape=shape_of((d, width)),
        scratch_shapes=[pltpu.VMEM((3 * w, 2 * rows), BF16)],
        compiler_params=params(),
        cost_estimate=cost(12 * rows * d * w, 12 * rows * d),
        name="weight_grad",
    )(own, other, dq, dk, dv, *extra)


def input_sum(w, grads, qk, vo):
    total = None
    for s in range(2):
        dq, dk, dv = grads[3 * s:3 * s + 3]
        both = jnp.concatenate([dq[...], dk[...]], axis=0)
        part = dot(both, qk[s][...], TT) + dot(dv[...], vo[s][:, :w], TT)
        total = part if total is None else total + part
    return total


def input_other_kernel(w, *refs):
    refs, out_ref = refs[:-1], refs[-1]
    out_ref[...] = input_sum(w, refs[:6], refs[6:8], refs[8:10]).astype(BF16)


def input_other(grads, qk, vo):
    w, length = grads[0].shape
    d, w2 = plain(qk)[0].shape[-2:]
    bt = 512
    steps = length // 2 // bt
    col = pl.BlockSpec((w, bt), lambda i: (0, i + steps))
    return pl.pallas_call(
        functools.partial(input_other_kernel, w),
        grid=(steps,),
        in_specs=[col] * 6 + [weight(a) for a in (*qk, *vo)],
        out_specs=pl.BlockSpec((bt, d), lambda i: (i, 0)),
        out_shape=shape_of((length // 2, d)),
        compiler_params=params(),
        cost_estimate=cost(3 * length * d * w2, 4 * length * d),
        name="input_other",
    )(*grads, *plain(qk), *plain(vo))


def input_own_kernel(w, *refs):
    grads, refs = refs[:6], refs[6:]
    got_ref, x_ref, g_ref, gain_ref, qk0, qk1, vo0, vo1, out_ref, sum_ref = refs

    @pl.when(pl.program_id(0) == 0)
    def _():
        sum_ref[...] = jnp.zeros_like(sum_ref)

    g_ha = input_sum(w, grads, (qk0, qk1), (vo0, vo1)) + got_ref[...].astype(F32)
    x = x_ref[...]
    inv = inverse_rms(x)
    normed = x * inv
    sum_ref[...] += eight(g_ha * normed)
    scaled = g_ha * gain_ref[...]
    out_ref[...] = g_ref[...] + inv * (scaled - normed * jnp.mean(scaled * normed, axis=-1, keepdims=True))


def input_own(grads, got, x, g, gain, qk, vo):
    w = grads[0].shape[0]
    rows, d = x.shape
    w2 = 2 * w
    bt = 256
    col = pl.BlockSpec((w, bt), lambda i: (0, i))
    row = pl.BlockSpec((bt, d), lambda i: (i, 0))
    return pl.pallas_call(
        functools.partial(input_own_kernel, w),
        grid=(rows // bt,),
        in_specs=[col] * 6 + [row] * 3 + [fixed((1, d))]
        + [weight(a) for a in (*qk, *vo)],
        out_specs=[row, fixed((8, d))],
        out_shape=[shape_of((rows, d), F32), shape_of((8, d), F32)],
        compiler_params=params(),
        cost_estimate=cost(6 * rows * d * w2, 24 * rows * d),
        name="input_own",
    )(*grads, got, x, g, gain, *plain(qk), *plain(vo))


def total_over_all(plan, a):
    n, f = plan.tp, plan.fsdp
    hop = 1
    while hop < n:
        a = a + lax.ppermute(a, "tp", [(t, t ^ hop) for t in range(n)])
        hop *= 2
    hop = 1
    while hop < f:
        a = a + lax.ppermute(a, "fsdp", [(t, t ^ hop) for t in range(f)])
        hop *= 2
    return a


def add_low(own, got):
    return (own.astype(F32) + got.astype(F32)).astype(BF16)


def scatter_rows(mine):
    return lax.psum_scatter(mine, "fsdp", scatter_dimension=0, tiled=True).astype(F32)


def after(*arrays):
    return lax.optimization_barrier(arrays)


def fast_body(plan, inputs, cotangent, w_qkv, w_out, w_up, w_down, norm_gain, query_scale, prefix_len):
    seqs, positions, d = inputs.shape
    layers, w = w_qkv.shape[0], w_qkv.shape[3]
    dh = query_scale.shape[1]
    unit = SOFT_ONE / math.sqrt(dh)
    factors = jax.nn.softplus(query_scale) * unit
    prefix = lax.dynamic_slice_in_dim(prefix_len, plan.seq, 1)
    order = plan.blocks(positions * plan.tp)
    out_shard, down_shard = jnp.swapaxes(w_out, 1, 2), jnp.swapaxes(w_down, 1, 2)
    pairs = jnp.concatenate(
        [
            jnp.concatenate([w_qkv[:, 0], w_qkv[:, 1]], axis=2)[:, None],
            jnp.concatenate([w_qkv[:, 2], out_shard], axis=2)[:, None],
            jnp.concatenate([w_up, down_shard], axis=2)[:, None],
        ],
        axis=1,
    )

    block = plan.pick(inputs, 1 - plan.seq).astype(BF16)
    got, other = gather_call(pairs[0, :2], block, pieces_of(2, pairs.shape[2]), plan.fsdp, plan.ring)
    qk0, vo0 = got[0:2], got[2:4]

    def along(l, m):
        return lax.all_gather(pairs[l, m], "fsdp", axis=0, tiled=True)

    def both(rows):
        return rows, plan.across(rows)

    def four(pair):
        return (*pair, plan.core(pair[0]), plan.core(pair[1]))

    def stacked(rows):
        return (rows, 0), (rows, 1)

    shards = jnp.stack([pairs[1, 1:], plan.across(pairs[1, 1:])], axis=1)
    un0_rows, qk1_rows = along(0, 2), along(1, 0)
    vo1_rows, un1_rows = (lax.all_gather(shards[m], "fsdp", axis=1, tiled=True) for m in range(2))
    x = plan.order(plan.pick(inputs, plan.seq), other.astype(F32))
    h = (x * inverse_rms(x) * norm_gain[0, 0]).astype(BF16)
    h, un0_rows, qk1_rows, cotangent = after(h, un0_rows, qk1_rows, cotangent)
    un0 = both(un0_rows)
    cot_block = plan.pick(cotangent, 1 - plan.seq).astype(BF16)
    kept, weights = [], []
    for l in range(layers):
        qk, vo = (qk0, vo0) if l == 0 else (qk1, vo1)
        scale = jnp.tile(factors[l] * LOG2E, 2 * w // dh)[:, None]
        h_other = plan.core(h)
        qkv = project(h, qk, vo, scale, 0)
        q, k, v = project(h_other, qk, vo, scale, 1, qkv)
        att, lse = attention_forward(q, k, v, prefix, order, dh)
        if l == 0:
            att, un0_got, qk1_rows = after(att, un0[1], qk1_rows)
            un, qk1 = four((un0[0], un0_got)), both(qk1_rows)
        else:
            att, un1_rows, cot_got = after(att, un1_rows, cot_got)
            un = (*stacked(un1_rows), *stacked(plan.core(un1_rows)))
        part = plan.core(out_project(att, vo, 1))
        next_gain = norm_gain[(l + 1) % layers, 0][None]
        mid, pre, res, h_next = middle_call(x, att, part, norm_gain[l, 1][None], next_gain, vo, un)
        if l == 0:
            h_next, qk1_got, vo1_rows, cot_block = after(h_next, qk1[1], vo1_rows, cot_block)
            qk1, vo1 = (qk1[0], qk1_got), stacked(vo1_rows)
            cot_got = plan.across(cot_block)
        kept.append((x, h, h_other, q, k, v, att, lse, mid, pre))
        weights.append((qk, vo, un))
        x, h = res, h_next
    g = plan.order(plan.pick(cotangent, plan.seq), cot_got.astype(F32))
    out_blocks = x.reshape(seqs, positions, d)
    out_send = plan.pick(out_blocks, 1 - plan.seq).astype(BF16)
    g, out_send = after(g, out_send)
    out_got = plan.across(out_send)
    outputs = None
    width = -(-3 * w // 128) * 128
    grads = [None] * layers
    for l in reversed(range(layers)):
        qk, vo, un = weights[l]
        x, h, h_other, q, k, v, att, lse, mid, pre = kept[l]
        g_mid, gain_m, g_att, *early = mlp_back(g, mid, pre, norm_gain[l, 1][None], att, vo, un, width, 1 + l)
        early = [early[1], early[0]]
        if outputs is None:
            g_att, out_got = after(g_att, out_got)
            outputs = plan.order(plan.pick(out_blocks, plan.seq), out_got.astype(F32)).reshape(out_blocks.shape)
        early_got = plan.across(early[0])
        g_att, early[1] = after(g_att, early[1])
        dgrads, fgs, pieces = [None] * 6, [], [None] * 2
        for s in (1, 0):
            dq, dk, dv, fg = attention_backward(
                q, k, v, att, g_att, lse, factors[l], prefix, order, dh, s * w, w
            )
            if s == 0 and l + 1 < layers:
                dq, upper = after(dq, grads[l + 1][1])
                grads[l + 1] = (grads[l + 1][0], upper, grads[l + 1][2])
            if s == 1:
                pieces[1] = weight_grad(h, h_other, dq, dk, dv, width)
                g_att, pieces[1], early_got = after(g_att, pieces[1], early_got)
                late_got = plan.across(pieces[1])
                mine, g_att = after(add_low(early[1], early_got), g_att)
                early = scatter_rows(mine)
            dgrads[3 * s:3 * s + 3] = [dq, dk, dv]
            fgs.append(fg)
        fg = fgs[0] + fgs[1]
        part = input_other(dgrads, qk, vo)
        part, dgrads[0], late_got = after(part, dgrads[0], late_got)
        part = plan.core(part)
        mine, dgrads[1] = after(weight_grad(h, h_other, *dgrads[:3], width, late_got), dgrads[1])
        late = scatter_rows(mine)
        g, gain_a = input_own(dgrads, part, x, g_mid, norm_gain[l, 0][None], qk, vo)
        if l > 0:
            g, early = after(g, early)
        factor_grad = jnp.sum(fg, axis=1) / (factors[l] * LOG2E)
        small = jnp.concatenate([jnp.sum(gain_a, axis=0), jnp.sum(gain_m, axis=0), factor_grad])
        grads[l] = (early, late, small)
    input_grad = plan.unswap(g)
    small = jnp.stack([entry[2] for entry in grads])
    small = total_over_all(plan, small)
    early, late = jnp.stack([e[0] for e in grads]), jnp.stack([e[1] for e in grads])
    qkv_g = jnp.stack([late[:, :, c * w:(c + 1) * w] for c in range(3)], axis=1)
    up_g, down_g, out_g = (early[:, :, c * w:(c + 1) * w] for c in range(3))
    scale_g = small[:, 2 * d:] * jax.nn.sigmoid(query_scale) * unit
    return (
        outputs, input_grad, qkv_g, jnp.swapaxes(out_g, 1, 2), up_g, jnp.swapaxes(down_g, 1, 2),
        small[:, :d], small[:, d:2 * d], scale_g,
    )


def body(inputs, cotangent, w_qkv, w_out, w_up, w_down, norm_gain, query_scale, prefix_len):
    seqs, positions, d = inputs.shape
    fsdp, tp = lax.axis_size("fsdp"), lax.axis_size("tp")
    layers = w_qkv.shape[0]
    plan = Plan(seqs, tp, fsdp, w_qkv.shape[2])
    if plan.fast:
        return fast_body(
            plan, inputs, cotangent, w_qkv, w_out, w_up, w_down, norm_gain, query_scale, prefix_len
        )
    dh = query_scale.shape[1]
    unit = SOFT_ONE / math.sqrt(dh)
    factors = jax.nn.softplus(query_scale) * unit
    prefix = lax.dynamic_slice_in_dim(prefix_len, plan.seq, 1)
    order = plan.blocks(positions * tp)
    out_shard, down_shard = jnp.swapaxes(w_out, 1, 2), jnp.swapaxes(w_down, 1, 2)

    weights = []
    for l in range(layers):
        qkv = plan.gather_heads(w_qkv[l])
        out_t = plan.gather_heads(out_shard[l][None])[:, 0]
        up, down_t = plan.gather_full(jnp.stack([w_up[l], down_shard[l]]))
        weights.append(([qkv[:, c] for c in range(3)], out_t, up, down_t))

    x = plan.swap(inputs)
    g = plan.swap(cotangent)
    kept = []
    for l in range(layers):
        x, saved = layer_forward(plan, x, prefix, order, *weights[l], norm_gain[l], factors[l])
        kept.append(saved)
    outputs = plan.unswap(x)
    grads = [None] * layers
    for l in reversed(range(layers)):
        g, grads[l] = layer_backward(
            plan, g, kept[l], prefix, order, *weights[l], norm_gain[l], factors[l]
        )
    input_grad = plan.unswap(g)
    qkv_g, out_g, up_g, down_g, gain_a, gain_m, f_g = (jnp.stack(a) for a in zip(*grads))
    scale_g = f_g * jax.nn.sigmoid(query_scale) * unit
    gain_a, gain_m, scale_g = lax.psum((gain_a, gain_m, scale_g), ("fsdp", "tp"))
    return outputs, input_grad, qkv_g, out_g, up_g, down_g, gain_a, gain_m, scale_g


def solution(mesh):
    placed = (
        P("fsdp", "tp", None),
        P("fsdp", "tp", None),
        P(None, None, "fsdp", "tp"),
        P(None, "tp", "fsdp"),
        P(None, "fsdp", "tp"),
        P(None, "tp", "fsdp"),
        P(),
        P(),
        P("fsdp"),
    )
    return jax.shard_map(
        body,
        mesh=mesh,
        in_specs=placed,
        out_specs=placed[:6] + (P(), P(), P()),
        check_vma=False,
    )
```

```python
import functools, math
import jax
import jax.numpy as jnp
from jax import lax
from jax.experimental import pallas as pl
from jax.experimental.pallas import tpu as pltpu
from jax.sharding import PartitionSpec as P

MASKED = -1e30
F32, BF16 = jnp.float32, jnp.bfloat16
EPSILON = 1e-06
SOFT_ONE = 1.442695041
LOG2E = math.log2(math.e)
MESH = pl.DeviceIdType.MESH
HINT = 1
VMEM_LIMIT = 60 * 2**20

def dot(a, b, dims=((1,), (0,))):
    return lax.dot_general(a, b, (dims, ((), ())), preferred_element_type=F32)

def key_range(row_start, rows, prefix, block):
    full = jnp.maximum(row_start + 1, prefix) // block
    stop = (jnp.maximum(row_start + rows, prefix) + block - 1) // block
    return full, stop

def forward_kernel(prefix_ref, order_ref, q_ref, k_ref, v_ref, o_ref, lse_ref, key_rows, value_ext, *, pair, dh, bq, bk):
    length = q_ref.shape[1]
    prefix = prefix_ref[0]
    ext = value_ext.shape[1]
    bound = 0.0
    for h in range(pair):
        rows = slice(h * dh, (h + 1) * dh)
        q, k = q_ref[rows, :].astype(F32), k_ref[rows, :].astype(F32)
        bound = jnp.maximum(bound, jnp.max(jnp.sum(q * q, axis=0)) * jnp.max(jnp.sum(k * k, axis=0)))
        key_rows[h] = k_ref[rows, :].T
        value_ext[h, :dh] = v_ref[rows, :]
        value_ext[h, dh:] = jnp.ones((ext - dh, length), BF16)

    def one_query(shifted, qi, carry):
        start = qi * bq
        here = pl.ds(pl.multiple_of(order_ref[qi] * bq, bq), bq)
        queries = [q_ref[h * dh:(h + 1) * dh, here] for h in range(pair)]
        full, stop = key_range(start, bq, prefix, bk)

        def step(masked, ki, state):
            first = ki * bk
            there = pl.ds(pl.multiple_of(order_ref[ki] * bk, bk), bk)
            if masked:
                rows = first + lax.broadcasted_iota(jnp.int32, (bk, bq), 0)
                cols = start + lax.broadcasted_iota(jnp.int32, (bk, bq), 1)
                allowed = rows <= jnp.maximum(cols, prefix - 1)
            scores = [dot(key_rows[h, there], queries[h]) for h in range(pair)]
            fresh = []
            for h in range(pair):
                s = jnp.where(allowed, scores[h], MASKED) if masked else scores[h]
                if shifted:
                    top, total = state[h]
                    new_top = jnp.maximum(top, jnp.max(s, axis=0, keepdims=True))
                    p = jnp.exp2(s - new_top).astype(BF16)
                    total = total * jnp.exp2(top - new_top) + dot(value_ext[h, :, there], p)
                    fresh.append((new_top, total))
                else:
                    fresh.append(state[h] + dot(value_ext[h, :, there], jnp.exp2(s).astype(BF16)))
            return tuple(fresh)

        zero = jnp.zeros((ext, bq), F32)
        state = tuple((jnp.full((1, bq), MASKED, F32), zero) if shifted else zero for _ in range(pair))
        state = lax.fori_loop(0, full, functools.partial(step, False), state)
        state = lax.fori_loop(full, stop, functools.partial(step, True), state)
        for h in range(pair):
            top, total = state[h] if shifted else (0.0, state[h])
            norm = total[dh:dh + 1]
            o_ref[h * dh:(h + 1) * dh, here] = (total[:dh] / norm).astype(BF16)
            lse_ref[h, :, here] = top + jnp.log2(norm)
        return carry

    small = bound <= 3600.0

    @pl.when(small)
    def _():
        lax.fori_loop(0, length // bq, functools.partial(one_query, False), 0)

    @pl.when(jnp.logical_not(small))
    def _():
        lax.fori_loop(0, length // bq, functools.partial(one_query, True), 0)


def attention_forward(q, k, v, prefix, order, dh, pair=4):
    width, length = q.shape
    heads = width // dh
    pair = min(pair, heads)
    bq = bk = length // order.shape[0]
    ext = dh + 16
    spec = pl.BlockSpec((pair * dh, length), lambda i, p, o: (i, 0))
    return pl.pallas_call(
        functools.partial(forward_kernel, pair=pair, dh=dh, bq=bq, bk=bk),
        grid_spec=pltpu.PrefetchScalarGridSpec(
            num_scalar_prefetch=2, grid=(heads // pair,),
            in_specs=[spec, spec, spec],
            out_specs=[spec, pl.BlockSpec((pair, 1, length), lambda i, p, o: (i, 0, 0))],
            scratch_shapes=[pltpu.VMEM((pair, length, dh), BF16), pltpu.VMEM((pair, ext, length), BF16)],
        ),
        out_shape=[jax.ShapeDtypeStruct((width, length), BF16), jax.ShapeDtypeStruct((heads, 1, length), F32)],
        compiler_params=pltpu.CompilerParams(vmem_limit_bytes=VMEM_LIMIT),
        cost_estimate=pl.CostEstimate(flops=int(HINT * 600 * length * length * heads), bytes_accessed=int(HINT * 8 * width * length), transcendentals=0),
        name="attention_forward",
    )(prefix, order, q, k, v)

def split3(x):
    a = x.astype(BF16)
    r = x - a.astype(F32)
    b = r.astype(BF16)
    c = (r - b.astype(F32)).astype(BF16)
    return a, b, c

def backward_kernel(prefix_ref, order_ref, q_ref, k_ref, v_ref, o_ref, g_ref, lse_ref, scale_ref, dq_ref, dk_ref, dv_ref, fg_ref,
                    key_ext, value_ext, query_ext, grad_ext, dk_acc, dv_acc, *, pair, dh, bq, bk):
    length = q_ref.shape[1]
    prefix = prefix_ref[0]
    pad = key_ext.shape[1] - dh
    index = lax.broadcasted_iota(jnp.int32, (pad, length), 0)
    ones = (index < 3).astype(F32).astype(BF16)

    @pl.when(pl.program_id(0) == 0)
    def _():
        fg_ref[...] = jnp.zeros_like(fg_ref)

    def tail(row):
        high, mid, low = (part.astype(F32) for part in split3(-row))
        rest = jnp.where(index == 1, mid, jnp.where(index == 2, low, 0.0))
        return jnp.where(index == 0, high, rest).astype(BF16)

    for h in range(pair):
        rows = slice(h * dh, (h + 1) * dh)
        g = g_ref[rows, :]
        key_ext[h, :dh] = k_ref[rows, :]
        key_ext[h, dh:] = ones
        value_ext[h, :dh] = v_ref[rows, :]
        value_ext[h, dh:] = ones
        delta = jnp.sum(o_ref[rows, :].astype(F32) * g.astype(F32), axis=0, keepdims=True)
        query_ext[h, :dh] = q_ref[rows, :]
        query_ext[h, dh:] = tail(lse_ref[h])
        grad_ext[h, :dh] = g
        grad_ext[h, dh:] = tail(delta)
        dk_acc[h] = jnp.zeros((dh, length), F32)
        dv_acc[h] = jnp.zeros((dh, length), F32)

    def one_query(qi, carry):
        start = qi * bq
        here = pl.ds(pl.multiple_of(order_ref[qi] * bq, bq), bq)
        full, stop = key_range(start, bq, prefix, bk)

        def step(masked, ki, state):
            first = ki * bk
            there = pl.ds(pl.multiple_of(order_ref[ki] * bk, bk), bk)
            if masked:
                rows = start + lax.broadcasted_iota(jnp.int32, (bq, bk), 0)
                cols = first + lax.broadcasted_iota(jnp.int32, (bq, bk), 1)
                allowed = cols <= jnp.maximum(rows, prefix - 1)
            fresh = []
            s = [dot(query_ext[h, :, here], key_ext[h, :, there], ((0,), (0,))) for h in range(pair)]
            gp = [dot(grad_ext[h, :, here], value_ext[h, :, there], ((0,), (0,))) for h in range(pair)]
            for h in range(pair):
                x = jnp.where(allowed, s[h], MASKED) if masked else s[h]
                p = jnp.exp2(x)
                ds = (p * gp[h]).astype(BF16)
                rows = slice(h * dh, (h + 1) * dh)
                dv_acc[h, :, there] += dot(g_ref[rows, here], p.astype(BF16))
                dk_acc[h, :, there] += dot(q_ref[rows, here], ds)
                fresh.append(state[h] + dot(ds, k_ref[rows, there], ((1,), (1,))))
            return tuple(fresh)

        state = tuple(jnp.zeros((bq, dh), F32) for _ in range(pair))
        state = lax.fori_loop(0, full, functools.partial(step, False), state)
        state = lax.fori_loop(full, stop, functools.partial(step, True), state)
        for h in range(pair):
            rows = slice(h * dh, (h + 1) * dh)
            dq = state[h].T
            prod = dq * q_ref[rows, here].astype(F32)
            part = prod[:, :128]
            for c in range(1, bq // 128):
                part = part + prod[:, c * 128:(c + 1) * 128]
            fg_ref[...] += part
            dq_ref[rows, here] = (dq * scale_ref[...]).astype(BF16)
        return carry

    lax.fori_loop(0, length // bq, one_query, 0)
    for h in range(pair):
        rows = slice(h * dh, (h + 1) * dh)
        dk_ref[rows, :] = (dk_acc[h] * math.log(2.0)).astype(BF16)
        dv_ref[rows, :] = dv_acc[h].astype(BF16)


def attention_backward(q, k, v, o, g, lse, factor, prefix, order, dh, base=0, width=None, pair=2):
    full, length = q.shape
    width = width or full
    heads = width // dh
    pair = min(pair, heads)
    bq = bk = length // order.shape[0]
    ext = dh + 16
    spec = pl.BlockSpec((pair * dh, length), lambda i, p, o: (i, 0))
    skip = base // (pair * dh)
    source = pl.BlockSpec((pair * dh, length), lambda i, p, o: (i + skip, 0))
    wide = jax.ShapeDtypeStruct((width, length), BF16)
    return pl.pallas_call(
        functools.partial(backward_kernel, pair=pair, dh=dh, bq=bq, bk=bk),
        grid_spec=pltpu.PrefetchScalarGridSpec(
            num_scalar_prefetch=2, grid=(heads // pair,),
            in_specs=[source] * 5 + [pl.BlockSpec((pair, 1, length), lambda i, p, o: (i + skip, 0, 0)), pl.BlockSpec((dh, 1), lambda i, p, o: (0, 0))],
            out_specs=[spec] * 3 + [pl.BlockSpec((dh, 128), lambda i, p, o: (0, 0))],
            scratch_shapes=[
                pltpu.VMEM((pair, ext, length), BF16),
                pltpu.VMEM((pair, ext, length), BF16),
                pltpu.VMEM((pair, ext, length), BF16),
                pltpu.VMEM((pair, ext, length), BF16),
                pltpu.VMEM((pair, dh, length), F32),
                pltpu.VMEM((pair, dh, length), F32)],
        ),
        out_shape=[wide] * 3 + [jax.ShapeDtypeStruct((dh, 128), F32)],
        compiler_params=pltpu.CompilerParams(vmem_limit_bytes=VMEM_LIMIT),
        cost_estimate=pl.CostEstimate(flops=int(HINT * 1600 * length * length * heads), bytes_accessed=int(HINT * 16 * width * length), transcendentals=0),
        name="attention_backward",
    )(prefix, order, q, k, v, o, g, lse, factor.reshape(dh, 1))


def rms(x):
    inv = lax.rsqrt(jnp.mean(x * x, axis=-1, keepdims=True) + EPSILON)
    return x * inv, inv


def rms_back(normed, inv, gain, grad):
    scaled = grad * gain
    out = inv * (scaled - normed * jnp.mean(scaled * normed, axis=-1, keepdims=True))
    return out, jnp.sum(grad * normed, axis=0)


def ein(spec, *args):
    return jnp.einsum(spec, *args, preferred_element_type=F32)


def gather_kernel(pieces, pairs, outer, ring, shard_ref, block_ref, *refs):
    outs = [refs[2 * m:2 * m + 2] for m in range(pairs)]
    got_ref = refs[2 * pairs]
    send, recv, local = refs[2 * pairs + 1:]
    f, t = lax.axis_index("fsdp"), lax.axis_index("tp")
    zz, yy = f // 2, f % 2
    across = {"tp": lax.rem(t + ring, 2 * ring)}
    beside = {"fsdp": zz * 2 + 1 - yy}
    along = [{"fsdp": lax.rem(zz + k, outer) * 2 + yy} for k in range(1, outer)]
    peers = along + [across, beside]
    barrier = pltpu.get_barrier_semaphore()
    for peer in peers:
        pl.semaphore_signal(barrier, inc=1, device_id=peer, device_id_type=MESH)
    pl.semaphore_wait(barrier, len(peers))
    used = [0]

    def copy(src, dst, peer):
        slot = used[0]
        used[0] += 1
        return pltpu.make_async_remote_copy(
            src_ref=src, dst_ref=dst, send_sem=send.at[slot], recv_sem=recv.at[slot],
            device_id=peer, device_id_type=MESH,
        )

    count = len(pieces)
    chunks = 4
    step = block_ref.shape[0] // chunks
    blocks = [
        copy(block_ref.at[pl.ds(i * step, step)], got_ref.at[pl.ds(i * step, step)], across)
        for i in range(chunks)
    ]
    own, first, second, third = [], [], [], []
    for i, (m, low, rows, route) in enumerate(pieces):
        part = pl.ds(low, rows)
        w = [out.at[:, :, part] for out in outs[m]]
        src = shard_ref.at[m, part]
        own.append(pltpu.make_async_copy(src, w[0].at[zz, yy], local.at[i]))
        first.append([copy(src, w[0].at[zz, yy], peer) for peer in along])
        if route:
            second.append([copy(w[0].at[:, yy], w[0].at[:, yy], beside)])
            third.append([copy(w[0], w[1], across)])
        else:
            second.append([copy(w[0].at[:, yy], w[1].at[:, yy], across)])
            third.append([copy(w[s].at[:, yy], w[s].at[:, yy], beside) for s in range(2)])

    def begin(i):
        own[i].start()
        for c in first[i]:
            c.start()

    ahead = 3
    for i in range(min(ahead, count)):
        begin(i)
    started = 0
    for b in blocks[:2]:
        b.start()
    started = 2
    for i in range(count + 2):
        if i < count:
            own[i].wait()
            for c in first[i]:
                c.wait_recv()
            for c in second[i]:
                c.start()
            if i + ahead < count:
                begin(i + ahead)
            if started < chunks:
                blocks[started].start()
                started += 1
        if 0 <= i - 1 < count:
            for c in second[i - 1]:
                c.wait_recv()
            for c in third[i - 1]:
                c.start()
        if 0 <= i - 2 < count:
            for c in third[i - 2]:
                c.wait_recv()
    for b in blocks[started:]:
        b.start()
    for i in range(count):
        for c in first[i] + second[i] + third[i]:
            c.wait_send()
    for b in blocks:
        b.wait()


def pieces_of(pairs, rows):
    half = rows // 32 * 16
    return tuple(
        (m, low, size, m_part) for m in range(pairs) for m_part, (low, size) in enumerate(((0, half), (half, rows - half)))
    )


def gather_call(shards, block, pieces, fsdp, ring):
    pairs, rows, w = shards.shape
    outer = fsdp // 2
    slots = 4 + len(pieces) * (outer + 2)
    any_spec = pl.BlockSpec(memory_space=pl.ANY)
    got = pl.pallas_call(
        functools.partial(gather_kernel, pieces, pairs, outer, ring),
        out_shape=[jax.ShapeDtypeStruct((outer, 2, rows, w), BF16)] * (2 * pairs)
        + [jax.ShapeDtypeStruct(block.shape, block.dtype)],
        in_specs=[any_spec] * 2,
        out_specs=[any_spec] * (2 * pairs + 1),
        scratch_shapes=[
            pltpu.SemaphoreType.DMA((slots,)),
            pltpu.SemaphoreType.DMA((slots,)),
            pltpu.SemaphoreType.DMA((len(pieces),)),
        ],
        compiler_params=pltpu.CompilerParams(collective_id=0, has_side_effects=True),
        name="gather_weights",
    )(shards, block)
    return [a.reshape(outer * 2 * rows, w) for a in got[:-1]], got[-1]


class Plan:
    def __init__(self, seqs, tp, fsdp, rows):
        self.seqs, self.tp, self.ring, self.fsdp = seqs, tp, tp // seqs, fsdp
        self.same_member = [[s * self.ring + r for s in range(seqs)] for r in range(self.ring)]
        self.same_seq = [[s * self.ring + r for r in range(self.ring)] for s in range(seqs)]
        self.fast = seqs == 2 and self.ring == 2 and fsdp % 2 == 0 and rows % 32 == 0
        t = lax.axis_index("tp")
        self.seq, self.member = t // self.ring, lax.rem(t, self.ring)

    def across(self, a):
        n = self.tp
        return lax.ppermute(a, "tp", [(t, (t + self.ring) % n) for t in range(n)])

    def core(self, a):
        return lax.ppermute(a, "tp", [(t, t ^ 1) for t in range(self.tp)])

    def pick(self, blocks, index):
        return lax.dynamic_index_in_dim(blocks, index, 0, keepdims=False)

    def order(self, own, other):
        first = self.seq == 0
        return jnp.concatenate([jnp.where(first, own, other), jnp.where(first, other, own)])

    def swap(self, blocks):
        if self.seqs == 2:
            other = self.across(self.pick(blocks, 1 - self.seq).astype(BF16))
            return self.order(self.pick(blocks, self.seq), other.astype(F32))
        got = lax.all_to_all(
            blocks.astype(BF16), "tp", 0, 0, tiled=True, axis_index_groups=self.same_member
        )
        return got.reshape(-1, got.shape[-1]).astype(F32)

    def unswap(self, rows):
        blocks = rows.reshape(self.seqs, -1, rows.shape[-1])
        return self.swap(blocks).reshape(blocks.shape)

    def whole(self, rows):
        if self.fast:
            return jnp.concatenate([rows, self.core(rows)])
        cut = rows.reshape(self.seqs, -1, rows.shape[-1])
        got = lax.all_gather(cut, "tp", axis=1, axis_index_groups=self.same_seq)
        return got.reshape(-1, rows.shape[-1])

    def share(self, full):
        if self.fast:
            own = full.shape[0] // 2
            return full[:own].astype(F32) + self.core(full[own:].astype(BF16)).astype(F32)
        cut = full.astype(BF16).reshape(self.seqs, self.ring, -1, full.shape[-1])
        got = lax.psum_scatter(cut, "tp", scatter_dimension=1, axis_index_groups=self.same_seq)
        return got.reshape(-1, full.shape[-1]).astype(F32)

    def blocks(self, length):
        if self.fast:
            j = jnp.arange(self.tp, dtype=jnp.int32)
            apart = (j % self.ring != self.member).astype(jnp.int32)
            return apart * self.seqs + j // self.ring
        return jnp.arange(max(1, length // 512), dtype=jnp.int32)

    def gather_heads(self, shards):
        rows = lax.all_gather(shards, "fsdp", axis=1, tiled=True)
        if self.fast:
            return jnp.stack([rows, self.across(rows)])
        return lax.all_gather(rows, "tp", axis_index_groups=self.same_member)

    def join(self, every):
        r, s, m, d, w = every.shape
        return every.transpose(2, 3, 0, 1, 4).reshape(m, d, r * s * w)

    def gather_full(self, shards):
        part = self.gather_heads(shards)
        if self.fast:
            return self.join(jnp.stack([part, self.core(part)]))
        return self.join(lax.all_gather(part, "tp", axis_index_groups=self.same_seq))

    def scatter_heads(self, grads):
        if self.fast:
            other = self.across(grads[1].astype(BF16))
            mine = (grads[0].astype(F32) + other.astype(F32)).astype(BF16)
        else:
            mine = lax.psum_scatter(
                grads.astype(BF16), "tp", scatter_dimension=0, axis_index_groups=self.same_member
            )
        return lax.psum_scatter(mine, "fsdp", scatter_dimension=1, tiled=True).astype(F32)

    def scatter_full(self, grads):
        m, d, cols = grads.shape
        if self.fast:
            half = cols // 2
            other = self.core(grads[:, :, half:].astype(BF16))
            mine = grads[:, :, :half].astype(F32) + other.astype(F32)
            mine = mine.astype(BF16).reshape(m, d, self.seqs, -1).transpose(2, 0, 1, 3)
        else:
            cut = grads.astype(BF16).reshape(m, d, self.ring, self.seqs, -1).transpose(2, 3, 0, 1, 4)
            mine = lax.psum_scatter(cut, "tp", scatter_dimension=0, axis_index_groups=self.same_seq)
        return self.scatter_heads(mine)


def layer_forward(plan, x, prefix, order, qkv, out_t, up, down_t, gains, factor):
    dh = factor.shape[0]
    normed, inv = rms(x)
    h = plan.whole((normed * gains[0]).astype(BF16))
    seqs, d, w = out_t.shape
    raw = [ein("sdc,td->sct", qkv[c], h).reshape(seqs * w, -1) for c in range(3)]
    scale = jnp.tile(factor * LOG2E, seqs * w // dh)[:, None]
    q, k, v = (raw[0] * scale).astype(BF16), raw[1].astype(BF16), raw[2].astype(BF16)
    att, lse = attention_forward(q, k, v, prefix, order, dh)
    middle = x + plan.share(ein("sct,sdc->td", att.reshape(seqs, w, -1), out_t))
    normed_m, inv_m = rms(middle)
    h_m = (normed_m * gains[1]).astype(BF16)
    pre = ein("td,df->tf", h_m, up)
    hidden = jax.nn.silu(pre).astype(BF16)
    result = middle + ein("tf,df->td", hidden, down_t)
    return result, (x, inv, h, q, k, v, att, lse, middle, inv_m, h_m, pre, hidden)


def layer_backward(plan, g, saved, prefix, order, qkv, out_t, up, down_t, gains, factor):
    x, inv, h, q, k, v, att, lse, middle, inv_m, h_m, pre, hidden = saved
    dh = factor.shape[0]
    seqs, d, w = out_t.shape
    length = h.shape[0]
    g_low = g.astype(BF16)
    down_grad = ein("td,tf->df", g_low, hidden)
    g_hidden = ein("td,df->tf", g_low, down_t)
    sig = jax.nn.sigmoid(pre)
    g_pre = (g_hidden * sig * (1.0 + pre * (1.0 - sig))).astype(BF16)
    up_grad = ein("td,tf->df", h_m, g_pre)
    mlp_grads = plan.scatter_full(jnp.stack([up_grad, down_grad]))
    g_hm = ein("tf,df->td", g_pre, up)
    back_m, gain_m = rms_back(middle * inv_m, inv_m, gains[1], g_hm)
    g_mid = g + back_m
    g_all = plan.whole(g_mid.astype(BF16))
    att3 = att.reshape(seqs, w, length)
    out_grad = plan.scatter_heads(ein("td,sct->sdc", g_all, att3)[:, None])[0]
    g_att = ein("td,sdc->sct", g_all, out_t).astype(BF16).reshape(seqs * w, length)
    dq, dk, dv, fg = attention_backward(q, k, v, att, g_att, lse, factor, prefix, order, dh)
    factor_grad = jnp.sum(fg, axis=1) / (factor * LOG2E)
    parts = [a.reshape(seqs, w, length) for a in (dq, dk, dv)]
    qkv_grad = plan.scatter_heads(jnp.stack([ein("td,sct->sdc", h, a) for a in parts], axis=1))
    g_ha = plan.share(sum(ein("sct,sdc->td", a, b) for a, b in zip(parts, qkv)))
    back_a, gain_a = rms_back(x * inv, inv, gains[0], g_ha)
    return g_mid + back_a, (qkv_grad, out_grad.T, mlp_grads[0], mlp_grads[1].T, gain_a, gain_m, factor_grad)


TN, NT, TT = ((0,), (0,)), ((1,), (1,)), ((0,), (1,))
ONE = pl.Buffered(1)


def cost(flops, nbytes):
    return pl.CostEstimate(flops=int(flops * HINT), bytes_accessed=int(nbytes * HINT), transcendentals=0)


def params(mib=60):
    return pltpu.CompilerParams(vmem_limit_bytes=mib * 2**20)


def fixed(shape):
    return pl.BlockSpec(shape, lambda *a: (0,) * len(shape), pipeline_mode=ONE)


def weight(w, lanes=None):
    stack, index = w if isinstance(w, tuple) else (w, None)
    shape = (stack.shape[-2], lanes or stack.shape[-1])
    if index is None:
        return fixed(shape)
    return pl.BlockSpec((None,) + shape, lambda *a: (index, 0, 0), pipeline_mode=ONE)


def plain(weights):
    return [w[0] if isinstance(w, tuple) else w for w in weights]


def shape_of(shape, dtype=BF16):
    return jax.ShapeDtypeStruct(shape, dtype)


def inverse_rms(x):
    return lax.rsqrt(jnp.mean(x * x, axis=-1, keepdims=True) + EPSILON)


def eight(x):
    return jnp.sum(x.reshape(-1, 8, x.shape[-1]), axis=0)


def join_lanes(dst, refs, low, high):
    width = high - low
    for i, ref in enumerate(refs):
        dst[:, i * width:(i + 1) * width] = ref[:, low:high]


def core_of():
    t = lax.axis_index("tp")
    return {"tp": t + 1 - 2 * lax.rem(t, 2)}


def pushes(send, recv, core):
    def push(src, dst, slot):
        return pltpu.make_async_remote_copy(
            src_ref=src, dst_ref=dst, send_sem=send.at[slot], recv_sem=recv.at[slot],
            device_id=core, device_id_type=MESH,
        )

    return push


def greet(core):
    barrier = pltpu.get_barrier_semaphore()
    pl.semaphore_signal(barrier, inc=1, device_id=core, device_id_type=MESH)
    pl.semaphore_wait(barrier, 1)


def stack_index(weights):
    return tuple(a[1] if isinstance(a, tuple) else None for a in weights)


def entry(ref, k):
    return ref if k is None else ref.at[k]


def stages(steps):
    starts = [sum(steps[:n]) for n in range(len(steps))]

    def at(n, make):
        return lambda i: make(jnp.clip(i - starts[n], 0, steps[n] - 1))

    return at


ANY = pl.BlockSpec(memory_space=pl.ANY)


def project_kernel(w, low, steps, index, x_ref, gain_ref, scale_ref, *refs):
    weights, refs = refs[:4], refs[4:]
    own_ref, other_ref, q_ref, k_ref, v_ref = refs[:5]
    own, other, qk, vo, load, send, recv = refs[5:]
    i = pl.program_id(0)
    rows_steps, half, _ = steps
    bt, ba = x_ref.shape[0], q_ref.shape[1]
    core = core_of()
    push = pushes(send, recv, core)

    def loads():
        copies = [pltpu.make_async_copy(entry(weights[s], index[s]), qk.at[s], load.at[s]) for s in range(2)]
        for s in range(2):
            src = entry(weights[2 + s], index[2 + s]).at[:, pl.ds(0, low)]
            copies.append(pltpu.make_async_copy(src, vo.at[s], load.at[2 + s]))
        return copies

    def push_rows(k):
        part = pl.ds(pl.multiple_of(k * bt, bt), bt)
        return push(own.at[part], other.at[part], k)

    @pl.when(i == 0)
    def _():
        for c in loads():
            c.start()
        greet(core)

    @pl.when(i < rows_steps)
    def _():
        x = x_ref[...]
        h = (x * inverse_rms(x) * gain_ref[...]).astype(BF16)
        own[pl.ds(pl.multiple_of(i * bt, bt), bt)] = h
        own_ref[...] = h
        push_rows(i).start()

    at = i - rows_steps

    @pl.when(at == 0)
    def _():
        for c in loads():
            c.wait()

    @pl.when(at == half)
    def _():
        for k in range(rows_steps):
            push_rows(k).wait()

    def project(h):
        for s in range(2):
            rows = slice(s * w, (s + 1) * w)
            both = dot(qk[s], h, TT)
            q_ref[rows] = (both[:w] * scale_ref[rows]).astype(BF16)
            k_ref[rows] = both[w:].astype(BF16)
            v_ref[rows] = dot(vo[s, :, :w], h, TT).astype(BF16)

    @pl.when((at >= 0) & (at < half))
    def _():
        project(own[pl.ds(pl.multiple_of(at * ba, ba), ba)])

    @pl.when(at >= half)
    def _():
        h = other[pl.ds(pl.multiple_of((at - half) * ba, ba), ba)]
        other_ref[...] = h
        project(h)


def project(x, gain, qk, vo, scale, call):
    rows, d = x.shape
    w2 = plain(qk)[0].shape[-1]
    w = w2 // 2
    low = -(-w // 128) * 128
    bt, ba = 256, 512
    half = rows // ba
    steps = (rows // bt, half, half)
    row = pl.BlockSpec((bt, d), lambda i: (jnp.minimum(i, steps[0] - 1), 0))
    wide = pl.BlockSpec((w2, ba), lambda i: (0, jnp.clip(i - steps[0], 0, 2 * half - 1)))
    tall = pl.BlockSpec((ba, d), lambda i: (jnp.clip(i - steps[0] - half, 0, half - 1), 0))
    weights = (*qk, *vo)
    return pl.pallas_call(
        functools.partial(project_kernel, w, low, steps, stack_index(weights)),
        grid=(sum(steps),),
        in_specs=[row, fixed((1, d)), fixed((w2, 1))] + [ANY] * 4,
        out_specs=[row, tall] + [wide] * 3,
        out_shape=[shape_of((rows, d))] * 2 + [shape_of((w2, 2 * rows))] * 3,
        scratch_shapes=[
            pltpu.VMEM((rows, d), BF16), pltpu.VMEM((rows, d), BF16),
            pltpu.VMEM((2, d, w2), BF16), pltpu.VMEM((2, d, low), BF16),
            pltpu.SemaphoreType.DMA((4,)), pltpu.SemaphoreType.DMA((steps[0],)), pltpu.SemaphoreType.DMA((steps[0],)),
        ],
        compiler_params=pltpu.CompilerParams(vmem_limit_bytes=VMEM_LIMIT, collective_id=call, has_side_effects=True),
        cost_estimate=cost(4 * rows * d * 3 * w2, 12 * rows * d),
        name="project",
    )(x, gain, scale, *plain(weights))


def middle_kernel(w, low, steps, index, x_ref, gm_ref, att_any, *refs):
    weights, refs = refs[:4], refs[4:]
    mid_ref, pre_ref, res_ref, up_out, down_out, out_out = refs[:6]
    (up_mat, down_mat, out_mat, blocks, vo_side, att, part, got, load, store, send, recv) = refs[6:]
    i = pl.program_id(0)
    far, rows_steps = steps
    bt = x_ref.shape[0]
    ba = part.shape[0] // far
    rows = part.shape[0]
    core = core_of()
    push = pushes(send, recv, core)

    def loads():
        copies = [pltpu.make_async_copy(att_any, att, load.at[0])]
        for s in range(2):
            src = entry(weights[s], index[s]).at[:, pl.ds(low, vo_side.shape[2])]
            copies.append(pltpu.make_async_copy(src, vo_side.at[s], load.at[1 + s]))
        for s in range(2):
            copies.append(pltpu.make_async_copy(entry(weights[2 + s], index[2 + s]), blocks.at[s], load.at[3 + s]))
        return copies

    def stores():
        pairs = ((up_mat, up_out), (down_mat, down_out), (out_mat, out_out))
        return [pltpu.make_async_copy(src, dst, store.at[n]) for n, (src, dst) in enumerate(pairs)]

    def push_block(s):
        return push(blocks.at[s], blocks.at[2 + s], s)

    def push_part(k):
        here = pl.ds(pl.multiple_of(k * ba, ba), ba)
        return push(part.at[here], got.at[here], 2 + k)

    @pl.when(i == 0)
    def _():
        copies = loads()
        for c in copies:
            c.start()
        greet(core)
        for c in copies[:3]:
            c.wait()
        for s in range(2):
            out_mat[:, s * w:(s + 1) * w] = vo_side[s, :, 2 * w - low - w:2 * w - low]
        for s in range(2):
            copies[3 + s].wait()
            push_block(s).start()

    @pl.when(i < far)
    def _():
        here = pl.ds(pl.multiple_of(i * ba, ba), ba)
        cols = pl.ds(pl.multiple_of(rows + i * ba, ba), ba)
        part[here] = dot(att[:, cols], out_mat[...], TT).astype(BF16)
        push_part(i).start()

    at = i - far

    @pl.when(at == 0)
    def _():
        for s in range(2):
            push_block(s).wait()
        for b in range(4):
            up_mat[:, b * w:(b + 1) * w] = blocks[b, :, 0:w]
            down_mat[:, b * w:(b + 1) * w] = blocks[b, :, w:2 * w]
        for c in stores():
            c.start()

    for k in range(far):
        @pl.when(at == k * (ba // bt))
        def _():
            push_part(k).wait()

    @pl.when(at >= 0)
    def _():
        here = pl.ds(pl.multiple_of(at * bt, bt), bt)
        mid = x_ref[...] + got[here].astype(F32) + dot(att[:, here], out_mat[...], TT)
        mid_ref[...] = mid
        h_m = (mid * inverse_rms(mid) * gm_ref[...]).astype(BF16)
        pre = dot(h_m, up_mat[...])
        pre_ref[...] = pre
        hidden = (pre / (1.0 + jnp.exp(-pre))).astype(BF16)
        res_ref[...] = mid + dot(hidden, down_mat[...], NT)

    @pl.when(at == rows_steps - 1)
    def _():
        for c in stores():
            c.wait()


def middle_call(x, att, gain_m, vo, un, call):
    rows, d = x.shape
    w2 = plain(vo)[0].shape[-1]
    w, ff = w2 // 2, 2 * w2
    low = w // 128 * 128
    bt, ba = 256, 512
    steps = (rows // ba, rows // bt)
    row = pl.BlockSpec((bt, d), lambda i: (jnp.maximum(i - steps[0], 0), 0))
    wide = pl.BlockSpec((bt, ff), lambda i: (jnp.maximum(i - steps[0], 0), 0))
    weights = (*vo, *un)
    mats = [(d, ff), (d, ff), (d, w2)]
    slots = 2 + steps[0]
    return pl.pallas_call(
        functools.partial(middle_kernel, w, low, steps, stack_index(weights)),
        grid=(sum(steps),),
        in_specs=[row, fixed((1, d))] + [ANY] * 5,
        out_specs=[row, wide, row] + [ANY] * 3,
        out_shape=[shape_of((rows, d), F32), shape_of((rows, ff), F32), shape_of((rows, d), F32)] + [shape_of(m) for m in mats],
        scratch_shapes=[pltpu.VMEM(m, BF16) for m in mats]
        + [pltpu.VMEM((4, d, w2), BF16), pltpu.VMEM((2, d, w2 - low), BF16), pltpu.VMEM(att.shape, BF16)]
        + [pltpu.VMEM((rows, d), BF16)] * 2
        + [pltpu.SemaphoreType.DMA((5,)), pltpu.SemaphoreType.DMA((3,)), pltpu.SemaphoreType.DMA((slots,)), pltpu.SemaphoreType.DMA((slots,))],
        compiler_params=pltpu.CompilerParams(vmem_limit_bytes=VMEM_LIMIT, collective_id=call, has_side_effects=True),
        cost_estimate=cost(2 * rows * d * (2 * w2 + 2 * ff), 30 * rows * d),
        name="middle",
    )(x, gain_m, att, *plain(weights))


def mlp_back_kernel(w, steps, g_ref, mid_ref, pre_ref, gm_ref, att_any, *refs):
    mats, refs = refs[:3], refs[3:]
    g_mid_ref, gain_ref, g_att_ref, o0, o1 = refs[:5]
    (up_mat, down_mat, out_mat, g_all, hid_all, hm_all, gpre_all, low_own, low_other, blocks, got, att,
     load, send, recv) = refs[5:]
    i = pl.program_id(0)
    rows_steps, grad_steps, att_steps, _ = steps
    bt, bd, ba = g_ref.shape[0], o0.shape[0], g_att_ref.shape[1]
    core = core_of()
    push = pushes(send, recv, core)

    def loads():
        pairs = (*zip(mats, (up_mat, down_mat, out_mat)), (att_any, att))
        return [pltpu.make_async_copy(src, dst, load.at[n]) for n, (src, dst) in enumerate(pairs)]

    def push_rows(k):
        part = pl.ds(pl.multiple_of(k * bt, bt), bt)
        return push(low_own.at[part], low_other.at[part], k)

    def push_block(c, s):
        part = pl.ds(pl.multiple_of(c * bd, bd), bd)
        return push(blocks.at[2 + s, part], got.at[s, part], rows_steps + 2 * c + s)

    @pl.when(i == 0)
    def _():
        copies = loads()
        for c in copies:
            c.start()
        gain_ref[...] = jnp.zeros_like(gain_ref)
        greet(core)
        for c in copies[:2]:
            c.wait()

    @pl.when(i < rows_steps)
    def _():
        here = pl.ds(pl.multiple_of(i * bt, bt), bt)
        g = g_ref[...]
        g_low = g.astype(BF16)
        g_all[here] = g_low
        pre = pre_ref[...]
        sig = 1.0 / (1.0 + jnp.exp(-pre))
        hid_all[here] = (pre * sig).astype(BF16)
        g_hidden = dot(g_low, down_mat[...])
        g_pre = (g_hidden * sig * (1.0 + pre * (1.0 - sig))).astype(BF16)
        gpre_all[here] = g_pre
        mid = mid_ref[...]
        inv = inverse_rms(mid)
        normed = mid * inv
        gain = gm_ref[...]
        hm_all[here] = (normed * gain).astype(BF16)
        g_hm = dot(g_pre, up_mat[...], NT)
        gain_ref[...] += eight(g_hm * normed)
        scaled = g_hm * gain
        g_mid = g + inv * (scaled - normed * jnp.mean(scaled * normed, axis=-1, keepdims=True))
        g_mid_ref[...] = g_mid
        low_own[here] = g_mid.astype(BF16)
        push_rows(i).start()

    at = i - rows_steps

    @pl.when((at >= 0) & (at < grad_steps))
    def _():
        cols = pl.ds(pl.multiple_of(at * bd, bd), bd)
        up = dot(hm_all[:, cols], gpre_all[...], TN).astype(BF16)
        down = dot(g_all[:, cols], hid_all[...], TN).astype(BF16)
        for b in range(4):
            blocks[b, cols, 0:w] = up[:, b * w:(b + 1) * w]
            blocks[b, cols, w:2 * w] = down[:, b * w:(b + 1) * w]
        for s in range(2):
            push_block(at, s).start()

    to = at - grad_steps

    @pl.when(to == 0)
    def _():
        loads()[2].wait()

    half = att_steps // 2

    @pl.when((to >= 0) & (to < half))
    def _():
        here = pl.ds(pl.multiple_of(to * ba, ba), ba)
        g_att_ref[...] = dot(out_mat[...], low_own[here], TT).astype(BF16)

    @pl.when(to == half)
    def _():
        for k in range(rows_steps):
            push_rows(k).wait()

    @pl.when((to >= half) & (to < att_steps))
    def _():
        here = pl.ds(pl.multiple_of((to - half) * ba, ba), ba)
        g_att_ref[...] = dot(out_mat[...], low_other[here], TT).astype(BF16)

    last = to - att_steps

    @pl.when(last == 0)
    def _():
        loads()[3].wait()

    @pl.when(last >= 0)
    def _():
        cols = pl.ds(pl.multiple_of(last * bd, bd), bd)
        rows = low_own.shape[0]
        grad = dot(low_own[:, cols], att[:, :rows], TT) + dot(low_other[:, cols], att[:, rows:], TT)
        grad = grad.astype(BF16)
        for s, out in enumerate((o0, o1)):
            push_block(last, s).wait()
            out[:, :2 * w] = (blocks[s, cols].astype(F32) + got[s, cols].astype(F32)).astype(BF16)
            out[:, 2 * w:3 * w] = grad[:, s * w:(s + 1) * w]
            out[:, 3 * w:] = jnp.zeros((bd, out.shape[1] - 3 * w), BF16)


def mlp_back(g, mid, pre, gain, att, mats, width, call):
    rows, d = g.shape
    ff = pre.shape[1]
    w2 = att.shape[0]
    w = w2 // 2
    bt, bd, ba = 256, 256, 512
    steps = (rows // bt, d // bd, 2 * rows // ba, d // bd)
    at = stages(steps)
    row = pl.BlockSpec((bt, d), at(0, lambda k: (k, 0)))
    wide = pl.BlockSpec((bt, ff), at(0, lambda k: (k, 0)))
    block = pl.BlockSpec((bd, width), at(3, lambda k: (k, 0)))
    slots = steps[0] + 2 * steps[1]
    return pl.pallas_call(
        functools.partial(mlp_back_kernel, w, steps),
        grid=(sum(steps),),
        in_specs=[row, row, wide, fixed((1, d))] + [ANY] * 4,
        out_specs=[row, fixed((8, d)), pl.BlockSpec((w2, ba), at(2, lambda k: (0, k))), block, block],
        out_shape=[shape_of((rows, d), F32), shape_of((8, d), F32), shape_of((w2, 2 * rows))] + [shape_of((d, width))] * 2,
        scratch_shapes=[pltpu.VMEM((d, ff), BF16)] * 2
        + [pltpu.VMEM((d, w2), BF16)]
        + [pltpu.VMEM((rows, d), BF16), pltpu.VMEM((rows, ff), BF16)] * 2
        + [pltpu.VMEM((rows, d), BF16)] * 2
        + [pltpu.VMEM((4, d, w2), BF16), pltpu.VMEM((2, d, w2), BF16)]
        + [pltpu.VMEM(att.shape, BF16)]
        + [pltpu.SemaphoreType.DMA((4,)), pltpu.SemaphoreType.DMA((slots,)), pltpu.SemaphoreType.DMA((slots,))],
        compiler_params=pltpu.CompilerParams(vmem_limit_bytes=62 * 2**20, collective_id=call, has_side_effects=True),
        cost_estimate=cost(8 * rows * d * ff + 8 * rows * d * w2, 40 * rows * d),
        name="mlp_back",
    )(g, mid, pre, gain, att, *mats)


def weight_grad_kernel(w, own_ref, other_ref, dq_ref, dk_ref, dv_ref, *refs):
    out, stacked = refs[-2:]
    half = own_ref.shape[0]

    @pl.when(pl.program_id(0) == 0)
    def _():
        for j, ref in enumerate((dq_ref, dk_ref, dv_ref)):
            stacked[j * w:(j + 1) * w, :] = ref[...]

    grad = dot(own_ref[...], stacked[:, :half], TT) + dot(other_ref[...], stacked[:, half:], TT)
    if len(refs) == 3:
        grad = grad + refs[0][:, :3 * w].astype(F32)
    out[:, :3 * w] = grad.astype(BF16)
    out[:, 3 * w:] = jnp.zeros((out.shape[0], out.shape[1] - 3 * w), BF16)


def weight_grad(own, other, dq, dk, dv, width, got=None):
    rows, d = own.shape
    w = dq.shape[0]
    bd = 256
    col = pl.BlockSpec((rows, bd), lambda i: (0, i))
    flat = pl.BlockSpec((bd, width), lambda i: (i, 0))
    extra = [] if got is None else [got]
    return pl.pallas_call(
        functools.partial(weight_grad_kernel, w),
        grid=(d // bd,),
        in_specs=[col, col] + [fixed(dq.shape)] * 3 + [flat] * len(extra),
        out_specs=flat,
        out_shape=shape_of((d, width)),
        scratch_shapes=[pltpu.VMEM((3 * w, 2 * rows), BF16)],
        compiler_params=params(),
        cost_estimate=cost(12 * rows * d * w, 12 * rows * d),
        name="weight_grad",
    )(own, other, dq, dk, dv, *extra)


def input_sum(w, grads, qk, vo):
    total = None
    for s in range(2):
        dq, dk, dv = grads[3 * s:3 * s + 3]
        both = jnp.concatenate([dq[...], dk[...]], axis=0)
        part = dot(both, qk[s][...], TT) + dot(dv[...], vo[s][:, :w], TT)
        total = part if total is None else total + part
    return total


def input_other_kernel(w, *refs):
    refs, out_ref = refs[:-1], refs[-1]
    out_ref[...] = input_sum(w, refs[:6], refs[6:8], refs[8:10]).astype(BF16)


def input_other(grads, qk, vo):
    w, length = grads[0].shape
    d, w2 = plain(qk)[0].shape[-2:]
    bt = 512
    steps = length // 2 // bt
    col = pl.BlockSpec((w, bt), lambda i: (0, i + steps))
    return pl.pallas_call(
        functools.partial(input_other_kernel, w),
        grid=(steps,),
        in_specs=[col] * 6 + [weight(a) for a in (*qk, *vo)],
        out_specs=pl.BlockSpec((bt, d), lambda i: (i, 0)),
        out_shape=shape_of((length // 2, d)),
        compiler_params=params(),
        cost_estimate=cost(3 * length * d * w2, 4 * length * d),
        name="input_other",
    )(*grads, *plain(qk), *plain(vo))


def input_own_kernel(w, *refs):
    grads, refs = refs[:6], refs[6:]
    got_ref, x_ref, g_ref, gain_ref, qk0, qk1, vo0, vo1, out_ref, sum_ref = refs

    @pl.when(pl.program_id(0) == 0)
    def _():
        sum_ref[...] = jnp.zeros_like(sum_ref)

    g_ha = input_sum(w, grads, (qk0, qk1), (vo0, vo1)) + got_ref[...].astype(F32)
    x = x_ref[...]
    inv = inverse_rms(x)
    normed = x * inv
    sum_ref[...] += eight(g_ha * normed)
    scaled = g_ha * gain_ref[...]
    out_ref[...] = g_ref[...] + inv * (scaled - normed * jnp.mean(scaled * normed, axis=-1, keepdims=True))


def input_own(grads, got, x, g, gain, qk, vo):
    w = grads[0].shape[0]
    rows, d = x.shape
    w2 = 2 * w
    bt = 256
    col = pl.BlockSpec((w, bt), lambda i: (0, i))
    row = pl.BlockSpec((bt, d), lambda i: (i, 0))
    return pl.pallas_call(
        functools.partial(input_own_kernel, w),
        grid=(rows // bt,),
        in_specs=[col] * 6 + [row] * 3 + [fixed((1, d))]
        + [weight(a) for a in (*qk, *vo)],
        out_specs=[row, fixed((8, d))],
        out_shape=[shape_of((rows, d), F32), shape_of((8, d), F32)],
        compiler_params=params(),
        cost_estimate=cost(6 * rows * d * w2, 24 * rows * d),
        name="input_own",
    )(*grads, got, x, g, gain, *plain(qk), *plain(vo))


def total_over_all(plan, a):
    n, f = plan.tp, plan.fsdp
    hop = 1
    while hop < n:
        a = a + lax.ppermute(a, "tp", [(t, t ^ hop) for t in range(n)])
        hop *= 2
    hop = 1
    while hop < f:
        a = a + lax.ppermute(a, "fsdp", [(t, t ^ hop) for t in range(f)])
        hop *= 2
    return a


def add_low(own, got):
    return (own.astype(F32) + got.astype(F32)).astype(BF16)


def scatter_rows(mine):
    return lax.psum_scatter(mine, "fsdp", scatter_dimension=0, tiled=True).astype(F32)


def after(*arrays):
    return lax.optimization_barrier(arrays)


def fast_body(plan, inputs, cotangent, w_qkv, w_out, w_up, w_down, norm_gain, query_scale, prefix_len):
    seqs, positions, d = inputs.shape
    layers, w = w_qkv.shape[0], w_qkv.shape[3]
    dh = query_scale.shape[1]
    unit = SOFT_ONE / math.sqrt(dh)
    factors = jax.nn.softplus(query_scale) * unit
    prefix = lax.dynamic_slice_in_dim(prefix_len, plan.seq, 1)
    order = plan.blocks(positions * plan.tp)
    out_shard, down_shard = jnp.swapaxes(w_out, 1, 2), jnp.swapaxes(w_down, 1, 2)
    pairs = jnp.concatenate(
        [
            jnp.concatenate([w_qkv[:, 0], w_qkv[:, 1]], axis=2)[:, None],
            jnp.concatenate([w_qkv[:, 2], out_shard], axis=2)[:, None],
            jnp.concatenate([w_up, down_shard], axis=2)[:, None],
        ],
        axis=1,
    )

    block = plan.pick(inputs, 1 - plan.seq).astype(BF16)
    got, other = gather_call(pairs[0, :2], block, pieces_of(2, pairs.shape[2]), plan.fsdp, plan.ring)
    qk0, vo0 = got[0:2], got[2:4]

    def along(l, m):
        return lax.all_gather(pairs[l, m], "fsdp", axis=0, tiled=True)

    def both(rows):
        return rows, plan.across(rows)

    def stacked(rows):
        return (rows, 0), (rows, 1)

    un0_rows, qk1_rows = along(0, 2), along(1, 0)
    x = plan.order(plan.pick(inputs, plan.seq), other.astype(F32))
    x, un0_rows, cotangent, shards = after(x, un0_rows, cotangent, pairs[1, 1:])
    shards_got, un0 = plan.across(shards), both(un0_rows)
    cot_block = plan.pick(cotangent, 1 - plan.seq).astype(BF16)
    kept, weights = [], []
    for l in range(layers):
        qk, vo = (qk0, vo0) if l == 0 else (qk1, vo1)
        scale = jnp.tile(factors[l] * LOG2E, 2 * w // dh)[:, None]
        h, h_other, q, k, v = project(x, norm_gain[l, 0][None], qk, vo, scale, 3 + l)
        if l == 0:
            q, shards_got, qk1_rows = after(q, shards_got, qk1_rows)
            shards = jnp.stack([shards, shards_got], axis=1)
            vo1_rows, un1_rows = (lax.all_gather(shards[m], "fsdp", axis=1, tiled=True) for m in range(2))
            qk1 = both(qk1_rows)
        att, lse = attention_forward(q, k, v, prefix, order, dh)
        if l == 0:
            att, un0_got = after(att, un0[1])
            un = un0[0], un0_got
        else:
            att, un1_rows, cot_got = after(att, un1_rows, cot_got)
            un = stacked(un1_rows)
        mid, pre, res, *mats = middle_call(x, att, norm_gain[l, 1][None], vo, un, 5 + l)
        if l == 0:
            res, qk1_got, vo1_rows, cot_block = after(res, qk1[1], vo1_rows, cot_block)
            qk1, vo1 = (qk1[0], qk1_got), stacked(vo1_rows)
            cot_got = plan.across(cot_block)
        kept.append((x, h, h_other, q, k, v, att, lse, mid, pre))
        weights.append((qk, vo, mats))
        x = res
    g = plan.order(plan.pick(cotangent, plan.seq), cot_got.astype(F32))
    out_blocks = x.reshape(seqs, positions, d)
    out_send = plan.pick(out_blocks, 1 - plan.seq).astype(BF16)
    g, out_send = after(g, out_send)
    out_got = plan.across(out_send)
    outputs = None
    width = -(-3 * w // 128) * 128
    grads = [None] * layers
    for l in reversed(range(layers)):
        qk, vo, mats = weights[l]
        x, h, h_other, q, k, v, att, lse, mid, pre = kept[l]
        g_mid, gain_m, g_att, *early = mlp_back(g, mid, pre, norm_gain[l, 1][None], att, mats, width, 1 + l)
        early = [early[1], early[0]]
        if outputs is None:
            g_att, out_got = after(g_att, out_got)
            outputs = plan.order(plan.pick(out_blocks, plan.seq), out_got.astype(F32)).reshape(out_blocks.shape)
        early_got = plan.across(early[0])
        g_att, early[1] = after(g_att, early[1])
        dgrads, fgs, pieces = [None] * 6, [], [None] * 2
        for s in (1, 0):
            dq, dk, dv, fg = attention_backward(
                q, k, v, att, g_att, lse, factors[l], prefix, order, dh, s * w, w
            )
            if s == 0 and l + 1 < layers:
                dq, upper = after(dq, grads[l + 1][1])
                grads[l + 1] = (grads[l + 1][0], upper, grads[l + 1][2])
            if s == 1:
                pieces[1] = weight_grad(h, h_other, dq, dk, dv, width)
                g_att, pieces[1], early_got = after(g_att, pieces[1], early_got)
                late_got = plan.across(pieces[1])
                mine, g_att = after(add_low(early[1], early_got), g_att)
                early = scatter_rows(mine)
            dgrads[3 * s:3 * s + 3] = [dq, dk, dv]
            fgs.append(fg)
        fg = fgs[0] + fgs[1]
        part = input_other(dgrads, qk, vo)
        part, dgrads[0], late_got = after(part, dgrads[0], late_got)
        part = plan.core(part)
        mine, dgrads[1] = after(weight_grad(h, h_other, *dgrads[:3], width, late_got), dgrads[1])
        late = scatter_rows(mine)
        g, gain_a = input_own(dgrads, part, x, g_mid, norm_gain[l, 0][None], qk, vo)
        if l > 0:
            g, early = after(g, early)
        factor_grad = jnp.sum(fg, axis=1) / (factors[l] * LOG2E)
        small = jnp.concatenate([jnp.sum(gain_a, axis=0), jnp.sum(gain_m, axis=0), factor_grad])
        grads[l] = (early, late, small)
    input_grad = plan.unswap(g)
    small = jnp.stack([entry[2] for entry in grads])
    small = total_over_all(plan, small)
    early, late = jnp.stack([e[0] for e in grads]), jnp.stack([e[1] for e in grads])
    qkv_g = jnp.stack([late[:, :, c * w:(c + 1) * w] for c in range(3)], axis=1)
    up_g, down_g, out_g = (early[:, :, c * w:(c + 1) * w] for c in range(3))
    scale_g = small[:, 2 * d:] * jax.nn.sigmoid(query_scale) * unit
    return (
        outputs, input_grad, qkv_g, jnp.swapaxes(out_g, 1, 2), up_g, jnp.swapaxes(down_g, 1, 2),
        small[:, :d], small[:, d:2 * d], scale_g,
    )


def body(inputs, cotangent, w_qkv, w_out, w_up, w_down, norm_gain, query_scale, prefix_len):
    seqs, positions, d = inputs.shape
    fsdp, tp = lax.axis_size("fsdp"), lax.axis_size("tp")
    layers = w_qkv.shape[0]
    plan = Plan(seqs, tp, fsdp, w_qkv.shape[2])
    if plan.fast:
        return fast_body(
            plan, inputs, cotangent, w_qkv, w_out, w_up, w_down, norm_gain, query_scale, prefix_len
        )
    dh = query_scale.shape[1]
    unit = SOFT_ONE / math.sqrt(dh)
    factors = jax.nn.softplus(query_scale) * unit
    prefix = lax.dynamic_slice_in_dim(prefix_len, plan.seq, 1)
    order = plan.blocks(positions * tp)
    out_shard, down_shard = jnp.swapaxes(w_out, 1, 2), jnp.swapaxes(w_down, 1, 2)

    weights = []
    for l in range(layers):
        qkv = plan.gather_heads(w_qkv[l])
        out_t = plan.gather_heads(out_shard[l][None])[:, 0]
        up, down_t = plan.gather_full(jnp.stack([w_up[l], down_shard[l]]))
        weights.append(([qkv[:, c] for c in range(3)], out_t, up, down_t))

    x = plan.swap(inputs)
    g = plan.swap(cotangent)
    kept = []
    for l in range(layers):
        x, saved = layer_forward(plan, x, prefix, order, *weights[l], norm_gain[l], factors[l])
        kept.append(saved)
    outputs = plan.unswap(x)
    grads = [None] * layers
    for l in reversed(range(layers)):
        g, grads[l] = layer_backward(
            plan, g, kept[l], prefix, order, *weights[l], norm_gain[l], factors[l]
        )
    input_grad = plan.unswap(g)
    qkv_g, out_g, up_g, down_g, gain_a, gain_m, f_g = (jnp.stack(a) for a in zip(*grads))
    scale_g = f_g * jax.nn.sigmoid(query_scale) * unit
    gain_a, gain_m, scale_g = lax.psum((gain_a, gain_m, scale_g), ("fsdp", "tp"))
    return outputs, input_grad, qkv_g, out_g, up_g, down_g, gain_a, gain_m, scale_g


def solution(mesh):
    placed = (
        P("fsdp", "tp", None),
        P("fsdp", "tp", None),
        P(None, None, "fsdp", "tp"),
        P(None, "tp", "fsdp"),
        P(None, "fsdp", "tp"),
        P(None, "tp", "fsdp"),
        P(),
        P(),
        P("fsdp"),
    )
    return jax.shard_map(
        body,
        mesh=mesh,
        in_specs=placed,
        out_specs=placed[:6] + (P(), P(), P()),
        check_vma=False,
    )
```

```python
import functools, math
import jax
import jax.numpy as jnp
from jax import lax
from jax.experimental import pallas as pl
from jax.experimental.pallas import tpu as pltpu
from jax.sharding import PartitionSpec as P

MASKED = -1e30
F32, BF16 = jnp.float32, jnp.bfloat16
EPSILON = 1e-06
SOFT_ONE = 1.442695041
LOG2E = math.log2(math.e)
MESH = pl.DeviceIdType.MESH
HINT = 1
VMEM_LIMIT = 60 * 2**20

def dot(a, b, dims=((1,), (0,))):
    return lax.dot_general(a, b, (dims, ((), ())), preferred_element_type=F32)

def key_range(row_start, rows, prefix, block):
    full = jnp.maximum(row_start + 1, prefix) // block
    stop = (jnp.maximum(row_start + rows, prefix) + block - 1) // block
    return full, stop

def forward_kernel(prefix_ref, order_ref, q_ref, k_ref, v_ref, o_ref, lse_ref, key_rows, value_ext, *, pair, dh, bq, bk):
    length = q_ref.shape[1]
    prefix = prefix_ref[0]
    ext = value_ext.shape[1]
    bound = 0.0
    for h in range(pair):
        rows = slice(h * dh, (h + 1) * dh)
        q, k = q_ref[rows, :].astype(F32), k_ref[rows, :].astype(F32)
        bound = jnp.maximum(bound, jnp.max(jnp.sum(q * q, axis=0)) * jnp.max(jnp.sum(k * k, axis=0)))
        key_rows[h] = k_ref[rows, :].T
        value_ext[h, :dh] = v_ref[rows, :]
        value_ext[h, dh:] = jnp.ones((ext - dh, length), BF16)

    def one_query(shifted, qi, carry):
        start = qi * bq
        here = pl.ds(pl.multiple_of(order_ref[qi] * bq, bq), bq)
        queries = [q_ref[h * dh:(h + 1) * dh, here] for h in range(pair)]
        full, stop = key_range(start, bq, prefix, bk)

        def step(masked, ki, state):
            first = ki * bk
            there = pl.ds(pl.multiple_of(order_ref[ki] * bk, bk), bk)
            if masked:
                rows = first + lax.broadcasted_iota(jnp.int32, (bk, bq), 0)
                cols = start + lax.broadcasted_iota(jnp.int32, (bk, bq), 1)
                allowed = rows <= jnp.maximum(cols, prefix - 1)
            scores = [dot(key_rows[h, there], queries[h]) for h in range(pair)]
            fresh = []
            for h in range(pair):
                s = jnp.where(allowed, scores[h], MASKED) if masked else scores[h]
                if shifted:
                    top, total = state[h]
                    new_top = jnp.maximum(top, jnp.max(s, axis=0, keepdims=True))
                    p = jnp.exp2(s - new_top).astype(BF16)
                    total = total * jnp.exp2(top - new_top) + dot(value_ext[h, :, there], p)
                    fresh.append((new_top, total))
                else:
                    fresh.append(state[h] + dot(value_ext[h, :, there], jnp.exp2(s).astype(BF16)))
            return tuple(fresh)

        zero = jnp.zeros((ext, bq), F32)
        state = tuple((jnp.full((1, bq), MASKED, F32), zero) if shifted else zero for _ in range(pair))
        state = lax.fori_loop(0, full, functools.partial(step, False), state)
        state = lax.fori_loop(full, stop, functools.partial(step, True), state)
        for h in range(pair):
            top, total = state[h] if shifted else (0.0, state[h])
            norm = total[dh:dh + 1]
            o_ref[h * dh:(h + 1) * dh, here] = (total[:dh] / norm).astype(BF16)
            lse_ref[h, :, here] = top + jnp.log2(norm)
        return carry

    small = bound <= 3600.0

    @pl.when(small)
    def _():
        lax.fori_loop(0, length // bq, functools.partial(one_query, False), 0)

    @pl.when(jnp.logical_not(small))
    def _():
        lax.fori_loop(0, length // bq, functools.partial(one_query, True), 0)


def attention_forward(q, k, v, prefix, order, dh, pair=4):
    width, length = q.shape
    heads = width // dh
    pair = min(pair, heads)
    bq = bk = length // order.shape[0]
    ext = dh + 16
    spec = pl.BlockSpec((pair * dh, length), lambda i, p, o: (i, 0))
    return pl.pallas_call(
        functools.partial(forward_kernel, pair=pair, dh=dh, bq=bq, bk=bk),
        grid_spec=pltpu.PrefetchScalarGridSpec(
            num_scalar_prefetch=2, grid=(heads // pair,),
            in_specs=[spec, spec, spec],
            out_specs=[spec, pl.BlockSpec((pair, 1, length), lambda i, p, o: (i, 0, 0))],
            scratch_shapes=[pltpu.VMEM((pair, length, dh), BF16), pltpu.VMEM((pair, ext, length), BF16)],
        ),
        out_shape=[jax.ShapeDtypeStruct((width, length), BF16), jax.ShapeDtypeStruct((heads, 1, length), F32)],
        compiler_params=pltpu.CompilerParams(vmem_limit_bytes=VMEM_LIMIT),
        cost_estimate=pl.CostEstimate(flops=int(HINT * 600 * length * length * heads), bytes_accessed=int(HINT * 8 * width * length), transcendentals=0),
        name="attention_forward",
    )(prefix, order, q, k, v)

def split3(x):
    a = x.astype(BF16)
    r = x - a.astype(F32)
    b = r.astype(BF16)
    c = (r - b.astype(F32)).astype(BF16)
    return a, b, c

def backward_kernel(prefix_ref, order_ref, q_ref, k_ref, v_ref, o_ref, g_ref, lse_ref, scale_ref, dq_ref, dk_ref, dv_ref, fg_ref,
                    key_ext, value_ext, query_ext, grad_ext, dk_acc, dv_acc, *, pair, dh, bq, bk):
    length = q_ref.shape[1]
    prefix = prefix_ref[0]
    pad = key_ext.shape[1] - dh
    index = lax.broadcasted_iota(jnp.int32, (pad, length), 0)
    ones = (index < 3).astype(F32).astype(BF16)

    @pl.when(pl.program_id(0) == 0)
    def _():
        fg_ref[...] = jnp.zeros_like(fg_ref)

    def tail(row):
        high, mid, low = (part.astype(F32) for part in split3(-row))
        rest = jnp.where(index == 1, mid, jnp.where(index == 2, low, 0.0))
        return jnp.where(index == 0, high, rest).astype(BF16)

    for h in range(pair):
        rows = slice(h * dh, (h + 1) * dh)
        g = g_ref[rows, :]
        key_ext[h, :dh] = k_ref[rows, :]
        key_ext[h, dh:] = ones
        value_ext[h, :dh] = v_ref[rows, :]
        value_ext[h, dh:] = ones
        delta = jnp.sum(o_ref[rows, :].astype(F32) * g.astype(F32), axis=0, keepdims=True)
        query_ext[h, :dh] = q_ref[rows, :]
        query_ext[h, dh:] = tail(lse_ref[h])
        grad_ext[h, :dh] = g
        grad_ext[h, dh:] = tail(delta)
        dk_acc[h] = jnp.zeros((dh, length), F32)
        dv_acc[h] = jnp.zeros((dh, length), F32)

    def one_query(qi, carry):
        start = qi * bq
        here = pl.ds(pl.multiple_of(order_ref[qi] * bq, bq), bq)
        full, stop = key_range(start, bq, prefix, bk)

        def step(masked, ki, state):
            first = ki * bk
            there = pl.ds(pl.multiple_of(order_ref[ki] * bk, bk), bk)
            if masked:
                rows = start + lax.broadcasted_iota(jnp.int32, (bq, bk), 0)
                cols = first + lax.broadcasted_iota(jnp.int32, (bq, bk), 1)
                allowed = cols <= jnp.maximum(rows, prefix - 1)
            fresh = []
            s = [dot(query_ext[h, :, here], key_ext[h, :, there], ((0,), (0,))) for h in range(pair)]
            gp = [dot(grad_ext[h, :, here], value_ext[h, :, there], ((0,), (0,))) for h in range(pair)]
            for h in range(pair):
                x = jnp.where(allowed, s[h], MASKED) if masked else s[h]
                p = jnp.exp2(x)
                ds = (p * gp[h]).astype(BF16)
                rows = slice(h * dh, (h + 1) * dh)
                dv_acc[h, :, there] += dot(g_ref[rows, here], p.astype(BF16))
                dk_acc[h, :, there] += dot(q_ref[rows, here], ds)
                fresh.append(state[h] + dot(ds, k_ref[rows, there], ((1,), (1,))))
            return tuple(fresh)

        state = tuple(jnp.zeros((bq, dh), F32) for _ in range(pair))
        state = lax.fori_loop(0, full, functools.partial(step, False), state)
        state = lax.fori_loop(full, stop, functools.partial(step, True), state)
        for h in range(pair):
            rows = slice(h * dh, (h + 1) * dh)
            dq = state[h].T
            prod = dq * q_ref[rows, here].astype(F32)
            part = prod[:, :128]
            for c in range(1, bq // 128):
                part = part + prod[:, c * 128:(c + 1) * 128]
            fg_ref[...] += part
            dq_ref[rows, here] = (dq * scale_ref[...]).astype(BF16)
        return carry

    lax.fori_loop(0, length // bq, one_query, 0)
    for h in range(pair):
        rows = slice(h * dh, (h + 1) * dh)
        dk_ref[rows, :] = (dk_acc[h] * math.log(2.0)).astype(BF16)
        dv_ref[rows, :] = dv_acc[h].astype(BF16)


def attention_backward(q, k, v, o, g, lse, factor, prefix, order, dh, base=0, width=None, pair=2):
    full, length = q.shape
    width = width or full
    heads = width // dh
    pair = min(pair, heads)
    bq = bk = length // order.shape[0]
    ext = dh + 16
    spec = pl.BlockSpec((pair * dh, length), lambda i, p, o: (i, 0))
    skip = base // (pair * dh)
    source = pl.BlockSpec((pair * dh, length), lambda i, p, o: (i + skip, 0))
    wide = jax.ShapeDtypeStruct((width, length), BF16)
    return pl.pallas_call(
        functools.partial(backward_kernel, pair=pair, dh=dh, bq=bq, bk=bk),
        grid_spec=pltpu.PrefetchScalarGridSpec(
            num_scalar_prefetch=2, grid=(heads // pair,),
            in_specs=[source] * 5 + [pl.BlockSpec((pair, 1, length), lambda i, p, o: (i + skip, 0, 0)), pl.BlockSpec((dh, 1), lambda i, p, o: (0, 0))],
            out_specs=[spec] * 3 + [pl.BlockSpec((dh, 128), lambda i, p, o: (0, 0))],
            scratch_shapes=[
                pltpu.VMEM((pair, ext, length), BF16),
                pltpu.VMEM((pair, ext, length), BF16),
                pltpu.VMEM((pair, ext, length), BF16),
                pltpu.VMEM((pair, ext, length), BF16),
                pltpu.VMEM((pair, dh, length), F32),
                pltpu.VMEM((pair, dh, length), F32)],
        ),
        out_shape=[wide] * 3 + [jax.ShapeDtypeStruct((dh, 128), F32)],
        compiler_params=pltpu.CompilerParams(vmem_limit_bytes=VMEM_LIMIT),
        cost_estimate=pl.CostEstimate(flops=int(HINT * 1600 * length * length * heads), bytes_accessed=int(HINT * 16 * width * length), transcendentals=0),
        name="attention_backward",
    )(prefix, order, q, k, v, o, g, lse, factor.reshape(dh, 1))


def rms(x):
    inv = lax.rsqrt(jnp.mean(x * x, axis=-1, keepdims=True) + EPSILON)
    return x * inv, inv


def rms_back(normed, inv, gain, grad):
    scaled = grad * gain
    out = inv * (scaled - normed * jnp.mean(scaled * normed, axis=-1, keepdims=True))
    return out, jnp.sum(grad * normed, axis=0)


def ein(spec, *args):
    return jnp.einsum(spec, *args, preferred_element_type=F32)


def gather_kernel(pieces, pairs, outer, ring, shard_ref, block_ref, *refs):
    outs = [refs[2 * m:2 * m + 2] for m in range(pairs)]
    got_ref = refs[2 * pairs]
    send, recv, local = refs[2 * pairs + 1:]
    f, t = lax.axis_index("fsdp"), lax.axis_index("tp")
    zz, yy = f // 2, f % 2
    across = {"tp": lax.rem(t + ring, 2 * ring)}
    beside = {"fsdp": zz * 2 + 1 - yy}
    along = [{"fsdp": lax.rem(zz + k, outer) * 2 + yy} for k in range(1, outer)]
    peers = along + [across, beside]
    barrier = pltpu.get_barrier_semaphore()
    for peer in peers:
        pl.semaphore_signal(barrier, inc=1, device_id=peer, device_id_type=MESH)
    pl.semaphore_wait(barrier, len(peers))
    used = [0]

    def copy(src, dst, peer):
        slot = used[0]
        used[0] += 1
        return pltpu.make_async_remote_copy(
            src_ref=src, dst_ref=dst, send_sem=send.at[slot], recv_sem=recv.at[slot],
            device_id=peer, device_id_type=MESH,
        )

    count = len(pieces)
    chunks = 4
    step = block_ref.shape[0] // chunks
    blocks = [
        copy(block_ref.at[pl.ds(i * step, step)], got_ref.at[pl.ds(i * step, step)], across)
        for i in range(chunks)
    ]
    own, first, second, third = [], [], [], []
    for i, (m, low, rows, route) in enumerate(pieces):
        part = pl.ds(low, rows)
        w = [out.at[:, :, part] for out in outs[m]]
        src = shard_ref.at[m, part]
        own.append(pltpu.make_async_copy(src, w[0].at[zz, yy], local.at[i]))
        first.append([copy(src, w[0].at[zz, yy], peer) for peer in along])
        if route:
            second.append([copy(w[0].at[:, yy], w[0].at[:, yy], beside)])
            third.append([copy(w[0], w[1], across)])
        else:
            second.append([copy(w[0].at[:, yy], w[1].at[:, yy], across)])
            third.append([copy(w[s].at[:, yy], w[s].at[:, yy], beside) for s in range(2)])

    def begin(i):
        own[i].start()
        for c in first[i]:
            c.start()

    ahead = 3
    for i in range(min(ahead, count)):
        begin(i)
    started = 0
    for b in blocks[:2]:
        b.start()
    started = 2
    for i in range(count + 2):
        if i < count:
            own[i].wait()
            for c in first[i]:
                c.wait_recv()
            for c in second[i]:
                c.start()
            if i + ahead < count:
                begin(i + ahead)
            if started < chunks:
                blocks[started].start()
                started += 1
        if 0 <= i - 1 < count:
            for c in second[i - 1]:
                c.wait_recv()
            for c in third[i - 1]:
                c.start()
        if 0 <= i - 2 < count:
            for c in third[i - 2]:
                c.wait_recv()
    for b in blocks[started:]:
        b.start()
    for i in range(count):
        for c in first[i] + second[i] + third[i]:
            c.wait_send()
    for b in blocks:
        b.wait()


def pieces_of(pairs, rows):
    half = rows // 32 * 16
    return tuple(
        (m, low, size, m_part) for m in range(pairs) for m_part, (low, size) in enumerate(((0, half), (half, rows - half)))
    )


def gather_call(shards, block, pieces, fsdp, ring):
    pairs, rows, w = shards.shape
    outer = fsdp // 2
    slots = 4 + len(pieces) * (outer + 2)
    any_spec = pl.BlockSpec(memory_space=pl.ANY)
    got = pl.pallas_call(
        functools.partial(gather_kernel, pieces, pairs, outer, ring),
        out_shape=[jax.ShapeDtypeStruct((outer, 2, rows, w), BF16)] * (2 * pairs)
        + [jax.ShapeDtypeStruct(block.shape, block.dtype)],
        in_specs=[any_spec] * 2,
        out_specs=[any_spec] * (2 * pairs + 1),
        scratch_shapes=[
            pltpu.SemaphoreType.DMA((slots,)),
            pltpu.SemaphoreType.DMA((slots,)),
            pltpu.SemaphoreType.DMA((len(pieces),)),
        ],
        compiler_params=pltpu.CompilerParams(collective_id=0, has_side_effects=True),
        name="gather_weights",
    )(shards, block)
    return [a.reshape(outer * 2 * rows, w) for a in got[:-1]], got[-1]


class Plan:
    def __init__(self, seqs, tp, fsdp, rows):
        self.seqs, self.tp, self.ring, self.fsdp = seqs, tp, tp // seqs, fsdp
        self.same_member = [[s * self.ring + r for s in range(seqs)] for r in range(self.ring)]
        self.same_seq = [[s * self.ring + r for r in range(self.ring)] for s in range(seqs)]
        self.fast = seqs == 2 and self.ring == 2 and fsdp % 2 == 0 and rows % 32 == 0
        t = lax.axis_index("tp")
        self.seq, self.member = t // self.ring, lax.rem(t, self.ring)

    def across(self, a):
        n = self.tp
        return lax.ppermute(a, "tp", [(t, (t + self.ring) % n) for t in range(n)])

    def core(self, a):
        return lax.ppermute(a, "tp", [(t, t ^ 1) for t in range(self.tp)])

    def pick(self, blocks, index):
        return lax.dynamic_index_in_dim(blocks, index, 0, keepdims=False)

    def order(self, own, other):
        first = self.seq == 0
        return jnp.concatenate([jnp.where(first, own, other), jnp.where(first, other, own)])

    def swap(self, blocks):
        if self.seqs == 2:
            other = self.across(self.pick(blocks, 1 - self.seq).astype(BF16))
            return self.order(self.pick(blocks, self.seq), other.astype(F32))
        got = lax.all_to_all(
            blocks.astype(BF16), "tp", 0, 0, tiled=True, axis_index_groups=self.same_member
        )
        return got.reshape(-1, got.shape[-1]).astype(F32)

    def unswap(self, rows):
        blocks = rows.reshape(self.seqs, -1, rows.shape[-1])
        return self.swap(blocks).reshape(blocks.shape)

    def whole(self, rows):
        if self.fast:
            return jnp.concatenate([rows, self.core(rows)])
        cut = rows.reshape(self.seqs, -1, rows.shape[-1])
        got = lax.all_gather(cut, "tp", axis=1, axis_index_groups=self.same_seq)
        return got.reshape(-1, rows.shape[-1])

    def share(self, full):
        if self.fast:
            own = full.shape[0] // 2
            return full[:own].astype(F32) + self.core(full[own:].astype(BF16)).astype(F32)
        cut = full.astype(BF16).reshape(self.seqs, self.ring, -1, full.shape[-1])
        got = lax.psum_scatter(cut, "tp", scatter_dimension=1, axis_index_groups=self.same_seq)
        return got.reshape(-1, full.shape[-1]).astype(F32)

    def blocks(self, length):
        if self.fast:
            j = jnp.arange(self.tp, dtype=jnp.int32)
            apart = (j % self.ring != self.member).astype(jnp.int32)
            return apart * self.seqs + j // self.ring
        return jnp.arange(max(1, length // 512), dtype=jnp.int32)

    def gather_heads(self, shards):
        rows = lax.all_gather(shards, "fsdp", axis=1, tiled=True)
        if self.fast:
            return jnp.stack([rows, self.across(rows)])
        return lax.all_gather(rows, "tp", axis_index_groups=self.same_member)

    def join(self, every):
        r, s, m, d, w = every.shape
        return every.transpose(2, 3, 0, 1, 4).reshape(m, d, r * s * w)

    def gather_full(self, shards):
        part = self.gather_heads(shards)
        if self.fast:
            return self.join(jnp.stack([part, self.core(part)]))
        return self.join(lax.all_gather(part, "tp", axis_index_groups=self.same_seq))

    def scatter_heads(self, grads):
        if self.fast:
            other = self.across(grads[1].astype(BF16))
            mine = (grads[0].astype(F32) + other.astype(F32)).astype(BF16)
        else:
            mine = lax.psum_scatter(
                grads.astype(BF16), "tp", scatter_dimension=0, axis_index_groups=self.same_member
            )
        return lax.psum_scatter(mine, "fsdp", scatter_dimension=1, tiled=True).astype(F32)

    def scatter_full(self, grads):
        m, d, cols = grads.shape
        if self.fast:
            half = cols // 2
            other = self.core(grads[:, :, half:].astype(BF16))
            mine = grads[:, :, :half].astype(F32) + other.astype(F32)
            mine = mine.astype(BF16).reshape(m, d, self.seqs, -1).transpose(2, 0, 1, 3)
        else:
            cut = grads.astype(BF16).reshape(m, d, self.ring, self.seqs, -1).transpose(2, 3, 0, 1, 4)
            mine = lax.psum_scatter(cut, "tp", scatter_dimension=0, axis_index_groups=self.same_seq)
        return self.scatter_heads(mine)


def layer_forward(plan, x, prefix, order, qkv, out_t, up, down_t, gains, factor):
    dh = factor.shape[0]
    normed, inv = rms(x)
    h = plan.whole((normed * gains[0]).astype(BF16))
    seqs, d, w = out_t.shape
    raw = [ein("sdc,td->sct", qkv[c], h).reshape(seqs * w, -1) for c in range(3)]
    scale = jnp.tile(factor * LOG2E, seqs * w // dh)[:, None]
    q, k, v = (raw[0] * scale).astype(BF16), raw[1].astype(BF16), raw[2].astype(BF16)
    att, lse = attention_forward(q, k, v, prefix, order, dh)
    middle = x + plan.share(ein("sct,sdc->td", att.reshape(seqs, w, -1), out_t))
    normed_m, inv_m = rms(middle)
    h_m = (normed_m * gains[1]).astype(BF16)
    pre = ein("td,df->tf", h_m, up)
    hidden = jax.nn.silu(pre).astype(BF16)
    result = middle + ein("tf,df->td", hidden, down_t)
    return result, (x, inv, h, q, k, v, att, lse, middle, inv_m, h_m, pre, hidden)


def layer_backward(plan, g, saved, prefix, order, qkv, out_t, up, down_t, gains, factor):
    x, inv, h, q, k, v, att, lse, middle, inv_m, h_m, pre, hidden = saved
    dh = factor.shape[0]
    seqs, d, w = out_t.shape
    length = h.shape[0]
    g_low = g.astype(BF16)
    down_grad = ein("td,tf->df", g_low, hidden)
    g_hidden = ein("td,df->tf", g_low, down_t)
    sig = jax.nn.sigmoid(pre)
    g_pre = (g_hidden * sig * (1.0 + pre * (1.0 - sig))).astype(BF16)
    up_grad = ein("td,tf->df", h_m, g_pre)
    mlp_grads = plan.scatter_full(jnp.stack([up_grad, down_grad]))
    g_hm = ein("tf,df->td", g_pre, up)
    back_m, gain_m = rms_back(middle * inv_m, inv_m, gains[1], g_hm)
    g_mid = g + back_m
    g_all = plan.whole(g_mid.astype(BF16))
    att3 = att.reshape(seqs, w, length)
    out_grad = plan.scatter_heads(ein("td,sct->sdc", g_all, att3)[:, None])[0]
    g_att = ein("td,sdc->sct", g_all, out_t).astype(BF16).reshape(seqs * w, length)
    dq, dk, dv, fg = attention_backward(q, k, v, att, g_att, lse, factor, prefix, order, dh)
    factor_grad = jnp.sum(fg, axis=1) / (factor * LOG2E)
    parts = [a.reshape(seqs, w, length) for a in (dq, dk, dv)]
    qkv_grad = plan.scatter_heads(jnp.stack([ein("td,sct->sdc", h, a) for a in parts], axis=1))
    g_ha = plan.share(sum(ein("sct,sdc->td", a, b) for a, b in zip(parts, qkv)))
    back_a, gain_a = rms_back(x * inv, inv, gains[0], g_ha)
    return g_mid + back_a, (qkv_grad, out_grad.T, mlp_grads[0], mlp_grads[1].T, gain_a, gain_m, factor_grad)


TN, NT, TT = ((0,), (0,)), ((1,), (1,)), ((0,), (1,))
ONE = pl.Buffered(1)


def cost(flops, nbytes):
    return pl.CostEstimate(flops=int(flops * HINT), bytes_accessed=int(nbytes * HINT), transcendentals=0)


def params(mib=60):
    return pltpu.CompilerParams(vmem_limit_bytes=mib * 2**20)


def fixed(shape):
    return pl.BlockSpec(shape, lambda *a: (0,) * len(shape), pipeline_mode=ONE)


def weight(w, lanes=None):
    stack, index = w if isinstance(w, tuple) else (w, None)
    shape = (stack.shape[-2], lanes or stack.shape[-1])
    if index is None:
        return fixed(shape)
    return pl.BlockSpec((None,) + shape, lambda *a: (index, 0, 0), pipeline_mode=ONE)


def plain(weights):
    return [w[0] if isinstance(w, tuple) else w for w in weights]


def shape_of(shape, dtype=BF16):
    return jax.ShapeDtypeStruct(shape, dtype)


def inverse_rms(x):
    return lax.rsqrt(jnp.mean(x * x, axis=-1, keepdims=True) + EPSILON)


def eight(x):
    return jnp.sum(x.reshape(-1, 8, x.shape[-1]), axis=0)


def join_lanes(dst, refs, low, high):
    width = high - low
    for i, ref in enumerate(refs):
        dst[:, i * width:(i + 1) * width] = ref[:, low:high]


def core_of():
    t = lax.axis_index("tp")
    return {"tp": t + 1 - 2 * lax.rem(t, 2)}


def pushes(send, recv, core):
    def push(src, dst, slot):
        return pltpu.make_async_remote_copy(
            src_ref=src, dst_ref=dst, send_sem=send.at[slot], recv_sem=recv.at[slot],
            device_id=core, device_id_type=MESH,
        )

    return push


def greet(core):
    barrier = pltpu.get_barrier_semaphore()
    pl.semaphore_signal(barrier, inc=1, device_id=core, device_id_type=MESH)
    pl.semaphore_wait(barrier, 1)


def stack_index(weights):
    return tuple(a[1] if isinstance(a, tuple) else None for a in weights)


def entry(ref, k):
    return ref if k is None else ref.at[k]


def stages(steps):
    starts = [sum(steps[:n]) for n in range(len(steps))]

    def at(n, make):
        return lambda i: make(jnp.clip(i - starts[n], 0, steps[n] - 1))

    return at


ANY = pl.BlockSpec(memory_space=pl.ANY)


class Halves:
    def __init__(self, own_any, got_any, own, got, load, ring):
        self.seq = lax.axis_index("tp") // ring
        self.own, self.got = own, got
        self.copies = [
            pltpu.make_async_copy(own_any.at[self.seq], own, load.at[0]),
            pltpu.make_async_copy(got_any, got, load.at[1]),
        ]

    def rows(self, k, size):
        per = self.own.shape[0] // size
        here = pl.ds(pl.multiple_of(lax.rem(k, per) * size, size), size)
        return jnp.where(k // per == self.seq, self.own[here], self.got[here].astype(F32))


def halves_scratch(rows, d):
    return [pltpu.VMEM((rows // 2, d), F32), pltpu.VMEM((rows // 2, d), BF16), pltpu.SemaphoreType.DMA((2,))]


def project_kernel(w, low, steps, index, bt, ring, gain_ref, scale_ref, *refs):
    weights, refs = refs[:4], refs[4:]
    if ring:
        own_any, got_any, own_ref, other_ref, q_ref, k_ref, v_ref, x_out = refs[:8]
        own, other, qk, vo, load, send, recv, *rest = refs[8:]
        halves = Halves(own_any, got_any, *rest, ring)
    else:
        x_ref, own_ref, other_ref, q_ref, k_ref, v_ref = refs[:6]
        own, other, qk, vo, load, send, recv = refs[6:]
    i = pl.program_id(0)
    rows_steps, half, _ = steps
    ba = q_ref.shape[1]
    core = core_of()
    push = pushes(send, recv, core)

    def loads():
        copies = [pltpu.make_async_copy(entry(weights[s], index[s]), qk.at[s], load.at[s]) for s in range(2)]
        for s in range(2):
            src = entry(weights[2 + s], index[2 + s]).at[:, pl.ds(0, low)]
            copies.append(pltpu.make_async_copy(src, vo.at[s], load.at[2 + s]))
        return copies

    def push_rows(k):
        part = pl.ds(pl.multiple_of(k * bt, bt), bt)
        return push(own.at[part], other.at[part], k)

    @pl.when(i == 0)
    def _():
        if ring:
            for c in halves.copies:
                c.start()
        for c in loads():
            c.start()
        greet(core)
        if ring:
            for c in halves.copies:
                c.wait()

    @pl.when(i < rows_steps)
    def _():
        if ring:
            x = halves.rows(i, bt)
            x_out[...] = x
        else:
            x = x_ref[...]
        h = (x * inverse_rms(x) * gain_ref[...]).astype(BF16)
        own[pl.ds(pl.multiple_of(i * bt, bt), bt)] = h
        own_ref[...] = h
        push_rows(i).start()

    at = i - rows_steps

    @pl.when(at == 0)
    def _():
        for c in loads():
            c.wait()

    @pl.when(at == half)
    def _():
        for k in range(rows_steps):
            push_rows(k).wait()

    def project(h):
        for s in range(2):
            rows = slice(s * w, (s + 1) * w)
            both = dot(qk[s], h, TT)
            q_ref[rows] = (both[:w] * scale_ref[rows]).astype(BF16)
            k_ref[rows] = both[w:].astype(BF16)
            v_ref[rows] = dot(vo[s, :, :w], h, TT).astype(BF16)

    @pl.when((at >= 0) & (at < half))
    def _():
        project(own[pl.ds(pl.multiple_of(at * ba, ba), ba)])

    @pl.when(at >= half)
    def _():
        h = other[pl.ds(pl.multiple_of((at - half) * ba, ba), ba)]
        other_ref[...] = h
        project(h)


def project(x, gain, qk, vo, scale, call, ring=0):
    xs = x if ring else (x,)
    d = xs[0].shape[-1]
    rows = 2 * xs[1].shape[0] if ring else x.shape[0]
    w2 = plain(qk)[0].shape[-1]
    w = w2 // 2
    low = -(-w // 128) * 128
    bt, ba = 256, 512
    half = rows // ba
    steps = (rows // bt, half, half)
    row = pl.BlockSpec((bt, d), lambda i: (jnp.minimum(i, steps[0] - 1), 0))
    wide = pl.BlockSpec((w2, ba), lambda i: (0, jnp.clip(i - steps[0], 0, 2 * half - 1)))
    tall = pl.BlockSpec((ba, d), lambda i: (jnp.clip(i - steps[0] - half, 0, half - 1), 0))
    weights = (*qk, *vo)
    return pl.pallas_call(
        functools.partial(project_kernel, w, low, steps, stack_index(weights), bt, ring),
        grid=(sum(steps),),
        in_specs=[fixed((1, d)), fixed((w2, 1))] + [ANY] * 4 + ([ANY] * 2 if ring else [row]),
        out_specs=[row, tall] + [wide] * 3 + ([row] if ring else []),
        out_shape=[shape_of((rows, d))] * 2 + [shape_of((w2, 2 * rows))] * 3 + ([shape_of((rows, d), F32)] if ring else []),
        scratch_shapes=[
            pltpu.VMEM((rows, d), BF16), pltpu.VMEM((rows, d), BF16),
            pltpu.VMEM((2, d, w2), BF16), pltpu.VMEM((2, d, low), BF16),
            pltpu.SemaphoreType.DMA((4,)), pltpu.SemaphoreType.DMA((steps[0],)), pltpu.SemaphoreType.DMA((steps[0],)),
        ]
        + (halves_scratch(rows, d) if ring else []),
        compiler_params=pltpu.CompilerParams(vmem_limit_bytes=VMEM_LIMIT, collective_id=call, has_side_effects=True),
        cost_estimate=cost(4 * rows * d * 3 * w2, 12 * rows * d),
        name="project",
    )(gain, scale, *plain(weights), *xs)


def middle_kernel(w, low, steps, index, x_ref, gm_ref, att_any, *refs):
    weights, refs = refs[:4], refs[4:]
    mid_ref, pre_ref, res_ref, up_out, down_out, out_out = refs[:6]
    (up_mat, down_mat, out_mat, blocks, vo_side, att, part, got, load, store, send, recv) = refs[6:]
    i = pl.program_id(0)
    far, rows_steps = steps
    bt = x_ref.shape[0]
    ba = part.shape[0] // far
    rows = part.shape[0]
    core = core_of()
    push = pushes(send, recv, core)

    def loads():
        copies = [pltpu.make_async_copy(att_any, att, load.at[0])]
        for s in range(2):
            src = entry(weights[s], index[s]).at[:, pl.ds(low, vo_side.shape[2])]
            copies.append(pltpu.make_async_copy(src, vo_side.at[s], load.at[1 + s]))
        for s in range(2):
            copies.append(pltpu.make_async_copy(entry(weights[2 + s], index[2 + s]), blocks.at[s], load.at[3 + s]))
        return copies

    def stores():
        pairs = ((up_mat, up_out), (down_mat, down_out), (out_mat, out_out))
        return [pltpu.make_async_copy(src, dst, store.at[n]) for n, (src, dst) in enumerate(pairs)]

    def push_block(s):
        return push(blocks.at[s], blocks.at[2 + s], s)

    def push_part(k):
        here = pl.ds(pl.multiple_of(k * ba, ba), ba)
        return push(part.at[here], got.at[here], 2 + k)

    @pl.when(i == 0)
    def _():
        copies = loads()
        for c in copies:
            c.start()
        greet(core)
        for c in copies[:3]:
            c.wait()
        for s in range(2):
            out_mat[:, s * w:(s + 1) * w] = vo_side[s, :, 2 * w - low - w:2 * w - low]
        for s in range(2):
            copies[3 + s].wait()
            push_block(s).start()

    @pl.when(i < far)
    def _():
        here = pl.ds(pl.multiple_of(i * ba, ba), ba)
        cols = pl.ds(pl.multiple_of(rows + i * ba, ba), ba)
        part[here] = dot(att[:, cols], out_mat[...], TT).astype(BF16)
        push_part(i).start()

    at = i - far

    @pl.when(at == 0)
    def _():
        for s in range(2):
            push_block(s).wait()
        for b in range(4):
            up_mat[:, b * w:(b + 1) * w] = blocks[b, :, 0:w]
            down_mat[:, b * w:(b + 1) * w] = blocks[b, :, w:2 * w]
        for c in stores():
            c.start()

    for k in range(far):
        @pl.when(at == k * (ba // bt))
        def _():
            push_part(k).wait()

    @pl.when(at >= 0)
    def _():
        here = pl.ds(pl.multiple_of(at * bt, bt), bt)
        mid = x_ref[...] + got[here].astype(F32) + dot(att[:, here], out_mat[...], TT)
        mid_ref[...] = mid
        h_m = (mid * inverse_rms(mid) * gm_ref[...]).astype(BF16)
        pre = dot(h_m, up_mat[...])
        pre_ref[...] = pre
        hidden = (pre / (1.0 + jnp.exp(-pre))).astype(BF16)
        res_ref[...] = mid + dot(hidden, down_mat[...], NT)

    @pl.when(at == rows_steps - 1)
    def _():
        for c in stores():
            c.wait()


def middle_call(x, att, gain_m, vo, un, call):
    rows, d = x.shape
    w2 = plain(vo)[0].shape[-1]
    w, ff = w2 // 2, 2 * w2
    low = w // 128 * 128
    bt, ba = 256, 512
    steps = (rows // ba, rows // bt)
    row = pl.BlockSpec((bt, d), lambda i: (jnp.maximum(i - steps[0], 0), 0))
    wide = pl.BlockSpec((bt, ff), lambda i: (jnp.maximum(i - steps[0], 0), 0))
    weights = (*vo, *un)
    mats = [(d, ff), (d, ff), (d, w2)]
    slots = 2 + steps[0]
    return pl.pallas_call(
        functools.partial(middle_kernel, w, low, steps, stack_index(weights)),
        grid=(sum(steps),),
        in_specs=[row, fixed((1, d))] + [ANY] * 5,
        out_specs=[row, wide, row] + [ANY] * 3,
        out_shape=[shape_of((rows, d), F32), shape_of((rows, ff), F32), shape_of((rows, d), F32)] + [shape_of(m) for m in mats],
        scratch_shapes=[pltpu.VMEM(m, BF16) for m in mats]
        + [pltpu.VMEM((4, d, w2), BF16), pltpu.VMEM((2, d, w2 - low), BF16), pltpu.VMEM(att.shape, BF16)]
        + [pltpu.VMEM((rows, d), BF16)] * 2
        + [pltpu.SemaphoreType.DMA((5,)), pltpu.SemaphoreType.DMA((3,)), pltpu.SemaphoreType.DMA((slots,)), pltpu.SemaphoreType.DMA((slots,))],
        compiler_params=pltpu.CompilerParams(vmem_limit_bytes=VMEM_LIMIT, collective_id=call, has_side_effects=True),
        cost_estimate=cost(2 * rows * d * (2 * w2 + 2 * ff), 30 * rows * d),
        name="middle",
    )(x, gain_m, att, *plain(weights))


def mlp_back_kernel(w, steps, ring, mid_ref, pre_ref, gm_ref, att_any, *refs):
    mats, refs = refs[:3], refs[3:]
    if ring:
        own_any, got_any, refs = refs[0], refs[1], refs[2:]
        halves = Halves(own_any, got_any, *refs[-3:], ring)
        refs = refs[:-3]
    else:
        g_ref, refs = refs[0], refs[1:]
    g_mid_ref, gain_ref, g_att_ref, o0, o1 = refs[:5]
    (up_mat, down_mat, out_mat, g_all, hid_all, hm_all, gpre_all, low_own, low_other, blocks, got, att,
     load, send, recv) = refs[5:]
    i = pl.program_id(0)
    rows_steps, grad_steps, att_steps, _ = steps
    bt, bd, ba = mid_ref.shape[0], o0.shape[0], g_att_ref.shape[1]
    core = core_of()
    push = pushes(send, recv, core)

    def loads():
        pairs = (*zip(mats, (up_mat, down_mat, out_mat)), (att_any, att))
        return [pltpu.make_async_copy(src, dst, load.at[n]) for n, (src, dst) in enumerate(pairs)]

    def push_rows(k):
        part = pl.ds(pl.multiple_of(k * bt, bt), bt)
        return push(low_own.at[part], low_other.at[part], k)

    def push_block(c, s):
        part = pl.ds(pl.multiple_of(c * bd, bd), bd)
        return push(blocks.at[2 + s, part], got.at[s, part], rows_steps + 2 * c + s)

    @pl.when(i == 0)
    def _():
        copies = loads()
        for c in copies:
            c.start()
        gain_ref[...] = jnp.zeros_like(gain_ref)
        if ring:
            for c in halves.copies:
                c.start()
        greet(core)
        for c in copies[:2] + (halves.copies if ring else []):
            c.wait()

    @pl.when(i < rows_steps)
    def _():
        here = pl.ds(pl.multiple_of(i * bt, bt), bt)
        g = halves.rows(i, bt) if ring else g_ref[...]
        g_low = g.astype(BF16)
        g_all[here] = g_low
        pre = pre_ref[...]
        sig = 1.0 / (1.0 + jnp.exp(-pre))
        hid_all[here] = (pre * sig).astype(BF16)
        g_hidden = dot(g_low, down_mat[...])
        g_pre = (g_hidden * sig * (1.0 + pre * (1.0 - sig))).astype(BF16)
        gpre_all[here] = g_pre
        mid = mid_ref[...]
        inv = inverse_rms(mid)
        normed = mid * inv
        gain = gm_ref[...]
        hm_all[here] = (normed * gain).astype(BF16)
        g_hm = dot(g_pre, up_mat[...], NT)
        gain_ref[...] += eight(g_hm * normed)
        scaled = g_hm * gain
        g_mid = g + inv * (scaled - normed * jnp.mean(scaled * normed, axis=-1, keepdims=True))
        g_mid_ref[...] = g_mid
        low_own[here] = g_mid.astype(BF16)
        push_rows(i).start()

    at = i - rows_steps

    @pl.when((at >= 0) & (at < grad_steps))
    def _():
        cols = pl.ds(pl.multiple_of(at * bd, bd), bd)
        up = dot(hm_all[:, cols], gpre_all[...], TN).astype(BF16)
        down = dot(g_all[:, cols], hid_all[...], TN).astype(BF16)
        for b in range(4):
            blocks[b, cols, 0:w] = up[:, b * w:(b + 1) * w]
            blocks[b, cols, w:2 * w] = down[:, b * w:(b + 1) * w]
        for s in range(2):
            push_block(at, s).start()

    to = at - grad_steps

    @pl.when(to == 0)
    def _():
        loads()[2].wait()

    half = att_steps // 2

    @pl.when((to >= 0) & (to < half))
    def _():
        here = pl.ds(pl.multiple_of(to * ba, ba), ba)
        g_att_ref[...] = dot(out_mat[...], low_own[here], TT).astype(BF16)

    @pl.when(to == half)
    def _():
        for k in range(rows_steps):
            push_rows(k).wait()

    @pl.when((to >= half) & (to < att_steps))
    def _():
        here = pl.ds(pl.multiple_of((to - half) * ba, ba), ba)
        g_att_ref[...] = dot(out_mat[...], low_other[here], TT).astype(BF16)

    last = to - att_steps

    @pl.when(last == 0)
    def _():
        loads()[3].wait()

    @pl.when(last >= 0)
    def _():
        cols = pl.ds(pl.multiple_of(last * bd, bd), bd)
        rows = low_own.shape[0]
        grad = dot(low_own[:, cols], att[:, :rows], TT) + dot(low_other[:, cols], att[:, rows:], TT)
        grad = grad.astype(BF16)
        for s, out in enumerate((o0, o1)):
            push_block(last, s).wait()
            out[:, :2 * w] = (blocks[s, cols].astype(F32) + got[s, cols].astype(F32)).astype(BF16)
            out[:, 2 * w:3 * w] = grad[:, s * w:(s + 1) * w]
            out[:, 3 * w:] = jnp.zeros((bd, out.shape[1] - 3 * w), BF16)


def mlp_back(g, mid, pre, gain, att, mats, width, call, ring=0):
    rows, d = mid.shape
    gs = g if ring else (g,)
    ff = pre.shape[1]
    w2 = att.shape[0]
    w = w2 // 2
    bt, bd, ba = 256, 256, 512
    steps = (rows // bt, d // bd, 2 * rows // ba, d // bd)
    at = stages(steps)
    row = pl.BlockSpec((bt, d), at(0, lambda k: (k, 0)))
    wide = pl.BlockSpec((bt, ff), at(0, lambda k: (k, 0)))
    block = pl.BlockSpec((bd, width), at(3, lambda k: (k, 0)))
    slots = steps[0] + 2 * steps[1]
    return pl.pallas_call(
        functools.partial(mlp_back_kernel, w, steps, ring),
        grid=(sum(steps),),
        in_specs=[row, wide, fixed((1, d))] + [ANY] * 4 + ([ANY] * 2 if ring else [row]),
        out_specs=[row, fixed((8, d)), pl.BlockSpec((w2, ba), at(2, lambda k: (0, k))), block, block],
        out_shape=[shape_of((rows, d), F32), shape_of((8, d), F32), shape_of((w2, 2 * rows))] + [shape_of((d, width))] * 2,
        scratch_shapes=[pltpu.VMEM((d, ff), BF16)] * 2
        + [pltpu.VMEM((d, w2), BF16)]
        + [pltpu.VMEM((rows, d), BF16), pltpu.VMEM((rows, ff), BF16)] * 2
        + [pltpu.VMEM((rows, d), BF16)] * 2
        + [pltpu.VMEM((4, d, w2), BF16), pltpu.VMEM((2, d, w2), BF16)]
        + [pltpu.VMEM(att.shape, BF16)]
        + [pltpu.SemaphoreType.DMA((4,)), pltpu.SemaphoreType.DMA((slots,)), pltpu.SemaphoreType.DMA((slots,))]
        + (halves_scratch(rows, d) if ring else []),
        compiler_params=pltpu.CompilerParams(vmem_limit_bytes=62 * 2**20, collective_id=call, has_side_effects=True),
        cost_estimate=cost(8 * rows * d * ff + 8 * rows * d * w2, 40 * rows * d),
        name="mlp_back",
    )(mid, pre, gain, att, *mats, *gs)


def weight_grad_kernel(w, own_ref, other_ref, dq_ref, dk_ref, dv_ref, *refs):
    out, stacked = refs[-2:]
    half = own_ref.shape[0]

    @pl.when(pl.program_id(0) == 0)
    def _():
        for j, ref in enumerate((dq_ref, dk_ref, dv_ref)):
            stacked[j * w:(j + 1) * w, :] = ref[...]

    grad = dot(own_ref[...], stacked[:, :half], TT) + dot(other_ref[...], stacked[:, half:], TT)
    if len(refs) == 3:
        grad = grad + refs[0][:, :3 * w].astype(F32)
    out[:, :3 * w] = grad.astype(BF16)
    out[:, 3 * w:] = jnp.zeros((out.shape[0], out.shape[1] - 3 * w), BF16)


def weight_grad(own, other, dq, dk, dv, width, got=None):
    rows, d = own.shape
    w = dq.shape[0]
    bd = 256
    col = pl.BlockSpec((rows, bd), lambda i: (0, i))
    flat = pl.BlockSpec((bd, width), lambda i: (i, 0))
    extra = [] if got is None else [got]
    return pl.pallas_call(
        functools.partial(weight_grad_kernel, w),
        grid=(d // bd,),
        in_specs=[col, col] + [fixed(dq.shape)] * 3 + [flat] * len(extra),
        out_specs=flat,
        out_shape=shape_of((d, width)),
        scratch_shapes=[pltpu.VMEM((3 * w, 2 * rows), BF16)],
        compiler_params=params(),
        cost_estimate=cost(12 * rows * d * w, 12 * rows * d),
        name="weight_grad",
    )(own, other, dq, dk, dv, *extra)


def input_back_kernel(w, low, steps, index, x_ref, g_ref, gain_ref, *refs):
    grads, weights, refs = refs[:6], refs[6:10], refs[10:]
    stacked, qk, vo, part, got, load, send, recv = refs[-8:]
    i = pl.program_id(0)
    chunk_steps, far, _ = steps
    if chunk_steps:
        own_ref, other_ref, out_ref, sum_ref, piece_ref = refs[:-8]
    else:
        out_ref, sum_ref = refs[:-8]
    bt, half = x_ref.shape[0], part.shape[0]
    ba = half // far
    push = pushes(send, recv, core_of())

    def loads():
        copies = [
            pltpu.make_async_copy(grads[n], stacked.at[n // 3, pl.ds(n % 3 * w, w)], load.at[n]) for n in range(6)
        ]
        for s in range(2):
            copies.append(pltpu.make_async_copy(entry(weights[s], index[s]), qk.at[s], load.at[6 + s]))
        for s in range(2):
            src = entry(weights[2 + s], index[2 + s]).at[:, pl.ds(0, low)]
            copies.append(pltpu.make_async_copy(src, vo.at[s], load.at[8 + s]))
        return copies

    def push_part(k):
        here = pl.ds(pl.multiple_of(k * ba, ba), ba)
        return push(part.at[here], got.at[here], k)

    def total(cols):
        parts = [
            dot(stacked[s, :2 * w, cols], qk[s], TT) + dot(stacked[s, 2 * w:, cols], vo[s, :, :w], TT) for s in range(2)
        ]
        return parts[0] + parts[1]

    @pl.when(i == 0)
    def _():
        copies = loads()
        for c in copies:
            c.start()
        sum_ref[...] = jnp.zeros_like(sum_ref)
        greet(core_of())
        for c in copies[:3]:
            c.wait()

    if chunk_steps:
        @pl.when(i < chunk_steps)
        def _():
            grad = dot(own_ref[...], stacked[0, :, :half], TT) + dot(other_ref[...], stacked[0, :, half:], TT)
            piece_ref[:, :3 * w] = grad.astype(BF16)
            piece_ref[:, 3 * w:] = jnp.zeros((piece_ref.shape[0], piece_ref.shape[1] - 3 * w), BF16)

    to = i - chunk_steps

    @pl.when(to == 0)
    def _():
        for c in loads()[3:]:
            c.wait()

    @pl.when((to >= 0) & (to < far))
    def _():
        cols = pl.ds(pl.multiple_of(half + to * ba, ba), ba)
        part[pl.ds(pl.multiple_of(to * ba, ba), ba)] = total(cols).astype(BF16)
        push_part(to).start()

    at = to - far
    for k in range(far):
        @pl.when(at == k * (ba // bt))
        def _():
            push_part(k).wait()

    @pl.when(at >= 0)
    def _():
        here = pl.ds(pl.multiple_of(at * bt, bt), bt)
        g_ha = total(here) + got[here].astype(F32)
        x = x_ref[...]
        inv = inverse_rms(x)
        normed = x * inv
        sum_ref[...] += eight(g_ha * normed)
        scaled = g_ha * gain_ref[...]
        out_ref[...] = g_ref[...] + inv * (scaled - normed * jnp.mean(scaled * normed, axis=-1, keepdims=True))


def input_back(grads, x, g, gain, qk, vo, call, normed=(), width=0):
    w, length = grads[0].shape
    rows, d = x.shape
    low = -(-w // 128) * 128
    bt, bd, ba = 256, 256, 512
    chunks = d // bd if normed else 0
    steps = (chunks, rows // ba, rows // bt)
    row = pl.BlockSpec((bt, d), lambda i: (jnp.maximum(i - steps[0] - steps[1], 0), 0))

    def chunk(k):
        return jnp.minimum(k, chunks - 1)

    weights = (*qk, *vo)
    in_specs = [row, row, fixed((1, d))] + [ANY] * 10
    out_specs, out_shape = [row, fixed((8, d))], [shape_of((rows, d), F32), shape_of((8, d), F32)]
    if normed:
        in_specs += [pl.BlockSpec((rows, bd), lambda i: (0, chunk(i)))] * 2
        out_specs.append(pl.BlockSpec((bd, width), lambda i: (chunk(i), 0)))
        out_shape.append(shape_of((d, width)))
    return pl.pallas_call(
        functools.partial(input_back_kernel, w, low, steps, stack_index(weights)),
        grid=(sum(steps),),
        in_specs=in_specs,
        out_specs=out_specs,
        out_shape=out_shape,
        scratch_shapes=[
            pltpu.VMEM((2, 3 * w, length), BF16), pltpu.VMEM((2, d, 2 * w), BF16), pltpu.VMEM((2, d, low), BF16),
            pltpu.VMEM((rows, d), BF16), pltpu.VMEM((rows, d), BF16),
            pltpu.SemaphoreType.DMA((10,)), pltpu.SemaphoreType.DMA((steps[1],)), pltpu.SemaphoreType.DMA((steps[1],)),
        ],
        compiler_params=pltpu.CompilerParams(vmem_limit_bytes=VMEM_LIMIT, collective_id=call, has_side_effects=True),
        cost_estimate=cost(9 * rows * d * 4 * w, 24 * rows * d),
        name="input_back",
    )(x, g, gain, *grads, *plain(weights), *normed)


def total_over_all(plan, a):
    n, f = plan.tp, plan.fsdp
    hop = 1
    while hop < n:
        a = a + lax.ppermute(a, "tp", [(t, t ^ hop) for t in range(n)])
        hop *= 2
    hop = 1
    while hop < f:
        a = a + lax.ppermute(a, "fsdp", [(t, t ^ hop) for t in range(f)])
        hop *= 2
    return a


def add_low(own, got):
    return (own.astype(F32) + got.astype(F32)).astype(BF16)


def scatter_rows(mine):
    return lax.psum_scatter(mine, "fsdp", scatter_dimension=0, tiled=True)


def after(*arrays):
    return lax.optimization_barrier(arrays)


def fast_body(plan, inputs, cotangent, w_qkv, w_out, w_up, w_down, norm_gain, query_scale, prefix_len):
    seqs, positions, d = inputs.shape
    layers, w = w_qkv.shape[0], w_qkv.shape[3]
    dh = query_scale.shape[1]
    unit = SOFT_ONE / math.sqrt(dh)
    factors = jax.nn.softplus(query_scale) * unit
    prefix = lax.dynamic_slice_in_dim(prefix_len, plan.seq, 1)
    order = plan.blocks(positions * plan.tp)
    out_shard, down_shard = jnp.swapaxes(w_out, 1, 2), jnp.swapaxes(w_down, 1, 2)
    pairs = jnp.concatenate(
        [
            jnp.concatenate([w_qkv[:, 0], w_qkv[:, 1]], axis=2)[:, None],
            jnp.concatenate([w_qkv[:, 2], out_shard], axis=2)[:, None],
            jnp.concatenate([w_up, down_shard], axis=2)[:, None],
        ],
        axis=1,
    )

    block = plan.pick(inputs, 1 - plan.seq).astype(BF16)
    got, other = gather_call(pairs[0, :2], block, pieces_of(2, pairs.shape[2]), plan.fsdp, plan.ring)
    qk0, vo0 = got[0:2], got[2:4]

    def along(l, m):
        return lax.all_gather(pairs[l, m], "fsdp", axis=0, tiled=True)

    def both(rows):
        return rows, plan.across(rows)

    def stacked(rows):
        return (rows, 0), (rows, 1)

    un0_rows, qk1_rows = along(0, 2), along(1, 0)
    other, un0_rows, cotangent, shards = after(other, un0_rows, cotangent, pairs[1, 1:])
    shards_got, un0 = plan.across(shards), both(un0_rows)
    cot_block = plan.pick(cotangent, 1 - plan.seq).astype(BF16)
    kept, weights = [], []
    for l in range(layers):
        qk, vo = (qk0, vo0) if l == 0 else (qk1, vo1)
        scale = jnp.tile(factors[l] * LOG2E, 2 * w // dh)[:, None]
        gain = norm_gain[l, 0][None]
        if l == 0:
            h, h_other, q, k, v, x = project((inputs, other), gain, qk, vo, scale, 3, plan.ring)
        else:
            h, h_other, q, k, v = project(x, gain, qk, vo, scale, 3 + l)
        if l == 0:
            q, shards_got, qk1_rows = after(q, shards_got, qk1_rows)
            shards = jnp.stack([shards, shards_got], axis=1)
            vo1_rows, un1_rows = (lax.all_gather(shards[m], "fsdp", axis=1, tiled=True) for m in range(2))
            qk1 = both(qk1_rows)
        att, lse = attention_forward(q, k, v, prefix, order, dh)
        if l == 0:
            att, un0_got = after(att, un0[1])
            un = un0[0], un0_got
        else:
            att, un1_rows, cot_got = after(att, un1_rows, cot_got)
            un = stacked(un1_rows)
        mid, pre, res, *mats = middle_call(x, att, norm_gain[l, 1][None], vo, un, 5 + l)
        if l == 0:
            res, qk1_got, vo1_rows, cot_block = after(res, qk1[1], vo1_rows, cot_block)
            qk1, vo1 = (qk1[0], qk1_got), stacked(vo1_rows)
            cot_got = plan.across(cot_block)
        kept.append((x, h, h_other, q, k, v, att, lse, mid, pre))
        weights.append((qk, vo, mats))
        x = res
    g = cotangent, cot_got
    out_blocks = x.reshape(seqs, positions, d)
    out_send = plan.pick(out_blocks, 1 - plan.seq).astype(BF16)
    cot_got, out_send = after(cot_got, out_send)
    g = cotangent, cot_got
    out_got = plan.across(out_send)
    outputs = None
    width = -(-3 * w // 128) * 128
    grads = [None] * layers
    for l in reversed(range(layers)):
        qk, vo, mats = weights[l]
        x, h, h_other, q, k, v, att, lse, mid, pre = kept[l]
        ring = plan.ring if l == layers - 1 else 0
        g_mid, gain_m, g_att, *early = mlp_back(g, mid, pre, norm_gain[l, 1][None], att, mats, width, 1 + l, ring)
        if l > 0:
            early = [scatter_rows(a) for a in early]
        else:
            early_got = plan.across(early[1])
        if l + 1 < layers:
            g_att, grads[l + 1][0][1] = after(g_att, grads[l + 1][0][1])
        dgrads, fgs, pieces = [None] * 6, [], [None] * 2
        for s in (1, 0):
            dq, dk, dv, fg = attention_backward(
                q, k, v, att, g_att, lse, factors[l], prefix, order, dh, s * w, w
            )
            if s == 1:
                pieces[1] = weight_grad(h, h_other, dq, dk, dv, width)
                if outputs is None:
                    pieces[1], out_got = after(pieces[1], out_got)
                    outputs = plan.order(plan.pick(out_blocks, plan.seq), out_got.astype(F32)).reshape(out_blocks.shape)
                g_att, pieces[1] = after(g_att, pieces[1])
                late_got = plan.across(pieces[1])
                if l + 1 < layers:
                    g_att, grads[l + 1][1] = after(g_att, grads[l + 1][1])
                if l == 0:
                    g_att, early_got = after(g_att, early_got)
                    mine, g_att = after(add_low(early[0], early_got), g_att)
                    early = scatter_rows(mine)
            elif l > 0:
                dq, early[0] = after(dq, early[0])
            dgrads[3 * s:3 * s + 3] = [dq, dk, dv]
            fgs.append(fg)
        fg = fgs[0] + fgs[1]
        back = (dgrads, x, g_mid, norm_gain[l, 0][None], qk, vo, 7 + l)
        if l > 0:
            g, gain_a, pieces[0] = input_back(*back, (h, h_other), width)
            pieces[0], late_got = after(pieces[0], late_got)
            mine, g = after(add_low(pieces[0], late_got), g)
        else:
            pieces[0] = weight_grad(h, h_other, *dgrads[:3], width)
            pieces[0], late_got, dgrads[3] = after(pieces[0], late_got, dgrads[3])
            mine, dgrads[3] = after(add_low(pieces[0], late_got), dgrads[3])
            g, gain_a = input_back(*back)
        late = scatter_rows(mine)
        if l == 0:
            g, early = after(g, early)
        factor_grad = jnp.sum(fg, axis=1) / (factors[l] * LOG2E)
        small = jnp.concatenate([jnp.sum(gain_a, axis=0), jnp.sum(gain_m, axis=0), factor_grad])
        grads[l] = [early, late, small]
    in_blocks = g.reshape(out_blocks.shape)
    in_got = plan.across(plan.pick(in_blocks, 1 - plan.seq).astype(BF16))
    input_grad = plan.order(plan.pick(in_blocks, plan.seq), in_got.astype(F32)).reshape(out_blocks.shape)
    small = jnp.stack([entry[2] for entry in grads])
    small = total_over_all(plan, small)
    early = []
    for entry, _, _ in grads:
        if isinstance(entry, list):
            early.append(entry[0].astype(F32) + plan.across(entry[1]).astype(F32))
        else:
            early.append(entry.astype(F32))
    early = jnp.stack(early)
    late = jnp.stack([entry[1].astype(F32) for entry in grads])
    qkv_g = jnp.stack([late[:, :, c * w:(c + 1) * w] for c in range(3)], axis=1)
    up_g, down_g, out_g = (early[:, :, c * w:(c + 1) * w] for c in range(3))
    scale_g = small[:, 2 * d:] * jax.nn.sigmoid(query_scale) * unit
    return (
        outputs, input_grad, qkv_g, jnp.swapaxes(out_g, 1, 2), up_g, jnp.swapaxes(down_g, 1, 2),
        small[:, :d], small[:, d:2 * d], scale_g,
    )


def body(inputs, cotangent, w_qkv, w_out, w_up, w_down, norm_gain, query_scale, prefix_len):
    seqs, positions, d = inputs.shape
    fsdp, tp = lax.axis_size("fsdp"), lax.axis_size("tp")
    layers = w_qkv.shape[0]
    plan = Plan(seqs, tp, fsdp, w_qkv.shape[2])
    if plan.fast:
        return fast_body(
            plan, inputs, cotangent, w_qkv, w_out, w_up, w_down, norm_gain, query_scale, prefix_len
        )
    dh = query_scale.shape[1]
    unit = SOFT_ONE / math.sqrt(dh)
    factors = jax.nn.softplus(query_scale) * unit
    prefix = lax.dynamic_slice_in_dim(prefix_len, plan.seq, 1)
    order = plan.blocks(positions * tp)
    out_shard, down_shard = jnp.swapaxes(w_out, 1, 2), jnp.swapaxes(w_down, 1, 2)

    weights = []
    for l in range(layers):
        qkv = plan.gather_heads(w_qkv[l])
        out_t = plan.gather_heads(out_shard[l][None])[:, 0]
        up, down_t = plan.gather_full(jnp.stack([w_up[l], down_shard[l]]))
        weights.append(([qkv[:, c] for c in range(3)], out_t, up, down_t))

    x = plan.swap(inputs)
    g = plan.swap(cotangent)
    kept = []
    for l in range(layers):
        x, saved = layer_forward(plan, x, prefix, order, *weights[l], norm_gain[l], factors[l])
        kept.append(saved)
    outputs = plan.unswap(x)
    grads = [None] * layers
    for l in reversed(range(layers)):
        g, grads[l] = layer_backward(
            plan, g, kept[l], prefix, order, *weights[l], norm_gain[l], factors[l]
        )
    input_grad = plan.unswap(g)
    qkv_g, out_g, up_g, down_g, gain_a, gain_m, f_g = (jnp.stack(a) for a in zip(*grads))
    scale_g = f_g * jax.nn.sigmoid(query_scale) * unit
    gain_a, gain_m, scale_g = lax.psum((gain_a, gain_m, scale_g), ("fsdp", "tp"))
    return outputs, input_grad, qkv_g, out_g, up_g, down_g, gain_a, gain_m, scale_g


def solution(mesh):
    placed = (
        P("fsdp", "tp", None),
        P("fsdp", "tp", None),
        P(None, None, "fsdp", "tp"),
        P(None, "tp", "fsdp"),
        P(None, "fsdp", "tp"),
        P(None, "tp", "fsdp"),
        P(),
        P(),
        P("fsdp"),
    )
    return jax.shard_map(
        body,
        mesh=mesh,
        in_specs=placed,
        out_specs=placed[:6] + (P(), P(), P()),
        check_vma=False,
    )
```

```python
import functools, math
import jax
import jax.numpy as jnp
from jax import lax
from jax.experimental import pallas as pl
from jax.experimental.pallas import tpu as pltpu
from jax.sharding import PartitionSpec as P

MASKED = -1e30
F32, BF16 = jnp.float32, jnp.bfloat16
EPSILON = 1e-06
SOFT_ONE = 1.442695041
LOG2E = math.log2(math.e)
MESH = pl.DeviceIdType.MESH
HINT = 1
VMEM_LIMIT = 60 * 2**20

def dot(a, b, dims=((1,), (0,))):
    return lax.dot_general(a, b, (dims, ((), ())), preferred_element_type=F32)

def key_range(row_start, rows, prefix, block):
    full = jnp.maximum(row_start + 1, prefix) // block
    stop = (jnp.maximum(row_start + rows, prefix) + block - 1) // block
    return full, stop

def forward_kernel(prefix_ref, order_ref, q_ref, k_ref, v_ref, o_ref, lse_ref, key_rows, value_ext, *, pair, dh, bq, bk):
    length = q_ref.shape[1]
    prefix = prefix_ref[0]
    ext = value_ext.shape[1]
    bound = 0.0
    for h in range(pair):
        rows = slice(h * dh, (h + 1) * dh)
        q, k = q_ref[rows, :].astype(F32), k_ref[rows, :].astype(F32)
        bound = jnp.maximum(bound, jnp.max(jnp.sum(q * q, axis=0)) * jnp.max(jnp.sum(k * k, axis=0)))
        key_rows[h] = k_ref[rows, :].T
        value_ext[h, :dh] = v_ref[rows, :]
        value_ext[h, dh:] = jnp.ones((ext - dh, length), BF16)

    def one_query(shifted, qi, carry):
        start = qi * bq
        here = pl.ds(pl.multiple_of(order_ref[qi] * bq, bq), bq)
        queries = [q_ref[h * dh:(h + 1) * dh, here] for h in range(pair)]
        full, stop = key_range(start, bq, prefix, bk)

        def step(masked, ki, state):
            first = ki * bk
            there = pl.ds(pl.multiple_of(order_ref[ki] * bk, bk), bk)
            if masked:
                rows = first + lax.broadcasted_iota(jnp.int32, (bk, bq), 0)
                cols = start + lax.broadcasted_iota(jnp.int32, (bk, bq), 1)
                allowed = rows <= jnp.maximum(cols, prefix - 1)
            scores = [dot(key_rows[h, there], queries[h]) for h in range(pair)]
            fresh = []
            for h in range(pair):
                s = jnp.where(allowed, scores[h], MASKED) if masked else scores[h]
                if shifted:
                    top, total = state[h]
                    new_top = jnp.maximum(top, jnp.max(s, axis=0, keepdims=True))
                    p = jnp.exp2(s - new_top).astype(BF16)
                    total = total * jnp.exp2(top - new_top) + dot(value_ext[h, :, there], p)
                    fresh.append((new_top, total))
                else:
                    fresh.append(state[h] + dot(value_ext[h, :, there], jnp.exp2(s).astype(BF16)))
            return tuple(fresh)

        zero = jnp.zeros((ext, bq), F32)
        state = tuple((jnp.full((1, bq), MASKED, F32), zero) if shifted else zero for _ in range(pair))
        state = lax.fori_loop(0, full, functools.partial(step, False), state)
        state = lax.fori_loop(full, stop, functools.partial(step, True), state)
        for h in range(pair):
            top, total = state[h] if shifted else (0.0, state[h])
            norm = total[dh:dh + 1]
            o_ref[h * dh:(h + 1) * dh, here] = (total[:dh] / norm).astype(BF16)
            lse_ref[h, :, here] = top + jnp.log2(norm)
        return carry

    small = bound <= 3600.0

    @pl.when(small)
    def _():
        lax.fori_loop(0, length // bq, functools.partial(one_query, False), 0)

    @pl.when(jnp.logical_not(small))
    def _():
        lax.fori_loop(0, length // bq, functools.partial(one_query, True), 0)


def attention_forward(q, k, v, prefix, order, dh, pair=4):
    width, length = q.shape
    heads = width // dh
    pair = min(pair, heads)
    bq = bk = length // order.shape[0]
    ext = dh + 16
    spec = pl.BlockSpec((pair * dh, length), lambda i, p, o: (i, 0))
    return pl.pallas_call(
        functools.partial(forward_kernel, pair=pair, dh=dh, bq=bq, bk=bk),
        grid_spec=pltpu.PrefetchScalarGridSpec(
            num_scalar_prefetch=2, grid=(heads // pair,),
            in_specs=[spec, spec, spec],
            out_specs=[spec, pl.BlockSpec((pair, 1, length), lambda i, p, o: (i, 0, 0))],
            scratch_shapes=[pltpu.VMEM((pair, length, dh), BF16), pltpu.VMEM((pair, ext, length), BF16)],
        ),
        out_shape=[jax.ShapeDtypeStruct((width, length), BF16), jax.ShapeDtypeStruct((heads, 1, length), F32)],
        compiler_params=pltpu.CompilerParams(vmem_limit_bytes=VMEM_LIMIT),
        cost_estimate=pl.CostEstimate(flops=int(HINT * 600 * length * length * heads), bytes_accessed=int(HINT * 8 * width * length), transcendentals=0),
        name="attention_forward",
    )(prefix, order, q, k, v)

def split3(x):
    a = x.astype(BF16)
    r = x - a.astype(F32)
    b = r.astype(BF16)
    c = (r - b.astype(F32)).astype(BF16)
    return a, b, c

def backward_kernel(prefix_ref, order_ref, q_ref, k_ref, v_ref, o_ref, g_ref, lse_ref, scale_ref, dq_ref, dk_ref, dv_ref, fg_ref,
                    key_ext, value_ext, query_ext, grad_ext, dk_acc, dv_acc, *, pair, dh, bq, bk):
    length = q_ref.shape[1]
    prefix = prefix_ref[0]
    pad = key_ext.shape[1] - dh
    index = lax.broadcasted_iota(jnp.int32, (pad, length), 0)
    ones = (index < 3).astype(F32).astype(BF16)

    @pl.when(pl.program_id(0) == 0)
    def _():
        fg_ref[...] = jnp.zeros_like(fg_ref)

    def tail(row):
        high, mid, low = (part.astype(F32) for part in split3(-row))
        rest = jnp.where(index == 1, mid, jnp.where(index == 2, low, 0.0))
        return jnp.where(index == 0, high, rest).astype(BF16)

    for h in range(pair):
        rows = slice(h * dh, (h + 1) * dh)
        g = g_ref[rows, :]
        key_ext[h, :dh] = k_ref[rows, :]
        key_ext[h, dh:] = ones
        value_ext[h, :dh] = v_ref[rows, :]
        value_ext[h, dh:] = ones
        delta = jnp.sum(o_ref[rows, :].astype(F32) * g.astype(F32), axis=0, keepdims=True)
        query_ext[h, :dh] = q_ref[rows, :]
        query_ext[h, dh:] = tail(lse_ref[h])
        grad_ext[h, :dh] = g
        grad_ext[h, dh:] = tail(delta)
        dk_acc[h] = jnp.zeros((dh, length), F32)
        dv_acc[h] = jnp.zeros((dh, length), F32)

    def one_query(qi, carry):
        start = qi * bq
        here = pl.ds(pl.multiple_of(order_ref[qi] * bq, bq), bq)
        full, stop = key_range(start, bq, prefix, bk)

        def step(masked, ki, state):
            first = ki * bk
            there = pl.ds(pl.multiple_of(order_ref[ki] * bk, bk), bk)
            if masked:
                rows = start + lax.broadcasted_iota(jnp.int32, (bq, bk), 0)
                cols = first + lax.broadcasted_iota(jnp.int32, (bq, bk), 1)
                allowed = cols <= jnp.maximum(rows, prefix - 1)
            fresh = []
            s = [dot(query_ext[h, :, here], key_ext[h, :, there], ((0,), (0,))) for h in range(pair)]
            gp = [dot(grad_ext[h, :, here], value_ext[h, :, there], ((0,), (0,))) for h in range(pair)]
            for h in range(pair):
                x = jnp.where(allowed, s[h], MASKED) if masked else s[h]
                p = jnp.exp2(x)
                ds = (p * gp[h]).astype(BF16)
                rows = slice(h * dh, (h + 1) * dh)
                dv_acc[h, :, there] += dot(g_ref[rows, here], p.astype(BF16))
                dk_acc[h, :, there] += dot(q_ref[rows, here], ds)
                fresh.append(state[h] + dot(ds, k_ref[rows, there], ((1,), (1,))))
            return tuple(fresh)

        state = tuple(jnp.zeros((bq, dh), F32) for _ in range(pair))
        state = lax.fori_loop(0, full, functools.partial(step, False), state)
        state = lax.fori_loop(full, stop, functools.partial(step, True), state)
        for h in range(pair):
            rows = slice(h * dh, (h + 1) * dh)
            dq = state[h].T
            prod = dq * q_ref[rows, here].astype(F32)
            part = prod[:, :128]
            for c in range(1, bq // 128):
                part = part + prod[:, c * 128:(c + 1) * 128]
            fg_ref[...] += part
            dq_ref[rows, here] = (dq * scale_ref[...]).astype(BF16)
        return carry

    lax.fori_loop(0, length // bq, one_query, 0)
    for h in range(pair):
        rows = slice(h * dh, (h + 1) * dh)
        dk_ref[rows, :] = (dk_acc[h] * math.log(2.0)).astype(BF16)
        dv_ref[rows, :] = dv_acc[h].astype(BF16)


def attention_backward(q, k, v, o, g, lse, factor, prefix, order, dh, base=0, width=None, pair=2):
    full, length = q.shape
    width = width or full
    heads = width // dh
    pair = min(pair, heads)
    bq = bk = length // order.shape[0]
    ext = dh + 16
    spec = pl.BlockSpec((pair * dh, length), lambda i, p, o: (i, 0))
    skip = base // (pair * dh)
    source = pl.BlockSpec((pair * dh, length), lambda i, p, o: (i + skip, 0))
    wide = jax.ShapeDtypeStruct((width, length), BF16)
    return pl.pallas_call(
        functools.partial(backward_kernel, pair=pair, dh=dh, bq=bq, bk=bk),
        grid_spec=pltpu.PrefetchScalarGridSpec(
            num_scalar_prefetch=2, grid=(heads // pair,),
            in_specs=[source] * 5 + [pl.BlockSpec((pair, 1, length), lambda i, p, o: (i + skip, 0, 0)), pl.BlockSpec((dh, 1), lambda i, p, o: (0, 0))],
            out_specs=[spec] * 3 + [pl.BlockSpec((dh, 128), lambda i, p, o: (0, 0))],
            scratch_shapes=[
                pltpu.VMEM((pair, ext, length), BF16),
                pltpu.VMEM((pair, ext, length), BF16),
                pltpu.VMEM((pair, ext, length), BF16),
                pltpu.VMEM((pair, ext, length), BF16),
                pltpu.VMEM((pair, dh, length), F32),
                pltpu.VMEM((pair, dh, length), F32)],
        ),
        out_shape=[wide] * 3 + [jax.ShapeDtypeStruct((dh, 128), F32)],
        compiler_params=pltpu.CompilerParams(vmem_limit_bytes=VMEM_LIMIT),
        cost_estimate=pl.CostEstimate(flops=int(HINT * 1600 * length * length * heads), bytes_accessed=int(HINT * 16 * width * length), transcendentals=0),
        name="attention_backward",
    )(prefix, order, q, k, v, o, g, lse, factor.reshape(dh, 1))


def rms(x):
    inv = lax.rsqrt(jnp.mean(x * x, axis=-1, keepdims=True) + EPSILON)
    return x * inv, inv


def rms_back(normed, inv, gain, grad):
    scaled = grad * gain
    out = inv * (scaled - normed * jnp.mean(scaled * normed, axis=-1, keepdims=True))
    return out, jnp.sum(grad * normed, axis=0)


def ein(spec, *args):
    return jnp.einsum(spec, *args, preferred_element_type=F32)


def gather_kernel(pieces, pairs, outer, ring, shard_ref, block_ref, *refs):
    outs = [refs[2 * m:2 * m + 2] for m in range(pairs)]
    got_ref = refs[2 * pairs]
    send, recv, local = refs[2 * pairs + 1:]
    f, t = lax.axis_index("fsdp"), lax.axis_index("tp")
    zz, yy = f // 2, f % 2
    across = {"tp": lax.rem(t + ring, 2 * ring)}
    beside = {"fsdp": zz * 2 + 1 - yy}
    along = [{"fsdp": lax.rem(zz + k, outer) * 2 + yy} for k in range(1, outer)]
    peers = along + [across, beside]
    barrier = pltpu.get_barrier_semaphore()
    for peer in peers:
        pl.semaphore_signal(barrier, inc=1, device_id=peer, device_id_type=MESH)
    pl.semaphore_wait(barrier, len(peers))
    used = [0]

    def copy(src, dst, peer):
        slot = used[0]
        used[0] += 1
        return pltpu.make_async_remote_copy(
            src_ref=src, dst_ref=dst, send_sem=send.at[slot], recv_sem=recv.at[slot],
            device_id=peer, device_id_type=MESH,
        )

    count = len(pieces)
    chunks = 4
    step = block_ref.shape[0] // chunks
    blocks = [
        copy(block_ref.at[pl.ds(i * step, step)], got_ref.at[pl.ds(i * step, step)], across)
        for i in range(chunks)
    ]
    own, first, second, third = [], [], [], []
    for i, (m, low, rows, route) in enumerate(pieces):
        part = pl.ds(low, rows)
        w = [out.at[:, :, part] for out in outs[m]]
        src = shard_ref.at[m, part]
        own.append(pltpu.make_async_copy(src, w[0].at[zz, yy], local.at[i]))
        first.append([copy(src, w[0].at[zz, yy], peer) for peer in along])
        if route:
            second.append([copy(w[0].at[:, yy], w[0].at[:, yy], beside)])
            third.append([copy(w[0], w[1], across)])
        else:
            second.append([copy(w[0].at[:, yy], w[1].at[:, yy], across)])
            third.append([copy(w[s].at[:, yy], w[s].at[:, yy], beside) for s in range(2)])

    def begin(i):
        own[i].start()
        for c in first[i]:
            c.start()

    ahead = 3
    for i in range(min(ahead, count)):
        begin(i)
    started = 0
    for b in blocks[:2]:
        b.start()
    started = 2
    for i in range(count + 2):
        if i < count:
            own[i].wait()
            for c in first[i]:
                c.wait_recv()
            for c in second[i]:
                c.start()
            if i + ahead < count:
                begin(i + ahead)
            if started < chunks:
                blocks[started].start()
                started += 1
        if 0 <= i - 1 < count:
            for c in second[i - 1]:
                c.wait_recv()
            for c in third[i - 1]:
                c.start()
        if 0 <= i - 2 < count:
            for c in third[i - 2]:
                c.wait_recv()
    for b in blocks[started:]:
        b.start()
    for i in range(count):
        for c in first[i] + second[i] + third[i]:
            c.wait_send()
    for b in blocks:
        b.wait()


def pieces_of(pairs, rows):
    half = rows // 32 * 16
    return tuple(
        (m, low, size, m_part) for m in range(pairs) for m_part, (low, size) in enumerate(((0, half), (half, rows - half)))
    )


def gather_call(shards, block, pieces, fsdp, ring):
    pairs, rows, w = shards.shape
    outer = fsdp // 2
    slots = 4 + len(pieces) * (outer + 2)
    any_spec = pl.BlockSpec(memory_space=pl.ANY)
    got = pl.pallas_call(
        functools.partial(gather_kernel, pieces, pairs, outer, ring),
        out_shape=[jax.ShapeDtypeStruct((outer, 2, rows, w), BF16)] * (2 * pairs)
        + [jax.ShapeDtypeStruct(block.shape, block.dtype)],
        in_specs=[any_spec] * 2,
        out_specs=[any_spec] * (2 * pairs + 1),
        scratch_shapes=[
            pltpu.SemaphoreType.DMA((slots,)),
            pltpu.SemaphoreType.DMA((slots,)),
            pltpu.SemaphoreType.DMA((len(pieces),)),
        ],
        compiler_params=pltpu.CompilerParams(collective_id=0, has_side_effects=True),
        name="gather_weights",
    )(shards, block)
    return [a.reshape(outer * 2 * rows, w) for a in got[:-1]], got[-1]


class Plan:
    def __init__(self, seqs, tp, fsdp, rows):
        self.seqs, self.tp, self.ring, self.fsdp = seqs, tp, tp // seqs, fsdp
        self.same_member = [[s * self.ring + r for s in range(seqs)] for r in range(self.ring)]
        self.same_seq = [[s * self.ring + r for r in range(self.ring)] for s in range(seqs)]
        self.fast = seqs == 2 and self.ring == 2 and fsdp % 2 == 0 and rows % 32 == 0
        t = lax.axis_index("tp")
        self.seq, self.member = t // self.ring, lax.rem(t, self.ring)

    def across(self, a):
        n = self.tp
        return lax.ppermute(a, "tp", [(t, (t + self.ring) % n) for t in range(n)])

    def core(self, a):
        return lax.ppermute(a, "tp", [(t, t ^ 1) for t in range(self.tp)])

    def pick(self, blocks, index):
        return lax.dynamic_index_in_dim(blocks, index, 0, keepdims=False)

    def order(self, own, other):
        first = self.seq == 0
        return jnp.concatenate([jnp.where(first, own, other), jnp.where(first, other, own)])

    def swap(self, blocks):
        if self.seqs == 2:
            other = self.across(self.pick(blocks, 1 - self.seq).astype(BF16))
            return self.order(self.pick(blocks, self.seq), other.astype(F32))
        got = lax.all_to_all(
            blocks.astype(BF16), "tp", 0, 0, tiled=True, axis_index_groups=self.same_member
        )
        return got.reshape(-1, got.shape[-1]).astype(F32)

    def unswap(self, rows):
        blocks = rows.reshape(self.seqs, -1, rows.shape[-1])
        return self.swap(blocks).reshape(blocks.shape)

    def whole(self, rows):
        if self.fast:
            return jnp.concatenate([rows, self.core(rows)])
        cut = rows.reshape(self.seqs, -1, rows.shape[-1])
        got = lax.all_gather(cut, "tp", axis=1, axis_index_groups=self.same_seq)
        return got.reshape(-1, rows.shape[-1])

    def share(self, full):
        if self.fast:
            own = full.shape[0] // 2
            return full[:own].astype(F32) + self.core(full[own:].astype(BF16)).astype(F32)
        cut = full.astype(BF16).reshape(self.seqs, self.ring, -1, full.shape[-1])
        got = lax.psum_scatter(cut, "tp", scatter_dimension=1, axis_index_groups=self.same_seq)
        return got.reshape(-1, full.shape[-1]).astype(F32)

    def blocks(self, length):
        if self.fast:
            j = jnp.arange(self.tp, dtype=jnp.int32)
            apart = (j % self.ring != self.member).astype(jnp.int32)
            return apart * self.seqs + j // self.ring
        return jnp.arange(max(1, length // 512), dtype=jnp.int32)

    def gather_heads(self, shards):
        rows = lax.all_gather(shards, "fsdp", axis=1, tiled=True)
        if self.fast:
            return jnp.stack([rows, self.across(rows)])
        return lax.all_gather(rows, "tp", axis_index_groups=self.same_member)

    def join(self, every):
        r, s, m, d, w = every.shape
        return every.transpose(2, 3, 0, 1, 4).reshape(m, d, r * s * w)

    def gather_full(self, shards):
        part = self.gather_heads(shards)
        if self.fast:
            return self.join(jnp.stack([part, self.core(part)]))
        return self.join(lax.all_gather(part, "tp", axis_index_groups=self.same_seq))

    def scatter_heads(self, grads):
        if self.fast:
            other = self.across(grads[1].astype(BF16))
            mine = (grads[0].astype(F32) + other.astype(F32)).astype(BF16)
        else:
            mine = lax.psum_scatter(
                grads.astype(BF16), "tp", scatter_dimension=0, axis_index_groups=self.same_member
            )
        return lax.psum_scatter(mine, "fsdp", scatter_dimension=1, tiled=True).astype(F32)

    def scatter_full(self, grads):
        m, d, cols = grads.shape
        if self.fast:
            half = cols // 2
            other = self.core(grads[:, :, half:].astype(BF16))
            mine = grads[:, :, :half].astype(F32) + other.astype(F32)
            mine = mine.astype(BF16).reshape(m, d, self.seqs, -1).transpose(2, 0, 1, 3)
        else:
            cut = grads.astype(BF16).reshape(m, d, self.ring, self.seqs, -1).transpose(2, 3, 0, 1, 4)
            mine = lax.psum_scatter(cut, "tp", scatter_dimension=0, axis_index_groups=self.same_seq)
        return self.scatter_heads(mine)


def layer_forward(plan, x, prefix, order, qkv, out_t, up, down_t, gains, factor):
    dh = factor.shape[0]
    normed, inv = rms(x)
    h = plan.whole((normed * gains[0]).astype(BF16))
    seqs, d, w = out_t.shape
    raw = [ein("sdc,td->sct", qkv[c], h).reshape(seqs * w, -1) for c in range(3)]
    scale = jnp.tile(factor * LOG2E, seqs * w // dh)[:, None]
    q, k, v = (raw[0] * scale).astype(BF16), raw[1].astype(BF16), raw[2].astype(BF16)
    att, lse = attention_forward(q, k, v, prefix, order, dh)
    middle = x + plan.share(ein("sct,sdc->td", att.reshape(seqs, w, -1), out_t))
    normed_m, inv_m = rms(middle)
    h_m = (normed_m * gains[1]).astype(BF16)
    pre = ein("td,df->tf", h_m, up)
    hidden = jax.nn.silu(pre).astype(BF16)
    result = middle + ein("tf,df->td", hidden, down_t)
    return result, (x, inv, h, q, k, v, att, lse, middle, inv_m, h_m, pre, hidden)


def layer_backward(plan, g, saved, prefix, order, qkv, out_t, up, down_t, gains, factor):
    x, inv, h, q, k, v, att, lse, middle, inv_m, h_m, pre, hidden = saved
    dh = factor.shape[0]
    seqs, d, w = out_t.shape
    length = h.shape[0]
    g_low = g.astype(BF16)
    down_grad = ein("td,tf->df", g_low, hidden)
    g_hidden = ein("td,df->tf", g_low, down_t)
    sig = jax.nn.sigmoid(pre)
    g_pre = (g_hidden * sig * (1.0 + pre * (1.0 - sig))).astype(BF16)
    up_grad = ein("td,tf->df", h_m, g_pre)
    mlp_grads = plan.scatter_full(jnp.stack([up_grad, down_grad]))
    g_hm = ein("tf,df->td", g_pre, up)
    back_m, gain_m = rms_back(middle * inv_m, inv_m, gains[1], g_hm)
    g_mid = g + back_m
    g_all = plan.whole(g_mid.astype(BF16))
    att3 = att.reshape(seqs, w, length)
    out_grad = plan.scatter_heads(ein("td,sct->sdc", g_all, att3)[:, None])[0]
    g_att = ein("td,sdc->sct", g_all, out_t).astype(BF16).reshape(seqs * w, length)
    dq, dk, dv, fg = attention_backward(q, k, v, att, g_att, lse, factor, prefix, order, dh)
    factor_grad = jnp.sum(fg, axis=1) / (factor * LOG2E)
    parts = [a.reshape(seqs, w, length) for a in (dq, dk, dv)]
    qkv_grad = plan.scatter_heads(jnp.stack([ein("td,sct->sdc", h, a) for a in parts], axis=1))
    g_ha = plan.share(sum(ein("sct,sdc->td", a, b) for a, b in zip(parts, qkv)))
    back_a, gain_a = rms_back(x * inv, inv, gains[0], g_ha)
    return g_mid + back_a, (qkv_grad, out_grad.T, mlp_grads[0], mlp_grads[1].T, gain_a, gain_m, factor_grad)


TN, NT, TT = ((0,), (0,)), ((1,), (1,)), ((0,), (1,))
ONE = pl.Buffered(1)


def cost(flops, nbytes):
    return pl.CostEstimate(flops=int(flops * HINT), bytes_accessed=int(nbytes * HINT), transcendentals=0)


def params(mib=60):
    return pltpu.CompilerParams(vmem_limit_bytes=mib * 2**20)


def fixed(shape):
    return pl.BlockSpec(shape, lambda *a: (0,) * len(shape), pipeline_mode=ONE)


def weight(w, lanes=None):
    stack, index = w if isinstance(w, tuple) else (w, None)
    shape = (stack.shape[-2], lanes or stack.shape[-1])
    if index is None:
        return fixed(shape)
    return pl.BlockSpec((None,) + shape, lambda *a: (index, 0, 0), pipeline_mode=ONE)


def plain(weights):
    return [w[0] if isinstance(w, tuple) else w for w in weights]


def shape_of(shape, dtype=BF16):
    return jax.ShapeDtypeStruct(shape, dtype)


def inverse_rms(x):
    return lax.rsqrt(jnp.mean(x * x, axis=-1, keepdims=True) + EPSILON)


def eight(x):
    return jnp.sum(x.reshape(-1, 8, x.shape[-1]), axis=0)


def join_lanes(dst, refs, low, high):
    width = high - low
    for i, ref in enumerate(refs):
        dst[:, i * width:(i + 1) * width] = ref[:, low:high]


def core_of():
    t = lax.axis_index("tp")
    return {"tp": t + 1 - 2 * lax.rem(t, 2)}


def pushes(send, recv, core):
    def push(src, dst, slot):
        return pltpu.make_async_remote_copy(
            src_ref=src, dst_ref=dst, send_sem=send.at[slot], recv_sem=recv.at[slot],
            device_id=core, device_id_type=MESH,
        )

    return push


def greet(core):
    barrier = pltpu.get_barrier_semaphore()
    pl.semaphore_signal(barrier, inc=1, device_id=core, device_id_type=MESH)
    pl.semaphore_wait(barrier, 1)


def stack_index(weights):
    return tuple(a[1] if isinstance(a, tuple) else None for a in weights)


def entry(ref, k):
    return ref if k is None else ref.at[k]


def stages(steps):
    starts = [sum(steps[:n]) for n in range(len(steps))]

    def at(n, make):
        return lambda i: make(jnp.clip(i - starts[n], 0, steps[n] - 1))

    return at


ANY = pl.BlockSpec(memory_space=pl.ANY)


class Halves:
    def __init__(self, own_any, got_any, own, got, load, ring):
        self.seq = lax.axis_index("tp") // ring
        self.own, self.got = own, got
        self.copies = [
            pltpu.make_async_copy(own_any.at[self.seq], own, load.at[0]),
            pltpu.make_async_copy(got_any, got, load.at[1]),
        ]

    def rows(self, k, size):
        per = self.own.shape[0] // size
        here = pl.ds(pl.multiple_of(lax.rem(k, per) * size, size), size)
        return jnp.where(k // per == self.seq, self.own[here], self.got[here].astype(F32))


def halves_scratch(rows, d):
    return [pltpu.VMEM((rows // 2, d), F32), pltpu.VMEM((rows // 2, d), BF16), pltpu.SemaphoreType.DMA((2,))]


def project_kernel(w, low, steps, index, bt, ring, gain_ref, scale_ref, *refs):
    weights, refs = refs[:4], refs[4:]
    if ring:
        own_any, got_any, own_ref, other_ref, q_ref, k_ref, v_ref, x_out = refs[:8]
        own, other, qk, vo, load, send, recv, *rest = refs[8:]
        halves = Halves(own_any, got_any, *rest, ring)
    else:
        x_ref, own_ref, other_ref, q_ref, k_ref, v_ref = refs[:6]
        own, other, qk, vo, load, send, recv = refs[6:]
    i = pl.program_id(0)
    rows_steps, half, _ = steps
    ba = q_ref.shape[1]
    core = core_of()
    push = pushes(send, recv, core)

    def loads():
        copies = [pltpu.make_async_copy(entry(weights[s], index[s]), qk.at[s], load.at[s]) for s in range(2)]
        for s in range(2):
            src = entry(weights[2 + s], index[2 + s]).at[:, pl.ds(0, low)]
            copies.append(pltpu.make_async_copy(src, vo.at[s], load.at[2 + s]))
        return copies

    def push_rows(k):
        part = pl.ds(pl.multiple_of(k * bt, bt), bt)
        return push(own.at[part], other.at[part], k)

    @pl.when(i == 0)
    def _():
        if ring:
            for c in halves.copies:
                c.start()
        for c in loads():
            c.start()
        greet(core)
        if ring:
            for c in halves.copies:
                c.wait()

    @pl.when(i < rows_steps)
    def _():
        if ring:
            x = halves.rows(i, bt)
            x_out[...] = x
        else:
            x = x_ref[...]
        h = (x * inverse_rms(x) * gain_ref[...]).astype(BF16)
        own[pl.ds(pl.multiple_of(i * bt, bt), bt)] = h
        own_ref[...] = h
        push_rows(i).start()

    at = i - rows_steps

    @pl.when(at == 0)
    def _():
        for c in loads():
            c.wait()

    @pl.when(at == half)
    def _():
        for k in range(rows_steps):
            push_rows(k).wait()

    def project(h):
        for s in range(2):
            rows = slice(s * w, (s + 1) * w)
            both = dot(qk[s], h, TT)
            q_ref[rows] = (both[:w] * scale_ref[rows]).astype(BF16)
            k_ref[rows] = both[w:].astype(BF16)
            v_ref[rows] = dot(vo[s, :, :w], h, TT).astype(BF16)

    @pl.when((at >= 0) & (at < half))
    def _():
        project(own[pl.ds(pl.multiple_of(at * ba, ba), ba)])

    @pl.when(at >= half)
    def _():
        h = other[pl.ds(pl.multiple_of((at - half) * ba, ba), ba)]
        other_ref[...] = h
        project(h)


def project(x, gain, qk, vo, scale, call, ring=0):
    xs = x if ring else (x,)
    d = xs[0].shape[-1]
    rows = 2 * xs[1].shape[0] if ring else x.shape[0]
    w2 = plain(qk)[0].shape[-1]
    w = w2 // 2
    low = -(-w // 128) * 128
    bt, ba = 256, 512
    half = rows // ba
    steps = (rows // bt, half, half)
    row = pl.BlockSpec((bt, d), lambda i: (jnp.minimum(i, steps[0] - 1), 0))
    wide = pl.BlockSpec((w2, ba), lambda i: (0, jnp.clip(i - steps[0], 0, 2 * half - 1)))
    tall = pl.BlockSpec((ba, d), lambda i: (jnp.clip(i - steps[0] - half, 0, half - 1), 0))
    weights = (*qk, *vo)
    return pl.pallas_call(
        functools.partial(project_kernel, w, low, steps, stack_index(weights), bt, ring),
        grid=(sum(steps),),
        in_specs=[fixed((1, d)), fixed((w2, 1))] + [ANY] * 4 + ([ANY] * 2 if ring else [row]),
        out_specs=[row, tall] + [wide] * 3 + ([row] if ring else []),
        out_shape=[shape_of((rows, d))] * 2 + [shape_of((w2, 2 * rows))] * 3 + ([shape_of((rows, d), F32)] if ring else []),
        scratch_shapes=[
            pltpu.VMEM((rows, d), BF16), pltpu.VMEM((rows, d), BF16),
            pltpu.VMEM((2, d, w2), BF16), pltpu.VMEM((2, d, low), BF16),
            pltpu.SemaphoreType.DMA((4,)), pltpu.SemaphoreType.DMA((steps[0],)), pltpu.SemaphoreType.DMA((steps[0],)),
        ]
        + (halves_scratch(rows, d) if ring else []),
        compiler_params=pltpu.CompilerParams(vmem_limit_bytes=VMEM_LIMIT, collective_id=call, has_side_effects=True),
        cost_estimate=cost(4 * rows * d * 3 * w2, 12 * rows * d),
        name="project",
    )(gain, scale, *plain(weights), *xs)


def middle_kernel(w, low, steps, index, x_ref, gm_ref, att_any, *refs):
    weights, refs = refs[:4], refs[4:]
    mid_ref, pre_ref, res_ref, up_out, down_out, out_out = refs[:6]
    (up_mat, down_mat, out_mat, blocks, vo_side, att, part, got, load, store, send, recv) = refs[6:]
    i = pl.program_id(0)
    far, rows_steps = steps
    bt = x_ref.shape[0]
    ba = part.shape[0] // far
    rows = part.shape[0]
    core = core_of()
    push = pushes(send, recv, core)

    def loads():
        copies = [pltpu.make_async_copy(att_any, att, load.at[0])]
        for s in range(2):
            src = entry(weights[s], index[s]).at[:, pl.ds(low, vo_side.shape[2])]
            copies.append(pltpu.make_async_copy(src, vo_side.at[s], load.at[1 + s]))
        for s in range(2):
            copies.append(pltpu.make_async_copy(entry(weights[2 + s], index[2 + s]), blocks.at[s], load.at[3 + s]))
        return copies

    def stores():
        pairs = ((up_mat, up_out), (down_mat, down_out), (out_mat, out_out))
        return [pltpu.make_async_copy(src, dst, store.at[n]) for n, (src, dst) in enumerate(pairs)]

    def push_block(s):
        return push(blocks.at[s], blocks.at[2 + s], s)

    def push_part(k):
        here = pl.ds(pl.multiple_of(k * ba, ba), ba)
        return push(part.at[here], got.at[here], 2 + k)

    @pl.when(i == 0)
    def _():
        copies = loads()
        for c in copies:
            c.start()
        greet(core)
        for c in copies[:3]:
            c.wait()
        for s in range(2):
            out_mat[:, s * w:(s + 1) * w] = vo_side[s, :, 2 * w - low - w:2 * w - low]
        for s in range(2):
            copies[3 + s].wait()
            push_block(s).start()

    @pl.when(i < far)
    def _():
        here = pl.ds(pl.multiple_of(i * ba, ba), ba)
        cols = pl.ds(pl.multiple_of(rows + i * ba, ba), ba)
        part[here] = dot(att[:, cols], out_mat[...], TT).astype(BF16)
        push_part(i).start()

    at = i - far

    @pl.when(at == 0)
    def _():
        for s in range(2):
            push_block(s).wait()
        for b in range(4):
            up_mat[:, b * w:(b + 1) * w] = blocks[b, :, 0:w]
            down_mat[:, b * w:(b + 1) * w] = blocks[b, :, w:2 * w]
        for c in stores():
            c.start()

    for k in range(far):
        @pl.when(at == k * (ba // bt))
        def _():
            push_part(k).wait()

    @pl.when(at >= 0)
    def _():
        here = pl.ds(pl.multiple_of(at * bt, bt), bt)
        mid = x_ref[...] + got[here].astype(F32) + dot(att[:, here], out_mat[...], TT)
        mid_ref[...] = mid
        h_m = (mid * inverse_rms(mid) * gm_ref[...]).astype(BF16)
        pre = dot(h_m, up_mat[...])
        pre_ref[...] = pre
        hidden = (pre / (1.0 + jnp.exp(-pre))).astype(BF16)
        res_ref[...] = mid + dot(hidden, down_mat[...], NT)

    @pl.when(at == rows_steps - 1)
    def _():
        for c in stores():
            c.wait()


def middle_call(x, att, gain_m, vo, un, call):
    rows, d = x.shape
    w2 = plain(vo)[0].shape[-1]
    w, ff = w2 // 2, 2 * w2
    low = w // 128 * 128
    bt, ba = 256, 512
    steps = (rows // ba, rows // bt)
    row = pl.BlockSpec((bt, d), lambda i: (jnp.maximum(i - steps[0], 0), 0))
    wide = pl.BlockSpec((bt, ff), lambda i: (jnp.maximum(i - steps[0], 0), 0))
    weights = (*vo, *un)
    mats = [(d, ff), (d, ff), (d, w2)]
    slots = 2 + steps[0]
    return pl.pallas_call(
        functools.partial(middle_kernel, w, low, steps, stack_index(weights)),
        grid=(sum(steps),),
        in_specs=[row, fixed((1, d))] + [ANY] * 5,
        out_specs=[row, wide, row] + [ANY] * 3,
        out_shape=[shape_of((rows, d), F32), shape_of((rows, ff), F32), shape_of((rows, d), F32)] + [shape_of(m) for m in mats],
        scratch_shapes=[pltpu.VMEM(m, BF16) for m in mats]
        + [pltpu.VMEM((4, d, w2), BF16), pltpu.VMEM((2, d, w2 - low), BF16), pltpu.VMEM(att.shape, BF16)]
        + [pltpu.VMEM((rows, d), BF16)] * 2
        + [pltpu.SemaphoreType.DMA((5,)), pltpu.SemaphoreType.DMA((3,)), pltpu.SemaphoreType.DMA((slots,)), pltpu.SemaphoreType.DMA((slots,))],
        compiler_params=pltpu.CompilerParams(vmem_limit_bytes=VMEM_LIMIT, collective_id=call, has_side_effects=True),
        cost_estimate=cost(2 * rows * d * (2 * w2 + 2 * ff), 30 * rows * d),
        name="middle",
    )(x, gain_m, att, *plain(weights))


def mlp_back_kernel(w, steps, ring, mid_ref, pre_ref, gm_ref, att_any, *refs):
    mats, refs = refs[:3], refs[3:]
    if ring:
        own_any, got_any, refs = refs[0], refs[1], refs[2:]
        halves = Halves(own_any, got_any, *refs[-3:], ring)
        refs = refs[:-3]
    else:
        g_ref, refs = refs[0], refs[1:]
    g_mid_ref, gain_ref, g_att_ref, o0, o1 = refs[:5]
    (up_mat, down_mat, out_mat, g_all, hid_all, hm_all, gpre_all, low_own, low_other, blocks, got, att,
     load, send, recv) = refs[5:]
    i = pl.program_id(0)
    rows_steps, grad_steps, att_steps, _ = steps
    bt, bd, ba = mid_ref.shape[0], o0.shape[0], g_att_ref.shape[1]
    core = core_of()
    push = pushes(send, recv, core)

    def loads():
        pairs = (*zip(mats, (up_mat, down_mat, out_mat)), (att_any, att))
        return [pltpu.make_async_copy(src, dst, load.at[n]) for n, (src, dst) in enumerate(pairs)]

    def push_rows(k):
        part = pl.ds(pl.multiple_of(k * bt, bt), bt)
        return push(low_own.at[part], low_other.at[part], k)

    def push_block(c, s):
        part = pl.ds(pl.multiple_of(c * bd, bd), bd)
        return push(blocks.at[2 + s, part], got.at[s, part], rows_steps + 2 * c + s)

    @pl.when(i == 0)
    def _():
        copies = loads()
        for c in copies:
            c.start()
        gain_ref[...] = jnp.zeros_like(gain_ref)
        if ring:
            for c in halves.copies:
                c.start()
        greet(core)
        for c in copies[:2] + (halves.copies if ring else []):
            c.wait()

    @pl.when(i < rows_steps)
    def _():
        here = pl.ds(pl.multiple_of(i * bt, bt), bt)
        g = halves.rows(i, bt) if ring else g_ref[...]
        g_low = g.astype(BF16)
        g_all[here] = g_low
        pre = pre_ref[...]
        sig = 1.0 / (1.0 + jnp.exp(-pre))
        hid_all[here] = (pre * sig).astype(BF16)
        g_hidden = dot(g_low, down_mat[...])
        g_pre = (g_hidden * sig * (1.0 + pre * (1.0 - sig))).astype(BF16)
        gpre_all[here] = g_pre
        mid = mid_ref[...]
        inv = inverse_rms(mid)
        normed = mid * inv
        gain = gm_ref[...]
        hm_all[here] = (normed * gain).astype(BF16)
        g_hm = dot(g_pre, up_mat[...], NT)
        gain_ref[...] += eight(g_hm * normed)
        scaled = g_hm * gain
        g_mid = g + inv * (scaled - normed * jnp.mean(scaled * normed, axis=-1, keepdims=True))
        g_mid_ref[...] = g_mid
        low_own[here] = g_mid.astype(BF16)
        push_rows(i).start()

    at = i - rows_steps

    @pl.when((at >= 0) & (at < grad_steps))
    def _():
        cols = pl.ds(pl.multiple_of(at * bd, bd), bd)
        up = dot(hm_all[:, cols], gpre_all[...], TN).astype(BF16)
        down = dot(g_all[:, cols], hid_all[...], TN).astype(BF16)
        for b in range(4):
            blocks[b, cols, 0:w] = up[:, b * w:(b + 1) * w]
            blocks[b, cols, w:2 * w] = down[:, b * w:(b + 1) * w]
        for s in range(2):
            push_block(at, s).start()

    to = at - grad_steps

    @pl.when(to == 0)
    def _():
        loads()[2].wait()

    half = att_steps // 2

    @pl.when((to >= 0) & (to < half))
    def _():
        here = pl.ds(pl.multiple_of(to * ba, ba), ba)
        g_att_ref[...] = dot(out_mat[...], low_own[here], TT).astype(BF16)

    @pl.when(to == half)
    def _():
        for k in range(rows_steps):
            push_rows(k).wait()

    @pl.when((to >= half) & (to < att_steps))
    def _():
        here = pl.ds(pl.multiple_of((to - half) * ba, ba), ba)
        g_att_ref[...] = dot(out_mat[...], low_other[here], TT).astype(BF16)

    last = to - att_steps

    @pl.when(last == 0)
    def _():
        loads()[3].wait()

    @pl.when(last >= 0)
    def _():
        cols = pl.ds(pl.multiple_of(last * bd, bd), bd)
        rows = low_own.shape[0]
        grad = dot(low_own[:, cols], att[:, :rows], TT) + dot(low_other[:, cols], att[:, rows:], TT)
        grad = grad.astype(BF16)
        for s, out in enumerate((o0, o1)):
            push_block(last, s).wait()
            out[:, :2 * w] = (blocks[s, cols].astype(F32) + got[s, cols].astype(F32)).astype(BF16)
            out[:, 2 * w:3 * w] = grad[:, s * w:(s + 1) * w]
            out[:, 3 * w:] = jnp.zeros((bd, out.shape[1] - 3 * w), BF16)


def mlp_back(g, mid, pre, gain, att, mats, width, call, ring=0):
    rows, d = mid.shape
    gs = g if ring else (g,)
    ff = pre.shape[1]
    w2 = att.shape[0]
    w = w2 // 2
    bt, bd, ba = 256, 256, 512
    steps = (rows // bt, d // bd, 2 * rows // ba, d // bd)
    at = stages(steps)
    row = pl.BlockSpec((bt, d), at(0, lambda k: (k, 0)))
    wide = pl.BlockSpec((bt, ff), at(0, lambda k: (k, 0)))
    block = pl.BlockSpec((bd, width), at(3, lambda k: (k, 0)))
    slots = steps[0] + 2 * steps[1]
    return pl.pallas_call(
        functools.partial(mlp_back_kernel, w, steps, ring),
        grid=(sum(steps),),
        in_specs=[row, wide, fixed((1, d))] + [ANY] * 4 + ([ANY] * 2 if ring else [row]),
        out_specs=[row, fixed((8, d)), pl.BlockSpec((w2, ba), at(2, lambda k: (0, k))), block, block],
        out_shape=[shape_of((rows, d), F32), shape_of((8, d), F32), shape_of((w2, 2 * rows))] + [shape_of((d, width))] * 2,
        scratch_shapes=[pltpu.VMEM((d, ff), BF16)] * 2
        + [pltpu.VMEM((d, w2), BF16)]
        + [pltpu.VMEM((rows, d), BF16), pltpu.VMEM((rows, ff), BF16)] * 2
        + [pltpu.VMEM((rows, d), BF16)] * 2
        + [pltpu.VMEM((4, d, w2), BF16), pltpu.VMEM((2, d, w2), BF16)]
        + [pltpu.VMEM(att.shape, BF16)]
        + [pltpu.SemaphoreType.DMA((4,)), pltpu.SemaphoreType.DMA((slots,)), pltpu.SemaphoreType.DMA((slots,))]
        + (halves_scratch(rows, d) if ring else []),
        compiler_params=pltpu.CompilerParams(vmem_limit_bytes=62 * 2**20, collective_id=call, has_side_effects=True),
        cost_estimate=cost(8 * rows * d * ff + 8 * rows * d * w2, 40 * rows * d),
        name="mlp_back",
    )(mid, pre, gain, att, *mats, *gs)


def weight_grad_kernel(w, own_ref, other_ref, dq_ref, dk_ref, dv_ref, *refs):
    out, stacked = refs[-2:]
    half = own_ref.shape[0]

    @pl.when(pl.program_id(0) == 0)
    def _():
        for j, ref in enumerate((dq_ref, dk_ref, dv_ref)):
            stacked[j * w:(j + 1) * w, :] = ref[...]

    grad = dot(own_ref[...], stacked[:, :half], TT) + dot(other_ref[...], stacked[:, half:], TT)
    if len(refs) == 3:
        grad = grad + refs[0][:, :3 * w].astype(F32)
    out[:, :3 * w] = grad.astype(BF16)
    out[:, 3 * w:] = jnp.zeros((out.shape[0], out.shape[1] - 3 * w), BF16)


def weight_grad(own, other, dq, dk, dv, width, got=None):
    rows, d = own.shape
    w = dq.shape[0]
    bd = 256
    col = pl.BlockSpec((rows, bd), lambda i: (0, i))
    flat = pl.BlockSpec((bd, width), lambda i: (i, 0))
    extra = [] if got is None else [got]
    return pl.pallas_call(
        functools.partial(weight_grad_kernel, w),
        grid=(d // bd,),
        in_specs=[col, col] + [fixed(dq.shape)] * 3 + [flat] * len(extra),
        out_specs=flat,
        out_shape=shape_of((d, width)),
        scratch_shapes=[pltpu.VMEM((3 * w, 2 * rows), BF16)],
        compiler_params=params(),
        cost_estimate=cost(12 * rows * d * w, 12 * rows * d),
        name="weight_grad",
    )(own, other, dq, dk, dv, *extra)


def input_back_kernel(w, low, steps, index, x_ref, g_ref, gain_ref, *refs):
    grads, weights, refs = refs[:6], refs[6:10], refs[10:]
    stacked, qk, vo, part, got, load, send, recv = refs[-8:]
    i = pl.program_id(0)
    chunk_steps, far, _ = steps
    if chunk_steps:
        own_ref, other_ref, out_ref, sum_ref, piece_ref = refs[:-8]
    else:
        out_ref, sum_ref = refs[:-8]
    bt, half = x_ref.shape[0], part.shape[0]
    ba = half // far
    push = pushes(send, recv, core_of())

    def loads():
        copies = [
            pltpu.make_async_copy(grads[n], stacked.at[n // 3, pl.ds(n % 3 * w, w)], load.at[n]) for n in range(6)
        ]
        for s in range(2):
            copies.append(pltpu.make_async_copy(entry(weights[s], index[s]), qk.at[s], load.at[6 + s]))
        for s in range(2):
            src = entry(weights[2 + s], index[2 + s]).at[:, pl.ds(0, low)]
            copies.append(pltpu.make_async_copy(src, vo.at[s], load.at[8 + s]))
        return copies

    def push_part(k):
        here = pl.ds(pl.multiple_of(k * ba, ba), ba)
        return push(part.at[here], got.at[here], k)

    def total(cols):
        parts = [
            dot(stacked[s, :2 * w, cols], qk[s], TT) + dot(stacked[s, 2 * w:, cols], vo[s, :, :w], TT) for s in range(2)
        ]
        return parts[0] + parts[1]

    @pl.when(i == 0)
    def _():
        copies = loads()
        for c in copies:
            c.start()
        sum_ref[...] = jnp.zeros_like(sum_ref)
        greet(core_of())
        for c in copies[:3]:
            c.wait()

    if chunk_steps:
        @pl.when(i < chunk_steps)
        def _():
            grad = dot(own_ref[...], stacked[0, :, :half], TT) + dot(other_ref[...], stacked[0, :, half:], TT)
            piece_ref[:, :3 * w] = grad.astype(BF16)
            piece_ref[:, 3 * w:] = jnp.zeros((piece_ref.shape[0], piece_ref.shape[1] - 3 * w), BF16)

    to = i - chunk_steps

    @pl.when(to == 0)
    def _():
        for c in loads()[3:]:
            c.wait()

    @pl.when((to >= 0) & (to < far))
    def _():
        cols = pl.ds(pl.multiple_of(half + to * ba, ba), ba)
        part[pl.ds(pl.multiple_of(to * ba, ba), ba)] = total(cols).astype(BF16)
        push_part(to).start()

    at = to - far
    for k in range(far):
        @pl.when(at == k * (ba // bt))
        def _():
            push_part(k).wait()

    @pl.when(at >= 0)
    def _():
        here = pl.ds(pl.multiple_of(at * bt, bt), bt)
        g_ha = total(here) + got[here].astype(F32)
        x = x_ref[...]
        inv = inverse_rms(x)
        normed = x * inv
        sum_ref[...] += eight(g_ha * normed)
        scaled = g_ha * gain_ref[...]
        out_ref[...] = g_ref[...] + inv * (scaled - normed * jnp.mean(scaled * normed, axis=-1, keepdims=True))


def input_back(grads, x, g, gain, qk, vo, call, normed=(), width=0):
    w, length = grads[0].shape
    rows, d = x.shape
    low = -(-w // 128) * 128
    bt, bd, ba = 256, 256, 512
    chunks = d // bd if normed else 0
    steps = (chunks, rows // ba, rows // bt)
    row = pl.BlockSpec((bt, d), lambda i: (jnp.maximum(i - steps[0] - steps[1], 0), 0))

    def chunk(k):
        return jnp.minimum(k, chunks - 1)

    weights = (*qk, *vo)
    in_specs = [row, row, fixed((1, d))] + [ANY] * 10
    out_specs, out_shape = [row, fixed((8, d))], [shape_of((rows, d), F32), shape_of((8, d), F32)]
    if normed:
        in_specs += [pl.BlockSpec((rows, bd), lambda i: (0, chunk(i)))] * 2
        out_specs.append(pl.BlockSpec((bd, width), lambda i: (chunk(i), 0)))
        out_shape.append(shape_of((d, width)))
    return pl.pallas_call(
        functools.partial(input_back_kernel, w, low, steps, stack_index(weights)),
        grid=(sum(steps),),
        in_specs=in_specs,
        out_specs=out_specs,
        out_shape=out_shape,
        scratch_shapes=[
            pltpu.VMEM((2, 3 * w, length), BF16), pltpu.VMEM((2, d, 2 * w), BF16), pltpu.VMEM((2, d, low), BF16),
            pltpu.VMEM((rows, d), BF16), pltpu.VMEM((rows, d), BF16),
            pltpu.SemaphoreType.DMA((10,)), pltpu.SemaphoreType.DMA((steps[1],)), pltpu.SemaphoreType.DMA((steps[1],)),
        ],
        compiler_params=pltpu.CompilerParams(vmem_limit_bytes=VMEM_LIMIT, collective_id=call, has_side_effects=True),
        cost_estimate=cost(9 * rows * d * 4 * w, 24 * rows * d),
        name="input_back",
    )(x, g, gain, *grads, *plain(weights), *normed)


def finish_kernel(w, low, far, own_steps, outer, ring, index, gain_ref, small_ref, x_any, g_any, mine_any, *refs):
    grads, weights, refs = refs[:6], refs[6:10], refs[10:]
    own_any, got_any, late_ref, sums_ref = refs[:4]
    (stacked, qk, vo, part, got, xs, gs, send_half, keep, near, hops, gain_sum, vec, vecs,
     load, store, send, recv) = refs[4:]
    i = pl.program_id(0)
    half = part.shape[0]
    ba, bt = half // far, half // own_steps
    f, t = lax.axis_index("fsdp"), lax.axis_index("tp")
    zz, yy, seq = f // 2, lax.rem(f, 2), t // ring
    across = {"tp": lax.rem(t + ring, 2 * ring)}
    beside = {"fsdp": zz * 2 + 1 - yy}
    along = [{"fsdp": lax.rem(zz + k, outer) * 2 + yy} for k in range(1, outer)]
    core = core_of()
    chunk = keep.shape[1]
    sends = far + outer + outer - 1
    pushed = own_steps // 2

    def push(src, dst, slot, peer):
        return pltpu.make_async_remote_copy(
            src_ref=src, dst_ref=dst, send_sem=send.at[slot], recv_sem=recv.at[slot],
            device_id=peer, device_id_type=MESH,
        )

    def rows_of(j, side):
        z = lax.rem(zz + 1 + j, outer)
        return pl.ds(pl.multiple_of((z * 2 + side) * chunk, chunk), chunk)

    def loads():
        def columns(first):
            cols = pl.ds(first, half)
            return [(grads[n].at[:, cols], stacked.at[n // 3, pl.ds(n % 3 * w, w), cols]) for n in range(6)]

        pairs = columns(half)
        pairs += [(entry(weights[s], index[s]), qk.at[s]) for s in range(2)]
        pairs += [(entry(weights[2 + s], index[2 + s]).at[:, pl.ds(0, low)], vo.at[s]) for s in range(2)]
        pairs += columns(0)
        pairs += [(x_any, xs), (g_any, gs)]
        pairs += [(mine_any.at[rows_of(j, yy)], keep.at[j]) for j in range(outer)]
        return [pltpu.make_async_copy(src, dst, load.at[n]) for n, (src, dst) in enumerate(pairs)]

    def push_part(k):
        here = pl.ds(pl.multiple_of(k * ba, ba), ba)
        return push(part.at[here], got.at[here], k, core)

    def push_near(j):
        return push(mine_any.at[rows_of(j, 1 - yy)], near.at[j], far + j, beside)

    def push_hop(j):
        return push(keep.at[j], hops.at[j], far + outer + j, along[j])

    def push_half(k):
        here = pl.ds(pl.multiple_of(k * bt, bt), bt)
        return push(send_half.at[here], got_any.at[here], sends + k, across)

    def push_small(n):
        peer = ([core, across, beside] + along)[n]
        return push(vec.at[min(n, 3)], vecs.at[n], sends + pushed + n, peer)

    def total(cols):
        parts = [
            dot(stacked[s, :2 * w, cols], qk[s], TT) + dot(stacked[s, 2 * w:, cols], vo[s, :, :w], TT) for s in range(2)
        ]
        return parts[0] + parts[1]

    @pl.when(i == 0)
    def _():
        copies = loads()
        for c in copies[:10]:
            c.start()
        gain_sum[...] = jnp.zeros_like(gain_sum)
        barrier = pltpu.get_barrier_semaphore()
        peers = [core, across, beside] + along
        for peer in peers:
            pl.semaphore_signal(barrier, inc=1, device_id=peer, device_id_type=MESH)
        pl.semaphore_wait(barrier, len(peers))
        for j in range(outer):
            push_near(j).start()
        for c in copies[:10]:
            c.wait()
        for c in copies[10:]:
            c.start()

    @pl.when(i < far)
    def _():
        cols = pl.ds(pl.multiple_of(half + i * ba, ba), ba)
        part[pl.ds(pl.multiple_of(i * ba, ba), ba)] = total(cols).astype(BF16)
        push_part(i).start()

    at = i - far

    @pl.when(at == 0)
    def _():
        for c in loads()[10:]:
            c.wait()
        for k in range(far):
            push_part(k).wait()

    for j in range(outer - 1):
        @pl.when(at == j + 1)
        def _():
            push_near(j).wait_recv()
            keep[j] = (keep[j].astype(F32) + near[j].astype(F32)).astype(BF16)
            push_hop(j).start()

    @pl.when((at >= 0) & (at < own_steps))
    def _():
        place = lax.rem(at + pushed * (1 - seq), own_steps)
        here = pl.ds(pl.multiple_of(place * bt, bt), bt)
        g_ha = total(here) + got[here].astype(F32)
        x = xs[here]
        inv = inverse_rms(x)
        normed = x * inv
        gain_sum[...] += eight(g_ha * normed)
        scaled = g_ha * gain_ref[...]
        gs[here] = gs[here] + inv * (scaled - normed * jnp.mean(scaled * normed, axis=-1, keepdims=True))

    @pl.when((at >= 0) & (at < pushed))
    def _():
        place = at + pushed * (1 - seq)
        send_half[pl.ds(pl.multiple_of(at * bt, bt), bt)] = gs[pl.ds(pl.multiple_of(place * bt, bt), bt)].astype(BF16)
        push_half(at).start()

    @pl.when(at == own_steps)
    def _():
        size = half // 2
        mine = pl.ds(pl.multiple_of(seq * size, size), size)
        out_own = pltpu.make_async_copy(gs.at[mine], own_any, store.at[0])
        out_own.start()
        first = lax.broadcasted_iota(jnp.int32, vec.shape[1:], 0) == 0
        vec[0] = small_ref[...] + jnp.where(first, jnp.sum(gain_sum[...], axis=0, keepdims=True), 0.0)
        for n in range(3):
            push_small(n).start()
            push_small(n).wait()
            vec[n + 1] = vec[n] + vecs[n]
        for n in range(3, 2 + outer):
            push_small(n).start()
        for n in range(3, 2 + outer):
            push_small(n).wait()
        sums = vec[3]
        for n in range(3, 2 + outer):
            sums = sums + vecs[n]
        sums_ref[...] = sums
        push_near(outer - 1).wait_recv()
        late = keep[outer - 1].astype(F32) + near[outer - 1].astype(F32)
        for j in range(outer - 1):
            push_hop(j).wait()
            late = late + hops[j].astype(F32)
        late_ref[...] = late
        for j in range(outer):
            push_near(j).wait_send()
        for k in range(pushed):
            push_half(k).wait()
        out_own.wait()


def finish(grads, x, g, gain, small, mine, qk, vo, fsdp, ring, call):
    w, length = grads[0].shape
    rows, d = x.shape
    width = mine.shape[1]
    low = -(-w // 128) * 128
    outer, chunk = fsdp // 2, mine.shape[0] // fsdp
    far, own_steps = rows // 512, rows // 256
    weights = (*qk, *vo)
    slots = far + 2 * outer - 1 + own_steps // 2 + 2 + outer
    dma = pltpu.SemaphoreType.DMA
    return pl.pallas_call(
        functools.partial(finish_kernel, w, low, far, own_steps, outer, ring, stack_index(weights)),
        grid=(far + own_steps + 1,),
        in_specs=[fixed((1, d)), fixed(small.shape)] + [ANY] * 13,
        out_specs=[ANY, ANY, fixed((chunk, width)), fixed(small.shape)],
        out_shape=[shape_of((rows // 2, d), F32), shape_of((rows // 2, d)), shape_of((chunk, width), F32), shape_of(small.shape, F32)],
        scratch_shapes=[
            pltpu.VMEM((2, 3 * w, length), BF16), pltpu.VMEM((2, d, 2 * w), BF16), pltpu.VMEM((2, d, low), BF16),
            pltpu.VMEM((rows, d), BF16), pltpu.VMEM((rows, d), BF16),
            pltpu.VMEM((rows, d), F32), pltpu.VMEM((rows, d), F32),
            pltpu.VMEM((rows // 2, d), BF16),
            pltpu.VMEM((outer, chunk, width), BF16), pltpu.VMEM((outer, chunk, width), BF16),
            pltpu.VMEM((outer - 1, chunk, width), BF16),
            pltpu.VMEM((8, d), F32), pltpu.VMEM((4,) + small.shape, F32), pltpu.VMEM((2 + outer,) + small.shape, F32),
            dma((18 + outer,)), dma((1,)), dma((slots,)), dma((slots,)),
        ],
        compiler_params=pltpu.CompilerParams(vmem_limit_bytes=VMEM_LIMIT, collective_id=call, has_side_effects=True),
        cost_estimate=cost(6 * rows * d * 4 * w, 24 * rows * d),
        name="finish",
    )(gain, small, x, g, mine, *grads, *plain(weights))


def total_over_all(plan, a):
    n, f = plan.tp, plan.fsdp
    hop = 1
    while hop < n:
        a = a + lax.ppermute(a, "tp", [(t, t ^ hop) for t in range(n)])
        hop *= 2
    hop = 1
    while hop < f:
        a = a + lax.ppermute(a, "fsdp", [(t, t ^ hop) for t in range(f)])
        hop *= 2
    return a


def add_low(own, got):
    return (own.astype(F32) + got.astype(F32)).astype(BF16)


def scatter_rows(mine):
    return lax.psum_scatter(mine, "fsdp", scatter_dimension=0, tiled=True)


def after(*arrays):
    return lax.optimization_barrier(arrays)


def fast_body(plan, inputs, cotangent, w_qkv, w_out, w_up, w_down, norm_gain, query_scale, prefix_len):
    seqs, positions, d = inputs.shape
    layers, w = w_qkv.shape[0], w_qkv.shape[3]
    dh = query_scale.shape[1]
    unit = SOFT_ONE / math.sqrt(dh)
    factors = jax.nn.softplus(query_scale) * unit
    prefix = lax.dynamic_slice_in_dim(prefix_len, plan.seq, 1)
    order = plan.blocks(positions * plan.tp)
    out_shard, down_shard = jnp.swapaxes(w_out, 1, 2), jnp.swapaxes(w_down, 1, 2)
    pairs = jnp.concatenate(
        [
            jnp.concatenate([w_qkv[:, 0], w_qkv[:, 1]], axis=2)[:, None],
            jnp.concatenate([w_qkv[:, 2], out_shard], axis=2)[:, None],
            jnp.concatenate([w_up, down_shard], axis=2)[:, None],
        ],
        axis=1,
    )

    block = plan.pick(inputs, 1 - plan.seq).astype(BF16)
    got, other = gather_call(pairs[0, :2], block, pieces_of(2, pairs.shape[2]), plan.fsdp, plan.ring)
    qk0, vo0 = got[0:2], got[2:4]

    def along(l, m):
        return lax.all_gather(pairs[l, m], "fsdp", axis=0, tiled=True)

    def both(rows):
        return rows, plan.across(rows)

    def stacked(rows):
        return (rows, 0), (rows, 1)

    un0_rows, qk1_rows = along(0, 2), along(1, 0)
    other, un0_rows, cotangent, shards = after(other, un0_rows, cotangent, pairs[1, 1:])
    shards_got, un0 = plan.across(shards), both(un0_rows)
    cot_block = plan.pick(cotangent, 1 - plan.seq).astype(BF16)
    kept, weights = [], []
    for l in range(layers):
        qk, vo = (qk0, vo0) if l == 0 else (qk1, vo1)
        scale = jnp.tile(factors[l] * LOG2E, 2 * w // dh)[:, None]
        gain = norm_gain[l, 0][None]
        if l == 0:
            h, h_other, q, k, v, x = project((inputs, other), gain, qk, vo, scale, 3, plan.ring)
        else:
            h, h_other, q, k, v = project(x, gain, qk, vo, scale, 3 + l)
        if l == 0:
            q, shards_got, qk1_rows = after(q, shards_got, qk1_rows)
            shards = jnp.stack([shards, shards_got], axis=1)
            vo1_rows, un1_rows = (lax.all_gather(shards[m], "fsdp", axis=1, tiled=True) for m in range(2))
            qk1 = both(qk1_rows)
        att, lse = attention_forward(q, k, v, prefix, order, dh)
        if l == 0:
            att, un0_got = after(att, un0[1])
            un = un0[0], un0_got
        else:
            att, un1_rows, cot_got = after(att, un1_rows, cot_got)
            un = stacked(un1_rows)
        mid, pre, res, *mats = middle_call(x, att, norm_gain[l, 1][None], vo, un, 5 + l)
        if l == 0:
            res, qk1_got, vo1_rows, cot_block = after(res, qk1[1], vo1_rows, cot_block)
            qk1, vo1 = (qk1[0], qk1_got), stacked(vo1_rows)
            cot_got = plan.across(cot_block)
        kept.append((x, h, h_other, q, k, v, att, lse, mid, pre))
        weights.append((qk, vo, mats))
        x = res
    g = cotangent, cot_got
    out_blocks = x.reshape(seqs, positions, d)
    out_send = plan.pick(out_blocks, 1 - plan.seq).astype(BF16)
    cot_got, out_send = after(cot_got, out_send)
    g = cotangent, cot_got
    out_got = plan.across(out_send)
    outputs = None
    width = -(-3 * w // 128) * 128
    grads = [None] * layers
    for l in reversed(range(layers)):
        qk, vo, mats = weights[l]
        x, h, h_other, q, k, v, att, lse, mid, pre = kept[l]
        ring = plan.ring if l == layers - 1 else 0
        g_mid, gain_m, g_att, *early = mlp_back(g, mid, pre, norm_gain[l, 1][None], att, mats, width, 1 + l, ring)
        if l > 0:
            early = [scatter_rows(a) for a in early]
        else:
            early_got = plan.across(early[1])
        if l + 1 < layers:
            g_att, grads[l + 1][0][1] = after(g_att, grads[l + 1][0][1])
        dgrads, fgs, pieces = [None] * 6, [], [None] * 2
        for s in (1, 0):
            dq, dk, dv, fg = attention_backward(
                q, k, v, att, g_att, lse, factors[l], prefix, order, dh, s * w, w
            )
            if s == 1:
                pieces[1] = weight_grad(h, h_other, dq, dk, dv, width)
                if l > 0:
                    pieces[1], out_got = after(pieces[1], out_got)
                    g_att, pieces[1] = after(g_att, pieces[1])
                else:
                    g_att, pieces[1], out_got = after(g_att, pieces[1], out_got)
                    outputs = plan.order(plan.pick(out_blocks, plan.seq), out_got.astype(F32)).reshape(out_blocks.shape)
                    pieces[1], early_got, outputs = after(pieces[1], early_got, outputs)
                late_got = plan.across(pieces[1])
                if l + 1 < layers:
                    g_att, grads[l + 1][1] = after(g_att, grads[l + 1][1])
                if l == 0:
                    g_att, early_got = after(g_att, early_got)
                    mine, g_att = after(add_low(early[0], early_got), g_att)
                    early = scatter_rows(mine)
            elif l > 0:
                dq, early[0] = after(dq, early[0])
            dgrads[3 * s:3 * s + 3] = [dq, dk, dv]
            fgs.append(fg)
        fg = fgs[0] + fgs[1]
        if l > 0:
            g, gain_a, pieces[0] = input_back(
                dgrads, x, g_mid, norm_gain[l, 0][None], qk, vo, 7 + l, (h, h_other), width
            )
            pieces[0], late_got = after(pieces[0], late_got)
            mine, g = after(add_low(pieces[0], late_got), g)
        else:
            pieces[0] = weight_grad(h, h_other, *dgrads[:3], width)
            pieces[0], late_got, dgrads[3] = after(pieces[0], late_got, dgrads[3])
            mine, dgrads[3] = after(add_low(pieces[0], late_got), dgrads[3])
        row = lambda a: jnp.pad(a, (0, d - a.shape[0]))[None]
        small = [row(jnp.sum(gain_m, axis=0)), row(jnp.sum(fg, axis=1) / (factors[l] * LOG2E))]
        if l > 0:
            late = scatter_rows(mine)
            small.append(row(jnp.sum(gain_a, axis=0)))
            grads[l] = [early, late, small]
    upper = grads[1][2]
    zero = jnp.zeros((1, d), F32)
    small = jnp.concatenate([zero, upper[2], small[0], upper[0], small[1], upper[1], zero, zero])
    own_half, got_half, late, small = finish(
        dgrads, x, g_mid, norm_gain[0, 0][None], small, mine, qk, vo, plan.fsdp, plan.ring, 9
    )
    grads[0] = [early, late, small]
    input_grad = plan.order(own_half, got_half.astype(F32)).reshape(out_blocks.shape)
    early = []
    for entry, _, _ in grads:
        if isinstance(entry, list):
            early.append(entry[0].astype(F32) + plan.across(entry[1]).astype(F32))
        else:
            early.append(entry.astype(F32))
    early = jnp.stack(early)
    late = jnp.stack([entry[1].astype(F32) for entry in grads])
    qkv_g = jnp.stack([late[:, :, c * w:(c + 1) * w] for c in range(3)], axis=1)
    up_g, down_g, out_g = (early[:, :, c * w:(c + 1) * w] for c in range(3))
    scale_g = small[4:6, :dh] * jax.nn.sigmoid(query_scale) * unit
    return (
        outputs, input_grad, qkv_g, jnp.swapaxes(out_g, 1, 2), up_g, jnp.swapaxes(down_g, 1, 2),
        small[:2], small[2:4], scale_g,
    )


def body(inputs, cotangent, w_qkv, w_out, w_up, w_down, norm_gain, query_scale, prefix_len):
    seqs, positions, d = inputs.shape
    fsdp, tp = lax.axis_size("fsdp"), lax.axis_size("tp")
    layers = w_qkv.shape[0]
    plan = Plan(seqs, tp, fsdp, w_qkv.shape[2])
    if plan.fast:
        return fast_body(
            plan, inputs, cotangent, w_qkv, w_out, w_up, w_down, norm_gain, query_scale, prefix_len
        )
    dh = query_scale.shape[1]
    unit = SOFT_ONE / math.sqrt(dh)
    factors = jax.nn.softplus(query_scale) * unit
    prefix = lax.dynamic_slice_in_dim(prefix_len, plan.seq, 1)
    order = plan.blocks(positions * tp)
    out_shard, down_shard = jnp.swapaxes(w_out, 1, 2), jnp.swapaxes(w_down, 1, 2)

    weights = []
    for l in range(layers):
        qkv = plan.gather_heads(w_qkv[l])
        out_t = plan.gather_heads(out_shard[l][None])[:, 0]
        up, down_t = plan.gather_full(jnp.stack([w_up[l], down_shard[l]]))
        weights.append(([qkv[:, c] for c in range(3)], out_t, up, down_t))

    x = plan.swap(inputs)
    g = plan.swap(cotangent)
    kept = []
    for l in range(layers):
        x, saved = layer_forward(plan, x, prefix, order, *weights[l], norm_gain[l], factors[l])
        kept.append(saved)
    outputs = plan.unswap(x)
    grads = [None] * layers
    for l in reversed(range(layers)):
        g, grads[l] = layer_backward(
            plan, g, kept[l], prefix, order, *weights[l], norm_gain[l], factors[l]
        )
    input_grad = plan.unswap(g)
    qkv_g, out_g, up_g, down_g, gain_a, gain_m, f_g = (jnp.stack(a) for a in zip(*grads))
    scale_g = f_g * jax.nn.sigmoid(query_scale) * unit
    gain_a, gain_m, scale_g = lax.psum((gain_a, gain_m, scale_g), ("fsdp", "tp"))
    return outputs, input_grad, qkv_g, out_g, up_g, down_g, gain_a, gain_m, scale_g


def solution(mesh):
    placed = (
        P("fsdp", "tp", None),
        P("fsdp", "tp", None),
        P(None, None, "fsdp", "tp"),
        P(None, "tp", "fsdp"),
        P(None, "fsdp", "tp"),
        P(None, "tp", "fsdp"),
        P(),
        P(),
        P("fsdp"),
    )
    return jax.shard_map(
        body,
        mesh=mesh,
        in_specs=placed,
        out_specs=placed[:6] + (P(), P(), P()),
        check_vma=False,
    )
```

```python
import functools, math
import jax
import jax.numpy as jnp
from jax import lax
from jax.experimental import pallas as pl
from jax.experimental.pallas import tpu as pltpu
from jax.sharding import PartitionSpec as P

MASKED = -1e30
F32, BF16 = jnp.float32, jnp.bfloat16
EPSILON = 1e-06
SOFT_ONE = 1.442695041
LOG2E = math.log2(math.e)
MESH = pl.DeviceIdType.MESH
HINT = 1
VMEM_LIMIT = 60 * 2**20

def dot(a, b, dims=((1,), (0,))):
    return lax.dot_general(a, b, (dims, ((), ())), preferred_element_type=F32)

def key_range(row_start, rows, prefix, block):
    full = jnp.maximum(row_start + 1, prefix) // block
    stop = (jnp.maximum(row_start + rows, prefix) + block - 1) // block
    return full, stop

def forward_kernel(prefix_ref, order_ref, q_ref, k_ref, v_ref, o_ref, lse_ref, key_rows, value_ext, *, pair, dh, bq, bk):
    length = q_ref.shape[1]
    prefix = prefix_ref[0]
    ext = value_ext.shape[1]
    bound = 0.0
    for h in range(pair):
        rows = slice(h * dh, (h + 1) * dh)
        q, k = q_ref[rows, :].astype(F32), k_ref[rows, :].astype(F32)
        bound = jnp.maximum(bound, jnp.max(jnp.sum(q * q, axis=0)) * jnp.max(jnp.sum(k * k, axis=0)))
        key_rows[h] = k_ref[rows, :].T
        value_ext[h, :dh] = v_ref[rows, :]
        value_ext[h, dh:] = jnp.ones((ext - dh, length), BF16)

    def one_query(shifted, qi, carry):
        start = qi * bq
        here = pl.ds(pl.multiple_of(order_ref[qi] * bq, bq), bq)
        queries = [q_ref[h * dh:(h + 1) * dh, here] for h in range(pair)]
        full, stop = key_range(start, bq, prefix, bk)

        def step(masked, ki, state):
            first = ki * bk
            there = pl.ds(pl.multiple_of(order_ref[ki] * bk, bk), bk)
            if masked:
                rows = first + lax.broadcasted_iota(jnp.int32, (bk, bq), 0)
                cols = start + lax.broadcasted_iota(jnp.int32, (bk, bq), 1)
                allowed = rows <= jnp.maximum(cols, prefix - 1)
            scores = [dot(key_rows[h, there], queries[h]) for h in range(pair)]
            fresh = []
            for h in range(pair):
                s = jnp.where(allowed, scores[h], MASKED) if masked else scores[h]
                if shifted:
                    top, total = state[h]
                    new_top = jnp.maximum(top, jnp.max(s, axis=0, keepdims=True))
                    p = jnp.exp2(s - new_top).astype(BF16)
                    total = total * jnp.exp2(top - new_top) + dot(value_ext[h, :, there], p)
                    fresh.append((new_top, total))
                else:
                    fresh.append(state[h] + dot(value_ext[h, :, there], jnp.exp2(s).astype(BF16)))
            return tuple(fresh)

        zero = jnp.zeros((ext, bq), F32)
        state = tuple((jnp.full((1, bq), MASKED, F32), zero) if shifted else zero for _ in range(pair))
        state = lax.fori_loop(0, full, functools.partial(step, False), state)
        state = lax.fori_loop(full, stop, functools.partial(step, True), state)
        for h in range(pair):
            top, total = state[h] if shifted else (0.0, state[h])
            norm = total[dh:dh + 1]
            o_ref[h * dh:(h + 1) * dh, here] = (total[:dh] / norm).astype(BF16)
            lse_ref[h, :, here] = top + jnp.log2(norm)
        return carry

    small = bound <= 3600.0

    @pl.when(small)
    def _():
        lax.fori_loop(0, length // bq, functools.partial(one_query, False), 0)

    @pl.when(jnp.logical_not(small))
    def _():
        lax.fori_loop(0, length // bq, functools.partial(one_query, True), 0)


def attention_forward(q, k, v, prefix, order, dh, pair=4):
    width, length = q.shape
    heads = width // dh
    pair = min(pair, heads)
    bq = bk = length // order.shape[0]
    ext = dh + 16
    spec = pl.BlockSpec((pair * dh, length), lambda i, p, o: (i, 0))
    return pl.pallas_call(
        functools.partial(forward_kernel, pair=pair, dh=dh, bq=bq, bk=bk),
        grid_spec=pltpu.PrefetchScalarGridSpec(
            num_scalar_prefetch=2, grid=(heads // pair,),
            in_specs=[spec, spec, spec],
            out_specs=[spec, pl.BlockSpec((pair, 1, length), lambda i, p, o: (i, 0, 0))],
            scratch_shapes=[pltpu.VMEM((pair, length, dh), BF16), pltpu.VMEM((pair, ext, length), BF16)],
        ),
        out_shape=[jax.ShapeDtypeStruct((width, length), BF16), jax.ShapeDtypeStruct((heads, 1, length), F32)],
        compiler_params=pltpu.CompilerParams(vmem_limit_bytes=VMEM_LIMIT),
        cost_estimate=pl.CostEstimate(flops=int(HINT * 600 * length * length * heads), bytes_accessed=int(HINT * 8 * width * length), transcendentals=0),
        name="attention_forward",
    )(prefix, order, q, k, v)

def split3(x):
    a = x.astype(BF16)
    r = x - a.astype(F32)
    b = r.astype(BF16)
    c = (r - b.astype(F32)).astype(BF16)
    return a, b, c

def backward_kernel(prefix_ref, order_ref, q_ref, k_ref, v_ref, o_ref, g_ref, lse_ref, scale_ref, dq_ref, dk_ref, dv_ref, fg_ref,
                    key_ext, value_ext, query_ext, grad_ext, dk_acc, dv_acc, *, pair, dh, bq, bk):
    length = q_ref.shape[1]
    prefix = prefix_ref[0]
    pad = key_ext.shape[1] - dh
    index = lax.broadcasted_iota(jnp.int32, (pad, length), 0)
    ones = (index < 3).astype(F32).astype(BF16)

    @pl.when(pl.program_id(0) == 0)
    def _():
        fg_ref[...] = jnp.zeros_like(fg_ref)

    def tail(row):
        high, mid, low = (part.astype(F32) for part in split3(-row))
        rest = jnp.where(index == 1, mid, jnp.where(index == 2, low, 0.0))
        return jnp.where(index == 0, high, rest).astype(BF16)

    for h in range(pair):
        rows = slice(h * dh, (h + 1) * dh)
        g = g_ref[rows, :]
        key_ext[h, :dh] = k_ref[rows, :]
        key_ext[h, dh:] = ones
        value_ext[h, :dh] = v_ref[rows, :]
        value_ext[h, dh:] = ones
        delta = jnp.sum(o_ref[rows, :].astype(F32) * g.astype(F32), axis=0, keepdims=True)
        query_ext[h, :dh] = q_ref[rows, :]
        query_ext[h, dh:] = tail(lse_ref[h])
        grad_ext[h, :dh] = g
        grad_ext[h, dh:] = tail(delta)
        dk_acc[h] = jnp.zeros((dh, length), F32)
        dv_acc[h] = jnp.zeros((dh, length), F32)

    def one_query(qi, carry):
        start = qi * bq
        here = pl.ds(pl.multiple_of(order_ref[qi] * bq, bq), bq)
        full, stop = key_range(start, bq, prefix, bk)

        def step(masked, ki, state):
            first = ki * bk
            there = pl.ds(pl.multiple_of(order_ref[ki] * bk, bk), bk)
            if masked:
                rows = start + lax.broadcasted_iota(jnp.int32, (bq, bk), 0)
                cols = first + lax.broadcasted_iota(jnp.int32, (bq, bk), 1)
                allowed = cols <= jnp.maximum(rows, prefix - 1)
            fresh = []
            s = [dot(query_ext[h, :, here], key_ext[h, :, there], ((0,), (0,))) for h in range(pair)]
            gp = [dot(grad_ext[h, :, here], value_ext[h, :, there], ((0,), (0,))) for h in range(pair)]
            for h in range(pair):
                x = jnp.where(allowed, s[h], MASKED) if masked else s[h]
                p = jnp.exp2(x)
                ds = (p * gp[h]).astype(BF16)
                rows = slice(h * dh, (h + 1) * dh)
                dv_acc[h, :, there] += dot(g_ref[rows, here], p.astype(BF16))
                dk_acc[h, :, there] += dot(q_ref[rows, here], ds)
                fresh.append(state[h] + dot(ds, k_ref[rows, there], ((1,), (1,))))
            return tuple(fresh)

        state = tuple(jnp.zeros((bq, dh), F32) for _ in range(pair))
        state = lax.fori_loop(0, full, functools.partial(step, False), state)
        state = lax.fori_loop(full, stop, functools.partial(step, True), state)
        for h in range(pair):
            rows = slice(h * dh, (h + 1) * dh)
            dq = state[h].T
            prod = dq * q_ref[rows, here].astype(F32)
            part = prod[:, :128]
            for c in range(1, bq // 128):
                part = part + prod[:, c * 128:(c + 1) * 128]
            fg_ref[...] += part
            dq_ref[rows, here] = (dq * scale_ref[...]).astype(BF16)
        return carry

    lax.fori_loop(0, length // bq, one_query, 0)
    for h in range(pair):
        rows = slice(h * dh, (h + 1) * dh)
        dk_ref[rows, :] = (dk_acc[h] * math.log(2.0)).astype(BF16)
        dv_ref[rows, :] = dv_acc[h].astype(BF16)


def attention_backward(q, k, v, o, g, lse, factor, prefix, order, dh, base=0, width=None, pair=2):
    full, length = q.shape
    width = width or full
    heads = width // dh
    pair = min(pair, heads)
    bq = bk = length // order.shape[0]
    ext = dh + 16
    spec = pl.BlockSpec((pair * dh, length), lambda i, p, o: (i, 0))
    skip = base // (pair * dh)
    source = pl.BlockSpec((pair * dh, length), lambda i, p, o: (i + skip, 0))
    wide = jax.ShapeDtypeStruct((width, length), BF16)
    return pl.pallas_call(
        functools.partial(backward_kernel, pair=pair, dh=dh, bq=bq, bk=bk),
        grid_spec=pltpu.PrefetchScalarGridSpec(
            num_scalar_prefetch=2, grid=(heads // pair,),
            in_specs=[source] * 5 + [pl.BlockSpec((pair, 1, length), lambda i, p, o: (i + skip, 0, 0)), pl.BlockSpec((dh, 1), lambda i, p, o: (0, 0))],
            out_specs=[spec] * 3 + [pl.BlockSpec((dh, 128), lambda i, p, o: (0, 0))],
            scratch_shapes=[
                pltpu.VMEM((pair, ext, length), BF16),
                pltpu.VMEM((pair, ext, length), BF16),
                pltpu.VMEM((pair, ext, length), BF16),
                pltpu.VMEM((pair, ext, length), BF16),
                pltpu.VMEM((pair, dh, length), F32),
                pltpu.VMEM((pair, dh, length), F32)],
        ),
        out_shape=[wide] * 3 + [jax.ShapeDtypeStruct((dh, 128), F32)],
        compiler_params=pltpu.CompilerParams(vmem_limit_bytes=VMEM_LIMIT),
        cost_estimate=pl.CostEstimate(flops=int(HINT * 1600 * length * length * heads), bytes_accessed=int(HINT * 16 * width * length), transcendentals=0),
        name="attention_backward",
    )(prefix, order, q, k, v, o, g, lse, factor.reshape(dh, 1))


def rms(x):
    inv = lax.rsqrt(jnp.mean(x * x, axis=-1, keepdims=True) + EPSILON)
    return x * inv, inv


def rms_back(normed, inv, gain, grad):
    scaled = grad * gain
    out = inv * (scaled - normed * jnp.mean(scaled * normed, axis=-1, keepdims=True))
    return out, jnp.sum(grad * normed, axis=0)


def ein(spec, *args):
    return jnp.einsum(spec, *args, preferred_element_type=F32)


def gather_kernel(pieces, pairs, outer, ring, shard_ref, block_ref, *refs):
    outs = [refs[2 * m:2 * m + 2] for m in range(pairs)]
    got_ref = refs[2 * pairs]
    send, recv, local = refs[2 * pairs + 1:]
    f, t = lax.axis_index("fsdp"), lax.axis_index("tp")
    zz, yy = f // 2, f % 2
    across = {"tp": lax.rem(t + ring, 2 * ring)}
    beside = {"fsdp": zz * 2 + 1 - yy}
    along = [{"fsdp": lax.rem(zz + k, outer) * 2 + yy} for k in range(1, outer)]
    peers = along + [across, beside]
    barrier = pltpu.get_barrier_semaphore()
    for peer in peers:
        pl.semaphore_signal(barrier, inc=1, device_id=peer, device_id_type=MESH)
    pl.semaphore_wait(barrier, len(peers))
    used = [0]

    def copy(src, dst, peer):
        slot = used[0]
        used[0] += 1
        return pltpu.make_async_remote_copy(
            src_ref=src, dst_ref=dst, send_sem=send.at[slot], recv_sem=recv.at[slot],
            device_id=peer, device_id_type=MESH,
        )

    count = len(pieces)
    chunks = 4
    step = block_ref.shape[0] // chunks
    blocks = [
        copy(block_ref.at[pl.ds(i * step, step)], got_ref.at[pl.ds(i * step, step)], across)
        for i in range(chunks)
    ]
    own, first, second, third = [], [], [], []
    for i, (m, low, rows, route) in enumerate(pieces):
        part = pl.ds(low, rows)
        w = [out.at[:, :, part] for out in outs[m]]
        src = shard_ref.at[m, part]
        own.append(pltpu.make_async_copy(src, w[0].at[zz, yy], local.at[i]))
        first.append([copy(src, w[0].at[zz, yy], peer) for peer in along])
        if route:
            second.append([copy(w[0].at[:, yy], w[0].at[:, yy], beside)])
            third.append([copy(w[0], w[1], across)])
        else:
            second.append([copy(w[0].at[:, yy], w[1].at[:, yy], across)])
            third.append([copy(w[s].at[:, yy], w[s].at[:, yy], beside) for s in range(2)])

    def begin(i):
        own[i].start()
        for c in first[i]:
            c.start()

    ahead = 3
    for i in range(min(ahead, count)):
        begin(i)
    started = 0
    for b in blocks[:2]:
        b.start()
    started = 2
    for i in range(count + 2):
        if i < count:
            own[i].wait()
            for c in first[i]:
                c.wait_recv()
            for c in second[i]:
                c.start()
            if i + ahead < count:
                begin(i + ahead)
            if started < chunks:
                blocks[started].start()
                started += 1
        if 0 <= i - 1 < count:
            for c in second[i - 1]:
                c.wait_recv()
            for c in third[i - 1]:
                c.start()
        if 0 <= i - 2 < count:
            for c in third[i - 2]:
                c.wait_recv()
    for b in blocks[started:]:
        b.start()
    for i in range(count):
        for c in first[i] + second[i] + third[i]:
            c.wait_send()
    for b in blocks:
        b.wait()


def pieces_of(pairs, rows):
    half = rows // 32 * 16
    return tuple(
        (m, low, size, m_part) for m in range(pairs) for m_part, (low, size) in enumerate(((0, half), (half, rows - half)))
    )


def gather_call(shards, block, pieces, fsdp, ring):
    pairs, rows, w = shards.shape
    outer = fsdp // 2
    slots = 4 + len(pieces) * (outer + 2)
    any_spec = pl.BlockSpec(memory_space=pl.ANY)
    got = pl.pallas_call(
        functools.partial(gather_kernel, pieces, pairs, outer, ring),
        out_shape=[jax.ShapeDtypeStruct((outer, 2, rows, w), BF16)] * (2 * pairs)
        + [jax.ShapeDtypeStruct(block.shape, block.dtype)],
        in_specs=[any_spec] * 2,
        out_specs=[any_spec] * (2 * pairs + 1),
        scratch_shapes=[
            pltpu.SemaphoreType.DMA((slots,)),
            pltpu.SemaphoreType.DMA((slots,)),
            pltpu.SemaphoreType.DMA((len(pieces),)),
        ],
        compiler_params=pltpu.CompilerParams(collective_id=0, has_side_effects=True),
        name="gather_weights",
    )(shards, block)
    return [a.reshape(outer * 2 * rows, w) for a in got[:-1]], got[-1]


class Plan:
    def __init__(self, seqs, tp, fsdp, rows):
        self.seqs, self.tp, self.ring, self.fsdp = seqs, tp, tp // seqs, fsdp
        self.same_member = [[s * self.ring + r for s in range(seqs)] for r in range(self.ring)]
        self.same_seq = [[s * self.ring + r for r in range(self.ring)] for s in range(seqs)]
        self.fast = seqs == 2 and self.ring == 2 and fsdp % 2 == 0 and rows % 32 == 0
        t = lax.axis_index("tp")
        self.seq, self.member = t // self.ring, lax.rem(t, self.ring)

    def across(self, a):
        n = self.tp
        return lax.ppermute(a, "tp", [(t, (t + self.ring) % n) for t in range(n)])

    def core(self, a):
        return lax.ppermute(a, "tp", [(t, t ^ 1) for t in range(self.tp)])

    def pick(self, blocks, index):
        return lax.dynamic_index_in_dim(blocks, index, 0, keepdims=False)

    def order(self, own, other):
        first = self.seq == 0
        return jnp.concatenate([jnp.where(first, own, other), jnp.where(first, other, own)])

    def swap(self, blocks):
        if self.seqs == 2:
            other = self.across(self.pick(blocks, 1 - self.seq).astype(BF16))
            return self.order(self.pick(blocks, self.seq), other.astype(F32))
        got = lax.all_to_all(
            blocks.astype(BF16), "tp", 0, 0, tiled=True, axis_index_groups=self.same_member
        )
        return got.reshape(-1, got.shape[-1]).astype(F32)

    def unswap(self, rows):
        blocks = rows.reshape(self.seqs, -1, rows.shape[-1])
        return self.swap(blocks).reshape(blocks.shape)

    def whole(self, rows):
        if self.fast:
            return jnp.concatenate([rows, self.core(rows)])
        cut = rows.reshape(self.seqs, -1, rows.shape[-1])
        got = lax.all_gather(cut, "tp", axis=1, axis_index_groups=self.same_seq)
        return got.reshape(-1, rows.shape[-1])

    def share(self, full):
        if self.fast:
            own = full.shape[0] // 2
            return full[:own].astype(F32) + self.core(full[own:].astype(BF16)).astype(F32)
        cut = full.astype(BF16).reshape(self.seqs, self.ring, -1, full.shape[-1])
        got = lax.psum_scatter(cut, "tp", scatter_dimension=1, axis_index_groups=self.same_seq)
        return got.reshape(-1, full.shape[-1]).astype(F32)

    def blocks(self, length):
        if self.fast:
            j = jnp.arange(self.tp, dtype=jnp.int32)
            apart = (j % self.ring != self.member).astype(jnp.int32)
            return apart * self.seqs + j // self.ring
        return jnp.arange(max(1, length // 512), dtype=jnp.int32)

    def gather_heads(self, shards):
        rows = lax.all_gather(shards, "fsdp", axis=1, tiled=True)
        if self.fast:
            return jnp.stack([rows, self.across(rows)])
        return lax.all_gather(rows, "tp", axis_index_groups=self.same_member)

    def join(self, every):
        r, s, m, d, w = every.shape
        return every.transpose(2, 3, 0, 1, 4).reshape(m, d, r * s * w)

    def gather_full(self, shards):
        part = self.gather_heads(shards)
        if self.fast:
            return self.join(jnp.stack([part, self.core(part)]))
        return self.join(lax.all_gather(part, "tp", axis_index_groups=self.same_seq))

    def scatter_heads(self, grads):
        if self.fast:
            other = self.across(grads[1].astype(BF16))
            mine = (grads[0].astype(F32) + other.astype(F32)).astype(BF16)
        else:
            mine = lax.psum_scatter(
                grads.astype(BF16), "tp", scatter_dimension=0, axis_index_groups=self.same_member
            )
        return lax.psum_scatter(mine, "fsdp", scatter_dimension=1, tiled=True).astype(F32)

    def scatter_full(self, grads):
        m, d, cols = grads.shape
        if self.fast:
            half = cols // 2
            other = self.core(grads[:, :, half:].astype(BF16))
            mine = grads[:, :, :half].astype(F32) + other.astype(F32)
            mine = mine.astype(BF16).reshape(m, d, self.seqs, -1).transpose(2, 0, 1, 3)
        else:
            cut = grads.astype(BF16).reshape(m, d, self.ring, self.seqs, -1).transpose(2, 3, 0, 1, 4)
            mine = lax.psum_scatter(cut, "tp", scatter_dimension=0, axis_index_groups=self.same_seq)
        return self.scatter_heads(mine)


def layer_forward(plan, x, prefix, order, qkv, out_t, up, down_t, gains, factor):
    dh = factor.shape[0]
    normed, inv = rms(x)
    h = plan.whole((normed * gains[0]).astype(BF16))
    seqs, d, w = out_t.shape
    raw = [ein("sdc,td->sct", qkv[c], h).reshape(seqs * w, -1) for c in range(3)]
    scale = jnp.tile(factor * LOG2E, seqs * w // dh)[:, None]
    q, k, v = (raw[0] * scale).astype(BF16), raw[1].astype(BF16), raw[2].astype(BF16)
    att, lse = attention_forward(q, k, v, prefix, order, dh)
    middle = x + plan.share(ein("sct,sdc->td", att.reshape(seqs, w, -1), out_t))
    normed_m, inv_m = rms(middle)
    h_m = (normed_m * gains[1]).astype(BF16)
    pre = ein("td,df->tf", h_m, up)
    hidden = jax.nn.silu(pre).astype(BF16)
    result = middle + ein("tf,df->td", hidden, down_t)
    return result, (x, inv, h, q, k, v, att, lse, middle, inv_m, h_m, pre, hidden)


def layer_backward(plan, g, saved, prefix, order, qkv, out_t, up, down_t, gains, factor):
    x, inv, h, q, k, v, att, lse, middle, inv_m, h_m, pre, hidden = saved
    dh = factor.shape[0]
    seqs, d, w = out_t.shape
    length = h.shape[0]
    g_low = g.astype(BF16)
    down_grad = ein("td,tf->df", g_low, hidden)
    g_hidden = ein("td,df->tf", g_low, down_t)
    sig = jax.nn.sigmoid(pre)
    g_pre = (g_hidden * sig * (1.0 + pre * (1.0 - sig))).astype(BF16)
    up_grad = ein("td,tf->df", h_m, g_pre)
    mlp_grads = plan.scatter_full(jnp.stack([up_grad, down_grad]))
    g_hm = ein("tf,df->td", g_pre, up)
    back_m, gain_m = rms_back(middle * inv_m, inv_m, gains[1], g_hm)
    g_mid = g + back_m
    g_all = plan.whole(g_mid.astype(BF16))
    att3 = att.reshape(seqs, w, length)
    out_grad = plan.scatter_heads(ein("td,sct->sdc", g_all, att3)[:, None])[0]
    g_att = ein("td,sdc->sct", g_all, out_t).astype(BF16).reshape(seqs * w, length)
    dq, dk, dv, fg = attention_backward(q, k, v, att, g_att, lse, factor, prefix, order, dh)
    factor_grad = jnp.sum(fg, axis=1) / (factor * LOG2E)
    parts = [a.reshape(seqs, w, length) for a in (dq, dk, dv)]
    qkv_grad = plan.scatter_heads(jnp.stack([ein("td,sct->sdc", h, a) for a in parts], axis=1))
    g_ha = plan.share(sum(ein("sct,sdc->td", a, b) for a, b in zip(parts, qkv)))
    back_a, gain_a = rms_back(x * inv, inv, gains[0], g_ha)
    return g_mid + back_a, (qkv_grad, out_grad.T, mlp_grads[0], mlp_grads[1].T, gain_a, gain_m, factor_grad)


TN, NT, TT = ((0,), (0,)), ((1,), (1,)), ((0,), (1,))
ONE = pl.Buffered(1)


def cost(flops, nbytes):
    return pl.CostEstimate(flops=int(flops * HINT), bytes_accessed=int(nbytes * HINT), transcendentals=0)


def params(mib=60):
    return pltpu.CompilerParams(vmem_limit_bytes=mib * 2**20)


def fixed(shape):
    return pl.BlockSpec(shape, lambda *a: (0,) * len(shape), pipeline_mode=ONE)


def weight(w, lanes=None):
    stack, index = w if isinstance(w, tuple) else (w, None)
    shape = (stack.shape[-2], lanes or stack.shape[-1])
    if index is None:
        return fixed(shape)
    return pl.BlockSpec((None,) + shape, lambda *a: (index, 0, 0), pipeline_mode=ONE)


def plain(weights):
    return [w[0] if isinstance(w, tuple) else w for w in weights]


def shape_of(shape, dtype=BF16):
    return jax.ShapeDtypeStruct(shape, dtype)


def inverse_rms(x):
    return lax.rsqrt(jnp.mean(x * x, axis=-1, keepdims=True) + EPSILON)


def eight(x):
    return jnp.sum(x.reshape(-1, 8, x.shape[-1]), axis=0)


def join_lanes(dst, refs, low, high):
    width = high - low
    for i, ref in enumerate(refs):
        dst[:, i * width:(i + 1) * width] = ref[:, low:high]


def core_of():
    t = lax.axis_index("tp")
    return {"tp": t + 1 - 2 * lax.rem(t, 2)}


def pushes(send, recv, core):
    def push(src, dst, slot):
        return pltpu.make_async_remote_copy(
            src_ref=src, dst_ref=dst, send_sem=send.at[slot], recv_sem=recv.at[slot],
            device_id=core, device_id_type=MESH,
        )

    return push


def greet(core):
    barrier = pltpu.get_barrier_semaphore()
    pl.semaphore_signal(barrier, inc=1, device_id=core, device_id_type=MESH)
    pl.semaphore_wait(barrier, 1)


def stack_index(weights):
    return tuple(a[1] if isinstance(a, tuple) else None for a in weights)


def entry(ref, k):
    return ref if k is None else ref.at[k]


def stages(steps):
    starts = [sum(steps[:n]) for n in range(len(steps))]

    def at(n, make):
        return lambda i: make(jnp.clip(i - starts[n], 0, steps[n] - 1))

    return at


ANY = pl.BlockSpec(memory_space=pl.ANY)


class Halves:
    def __init__(self, own_any, got_any, own, got, load, ring):
        self.seq = lax.axis_index("tp") // ring
        self.own, self.got = own, got
        self.copies = [
            pltpu.make_async_copy(own_any.at[self.seq], own, load.at[0]),
            pltpu.make_async_copy(got_any, got, load.at[1]),
        ]

    def rows(self, k, size):
        per = self.own.shape[0] // size
        here = pl.ds(pl.multiple_of(lax.rem(k, per) * size, size), size)
        return jnp.where(k // per == self.seq, self.own[here], self.got[here].astype(F32))


def halves_scratch(rows, d):
    return [pltpu.VMEM((rows // 2, d), F32), pltpu.VMEM((rows // 2, d), BF16), pltpu.SemaphoreType.DMA((2,))]


def project_kernel(w, low, steps, index, bt, ring, gain_ref, scale_ref, *refs):
    weights, refs = refs[:4], refs[4:]
    if ring:
        own_any, got_any, own_ref, other_ref, q_ref, k_ref, v_ref, x_out = refs[:8]
        own, other, qk, vo, load, send, recv, *rest = refs[8:]
        halves = Halves(own_any, got_any, *rest, ring)
    else:
        x_ref, own_ref, other_ref, q_ref, k_ref, v_ref = refs[:6]
        own, other, qk, vo, load, send, recv = refs[6:]
    i = pl.program_id(0)
    rows_steps, half, _ = steps
    ba = q_ref.shape[1]
    core = core_of()
    push = pushes(send, recv, core)

    def loads():
        copies = [pltpu.make_async_copy(entry(weights[s], index[s]), qk.at[s], load.at[s]) for s in range(2)]
        for s in range(2):
            src = entry(weights[2 + s], index[2 + s]).at[:, pl.ds(0, low)]
            copies.append(pltpu.make_async_copy(src, vo.at[s], load.at[2 + s]))
        return copies

    def push_rows(k):
        part = pl.ds(pl.multiple_of(k * bt, bt), bt)
        return push(own.at[part], other.at[part], k)

    @pl.when(i == 0)
    def _():
        if ring:
            for c in halves.copies:
                c.start()
        for c in loads():
            c.start()
        greet(core)
        if ring:
            for c in halves.copies:
                c.wait()

    @pl.when(i < rows_steps)
    def _():
        if ring:
            x = halves.rows(i, bt)
            x_out[...] = x
        else:
            x = x_ref[...]
        h = (x * inverse_rms(x) * gain_ref[...]).astype(BF16)
        own[pl.ds(pl.multiple_of(i * bt, bt), bt)] = h
        own_ref[...] = h
        push_rows(i).start()

    at = i - rows_steps

    @pl.when(at == 0)
    def _():
        for c in loads():
            c.wait()

    @pl.when(at == half)
    def _():
        for k in range(rows_steps):
            push_rows(k).wait()

    def project(h):
        for s in range(2):
            rows = slice(s * w, (s + 1) * w)
            both = dot(qk[s], h, TT)
            q_ref[rows] = (both[:w] * scale_ref[rows]).astype(BF16)
            k_ref[rows] = both[w:].astype(BF16)
            v_ref[rows] = dot(vo[s, :, :w], h, TT).astype(BF16)

    @pl.when((at >= 0) & (at < half))
    def _():
        project(own[pl.ds(pl.multiple_of(at * ba, ba), ba)])

    @pl.when(at >= half)
    def _():
        h = other[pl.ds(pl.multiple_of((at - half) * ba, ba), ba)]
        other_ref[...] = h
        project(h)


def project(x, gain, qk, vo, scale, call, ring=0):
    xs = x if ring else (x,)
    d = xs[0].shape[-1]
    rows = 2 * xs[1].shape[0] if ring else x.shape[0]
    w2 = plain(qk)[0].shape[-1]
    w = w2 // 2
    low = -(-w // 128) * 128
    bt, ba = 256, 512
    half = rows // ba
    steps = (rows // bt, half, half)
    row = pl.BlockSpec((bt, d), lambda i: (jnp.minimum(i, steps[0] - 1), 0))
    wide = pl.BlockSpec((w2, ba), lambda i: (0, jnp.clip(i - steps[0], 0, 2 * half - 1)))
    tall = pl.BlockSpec((ba, d), lambda i: (jnp.clip(i - steps[0] - half, 0, half - 1), 0))
    weights = (*qk, *vo)
    return pl.pallas_call(
        functools.partial(project_kernel, w, low, steps, stack_index(weights), bt, ring),
        grid=(sum(steps),),
        in_specs=[fixed((1, d)), fixed((w2, 1))] + [ANY] * 4 + ([ANY] * 2 if ring else [row]),
        out_specs=[row, tall] + [wide] * 3 + ([row] if ring else []),
        out_shape=[shape_of((rows, d))] * 2 + [shape_of((w2, 2 * rows))] * 3 + ([shape_of((rows, d), F32)] if ring else []),
        scratch_shapes=[
            pltpu.VMEM((rows, d), BF16), pltpu.VMEM((rows, d), BF16),
            pltpu.VMEM((2, d, w2), BF16), pltpu.VMEM((2, d, low), BF16),
            pltpu.SemaphoreType.DMA((4,)), pltpu.SemaphoreType.DMA((steps[0],)), pltpu.SemaphoreType.DMA((steps[0],)),
        ]
        + (halves_scratch(rows, d) if ring else []),
        compiler_params=pltpu.CompilerParams(vmem_limit_bytes=VMEM_LIMIT, collective_id=call, has_side_effects=True),
        cost_estimate=cost(4 * rows * d * 3 * w2, 12 * rows * d),
        name="project",
    )(gain, scale, *plain(weights), *xs)


def middle_kernel(w, low, steps, index, x_ref, gm_ref, att_any, *refs):
    weights, refs = refs[:4], refs[4:]
    mid_ref, pre_ref, res_ref, up_out, down_out, out_out = refs[:6]
    (up_mat, down_mat, out_mat, blocks, vo_side, att, part, got, load, store, send, recv) = refs[6:]
    i = pl.program_id(0)
    far, rows_steps = steps
    bt = x_ref.shape[0]
    ba = part.shape[0] // far
    rows = part.shape[0]
    core = core_of()
    push = pushes(send, recv, core)

    def loads():
        copies = [pltpu.make_async_copy(att_any, att, load.at[0])]
        for s in range(2):
            src = entry(weights[s], index[s]).at[:, pl.ds(low, vo_side.shape[2])]
            copies.append(pltpu.make_async_copy(src, vo_side.at[s], load.at[1 + s]))
        for s in range(2):
            copies.append(pltpu.make_async_copy(entry(weights[2 + s], index[2 + s]), blocks.at[s], load.at[3 + s]))
        return copies

    def stores():
        pairs = ((up_mat, up_out), (down_mat, down_out), (out_mat, out_out))
        return [pltpu.make_async_copy(src, dst, store.at[n]) for n, (src, dst) in enumerate(pairs)]

    def push_block(s):
        return push(blocks.at[s], blocks.at[2 + s], s)

    def push_part(k):
        here = pl.ds(pl.multiple_of(k * ba, ba), ba)
        return push(part.at[here], got.at[here], 2 + k)

    @pl.when(i == 0)
    def _():
        copies = loads()
        for c in copies:
            c.start()
        greet(core)
        for c in copies[:3]:
            c.wait()
        for s in range(2):
            out_mat[:, s * w:(s + 1) * w] = vo_side[s, :, 2 * w - low - w:2 * w - low]
        for s in range(2):
            copies[3 + s].wait()
            push_block(s).start()

    @pl.when(i < far)
    def _():
        here = pl.ds(pl.multiple_of(i * ba, ba), ba)
        cols = pl.ds(pl.multiple_of(rows + i * ba, ba), ba)
        part[here] = dot(att[:, cols], out_mat[...], TT).astype(BF16)
        push_part(i).start()

    at = i - far

    @pl.when(at == 0)
    def _():
        for s in range(2):
            push_block(s).wait()
        for b in range(4):
            up_mat[:, b * w:(b + 1) * w] = blocks[b, :, 0:w]
            down_mat[:, b * w:(b + 1) * w] = blocks[b, :, w:2 * w]
        for c in stores():
            c.start()

    for k in range(far):
        @pl.when(at == k * (ba // bt))
        def _():
            push_part(k).wait()

    @pl.when(at >= 0)
    def _():
        here = pl.ds(pl.multiple_of(at * bt, bt), bt)
        mid = x_ref[...] + got[here].astype(F32) + dot(att[:, here], out_mat[...], TT)
        mid_ref[...] = mid
        h_m = (mid * inverse_rms(mid) * gm_ref[...]).astype(BF16)
        pre = dot(h_m, up_mat[...])
        pre_ref[...] = pre
        hidden = (pre / (1.0 + jnp.exp(-pre))).astype(BF16)
        res_ref[...] = mid + dot(hidden, down_mat[...], NT)

    @pl.when(at == rows_steps - 1)
    def _():
        for c in stores():
            c.wait()


def middle_call(x, att, gain_m, vo, un, call):
    rows, d = x.shape
    w2 = plain(vo)[0].shape[-1]
    w, ff = w2 // 2, 2 * w2
    low = w // 128 * 128
    bt, ba = 256, 512
    steps = (rows // ba, rows // bt)
    row = pl.BlockSpec((bt, d), lambda i: (jnp.maximum(i - steps[0], 0), 0))
    wide = pl.BlockSpec((bt, ff), lambda i: (jnp.maximum(i - steps[0], 0), 0))
    weights = (*vo, *un)
    mats = [(d, ff), (d, ff), (d, w2)]
    slots = 2 + steps[0]
    return pl.pallas_call(
        functools.partial(middle_kernel, w, low, steps, stack_index(weights)),
        grid=(sum(steps),),
        in_specs=[row, fixed((1, d))] + [ANY] * 5,
        out_specs=[row, wide, row] + [ANY] * 3,
        out_shape=[shape_of((rows, d), F32), shape_of((rows, ff), F32), shape_of((rows, d), F32)] + [shape_of(m) for m in mats],
        scratch_shapes=[pltpu.VMEM(m, BF16) for m in mats]
        + [pltpu.VMEM((4, d, w2), BF16), pltpu.VMEM((2, d, w2 - low), BF16), pltpu.VMEM(att.shape, BF16)]
        + [pltpu.VMEM((rows, d), BF16)] * 2
        + [pltpu.SemaphoreType.DMA((5,)), pltpu.SemaphoreType.DMA((3,)), pltpu.SemaphoreType.DMA((slots,)), pltpu.SemaphoreType.DMA((slots,))],
        compiler_params=pltpu.CompilerParams(vmem_limit_bytes=VMEM_LIMIT, collective_id=call, has_side_effects=True),
        cost_estimate=cost(2 * rows * d * (2 * w2 + 2 * ff), 30 * rows * d),
        name="middle",
    )(x, gain_m, att, *plain(weights))


def mlp_back_kernel(w, steps, ring, mid_ref, pre_ref, gm_ref, att_any, *refs):
    mats, refs = refs[:3], refs[3:]
    if ring:
        own_any, got_any, refs = refs[0], refs[1], refs[2:]
        halves = Halves(own_any, got_any, *refs[-3:], ring)
        refs = refs[:-3]
    else:
        g_ref, refs = refs[0], refs[1:]
    g_mid_ref, gain_ref, g_att_ref, o0, o1 = refs[:5]
    (up_mat, down_mat, out_mat, g_all, hid_all, hm_all, gpre_all, low_own, low_other, blocks, got, att,
     load, send, recv) = refs[5:]
    i = pl.program_id(0)
    rows_steps, grad_steps, att_steps, _ = steps
    bt, bd, ba = mid_ref.shape[0], o0.shape[0], g_att_ref.shape[1]
    core = core_of()
    push = pushes(send, recv, core)

    def loads():
        pairs = (*zip(mats, (up_mat, down_mat, out_mat)), (att_any, att))
        return [pltpu.make_async_copy(src, dst, load.at[n]) for n, (src, dst) in enumerate(pairs)]

    def push_rows(k):
        part = pl.ds(pl.multiple_of(k * bt, bt), bt)
        return push(low_own.at[part], low_other.at[part], k)

    def push_block(c, s):
        part = pl.ds(pl.multiple_of(c * bd, bd), bd)
        return push(blocks.at[2 + s, part], got.at[s, part], rows_steps + 2 * c + s)

    @pl.when(i == 0)
    def _():
        copies = loads()
        for c in copies:
            c.start()
        gain_ref[...] = jnp.zeros_like(gain_ref)
        if ring:
            for c in halves.copies:
                c.start()
        greet(core)
        for c in copies[:2] + (halves.copies if ring else []):
            c.wait()

    @pl.when(i < rows_steps)
    def _():
        here = pl.ds(pl.multiple_of(i * bt, bt), bt)
        g = halves.rows(i, bt) if ring else g_ref[...]
        g_low = g.astype(BF16)
        g_all[here] = g_low
        pre = pre_ref[...]
        sig = 1.0 / (1.0 + jnp.exp(-pre))
        hid_all[here] = (pre * sig).astype(BF16)
        g_hidden = dot(g_low, down_mat[...])
        g_pre = (g_hidden * sig * (1.0 + pre * (1.0 - sig))).astype(BF16)
        gpre_all[here] = g_pre
        mid = mid_ref[...]
        inv = inverse_rms(mid)
        normed = mid * inv
        gain = gm_ref[...]
        hm_all[here] = (normed * gain).astype(BF16)
        g_hm = dot(g_pre, up_mat[...], NT)
        gain_ref[...] += eight(g_hm * normed)
        scaled = g_hm * gain
        g_mid = g + inv * (scaled - normed * jnp.mean(scaled * normed, axis=-1, keepdims=True))
        g_mid_ref[...] = g_mid
        low_own[here] = g_mid.astype(BF16)
        push_rows(i).start()

    at = i - rows_steps

    @pl.when((at >= 0) & (at < grad_steps))
    def _():
        cols = pl.ds(pl.multiple_of(at * bd, bd), bd)
        up = dot(hm_all[:, cols], gpre_all[...], TN).astype(BF16)
        down = dot(g_all[:, cols], hid_all[...], TN).astype(BF16)
        for b in range(4):
            blocks[b, cols, 0:w] = up[:, b * w:(b + 1) * w]
            blocks[b, cols, w:2 * w] = down[:, b * w:(b + 1) * w]
        for s in range(2):
            push_block(at, s).start()

    to = at - grad_steps

    @pl.when(to == 0)
    def _():
        loads()[2].wait()

    half = att_steps // 2

    @pl.when((to >= 0) & (to < half))
    def _():
        here = pl.ds(pl.multiple_of(to * ba, ba), ba)
        g_att_ref[...] = dot(out_mat[...], low_own[here], TT).astype(BF16)

    @pl.when(to == half)
    def _():
        for k in range(rows_steps):
            push_rows(k).wait()

    @pl.when((to >= half) & (to < att_steps))
    def _():
        here = pl.ds(pl.multiple_of((to - half) * ba, ba), ba)
        g_att_ref[...] = dot(out_mat[...], low_other[here], TT).astype(BF16)

    last = to - att_steps

    @pl.when(last == 0)
    def _():
        loads()[3].wait()

    @pl.when(last >= 0)
    def _():
        cols = pl.ds(pl.multiple_of(last * bd, bd), bd)
        rows = low_own.shape[0]
        grad = dot(low_own[:, cols], att[:, :rows], TT) + dot(low_other[:, cols], att[:, rows:], TT)
        grad = grad.astype(BF16)
        for s, out in enumerate((o0, o1)):
            push_block(last, s).wait()
            out[:, :2 * w] = (blocks[s, cols].astype(F32) + got[s, cols].astype(F32)).astype(BF16)
            out[:, 2 * w:3 * w] = grad[:, s * w:(s + 1) * w]
            out[:, 3 * w:] = jnp.zeros((bd, out.shape[1] - 3 * w), BF16)


def mlp_back(g, mid, pre, gain, att, mats, width, call, ring=0):
    rows, d = mid.shape
    gs = g if ring else (g,)
    ff = pre.shape[1]
    w2 = att.shape[0]
    w = w2 // 2
    bt, bd, ba = 256, 256, 512
    steps = (rows // bt, d // bd, 2 * rows // ba, d // bd)
    at = stages(steps)
    row = pl.BlockSpec((bt, d), at(0, lambda k: (k, 0)))
    wide = pl.BlockSpec((bt, ff), at(0, lambda k: (k, 0)))
    block = pl.BlockSpec((bd, width), at(3, lambda k: (k, 0)))
    slots = steps[0] + 2 * steps[1]
    return pl.pallas_call(
        functools.partial(mlp_back_kernel, w, steps, ring),
        grid=(sum(steps),),
        in_specs=[row, wide, fixed((1, d))] + [ANY] * 4 + ([ANY] * 2 if ring else [row]),
        out_specs=[row, fixed((8, d)), pl.BlockSpec((w2, ba), at(2, lambda k: (0, k))), block, block],
        out_shape=[shape_of((rows, d), F32), shape_of((8, d), F32), shape_of((w2, 2 * rows))] + [shape_of((d, width))] * 2,
        scratch_shapes=[pltpu.VMEM((d, ff), BF16)] * 2
        + [pltpu.VMEM((d, w2), BF16)]
        + [pltpu.VMEM((rows, d), BF16), pltpu.VMEM((rows, ff), BF16)] * 2
        + [pltpu.VMEM((rows, d), BF16)] * 2
        + [pltpu.VMEM((4, d, w2), BF16), pltpu.VMEM((2, d, w2), BF16)]
        + [pltpu.VMEM(att.shape, BF16)]
        + [pltpu.SemaphoreType.DMA((4,)), pltpu.SemaphoreType.DMA((slots,)), pltpu.SemaphoreType.DMA((slots,))]
        + (halves_scratch(rows, d) if ring else []),
        compiler_params=pltpu.CompilerParams(vmem_limit_bytes=62 * 2**20, collective_id=call, has_side_effects=True),
        cost_estimate=cost(8 * rows * d * ff + 8 * rows * d * w2, 40 * rows * d),
        name="mlp_back",
    )(mid, pre, gain, att, *mats, *gs)


def weight_grad_kernel(w, own_ref, other_ref, dq_ref, dk_ref, dv_ref, *refs):
    out, stacked = refs[-2:]
    half = own_ref.shape[0]

    @pl.when(pl.program_id(0) == 0)
    def _():
        for j, ref in enumerate((dq_ref, dk_ref, dv_ref)):
            stacked[j * w:(j + 1) * w, :] = ref[...]

    grad = dot(own_ref[...], stacked[:, :half], TT) + dot(other_ref[...], stacked[:, half:], TT)
    if len(refs) == 3:
        grad = grad + refs[0][:, :3 * w].astype(F32)
    out[:, :3 * w] = grad.astype(BF16)
    out[:, 3 * w:] = jnp.zeros((out.shape[0], out.shape[1] - 3 * w), BF16)


def weight_grad(own, other, dq, dk, dv, width, got=None):
    rows, d = own.shape
    w = dq.shape[0]
    bd = 256
    col = pl.BlockSpec((rows, bd), lambda i: (0, i))
    flat = pl.BlockSpec((bd, width), lambda i: (i, 0))
    extra = [] if got is None else [got]
    return pl.pallas_call(
        functools.partial(weight_grad_kernel, w),
        grid=(d // bd,),
        in_specs=[col, col] + [fixed(dq.shape)] * 3 + [flat] * len(extra),
        out_specs=flat,
        out_shape=shape_of((d, width)),
        scratch_shapes=[pltpu.VMEM((3 * w, 2 * rows), BF16)],
        compiler_params=params(),
        cost_estimate=cost(12 * rows * d * w, 12 * rows * d),
        name="weight_grad",
    )(own, other, dq, dk, dv, *extra)


def input_back_kernel(w, low, steps, index, x_ref, g_ref, gain_ref, *refs):
    grads, weights, refs = refs[:6], refs[6:10], refs[10:]
    stacked, qk, vo, part, got, load, send, recv = refs[-8:]
    i = pl.program_id(0)
    chunk_steps, far, _ = steps
    if chunk_steps:
        own_ref, other_ref, out_ref, sum_ref, piece_ref = refs[:-8]
    else:
        out_ref, sum_ref = refs[:-8]
    bt, half = x_ref.shape[0], part.shape[0]
    ba = half // far
    push = pushes(send, recv, core_of())

    def loads():
        copies = [
            pltpu.make_async_copy(grads[n], stacked.at[n // 3, pl.ds(n % 3 * w, w)], load.at[n]) for n in range(6)
        ]
        for s in range(2):
            copies.append(pltpu.make_async_copy(entry(weights[s], index[s]), qk.at[s], load.at[6 + s]))
        for s in range(2):
            src = entry(weights[2 + s], index[2 + s]).at[:, pl.ds(0, low)]
            copies.append(pltpu.make_async_copy(src, vo.at[s], load.at[8 + s]))
        return copies

    def push_part(k):
        here = pl.ds(pl.multiple_of(k * ba, ba), ba)
        return push(part.at[here], got.at[here], k)

    def total(cols):
        parts = [
            dot(stacked[s, :2 * w, cols], qk[s], TT) + dot(stacked[s, 2 * w:, cols], vo[s, :, :w], TT) for s in range(2)
        ]
        return parts[0] + parts[1]

    @pl.when(i == 0)
    def _():
        copies = loads()
        for c in copies:
            c.start()
        sum_ref[...] = jnp.zeros_like(sum_ref)
        greet(core_of())
        for c in copies[:3]:
            c.wait()

    if chunk_steps:
        @pl.when(i < chunk_steps)
        def _():
            grad = dot(own_ref[...], stacked[0, :, :half], TT) + dot(other_ref[...], stacked[0, :, half:], TT)
            piece_ref[:, :3 * w] = grad.astype(BF16)
            piece_ref[:, 3 * w:] = jnp.zeros((piece_ref.shape[0], piece_ref.shape[1] - 3 * w), BF16)

    to = i - chunk_steps

    @pl.when(to == 0)
    def _():
        for c in loads()[3:]:
            c.wait()

    @pl.when((to >= 0) & (to < far))
    def _():
        cols = pl.ds(pl.multiple_of(half + to * ba, ba), ba)
        part[pl.ds(pl.multiple_of(to * ba, ba), ba)] = total(cols).astype(BF16)
        push_part(to).start()

    at = to - far
    for k in range(far):
        @pl.when(at == k * (ba // bt))
        def _():
            push_part(k).wait()

    @pl.when(at >= 0)
    def _():
        here = pl.ds(pl.multiple_of(at * bt, bt), bt)
        g_ha = total(here) + got[here].astype(F32)
        x = x_ref[...]
        inv = inverse_rms(x)
        normed = x * inv
        sum_ref[...] += eight(g_ha * normed)
        scaled = g_ha * gain_ref[...]
        out_ref[...] = g_ref[...] + inv * (scaled - normed * jnp.mean(scaled * normed, axis=-1, keepdims=True))


def input_back(grads, x, g, gain, qk, vo, call, normed=(), width=0):
    w, length = grads[0].shape
    rows, d = x.shape
    low = -(-w // 128) * 128
    bt, bd, ba = 256, 256, 512
    chunks = d // bd if normed else 0
    steps = (chunks, rows // ba, rows // bt)
    row = pl.BlockSpec((bt, d), lambda i: (jnp.maximum(i - steps[0] - steps[1], 0), 0))

    def chunk(k):
        return jnp.minimum(k, chunks - 1)

    weights = (*qk, *vo)
    in_specs = [row, row, fixed((1, d))] + [ANY] * 10
    out_specs, out_shape = [row, fixed((8, d))], [shape_of((rows, d), F32), shape_of((8, d), F32)]
    if normed:
        in_specs += [pl.BlockSpec((rows, bd), lambda i: (0, chunk(i)))] * 2
        out_specs.append(pl.BlockSpec((bd, width), lambda i: (chunk(i), 0)))
        out_shape.append(shape_of((d, width)))
    return pl.pallas_call(
        functools.partial(input_back_kernel, w, low, steps, stack_index(weights)),
        grid=(sum(steps),),
        in_specs=in_specs,
        out_specs=out_specs,
        out_shape=out_shape,
        scratch_shapes=[
            pltpu.VMEM((2, 3 * w, length), BF16), pltpu.VMEM((2, d, 2 * w), BF16), pltpu.VMEM((2, d, low), BF16),
            pltpu.VMEM((rows, d), BF16), pltpu.VMEM((rows, d), BF16),
            pltpu.SemaphoreType.DMA((10,)), pltpu.SemaphoreType.DMA((steps[1],)), pltpu.SemaphoreType.DMA((steps[1],)),
        ],
        compiler_params=pltpu.CompilerParams(vmem_limit_bytes=VMEM_LIMIT, collective_id=call, has_side_effects=True),
        cost_estimate=cost(9 * rows * d * 4 * w, 24 * rows * d),
        name="input_back",
    )(x, g, gain, *grads, *plain(weights), *normed)


def finish_kernel(w, low, far, own_steps, outer, ring, index, gain_ref, small_ref, x_any, g_any, piece_any, came_any, *refs):
    grads, weights, refs = refs[:6], refs[6:10], refs[10:]
    own_any, got_any, late_ref, sums_ref = refs[:4]
    (stacked, qk, vo, part, got, xs, gs, send_half, keep, away, came, near, hops, gain_sum, vec, vecs,
     load, store, send, recv) = refs[4:]
    i = pl.program_id(0)
    half = part.shape[0]
    ba, bt = half // far, half // own_steps
    f, t = lax.axis_index("fsdp"), lax.axis_index("tp")
    zz, yy, seq = f // 2, lax.rem(f, 2), t // ring
    across = {"tp": lax.rem(t + ring, 2 * ring)}
    beside = {"fsdp": zz * 2 + 1 - yy}
    along = [{"fsdp": lax.rem(zz + k, outer) * 2 + yy} for k in range(1, outer)]
    core = core_of()
    chunk = keep.shape[1]
    sends = far + outer + outer - 1
    pushed = own_steps // 2

    def push(src, dst, slot, peer):
        return pltpu.make_async_remote_copy(
            src_ref=src, dst_ref=dst, send_sem=send.at[slot], recv_sem=recv.at[slot],
            device_id=peer, device_id_type=MESH,
        )

    def rows_of(j, side):
        z = lax.rem(zz + 1 + j, outer)
        return pl.ds(pl.multiple_of((z * 2 + side) * chunk, chunk), chunk)

    def loads():
        def columns(first):
            cols = pl.ds(first, half)
            return [(grads[n].at[:, cols], stacked.at[n // 3, pl.ds(n % 3 * w, w), cols]) for n in range(6)]

        pairs = columns(half)
        pairs += [(entry(weights[s], index[s]), qk.at[s]) for s in range(2)]
        pairs += [(entry(weights[2 + s], index[2 + s]).at[:, pl.ds(0, low)], vo.at[s]) for s in range(2)]
        pairs += columns(0)
        pairs += [(x_any, xs), (g_any, gs)]
        for j in range(outer):
            for n, (side, dst) in enumerate(((1 - yy, away), (yy, keep))):
                pairs += [(piece_any.at[rows_of(j, side)], dst.at[j]), (came_any.at[rows_of(j, side)], came.at[n, j])]
        return [pltpu.make_async_copy(src, dst, load.at[n]) for n, (src, dst) in enumerate(pairs)]

    def chunk_of(k):
        return 1 - seq if k == 0 else seq

    def push_part(k):
        here = pl.ds(pl.multiple_of(chunk_of(k) * ba, ba), ba)
        return push(part.at[here], got.at[here], k, core)

    def push_near(j):
        return push(away.at[j], near.at[j], far + j, beside)

    def push_hop(j):
        return push(keep.at[j], hops.at[j], far + outer + j, along[j])

    def push_half(k):
        here = pl.ds(pl.multiple_of(k * bt, bt), bt)
        return push(send_half.at[here], got_any.at[here], sends + k, across)

    def push_small(n):
        peer = ([core, across, beside] + along)[n]
        return push(vec.at[min(n, 3)], vecs.at[n], sends + pushed + n, peer)

    def total(cols):
        parts = [
            dot(stacked[s, :2 * w, cols], qk[s], TT) + dot(stacked[s, 2 * w:, cols], vo[s, :, :w], TT) for s in range(2)
        ]
        return parts[0] + parts[1]

    @pl.when(i == 0)
    def _():
        copies = loads()
        for c in copies[18:] + copies[:10]:
            c.start()
        gain_sum[...] = jnp.zeros_like(gain_sum)
        barrier = pltpu.get_barrier_semaphore()
        peers = [core, across, beside] + along
        for peer in peers:
            pl.semaphore_signal(barrier, inc=1, device_id=peer, device_id_type=MESH)
        pl.semaphore_wait(barrier, len(peers))
        for c in copies[18:]:
            c.wait()
        for j in range(outer):
            away[j] = (away[j].astype(F32) + came[0, j].astype(F32)).astype(BF16)
            push_near(j).start()
        for c in copies[:10]:
            c.wait()
        for c in copies[10:18]:
            c.start()

    run = 1 + pushed
    for k in range(far):
        @pl.when(i == k * run)
        def _():
            cols = pl.ds(pl.multiple_of(half + chunk_of(k) * ba, ba), ba)
            part[pl.ds(pl.multiple_of(chunk_of(k) * ba, ba), ba)] = total(cols).astype(BF16)
            push_part(k).start()

    place_in_run = lax.rem(i, run)
    at = jnp.where(place_in_run == 0, -1, i // run * pushed + place_in_run - 1)
    at = jnp.where(i == far + own_steps, own_steps, at)

    @pl.when(at == 0)
    def _():
        for c in loads()[10:18]:
            c.wait()

    for k in range(far):
        @pl.when(at == k * pushed)
        def _():
            push_part(k).wait()

    for j in range(outer - 1):
        @pl.when(at == j + 1)
        def _():
            push_near(j).wait_recv()
            keep[j] = (keep[j].astype(F32) + came[1, j].astype(F32) + near[j].astype(F32)).astype(BF16)
            push_hop(j).start()

    @pl.when((at >= 0) & (at < own_steps))
    def _():
        place = lax.rem(at + pushed * (1 - seq), own_steps)
        here = pl.ds(pl.multiple_of(place * bt, bt), bt)
        g_ha = total(here) + got[here].astype(F32)
        x = xs[here]
        inv = inverse_rms(x)
        normed = x * inv
        gain_sum[...] += eight(g_ha * normed)
        scaled = g_ha * gain_ref[...]
        gs[here] = gs[here] + inv * (scaled - normed * jnp.mean(scaled * normed, axis=-1, keepdims=True))

    @pl.when((at >= 0) & (at < pushed))
    def _():
        place = at + pushed * (1 - seq)
        send_half[pl.ds(pl.multiple_of(at * bt, bt), bt)] = gs[pl.ds(pl.multiple_of(place * bt, bt), bt)].astype(BF16)
        push_half(at).start()

    @pl.when(at == own_steps)
    def _():
        size = half // 2
        mine = pl.ds(pl.multiple_of(seq * size, size), size)
        out_own = pltpu.make_async_copy(gs.at[mine], own_any, store.at[0])
        out_own.start()
        first = lax.broadcasted_iota(jnp.int32, vec.shape[1:], 0) == 0
        vec[0] = small_ref[...] + jnp.where(first, jnp.sum(gain_sum[...], axis=0, keepdims=True), 0.0)
        for n in range(3):
            push_small(n).start()
            push_small(n).wait()
            vec[n + 1] = vec[n] + vecs[n]
        for n in range(3, 2 + outer):
            push_small(n).start()
        for n in range(3, 2 + outer):
            push_small(n).wait()
        sums = vec[3]
        for n in range(3, 2 + outer):
            sums = sums + vecs[n]
        sums_ref[...] = sums
        push_near(outer - 1).wait_recv()
        late = keep[outer - 1].astype(F32) + came[1, outer - 1].astype(F32) + near[outer - 1].astype(F32)
        for j in range(outer - 1):
            push_hop(j).wait()
            late = late + hops[j].astype(F32)
        late_ref[...] = late
        for j in range(outer):
            push_near(j).wait_send()
        for k in range(pushed):
            push_half(k).wait()
        out_own.wait()


def finish(grads, x, g, gain, small, piece, came, qk, vo, fsdp, ring, call):
    w, length = grads[0].shape
    rows, d = x.shape
    width = piece.shape[1]
    low = -(-w // 128) * 128
    outer, chunk = fsdp // 2, piece.shape[0] // fsdp
    far, own_steps = rows // 512, rows // 256
    weights = (*qk, *vo)
    slots = far + 2 * outer - 1 + own_steps // 2 + 2 + outer
    dma = pltpu.SemaphoreType.DMA
    return pl.pallas_call(
        functools.partial(finish_kernel, w, low, far, own_steps, outer, ring, stack_index(weights)),
        grid=(far + own_steps + 1,),
        in_specs=[fixed((1, d)), fixed(small.shape)] + [ANY] * 14,
        out_specs=[ANY, ANY, fixed((chunk, width)), fixed(small.shape)],
        out_shape=[shape_of((rows // 2, d), F32), shape_of((rows // 2, d)), shape_of((chunk, width), F32), shape_of(small.shape, F32)],
        scratch_shapes=[
            pltpu.VMEM((2, 3 * w, length), BF16), pltpu.VMEM((2, d, 2 * w), BF16), pltpu.VMEM((2, d, low), BF16),
            pltpu.VMEM((rows, d), BF16), pltpu.VMEM((rows, d), BF16),
            pltpu.VMEM((rows, d), F32), pltpu.VMEM((rows, d), F32),
            pltpu.VMEM((rows // 2, d), BF16),
            pltpu.VMEM((outer, chunk, width), BF16), pltpu.VMEM((outer, chunk, width), BF16),
            pltpu.VMEM((2, outer, chunk, width), BF16), pltpu.VMEM((outer, chunk, width), BF16),
            pltpu.VMEM((outer - 1, chunk, width), BF16),
            pltpu.VMEM((8, d), F32), pltpu.VMEM((4,) + small.shape, F32), pltpu.VMEM((2 + outer,) + small.shape, F32),
            dma((18 + 4 * outer,)), dma((1,)), dma((slots,)), dma((slots,)),
        ],
        compiler_params=pltpu.CompilerParams(vmem_limit_bytes=VMEM_LIMIT, collective_id=call, has_side_effects=True),
        cost_estimate=cost(6 * rows * d * 4 * w, 24 * rows * d),
        name="finish",
    )(gain, small, x, g, piece, came, *grads, *plain(weights))


def total_over_all(plan, a):
    n, f = plan.tp, plan.fsdp
    hop = 1
    while hop < n:
        a = a + lax.ppermute(a, "tp", [(t, t ^ hop) for t in range(n)])
        hop *= 2
    hop = 1
    while hop < f:
        a = a + lax.ppermute(a, "fsdp", [(t, t ^ hop) for t in range(f)])
        hop *= 2
    return a


def add_low(own, got):
    return (own.astype(F32) + got.astype(F32)).astype(BF16)


def scatter_rows(mine):
    return lax.psum_scatter(mine, "fsdp", scatter_dimension=0, tiled=True)


def after(*arrays):
    return lax.optimization_barrier(arrays)


def fast_body(plan, inputs, cotangent, w_qkv, w_out, w_up, w_down, norm_gain, query_scale, prefix_len):
    seqs, positions, d = inputs.shape
    layers, w = w_qkv.shape[0], w_qkv.shape[3]
    dh = query_scale.shape[1]
    unit = SOFT_ONE / math.sqrt(dh)
    factors = jax.nn.softplus(query_scale) * unit
    prefix = lax.dynamic_slice_in_dim(prefix_len, plan.seq, 1)
    order = plan.blocks(positions * plan.tp)
    out_shard, down_shard = jnp.swapaxes(w_out, 1, 2), jnp.swapaxes(w_down, 1, 2)
    pairs = jnp.concatenate(
        [
            jnp.concatenate([w_qkv[:, 0], w_qkv[:, 1]], axis=2)[:, None],
            jnp.concatenate([w_qkv[:, 2], out_shard], axis=2)[:, None],
            jnp.concatenate([w_up, down_shard], axis=2)[:, None],
        ],
        axis=1,
    )

    block = plan.pick(inputs, 1 - plan.seq).astype(BF16)
    got, other = gather_call(pairs[0, :2], block, pieces_of(2, pairs.shape[2]), plan.fsdp, plan.ring)
    qk0, vo0 = got[0:2], got[2:4]

    def along(l, m):
        return lax.all_gather(pairs[l, m], "fsdp", axis=0, tiled=True)

    def both(rows):
        return rows, plan.across(rows)

    def stacked(rows):
        return (rows, 0), (rows, 1)

    un0_rows, qk1_rows = along(0, 2), along(1, 0)
    other, un0_rows, shards = after(other, un0_rows, pairs[1, 1:])
    shards_got, un0 = plan.across(shards), both(un0_rows)
    kept, weights = [], []
    for l in range(layers):
        qk, vo = (qk0, vo0) if l == 0 else (qk1, vo1)
        scale = jnp.tile(factors[l] * LOG2E, 2 * w // dh)[:, None]
        gain = norm_gain[l, 0][None]
        if l == 0:
            h, h_other, q, k, v, x = project((inputs, other), gain, qk, vo, scale, 3, plan.ring)
        else:
            h, h_other, q, k, v = project(x, gain, qk, vo, scale, 3 + l)
        if l == 0:
            q, shards_got, qk1_rows = after(q, shards_got, qk1_rows)
            shards = jnp.stack([shards, shards_got], axis=1)
            vo1_rows, un1_rows = (lax.all_gather(shards[m], "fsdp", axis=1, tiled=True) for m in range(2))
            qk1 = both(qk1_rows)
        att, lse = attention_forward(q, k, v, prefix, order, dh)
        if l == 0:
            att, un0_got = after(att, un0[1])
            un = un0[0], un0_got
        else:
            att, un1_rows, cot_got = after(att, un1_rows, cot_got)
            un = stacked(un1_rows)
        mid, pre, res, *mats = middle_call(x, att, norm_gain[l, 1][None], vo, un, 5 + l)
        if l == 0:
            res, cotangent = after(res, cotangent)
            cot_block = plan.pick(cotangent, 1 - plan.seq).astype(BF16)
            res, qk1_got, vo1_rows, cot_block = after(res, qk1[1], vo1_rows, cot_block)
            qk1, vo1 = (qk1[0], qk1_got), stacked(vo1_rows)
            cot_got = plan.across(cot_block)
        kept.append((x, h, h_other, q, k, v, att, lse, mid, pre))
        weights.append((qk, vo, mats))
        x = res
    g = cotangent, cot_got
    out_blocks = x.reshape(seqs, positions, d)
    out_send = plan.pick(out_blocks, 1 - plan.seq).astype(BF16)
    cot_got, out_send = after(cot_got, out_send)
    g = cotangent, cot_got
    out_got = plan.across(out_send)
    outputs = None
    width = -(-3 * w // 128) * 128
    grads = [None] * layers
    for l in reversed(range(layers)):
        qk, vo, mats = weights[l]
        x, h, h_other, q, k, v, att, lse, mid, pre = kept[l]
        ring = plan.ring if l == layers - 1 else 0
        g_mid, gain_m, g_att, *early = mlp_back(g, mid, pre, norm_gain[l, 1][None], att, mats, width, 1 + l, ring)
        if l > 0:
            early = [scatter_rows(a) for a in early]
        else:
            early_got = plan.across(early[1])
        if l + 1 < layers:
            g_att, grads[l + 1][0][1] = after(g_att, grads[l + 1][0][1])
        dgrads, fgs, pieces = [None] * 6, [], [None] * 2
        for s in (1, 0):
            dq, dk, dv, fg = attention_backward(
                q, k, v, att, g_att, lse, factors[l], prefix, order, dh, s * w, w
            )
            if s == 1:
                pieces[1] = weight_grad(h, h_other, dq, dk, dv, width)
                if l > 0:
                    pieces[1], out_got = after(pieces[1], out_got)
                    g_att, pieces[1] = after(g_att, pieces[1])
                else:
                    g_att, pieces[1], out_got = after(g_att, pieces[1], out_got)
                    outputs = plan.order(plan.pick(out_blocks, plan.seq), out_got.astype(F32)).reshape(out_blocks.shape)
                    pieces[1], early_got, outputs = after(pieces[1], early_got, outputs)
                late_got = plan.across(pieces[1])
                if l + 1 < layers:
                    g_att, grads[l + 1][1] = after(g_att, grads[l + 1][1])
                if l == 0:
                    g_att, early_got = after(g_att, early_got)
                    mine, g_att = after(add_low(early[0], early_got), g_att)
                    early = scatter_rows(mine)
            elif l > 0:
                dq, early[0] = after(dq, early[0])
            dgrads[3 * s:3 * s + 3] = [dq, dk, dv]
            fgs.append(fg)
        fg = fgs[0] + fgs[1]
        if l > 0:
            g, gain_a, pieces[0] = input_back(
                dgrads, x, g_mid, norm_gain[l, 0][None], qk, vo, 7 + l, (h, h_other), width
            )
            pieces[0], late_got = after(pieces[0], late_got)
            mine, g = after(add_low(pieces[0], late_got), g)
        else:
            pieces[0] = weight_grad(h, h_other, *dgrads[:3], width)
        row = lambda a: jnp.pad(a, (0, d - a.shape[0]))[None]
        small = [row(jnp.sum(gain_m, axis=0)), row(jnp.sum(fg, axis=1) / (factors[l] * LOG2E))]
        if l > 0:
            late = scatter_rows(mine)
            small.append(row(jnp.sum(gain_a, axis=0)))
            grads[l] = [early, late, small]
    upper = grads[1][2]
    zero = jnp.zeros((1, d), F32)
    small = jnp.concatenate([zero, upper[2], small[0], upper[0], small[1], upper[1], zero, zero])
    own_half, got_half, late, small = finish(
        dgrads, x, g_mid, norm_gain[0, 0][None], small, pieces[0], late_got, qk, vo, plan.fsdp, plan.ring, 9
    )
    grads[0] = [early, late, small]
    input_grad = plan.order(own_half, got_half.astype(F32)).reshape(out_blocks.shape)
    early = []
    for entry, _, _ in grads:
        if isinstance(entry, list):
            early.append(entry[0].astype(F32) + plan.across(entry[1]).astype(F32))
        else:
            early.append(entry.astype(F32))
    early = jnp.stack(early)
    late = jnp.stack([entry[1].astype(F32) for entry in grads])
    qkv_g = jnp.stack([late[:, :, c * w:(c + 1) * w] for c in range(3)], axis=1)
    up_g, down_g, out_g = (early[:, :, c * w:(c + 1) * w] for c in range(3))
    scale_g = small[4:6, :dh] * jax.nn.sigmoid(query_scale) * unit
    return (
        outputs, input_grad, qkv_g, jnp.swapaxes(out_g, 1, 2), up_g, jnp.swapaxes(down_g, 1, 2),
        small[:2], small[2:4], scale_g,
    )


def body(inputs, cotangent, w_qkv, w_out, w_up, w_down, norm_gain, query_scale, prefix_len):
    seqs, positions, d = inputs.shape
    fsdp, tp = lax.axis_size("fsdp"), lax.axis_size("tp")
    layers = w_qkv.shape[0]
    plan = Plan(seqs, tp, fsdp, w_qkv.shape[2])
    if plan.fast:
        return fast_body(
            plan, inputs, cotangent, w_qkv, w_out, w_up, w_down, norm_gain, query_scale, prefix_len
        )
    dh = query_scale.shape[1]
    unit = SOFT_ONE / math.sqrt(dh)
    factors = jax.nn.softplus(query_scale) * unit
    prefix = lax.dynamic_slice_in_dim(prefix_len, plan.seq, 1)
    order = plan.blocks(positions * tp)
    out_shard, down_shard = jnp.swapaxes(w_out, 1, 2), jnp.swapaxes(w_down, 1, 2)

    weights = []
    for l in range(layers):
        qkv = plan.gather_heads(w_qkv[l])
        out_t = plan.gather_heads(out_shard[l][None])[:, 0]
        up, down_t = plan.gather_full(jnp.stack([w_up[l], down_shard[l]]))
        weights.append(([qkv[:, c] for c in range(3)], out_t, up, down_t))

    x = plan.swap(inputs)
    g = plan.swap(cotangent)
    kept = []
    for l in range(layers):
        x, saved = layer_forward(plan, x, prefix, order, *weights[l], norm_gain[l], factors[l])
        kept.append(saved)
    outputs = plan.unswap(x)
    grads = [None] * layers
    for l in reversed(range(layers)):
        g, grads[l] = layer_backward(
            plan, g, kept[l], prefix, order, *weights[l], norm_gain[l], factors[l]
        )
    input_grad = plan.unswap(g)
    qkv_g, out_g, up_g, down_g, gain_a, gain_m, f_g = (jnp.stack(a) for a in zip(*grads))
    scale_g = f_g * jax.nn.sigmoid(query_scale) * unit
    gain_a, gain_m, scale_g = lax.psum((gain_a, gain_m, scale_g), ("fsdp", "tp"))
    return outputs, input_grad, qkv_g, out_g, up_g, down_g, gain_a, gain_m, scale_g


def solution(mesh):
    placed = (
        P("fsdp", "tp", None),
        P("fsdp", "tp", None),
        P(None, None, "fsdp", "tp"),
        P(None, "tp", "fsdp"),
        P(None, "fsdp", "tp"),
        P(None, "tp", "fsdp"),
        P(),
        P(),
        P("fsdp"),
    )
    return jax.shard_map(
        body,
        mesh=mesh,
        in_specs=placed,
        out_specs=placed[:6] + (P(), P(), P()),
        check_vma=False,
    )
```

```python
import functools, math
import jax
import jax.numpy as jnp
from jax import lax
from jax.experimental import pallas as pl
from jax.experimental.pallas import tpu as pltpu
from jax.sharding import PartitionSpec as P

MASKED = -1e30
F32, BF16 = jnp.float32, jnp.bfloat16
EPSILON = 1e-06
SOFT_ONE = 1.442695041
LOG2E = math.log2(math.e)
MESH = pl.DeviceIdType.MESH
HINT = 1
VMEM_LIMIT = 60 * 2**20

def dot(a, b, dims=((1,), (0,))):
    return lax.dot_general(a, b, (dims, ((), ())), preferred_element_type=F32)

def key_range(row_start, rows, prefix, block):
    full = jnp.maximum(row_start + 1, prefix) // block
    stop = (jnp.maximum(row_start + rows, prefix) + block - 1) // block
    return full, stop

def forward_kernel(prefix_ref, order_ref, q_ref, k_ref, v_ref, o_ref, lse_ref, key_rows, value_ext, *, pair, dh, bq, bk):
    length = q_ref.shape[1]
    prefix = prefix_ref[0]
    ext = value_ext.shape[1]
    bound = 0.0
    for h in range(pair):
        rows = slice(h * dh, (h + 1) * dh)
        q, k = q_ref[rows, :].astype(F32), k_ref[rows, :].astype(F32)
        bound = jnp.maximum(bound, jnp.max(jnp.sum(q * q, axis=0)) * jnp.max(jnp.sum(k * k, axis=0)))
        key_rows[h] = k_ref[rows, :].T
        value_ext[h, :dh] = v_ref[rows, :]
        value_ext[h, dh:] = jnp.ones((ext - dh, length), BF16)

    def one_query(shifted, qi, carry):
        start = qi * bq
        here = pl.ds(pl.multiple_of(order_ref[qi] * bq, bq), bq)
        queries = [q_ref[h * dh:(h + 1) * dh, here] for h in range(pair)]
        full, stop = key_range(start, bq, prefix, bk)

        def step(masked, ki, state):
            first = ki * bk
            there = pl.ds(pl.multiple_of(order_ref[ki] * bk, bk), bk)
            if masked:
                rows = first + lax.broadcasted_iota(jnp.int32, (bk, bq), 0)
                cols = start + lax.broadcasted_iota(jnp.int32, (bk, bq), 1)
                allowed = rows <= jnp.maximum(cols, prefix - 1)
            scores = [dot(key_rows[h, there], queries[h]) for h in range(pair)]
            fresh = []
            for h in range(pair):
                s = jnp.where(allowed, scores[h], MASKED) if masked else scores[h]
                if shifted:
                    top, total = state[h]
                    new_top = jnp.maximum(top, jnp.max(s, axis=0, keepdims=True))
                    p = jnp.exp2(s - new_top).astype(BF16)
                    total = total * jnp.exp2(top - new_top) + dot(value_ext[h, :, there], p)
                    fresh.append((new_top, total))
                else:
                    fresh.append(state[h] + dot(value_ext[h, :, there], jnp.exp2(s).astype(BF16)))
            return tuple(fresh)

        zero = jnp.zeros((ext, bq), F32)
        state = tuple((jnp.full((1, bq), MASKED, F32), zero) if shifted else zero for _ in range(pair))
        state = lax.fori_loop(0, full, functools.partial(step, False), state)
        state = lax.fori_loop(full, stop, functools.partial(step, True), state)
        for h in range(pair):
            top, total = state[h] if shifted else (0.0, state[h])
            norm = total[dh:dh + 1]
            o_ref[h * dh:(h + 1) * dh, here] = (total[:dh] / norm).astype(BF16)
            lse_ref[h, :, here] = top + jnp.log2(norm)
        return carry

    small = bound <= 3600.0

    @pl.when(small)
    def _():
        lax.fori_loop(0, length // bq, functools.partial(one_query, False), 0)

    @pl.when(jnp.logical_not(small))
    def _():
        lax.fori_loop(0, length // bq, functools.partial(one_query, True), 0)


def attention_forward(q, k, v, prefix, order, dh, pair=4):
    width, length = q.shape
    heads = width // dh
    pair = min(pair, heads)
    bq = bk = length // order.shape[0]
    ext = dh + 16
    spec = pl.BlockSpec((pair * dh, length), lambda i, p, o: (i, 0))
    return pl.pallas_call(
        functools.partial(forward_kernel, pair=pair, dh=dh, bq=bq, bk=bk),
        grid_spec=pltpu.PrefetchScalarGridSpec(
            num_scalar_prefetch=2, grid=(heads // pair,),
            in_specs=[spec, spec, spec],
            out_specs=[spec, pl.BlockSpec((pair, 1, length), lambda i, p, o: (i, 0, 0))],
            scratch_shapes=[pltpu.VMEM((pair, length, dh), BF16), pltpu.VMEM((pair, ext, length), BF16)],
        ),
        out_shape=[jax.ShapeDtypeStruct((width, length), BF16), jax.ShapeDtypeStruct((heads, 1, length), F32)],
        compiler_params=pltpu.CompilerParams(vmem_limit_bytes=VMEM_LIMIT),
        cost_estimate=pl.CostEstimate(flops=int(HINT * 600 * length * length * heads), bytes_accessed=int(HINT * 8 * width * length), transcendentals=0),
        name="attention_forward",
    )(prefix, order, q, k, v)

def split3(x):
    a = x.astype(BF16)
    r = x - a.astype(F32)
    b = r.astype(BF16)
    c = (r - b.astype(F32)).astype(BF16)
    return a, b, c

def backward_kernel(prefix_ref, order_ref, q_ref, k_ref, v_ref, o_ref, g_ref, lse_ref, scale_ref, dq_ref, dk_ref, dv_ref, fg_ref,
                    key_ext, value_ext, query_ext, grad_ext, dk_acc, dv_acc, *, pair, dh, bq, bk):
    length = q_ref.shape[1]
    prefix = prefix_ref[0]
    pad = key_ext.shape[1] - dh
    index = lax.broadcasted_iota(jnp.int32, (pad, length), 0)
    ones = (index < 3).astype(F32).astype(BF16)

    @pl.when(pl.program_id(0) == 0)
    def _():
        fg_ref[...] = jnp.zeros_like(fg_ref)

    def tail(row):
        high, mid, low = (part.astype(F32) for part in split3(-row))
        rest = jnp.where(index == 1, mid, jnp.where(index == 2, low, 0.0))
        return jnp.where(index == 0, high, rest).astype(BF16)

    for h in range(pair):
        rows = slice(h * dh, (h + 1) * dh)
        g = g_ref[rows, :]
        key_ext[h, :dh] = k_ref[rows, :]
        key_ext[h, dh:] = ones
        value_ext[h, :dh] = v_ref[rows, :]
        value_ext[h, dh:] = ones
        delta = jnp.sum(o_ref[rows, :].astype(F32) * g.astype(F32), axis=0, keepdims=True)
        query_ext[h, :dh] = q_ref[rows, :]
        query_ext[h, dh:] = tail(lse_ref[h])
        grad_ext[h, :dh] = g
        grad_ext[h, dh:] = tail(delta)
        dk_acc[h] = jnp.zeros((dh, length), F32)
        dv_acc[h] = jnp.zeros((dh, length), F32)

    def one_query(qi, carry):
        start = qi * bq
        here = pl.ds(pl.multiple_of(order_ref[qi] * bq, bq), bq)
        full, stop = key_range(start, bq, prefix, bk)

        def step(masked, ki, state):
            first = ki * bk
            there = pl.ds(pl.multiple_of(order_ref[ki] * bk, bk), bk)
            if masked:
                rows = start + lax.broadcasted_iota(jnp.int32, (bq, bk), 0)
                cols = first + lax.broadcasted_iota(jnp.int32, (bq, bk), 1)
                allowed = cols <= jnp.maximum(rows, prefix - 1)
            fresh = []
            s = [dot(query_ext[h, :, here], key_ext[h, :, there], ((0,), (0,))) for h in range(pair)]
            gp = [dot(grad_ext[h, :, here], value_ext[h, :, there], ((0,), (0,))) for h in range(pair)]
            for h in range(pair):
                x = jnp.where(allowed, s[h], MASKED) if masked else s[h]
                p = jnp.exp2(x)
                ds = (p * gp[h]).astype(BF16)
                rows = slice(h * dh, (h + 1) * dh)
                dv_acc[h, :, there] += dot(g_ref[rows, here], p.astype(BF16))
                dk_acc[h, :, there] += dot(q_ref[rows, here], ds)
                fresh.append(state[h] + dot(ds, k_ref[rows, there], ((1,), (1,))))
            return tuple(fresh)

        state = tuple(jnp.zeros((bq, dh), F32) for _ in range(pair))
        state = lax.fori_loop(0, full, functools.partial(step, False), state)
        state = lax.fori_loop(full, stop, functools.partial(step, True), state)
        for h in range(pair):
            rows = slice(h * dh, (h + 1) * dh)
            dq = state[h].T
            prod = dq * q_ref[rows, here].astype(F32)
            part = prod[:, :128]
            for c in range(1, bq // 128):
                part = part + prod[:, c * 128:(c + 1) * 128]
            fg_ref[...] += part
            dq_ref[rows, here] = (dq * scale_ref[...]).astype(BF16)
        return carry

    lax.fori_loop(0, length // bq, one_query, 0)
    for h in range(pair):
        rows = slice(h * dh, (h + 1) * dh)
        dk_ref[rows, :] = (dk_acc[h] * math.log(2.0)).astype(BF16)
        dv_ref[rows, :] = dv_acc[h].astype(BF16)


def attention_backward(q, k, v, o, g, lse, factor, prefix, order, dh, base=0, width=None, pair=2):
    full, length = q.shape
    width = width or full
    heads = width // dh
    pair = min(pair, heads)
    bq = bk = length // order.shape[0]
    ext = dh + 16
    spec = pl.BlockSpec((pair * dh, length), lambda i, p, o: (i, 0))
    skip = base // (pair * dh)
    source = pl.BlockSpec((pair * dh, length), lambda i, p, o: (i + skip, 0))
    wide = jax.ShapeDtypeStruct((width, length), BF16)
    return pl.pallas_call(
        functools.partial(backward_kernel, pair=pair, dh=dh, bq=bq, bk=bk),
        grid_spec=pltpu.PrefetchScalarGridSpec(
            num_scalar_prefetch=2, grid=(heads // pair,),
            in_specs=[source] * 5 + [pl.BlockSpec((pair, 1, length), lambda i, p, o: (i + skip, 0, 0)), pl.BlockSpec((dh, 1), lambda i, p, o: (0, 0))],
            out_specs=[spec] * 3 + [pl.BlockSpec((dh, 128), lambda i, p, o: (0, 0))],
            scratch_shapes=[
                pltpu.VMEM((pair, ext, length), BF16),
                pltpu.VMEM((pair, ext, length), BF16),
                pltpu.VMEM((pair, ext, length), BF16),
                pltpu.VMEM((pair, ext, length), BF16),
                pltpu.VMEM((pair, dh, length), F32),
                pltpu.VMEM((pair, dh, length), F32)],
        ),
        out_shape=[wide] * 3 + [jax.ShapeDtypeStruct((dh, 128), F32)],
        compiler_params=pltpu.CompilerParams(vmem_limit_bytes=VMEM_LIMIT),
        cost_estimate=pl.CostEstimate(flops=int(HINT * 1600 * length * length * heads), bytes_accessed=int(HINT * 16 * width * length), transcendentals=0),
        name="attention_backward",
    )(prefix, order, q, k, v, o, g, lse, factor.reshape(dh, 1))


def rms(x):
    inv = lax.rsqrt(jnp.mean(x * x, axis=-1, keepdims=True) + EPSILON)
    return x * inv, inv


def rms_back(normed, inv, gain, grad):
    scaled = grad * gain
    out = inv * (scaled - normed * jnp.mean(scaled * normed, axis=-1, keepdims=True))
    return out, jnp.sum(grad * normed, axis=0)


def ein(spec, *args):
    return jnp.einsum(spec, *args, preferred_element_type=F32)


def gather_kernel(pieces, pairs, outer, ring, shard_ref, input_ref, *refs):
    outs = [refs[2 * m:2 * m + 2] for m in range(pairs)]
    got_ref = refs[2 * pairs]
    wide_ref, block_ref, send, recv, local = refs[2 * pairs + 1:]
    f, t = lax.axis_index("fsdp"), lax.axis_index("tp")
    zz, yy = f // 2, f % 2
    across = {"tp": lax.rem(t + ring, 2 * ring)}
    beside = {"fsdp": zz * 2 + 1 - yy}
    along = [{"fsdp": lax.rem(zz + k, outer) * 2 + yy} for k in range(1, outer)]
    peers = along + [across, beside]
    barrier = pltpu.get_barrier_semaphore()
    for peer in peers:
        pl.semaphore_signal(barrier, inc=1, device_id=peer, device_id_type=MESH)
    pl.semaphore_wait(barrier, len(peers))
    used = [0]
    wide = pltpu.make_async_copy(input_ref.at[1 - t // ring], wide_ref, local.at[len(pieces)])
    wide.start()

    def copy(src, dst, peer):
        slot = used[0]
        used[0] += 1
        return pltpu.make_async_remote_copy(
            src_ref=src, dst_ref=dst, send_sem=send.at[slot], recv_sem=recv.at[slot],
            device_id=peer, device_id_type=MESH,
        )

    count = len(pieces)
    chunks = 4
    step = block_ref.shape[0] // chunks
    blocks = [
        copy(block_ref.at[pl.ds(i * step, step)], got_ref.at[pl.ds(i * step, step)], across)
        for i in range(chunks)
    ]
    own, first, second, third = [], [], [], []
    for i, (m, low, rows, route) in enumerate(pieces):
        part = pl.ds(low, rows)
        w = [out.at[:, :, part] for out in outs[m]]
        src = shard_ref.at[m, part]
        own.append(pltpu.make_async_copy(src, w[0].at[zz, yy], local.at[i]))
        first.append([copy(src, w[0].at[zz, yy], peer) for peer in along])
        if route:
            second.append([copy(w[0].at[:, yy], w[0].at[:, yy], beside)])
            third.append([copy(w[0], w[1], across)])
        else:
            second.append([copy(w[0].at[:, yy], w[1].at[:, yy], across)])
            third.append([copy(w[s].at[:, yy], w[s].at[:, yy], beside) for s in range(2)])

    def begin(i):
        own[i].start()
        for c in first[i]:
            c.start()

    ahead = 3
    for i in range(min(ahead, count)):
        begin(i)
    wide.wait()
    block_ref[...] = wide_ref[...].astype(BF16)
    for b in blocks[:2]:
        b.start()
    started = 2
    for i in range(count + 2):
        if i < count:
            own[i].wait()
            for c in first[i]:
                c.wait_recv()
            for c in second[i]:
                c.start()
            if i + ahead < count:
                begin(i + ahead)
            if started < chunks:
                blocks[started].start()
                started += 1
        if 0 <= i - 1 < count:
            for c in second[i - 1]:
                c.wait_recv()
            for c in third[i - 1]:
                c.start()
        if 0 <= i - 2 < count:
            for c in third[i - 2]:
                c.wait_recv()
    for b in blocks[started:]:
        b.start()
    for i in range(count):
        for c in first[i] + second[i] + third[i]:
            c.wait_send()
    for b in blocks:
        b.wait()


def pieces_of(pairs, rows):
    half = rows // 32 * 16
    return tuple(
        (m, low, size, m_part) for m in range(pairs) for m_part, (low, size) in enumerate(((0, half), (half, rows - half)))
    )


def gather_call(shards, inputs, pieces, fsdp, ring):
    pairs, rows, w = shards.shape
    outer = fsdp // 2
    slots = 4 + len(pieces) * (outer + 2)
    any_spec = pl.BlockSpec(memory_space=pl.ANY)
    got = pl.pallas_call(
        functools.partial(gather_kernel, pieces, pairs, outer, ring),
        out_shape=[jax.ShapeDtypeStruct((outer, 2, rows, w), BF16)] * (2 * pairs)
        + [jax.ShapeDtypeStruct(inputs.shape[1:], BF16)],
        in_specs=[any_spec] * 2,
        out_specs=[any_spec] * (2 * pairs + 1),
        scratch_shapes=[
            pltpu.VMEM(inputs.shape[1:], F32),
            pltpu.VMEM(inputs.shape[1:], BF16),
            pltpu.SemaphoreType.DMA((slots,)),
            pltpu.SemaphoreType.DMA((slots,)),
            pltpu.SemaphoreType.DMA((len(pieces) + 1,)),
        ],
        compiler_params=pltpu.CompilerParams(vmem_limit_bytes=VMEM_LIMIT, collective_id=0, has_side_effects=True),
        name="gather_weights",
    )(shards, inputs)
    return [a.reshape(outer * 2 * rows, w) for a in got[:-1]], got[-1]


class Plan:
    def __init__(self, seqs, tp, fsdp, rows):
        self.seqs, self.tp, self.ring, self.fsdp = seqs, tp, tp // seqs, fsdp
        self.same_member = [[s * self.ring + r for s in range(seqs)] for r in range(self.ring)]
        self.same_seq = [[s * self.ring + r for r in range(self.ring)] for s in range(seqs)]
        self.fast = seqs == 2 and self.ring == 2 and fsdp % 2 == 0 and rows % 32 == 0
        t = lax.axis_index("tp")
        self.seq, self.member = t // self.ring, lax.rem(t, self.ring)

    def across(self, a):
        n = self.tp
        return lax.ppermute(a, "tp", [(t, (t + self.ring) % n) for t in range(n)])

    def core(self, a):
        return lax.ppermute(a, "tp", [(t, t ^ 1) for t in range(self.tp)])

    def pick(self, blocks, index):
        return lax.dynamic_index_in_dim(blocks, index, 0, keepdims=False)

    def order(self, own, other):
        first = self.seq == 0
        return jnp.concatenate([jnp.where(first, own, other), jnp.where(first, other, own)])

    def swap(self, blocks):
        if self.seqs == 2:
            other = self.across(self.pick(blocks, 1 - self.seq).astype(BF16))
            return self.order(self.pick(blocks, self.seq), other.astype(F32))
        got = lax.all_to_all(
            blocks.astype(BF16), "tp", 0, 0, tiled=True, axis_index_groups=self.same_member
        )
        return got.reshape(-1, got.shape[-1]).astype(F32)

    def unswap(self, rows):
        blocks = rows.reshape(self.seqs, -1, rows.shape[-1])
        return self.swap(blocks).reshape(blocks.shape)

    def whole(self, rows):
        if self.fast:
            return jnp.concatenate([rows, self.core(rows)])
        cut = rows.reshape(self.seqs, -1, rows.shape[-1])
        got = lax.all_gather(cut, "tp", axis=1, axis_index_groups=self.same_seq)
        return got.reshape(-1, rows.shape[-1])

    def share(self, full):
        if self.fast:
            own = full.shape[0] // 2
            return full[:own].astype(F32) + self.core(full[own:].astype(BF16)).astype(F32)
        cut = full.astype(BF16).reshape(self.seqs, self.ring, -1, full.shape[-1])
        got = lax.psum_scatter(cut, "tp", scatter_dimension=1, axis_index_groups=self.same_seq)
        return got.reshape(-1, full.shape[-1]).astype(F32)

    def blocks(self, length):
        if self.fast:
            j = jnp.arange(self.tp, dtype=jnp.int32)
            apart = (j % self.ring != self.member).astype(jnp.int32)
            return apart * self.seqs + j // self.ring
        return jnp.arange(max(1, length // 512), dtype=jnp.int32)

    def gather_heads(self, shards):
        rows = lax.all_gather(shards, "fsdp", axis=1, tiled=True)
        if self.fast:
            return jnp.stack([rows, self.across(rows)])
        return lax.all_gather(rows, "tp", axis_index_groups=self.same_member)

    def join(self, every):
        r, s, m, d, w = every.shape
        return every.transpose(2, 3, 0, 1, 4).reshape(m, d, r * s * w)

    def gather_full(self, shards):
        part = self.gather_heads(shards)
        if self.fast:
            return self.join(jnp.stack([part, self.core(part)]))
        return self.join(lax.all_gather(part, "tp", axis_index_groups=self.same_seq))

    def scatter_heads(self, grads):
        if self.fast:
            other = self.across(grads[1].astype(BF16))
            mine = (grads[0].astype(F32) + other.astype(F32)).astype(BF16)
        else:
            mine = lax.psum_scatter(
                grads.astype(BF16), "tp", scatter_dimension=0, axis_index_groups=self.same_member
            )
        return lax.psum_scatter(mine, "fsdp", scatter_dimension=1, tiled=True).astype(F32)

    def scatter_full(self, grads):
        m, d, cols = grads.shape
        if self.fast:
            half = cols // 2
            other = self.core(grads[:, :, half:].astype(BF16))
            mine = grads[:, :, :half].astype(F32) + other.astype(F32)
            mine = mine.astype(BF16).reshape(m, d, self.seqs, -1).transpose(2, 0, 1, 3)
        else:
            cut = grads.astype(BF16).reshape(m, d, self.ring, self.seqs, -1).transpose(2, 3, 0, 1, 4)
            mine = lax.psum_scatter(cut, "tp", scatter_dimension=0, axis_index_groups=self.same_seq)
        return self.scatter_heads(mine)


def layer_forward(plan, x, prefix, order, qkv, out_t, up, down_t, gains, factor):
    dh = factor.shape[0]
    normed, inv = rms(x)
    h = plan.whole((normed * gains[0]).astype(BF16))
    seqs, d, w = out_t.shape
    raw = [ein("sdc,td->sct", qkv[c], h).reshape(seqs * w, -1) for c in range(3)]
    scale = jnp.tile(factor * LOG2E, seqs * w // dh)[:, None]
    q, k, v = (raw[0] * scale).astype(BF16), raw[1].astype(BF16), raw[2].astype(BF16)
    att, lse = attention_forward(q, k, v, prefix, order, dh)
    middle = x + plan.share(ein("sct,sdc->td", att.reshape(seqs, w, -1), out_t))
    normed_m, inv_m = rms(middle)
    h_m = (normed_m * gains[1]).astype(BF16)
    pre = ein("td,df->tf", h_m, up)
    hidden = jax.nn.silu(pre).astype(BF16)
    result = middle + ein("tf,df->td", hidden, down_t)
    return result, (x, inv, h, q, k, v, att, lse, middle, inv_m, h_m, pre, hidden)


def layer_backward(plan, g, saved, prefix, order, qkv, out_t, up, down_t, gains, factor):
    x, inv, h, q, k, v, att, lse, middle, inv_m, h_m, pre, hidden = saved
    dh = factor.shape[0]
    seqs, d, w = out_t.shape
    length = h.shape[0]
    g_low = g.astype(BF16)
    down_grad = ein("td,tf->df", g_low, hidden)
    g_hidden = ein("td,df->tf", g_low, down_t)
    sig = jax.nn.sigmoid(pre)
    g_pre = (g_hidden * sig * (1.0 + pre * (1.0 - sig))).astype(BF16)
    up_grad = ein("td,tf->df", h_m, g_pre)
    mlp_grads = plan.scatter_full(jnp.stack([up_grad, down_grad]))
    g_hm = ein("tf,df->td", g_pre, up)
    back_m, gain_m = rms_back(middle * inv_m, inv_m, gains[1], g_hm)
    g_mid = g + back_m
    g_all = plan.whole(g_mid.astype(BF16))
    att3 = att.reshape(seqs, w, length)
    out_grad = plan.scatter_heads(ein("td,sct->sdc", g_all, att3)[:, None])[0]
    g_att = ein("td,sdc->sct", g_all, out_t).astype(BF16).reshape(seqs * w, length)
    dq, dk, dv, fg = attention_backward(q, k, v, att, g_att, lse, factor, prefix, order, dh)
    factor_grad = jnp.sum(fg, axis=1) / (factor * LOG2E)
    parts = [a.reshape(seqs, w, length) for a in (dq, dk, dv)]
    qkv_grad = plan.scatter_heads(jnp.stack([ein("td,sct->sdc", h, a) for a in parts], axis=1))
    g_ha = plan.share(sum(ein("sct,sdc->td", a, b) for a, b in zip(parts, qkv)))
    back_a, gain_a = rms_back(x * inv, inv, gains[0], g_ha)
    return g_mid + back_a, (qkv_grad, out_grad.T, mlp_grads[0], mlp_grads[1].T, gain_a, gain_m, factor_grad)


TN, NT, TT = ((0,), (0,)), ((1,), (1,)), ((0,), (1,))
ONE = pl.Buffered(1)


def cost(flops, nbytes):
    return pl.CostEstimate(flops=int(flops * HINT), bytes_accessed=int(nbytes * HINT), transcendentals=0)


def params(mib=60):
    return pltpu.CompilerParams(vmem_limit_bytes=mib * 2**20)


def fixed(shape):
    return pl.BlockSpec(shape, lambda *a: (0,) * len(shape), pipeline_mode=ONE)


def weight(w, lanes=None):
    stack, index = w if isinstance(w, tuple) else (w, None)
    shape = (stack.shape[-2], lanes or stack.shape[-1])
    if index is None:
        return fixed(shape)
    return pl.BlockSpec((None,) + shape, lambda *a: (index, 0, 0), pipeline_mode=ONE)


def plain(weights):
    return [w[0] if isinstance(w, tuple) else w for w in weights]


def shape_of(shape, dtype=BF16):
    return jax.ShapeDtypeStruct(shape, dtype)


def inverse_rms(x):
    return lax.rsqrt(jnp.mean(x * x, axis=-1, keepdims=True) + EPSILON)


def eight(x):
    return jnp.sum(x.reshape(-1, 8, x.shape[-1]), axis=0)


def join_lanes(dst, refs, low, high):
    width = high - low
    for i, ref in enumerate(refs):
        dst[:, i * width:(i + 1) * width] = ref[:, low:high]


def core_of():
    t = lax.axis_index("tp")
    return {"tp": t + 1 - 2 * lax.rem(t, 2)}


def pushes(send, recv, core):
    def push(src, dst, slot):
        return pltpu.make_async_remote_copy(
            src_ref=src, dst_ref=dst, send_sem=send.at[slot], recv_sem=recv.at[slot],
            device_id=core, device_id_type=MESH,
        )

    return push


def greet(core):
    barrier = pltpu.get_barrier_semaphore()
    pl.semaphore_signal(barrier, inc=1, device_id=core, device_id_type=MESH)
    pl.semaphore_wait(barrier, 1)


def stack_index(weights):
    return tuple(a[1] if isinstance(a, tuple) else None for a in weights)


def entry(ref, k):
    return ref if k is None else ref.at[k]


def stages(steps):
    starts = [sum(steps[:n]) for n in range(len(steps))]

    def at(n, make):
        return lambda i: make(jnp.clip(i - starts[n], 0, steps[n] - 1))

    return at


ANY = pl.BlockSpec(memory_space=pl.ANY)


class Halves:
    def __init__(self, own_any, got_any, own, got, load, ring):
        self.seq = lax.axis_index("tp") // ring
        self.own, self.got = own, got
        self.copies = [
            pltpu.make_async_copy(own_any.at[self.seq], own, load.at[0]),
            pltpu.make_async_copy(got_any, got, load.at[1]),
        ]

    def rows(self, k, size):
        per = self.own.shape[0] // size
        here = pl.ds(pl.multiple_of(lax.rem(k, per) * size, size), size)
        return jnp.where(k // per == self.seq, self.own[here], self.got[here].astype(F32))


def halves_scratch(rows, d):
    return [pltpu.VMEM((rows // 2, d), F32), pltpu.VMEM((rows // 2, d), BF16), pltpu.SemaphoreType.DMA((2,))]


def project_kernel(w, low, steps, index, bt, ring, gain_ref, scale_ref, *refs):
    weights, refs = refs[:4], refs[4:]
    if ring:
        own_any, got_any, own_ref, other_ref, q_ref, k_ref, v_ref, x_out = refs[:8]
        own, other, qk, vo, load, send, recv, *rest = refs[8:]
        halves = Halves(own_any, got_any, *rest, ring)
    else:
        x_ref, own_ref, other_ref, q_ref, k_ref, v_ref = refs[:6]
        own, other, qk, vo, load, send, recv = refs[6:]
    i = pl.program_id(0)
    rows_steps, half, _ = steps
    ba = q_ref.shape[1]
    core = core_of()
    push = pushes(send, recv, core)

    def loads():
        copies = [pltpu.make_async_copy(entry(weights[s], index[s]), qk.at[s], load.at[s]) for s in range(2)]
        for s in range(2):
            src = entry(weights[2 + s], index[2 + s]).at[:, pl.ds(0, low)]
            copies.append(pltpu.make_async_copy(src, vo.at[s], load.at[2 + s]))
        return copies

    def push_rows(k):
        part = pl.ds(pl.multiple_of(k * bt, bt), bt)
        return push(own.at[part], other.at[part], k)

    @pl.when(i == 0)
    def _():
        if ring:
            for c in halves.copies:
                c.start()
        for c in loads():
            c.start()
        greet(core)
        if ring:
            for c in halves.copies:
                c.wait()

    @pl.when(i < rows_steps)
    def _():
        if ring:
            x = halves.rows(i, bt)
            x_out[...] = x
        else:
            x = x_ref[...]
        h = (x * inverse_rms(x) * gain_ref[...]).astype(BF16)
        own[pl.ds(pl.multiple_of(i * bt, bt), bt)] = h
        own_ref[...] = h
        push_rows(i).start()

    at = i - rows_steps

    @pl.when(at == 0)
    def _():
        for c in loads():
            c.wait()

    @pl.when(at == half)
    def _():
        for k in range(rows_steps):
            push_rows(k).wait()

    def project(h):
        for s in range(2):
            rows = slice(s * w, (s + 1) * w)
            both = dot(qk[s], h, TT)
            q_ref[rows] = (both[:w] * scale_ref[rows]).astype(BF16)
            k_ref[rows] = both[w:].astype(BF16)
            v_ref[rows] = dot(vo[s, :, :w], h, TT).astype(BF16)

    @pl.when((at >= 0) & (at < half))
    def _():
        project(own[pl.ds(pl.multiple_of(at * ba, ba), ba)])

    @pl.when(at >= half)
    def _():
        h = other[pl.ds(pl.multiple_of((at - half) * ba, ba), ba)]
        other_ref[...] = h
        project(h)


def project(x, gain, qk, vo, scale, call, ring=0):
    xs = x if ring else (x,)
    d = xs[0].shape[-1]
    rows = 2 * xs[1].shape[0] if ring else x.shape[0]
    w2 = plain(qk)[0].shape[-1]
    w = w2 // 2
    low = -(-w // 128) * 128
    bt, ba = 256, 512
    half = rows // ba
    steps = (rows // bt, half, half)
    row = pl.BlockSpec((bt, d), lambda i: (jnp.minimum(i, steps[0] - 1), 0))
    wide = pl.BlockSpec((w2, ba), lambda i: (0, jnp.clip(i - steps[0], 0, 2 * half - 1)))
    tall = pl.BlockSpec((ba, d), lambda i: (jnp.clip(i - steps[0] - half, 0, half - 1), 0))
    weights = (*qk, *vo)
    return pl.pallas_call(
        functools.partial(project_kernel, w, low, steps, stack_index(weights), bt, ring),
        grid=(sum(steps),),
        in_specs=[fixed((1, d)), fixed((w2, 1))] + [ANY] * 4 + ([ANY] * 2 if ring else [row]),
        out_specs=[row, tall] + [wide] * 3 + ([row] if ring else []),
        out_shape=[shape_of((rows, d))] * 2 + [shape_of((w2, 2 * rows))] * 3 + ([shape_of((rows, d), F32)] if ring else []),
        scratch_shapes=[
            pltpu.VMEM((rows, d), BF16), pltpu.VMEM((rows, d), BF16),
            pltpu.VMEM((2, d, w2), BF16), pltpu.VMEM((2, d, low), BF16),
            pltpu.SemaphoreType.DMA((4,)), pltpu.SemaphoreType.DMA((steps[0],)), pltpu.SemaphoreType.DMA((steps[0],)),
        ]
        + (halves_scratch(rows, d) if ring else []),
        compiler_params=pltpu.CompilerParams(vmem_limit_bytes=VMEM_LIMIT, collective_id=call, has_side_effects=True),
        cost_estimate=cost(4 * rows * d * 3 * w2, 12 * rows * d),
        name="project",
    )(gain, scale, *plain(weights), *xs)


def middle_kernel(w, low, steps, index, ring, x_ref, gm_ref, att_any, *refs):
    weights, refs = refs[:4], refs[4:]
    mid_ref, pre_ref, res_ref, up_out, down_out, out_out = refs[:6]
    if ring:
        half_out, half = refs[6], refs[-1]
        refs = refs[:6] + refs[7:-1]
    (up_mat, down_mat, out_mat, blocks, vo_side, att, part, got, load, store, send, recv) = refs[6:]
    i = pl.program_id(0)
    far, rows_steps = steps
    bt = x_ref.shape[0]
    ba = part.shape[0] // far
    rows = part.shape[0]
    core = core_of()
    push = pushes(send, recv, core)

    def loads():
        copies = [pltpu.make_async_copy(att_any, att, load.at[0])]
        for s in range(2):
            src = entry(weights[s], index[s]).at[:, pl.ds(low, vo_side.shape[2])]
            copies.append(pltpu.make_async_copy(src, vo_side.at[s], load.at[1 + s]))
        for s in range(2):
            copies.append(pltpu.make_async_copy(entry(weights[2 + s], index[2 + s]), blocks.at[s], load.at[3 + s]))
        return copies

    def stores():
        pairs = [(up_mat, up_out), (down_mat, down_out), (out_mat, out_out)]
        return [pltpu.make_async_copy(src, dst, store.at[n]) for n, (src, dst) in enumerate(pairs)]

    def push_block(s):
        return push(blocks.at[s], blocks.at[2 + s], s)

    def push_part(k):
        here = pl.ds(pl.multiple_of(k * ba, ba), ba)
        return push(part.at[here], got.at[here], 2 + k)

    @pl.when(i == 0)
    def _():
        copies = loads()
        for c in copies:
            c.start()
        greet(core)
        for c in copies[:3]:
            c.wait()
        for s in range(2):
            out_mat[:, s * w:(s + 1) * w] = vo_side[s, :, 2 * w - low - w:2 * w - low]
        for s in range(2):
            copies[3 + s].wait()
            push_block(s).start()

    @pl.when(i < far)
    def _():
        here = pl.ds(pl.multiple_of(i * ba, ba), ba)
        cols = pl.ds(pl.multiple_of(rows + i * ba, ba), ba)
        part[here] = dot(att[:, cols], out_mat[...], TT).astype(BF16)
        push_part(i).start()

    at = i - far

    @pl.when(at == 0)
    def _():
        for s in range(2):
            push_block(s).wait()
        for b in range(4):
            up_mat[:, b * w:(b + 1) * w] = blocks[b, :, 0:w]
            down_mat[:, b * w:(b + 1) * w] = blocks[b, :, w:2 * w]
        for c in stores():
            c.start()

    for k in range(far):
        @pl.when(at == k * (ba // bt))
        def _():
            push_part(k).wait()

    @pl.when(at >= 0)
    def _():
        here = pl.ds(pl.multiple_of(at * bt, bt), bt)
        mid = x_ref[...] + got[here].astype(F32) + dot(att[:, here], out_mat[...], TT)
        mid_ref[...] = mid
        h_m = (mid * inverse_rms(mid) * gm_ref[...]).astype(BF16)
        pre = dot(h_m, up_mat[...])
        pre_ref[...] = pre
        hidden = (pre / (1.0 + jnp.exp(-pre))).astype(BF16)
        res = mid + dot(hidden, down_mat[...], NT)
        res_ref[...] = res
        if ring:
            per = rows_steps // 2

            @pl.when(at // per == 1 - lax.axis_index("tp") // ring)
            def _():
                half[pl.ds(pl.multiple_of(lax.rem(at, per) * bt, bt), bt)] = res.astype(BF16)

    @pl.when(at == rows_steps - 1)
    def _():
        if ring:
            leave = pltpu.make_async_copy(half, half_out, store.at[3])
            leave.start()
            leave.wait()
        for c in stores():
            c.wait()


def middle_call(x, att, gain_m, vo, un, call, ring=0):
    rows, d = x.shape
    w2 = plain(vo)[0].shape[-1]
    w, ff = w2 // 2, 2 * w2
    low = w // 128 * 128
    bt, ba = 256, 512
    steps = (rows // ba, rows // bt)
    row = pl.BlockSpec((bt, d), lambda i: (jnp.maximum(i - steps[0], 0), 0))
    wide = pl.BlockSpec((bt, ff), lambda i: (jnp.maximum(i - steps[0], 0), 0))
    weights = (*vo, *un)
    mats = [(d, ff), (d, ff), (d, w2)]
    slots = 2 + steps[0]
    return pl.pallas_call(
        functools.partial(middle_kernel, w, low, steps, stack_index(weights), ring),
        grid=(sum(steps),),
        in_specs=[row, fixed((1, d))] + [ANY] * 5,
        out_specs=[row, wide, row] + [ANY] * (4 if ring else 3),
        out_shape=[shape_of((rows, d), F32), shape_of((rows, ff), F32), shape_of((rows, d), F32)] + [shape_of(m) for m in mats]
        + ([shape_of((rows // 2, d))] if ring else []),
        scratch_shapes=[pltpu.VMEM(m, BF16) for m in mats]
        + [pltpu.VMEM((4, d, w2), BF16), pltpu.VMEM((2, d, w2 - low), BF16), pltpu.VMEM(att.shape, BF16)]
        + [pltpu.VMEM((rows, d), BF16)] * 2
        + [pltpu.SemaphoreType.DMA((5,)), pltpu.SemaphoreType.DMA((4,)), pltpu.SemaphoreType.DMA((slots,)), pltpu.SemaphoreType.DMA((slots,))]
        + ([pltpu.VMEM((rows // 2, d), BF16)] if ring else []),
        compiler_params=pltpu.CompilerParams(vmem_limit_bytes=VMEM_LIMIT, collective_id=call, has_side_effects=True),
        cost_estimate=cost(2 * rows * d * (2 * w2 + 2 * ff), 30 * rows * d),
        name="middle",
    )(x, gain_m, att, *plain(weights))


def mlp_back_kernel(w, steps, ring, mid_ref, pre_ref, gm_ref, att_any, *refs):
    mats, refs = refs[:3], refs[3:]
    if ring:
        own_any, got_any, refs = refs[0], refs[1], refs[2:]
        halves = Halves(own_any, got_any, *refs[-3:], ring)
        refs = refs[:-3]
    else:
        g_ref, refs = refs[0], refs[1:]
    g_mid_ref, gain_ref, g_att_ref, o0, o1 = refs[:5]
    (up_mat, down_mat, out_mat, g_all, hid_all, hm_all, gpre_all, low_own, low_other, blocks, got, att,
     load, send, recv) = refs[5:]
    i = pl.program_id(0)
    rows_steps, grad_steps, att_steps, _ = steps
    bt, bd, ba = mid_ref.shape[0], o0.shape[0], g_att_ref.shape[1]
    core = core_of()
    push = pushes(send, recv, core)

    def loads():
        pairs = (*zip(mats, (up_mat, down_mat, out_mat)), (att_any, att))
        return [pltpu.make_async_copy(src, dst, load.at[n]) for n, (src, dst) in enumerate(pairs)]

    def push_rows(k):
        part = pl.ds(pl.multiple_of(k * bt, bt), bt)
        return push(low_own.at[part], low_other.at[part], k)

    def push_block(c, s):
        part = pl.ds(pl.multiple_of(c * bd, bd), bd)
        return push(blocks.at[2 + s, part], got.at[s, part], rows_steps + 2 * c + s)

    @pl.when(i == 0)
    def _():
        copies = loads()
        for c in copies:
            c.start()
        gain_ref[...] = jnp.zeros_like(gain_ref)
        if ring:
            for c in halves.copies:
                c.start()
        greet(core)
        for c in copies[:2] + (halves.copies if ring else []):
            c.wait()

    @pl.when(i < rows_steps)
    def _():
        here = pl.ds(pl.multiple_of(i * bt, bt), bt)
        g = halves.rows(i, bt) if ring else g_ref[...]
        g_low = g.astype(BF16)
        g_all[here] = g_low
        pre = pre_ref[...]
        sig = 1.0 / (1.0 + jnp.exp(-pre))
        hid_all[here] = (pre * sig).astype(BF16)
        g_hidden = dot(g_low, down_mat[...])
        g_pre = (g_hidden * sig * (1.0 + pre * (1.0 - sig))).astype(BF16)
        gpre_all[here] = g_pre
        mid = mid_ref[...]
        inv = inverse_rms(mid)
        normed = mid * inv
        gain = gm_ref[...]
        hm_all[here] = (normed * gain).astype(BF16)
        g_hm = dot(g_pre, up_mat[...], NT)
        gain_ref[...] += eight(g_hm * normed)
        scaled = g_hm * gain
        g_mid = g + inv * (scaled - normed * jnp.mean(scaled * normed, axis=-1, keepdims=True))
        g_mid_ref[...] = g_mid
        low_own[here] = g_mid.astype(BF16)
        push_rows(i).start()

    at = i - rows_steps

    @pl.when((at >= 0) & (at < grad_steps))
    def _():
        cols = pl.ds(pl.multiple_of(at * bd, bd), bd)
        up = dot(hm_all[:, cols], gpre_all[...], TN).astype(BF16)
        down = dot(g_all[:, cols], hid_all[...], TN).astype(BF16)
        for b in range(4):
            blocks[b, cols, 0:w] = up[:, b * w:(b + 1) * w]
            blocks[b, cols, w:2 * w] = down[:, b * w:(b + 1) * w]
        for s in range(2):
            push_block(at, s).start()

    to = at - grad_steps

    @pl.when(to == 0)
    def _():
        loads()[2].wait()

    half = att_steps // 2

    @pl.when((to >= 0) & (to < half))
    def _():
        here = pl.ds(pl.multiple_of(to * ba, ba), ba)
        g_att_ref[...] = dot(out_mat[...], low_own[here], TT).astype(BF16)

    @pl.when(to == half)
    def _():
        for k in range(rows_steps):
            push_rows(k).wait()

    @pl.when((to >= half) & (to < att_steps))
    def _():
        here = pl.ds(pl.multiple_of((to - half) * ba, ba), ba)
        g_att_ref[...] = dot(out_mat[...], low_other[here], TT).astype(BF16)

    last = to - att_steps

    @pl.when(last == 0)
    def _():
        loads()[3].wait()

    @pl.when(last >= 0)
    def _():
        cols = pl.ds(pl.multiple_of(last * bd, bd), bd)
        rows = low_own.shape[0]
        grad = dot(low_own[:, cols], att[:, :rows], TT) + dot(low_other[:, cols], att[:, rows:], TT)
        grad = grad.astype(BF16)
        for s, out in enumerate((o0, o1)):
            push_block(last, s).wait()
            out[:, :2 * w] = (blocks[s, cols].astype(F32) + got[s, cols].astype(F32)).astype(BF16)
            out[:, 2 * w:3 * w] = grad[:, s * w:(s + 1) * w]
            out[:, 3 * w:] = jnp.zeros((bd, out.shape[1] - 3 * w), BF16)


def mlp_back(g, mid, pre, gain, att, mats, width, call, ring=0):
    rows, d = mid.shape
    gs = g if ring else (g,)
    ff = pre.shape[1]
    w2 = att.shape[0]
    w = w2 // 2
    bt, bd, ba = 256, 256, 512
    steps = (rows // bt, d // bd, 2 * rows // ba, d // bd)
    at = stages(steps)
    row = pl.BlockSpec((bt, d), at(0, lambda k: (k, 0)))
    wide = pl.BlockSpec((bt, ff), at(0, lambda k: (k, 0)))
    block = pl.BlockSpec((bd, width), at(3, lambda k: (k, 0)))
    slots = steps[0] + 2 * steps[1]
    return pl.pallas_call(
        functools.partial(mlp_back_kernel, w, steps, ring),
        grid=(sum(steps),),
        in_specs=[row, wide, fixed((1, d))] + [ANY] * 4 + ([ANY] * 2 if ring else [row]),
        out_specs=[row, fixed((8, d)), pl.BlockSpec((w2, ba), at(2, lambda k: (0, k))), block, block],
        out_shape=[shape_of((rows, d), F32), shape_of((8, d), F32), shape_of((w2, 2 * rows))] + [shape_of((d, width))] * 2,
        scratch_shapes=[pltpu.VMEM((d, ff), BF16)] * 2
        + [pltpu.VMEM((d, w2), BF16)]
        + [pltpu.VMEM((rows, d), BF16), pltpu.VMEM((rows, ff), BF16)] * 2
        + [pltpu.VMEM((rows, d), BF16)] * 2
        + [pltpu.VMEM((4, d, w2), BF16), pltpu.VMEM((2, d, w2), BF16)]
        + [pltpu.VMEM(att.shape, BF16)]
        + [pltpu.SemaphoreType.DMA((4,)), pltpu.SemaphoreType.DMA((slots,)), pltpu.SemaphoreType.DMA((slots,))]
        + (halves_scratch(rows, d) if ring else []),
        compiler_params=pltpu.CompilerParams(vmem_limit_bytes=62 * 2**20, collective_id=call, has_side_effects=True),
        cost_estimate=cost(8 * rows * d * ff + 8 * rows * d * w2, 40 * rows * d),
        name="mlp_back",
    )(mid, pre, gain, att, *mats, *gs)


def weight_grad_kernel(w, own_ref, other_ref, dq_ref, dk_ref, dv_ref, *refs):
    out, stacked = refs[-2:]
    half = own_ref.shape[0]

    @pl.when(pl.program_id(0) == 0)
    def _():
        for j, ref in enumerate((dq_ref, dk_ref, dv_ref)):
            stacked[j * w:(j + 1) * w, :] = ref[...]

    grad = dot(own_ref[...], stacked[:, :half], TT) + dot(other_ref[...], stacked[:, half:], TT)
    if len(refs) == 3:
        grad = grad + refs[0][:, :3 * w].astype(F32)
    out[:, :3 * w] = grad.astype(BF16)
    out[:, 3 * w:] = jnp.zeros((out.shape[0], out.shape[1] - 3 * w), BF16)


def weight_grad(own, other, dq, dk, dv, width, got=None):
    rows, d = own.shape
    w = dq.shape[0]
    bd = 256
    col = pl.BlockSpec((rows, bd), lambda i: (0, i))
    flat = pl.BlockSpec((bd, width), lambda i: (i, 0))
    extra = [] if got is None else [got]
    return pl.pallas_call(
        functools.partial(weight_grad_kernel, w),
        grid=(d // bd,),
        in_specs=[col, col] + [fixed(dq.shape)] * 3 + [flat] * len(extra),
        out_specs=flat,
        out_shape=shape_of((d, width)),
        scratch_shapes=[pltpu.VMEM((3 * w, 2 * rows), BF16)],
        compiler_params=params(),
        cost_estimate=cost(12 * rows * d * w, 12 * rows * d),
        name="weight_grad",
    )(own, other, dq, dk, dv, *extra)


def input_back_kernel(w, low, steps, index, x_ref, g_ref, gain_ref, *refs):
    grads, weights, refs = refs[:6], refs[6:10], refs[10:]
    stacked, qk, vo, part, got, load, send, recv = refs[-8:]
    i = pl.program_id(0)
    chunk_steps, far, _ = steps
    if chunk_steps:
        own_ref, other_ref, out_ref, sum_ref, piece_ref = refs[:-8]
    else:
        out_ref, sum_ref = refs[:-8]
    bt, half = x_ref.shape[0], part.shape[0]
    ba = half // far
    push = pushes(send, recv, core_of())

    def loads():
        copies = [
            pltpu.make_async_copy(grads[n], stacked.at[n // 3, pl.ds(n % 3 * w, w)], load.at[n]) for n in range(6)
        ]
        for s in range(2):
            copies.append(pltpu.make_async_copy(entry(weights[s], index[s]), qk.at[s], load.at[6 + s]))
        for s in range(2):
            src = entry(weights[2 + s], index[2 + s]).at[:, pl.ds(0, low)]
            copies.append(pltpu.make_async_copy(src, vo.at[s], load.at[8 + s]))
        return copies

    def push_part(k):
        here = pl.ds(pl.multiple_of(k * ba, ba), ba)
        return push(part.at[here], got.at[here], k)

    def total(cols):
        parts = [
            dot(stacked[s, :2 * w, cols], qk[s], TT) + dot(stacked[s, 2 * w:, cols], vo[s, :, :w], TT) for s in range(2)
        ]
        return parts[0] + parts[1]

    @pl.when(i == 0)
    def _():
        copies = loads()
        for c in copies:
            c.start()
        sum_ref[...] = jnp.zeros_like(sum_ref)
        greet(core_of())
        for c in copies[:3]:
            c.wait()

    if chunk_steps:
        @pl.when(i < chunk_steps)
        def _():
            grad = dot(own_ref[...], stacked[0, :, :half], TT) + dot(other_ref[...], stacked[0, :, half:], TT)
            piece_ref[:, :3 * w] = grad.astype(BF16)
            piece_ref[:, 3 * w:] = jnp.zeros((piece_ref.shape[0], piece_ref.shape[1] - 3 * w), BF16)

    to = i - chunk_steps

    @pl.when(to == 0)
    def _():
        for c in loads()[3:]:
            c.wait()

    @pl.when((to >= 0) & (to < far))
    def _():
        cols = pl.ds(pl.multiple_of(half + to * ba, ba), ba)
        part[pl.ds(pl.multiple_of(to * ba, ba), ba)] = total(cols).astype(BF16)
        push_part(to).start()

    at = to - far
    for k in range(far):
        @pl.when(at == k * (ba // bt))
        def _():
            push_part(k).wait()

    @pl.when(at >= 0)
    def _():
        here = pl.ds(pl.multiple_of(at * bt, bt), bt)
        g_ha = total(here) + got[here].astype(F32)
        x = x_ref[...]
        inv = inverse_rms(x)
        normed = x * inv
        sum_ref[...] += eight(g_ha * normed)
        scaled = g_ha * gain_ref[...]
        out_ref[...] = g_ref[...] + inv * (scaled - normed * jnp.mean(scaled * normed, axis=-1, keepdims=True))


def input_back(grads, x, g, gain, qk, vo, call, normed=(), width=0):
    w, length = grads[0].shape
    rows, d = x.shape
    low = -(-w // 128) * 128
    bt, bd, ba = 256, 256, 512
    chunks = d // bd if normed else 0
    steps = (chunks, rows // ba, rows // bt)
    row = pl.BlockSpec((bt, d), lambda i: (jnp.maximum(i - steps[0] - steps[1], 0), 0))

    def chunk(k):
        return jnp.minimum(k, chunks - 1)

    weights = (*qk, *vo)
    in_specs = [row, row, fixed((1, d))] + [ANY] * 10
    out_specs, out_shape = [row, fixed((8, d))], [shape_of((rows, d), F32), shape_of((8, d), F32)]
    if normed:
        in_specs += [pl.BlockSpec((rows, bd), lambda i: (0, chunk(i)))] * 2
        out_specs.append(pl.BlockSpec((bd, width), lambda i: (chunk(i), 0)))
        out_shape.append(shape_of((d, width)))
    return pl.pallas_call(
        functools.partial(input_back_kernel, w, low, steps, stack_index(weights)),
        grid=(sum(steps),),
        in_specs=in_specs,
        out_specs=out_specs,
        out_shape=out_shape,
        scratch_shapes=[
            pltpu.VMEM((2, 3 * w, length), BF16), pltpu.VMEM((2, d, 2 * w), BF16), pltpu.VMEM((2, d, low), BF16),
            pltpu.VMEM((rows, d), BF16), pltpu.VMEM((rows, d), BF16),
            pltpu.SemaphoreType.DMA((10,)), pltpu.SemaphoreType.DMA((steps[1],)), pltpu.SemaphoreType.DMA((steps[1],)),
        ],
        compiler_params=pltpu.CompilerParams(vmem_limit_bytes=VMEM_LIMIT, collective_id=call, has_side_effects=True),
        cost_estimate=cost(9 * rows * d * 4 * w, 24 * rows * d),
        name="input_back",
    )(x, g, gain, *grads, *plain(weights), *normed)


def finish_kernel(w, low, far, own_steps, outer, ring, index, gain_ref, small_ref, x_any, g_any, piece_any, came_any, *refs):
    grads, weights, refs = refs[:6], refs[6:10], refs[10:]
    own_any, got_any, late_ref, sums_ref = refs[:4]
    (stacked, qk, vo, part, got, xs, gs, send_half, keep, away, came, near, hops, gain_sum, vec, vecs,
     load, store, send, recv) = refs[4:]
    i = pl.program_id(0)
    half = part.shape[0]
    ba, bt = half // far, half // own_steps
    f, t = lax.axis_index("fsdp"), lax.axis_index("tp")
    zz, yy, seq = f // 2, lax.rem(f, 2), t // ring
    across = {"tp": lax.rem(t + ring, 2 * ring)}
    beside = {"fsdp": zz * 2 + 1 - yy}
    along = [{"fsdp": lax.rem(zz + k, outer) * 2 + yy} for k in range(1, outer)]
    core = core_of()
    chunk = keep.shape[1]
    sends = far + outer + outer - 1
    pushed = own_steps // 2

    def push(src, dst, slot, peer):
        return pltpu.make_async_remote_copy(
            src_ref=src, dst_ref=dst, send_sem=send.at[slot], recv_sem=recv.at[slot],
            device_id=peer, device_id_type=MESH,
        )

    def rows_of(j, side):
        z = lax.rem(zz + 1 + j, outer)
        return pl.ds(pl.multiple_of((z * 2 + side) * chunk, chunk), chunk)

    def loads():
        def columns(first):
            cols = pl.ds(first, half)
            return [(grads[n].at[:, cols], stacked.at[n // 3, pl.ds(n % 3 * w, w), cols]) for n in range(6)]

        pairs = columns(half)
        pairs += [(entry(weights[s], index[s]), qk.at[s]) for s in range(2)]
        pairs += [(entry(weights[2 + s], index[2 + s]).at[:, pl.ds(0, low)], vo.at[s]) for s in range(2)]
        pairs += columns(0)
        pairs += [(x_any, xs), (g_any, gs)]
        for j in range(outer):
            for n, (side, dst) in enumerate(((1 - yy, away), (yy, keep))):
                pairs += [(piece_any.at[rows_of(j, side)], dst.at[j]), (came_any.at[rows_of(j, side)], came.at[n, j])]
        return [pltpu.make_async_copy(src, dst, load.at[n]) for n, (src, dst) in enumerate(pairs)]

    def chunk_of(k):
        return 1 - seq if k == 0 else seq

    def push_part(k):
        here = pl.ds(pl.multiple_of(chunk_of(k) * ba, ba), ba)
        return push(part.at[here], got.at[here], k, core)

    def push_near(j):
        return push(away.at[j], near.at[j], far + j, beside)

    def push_hop(j):
        return push(keep.at[j], hops.at[j], far + outer + j, along[j])

    def push_half(k):
        here = pl.ds(pl.multiple_of(k * bt, bt), bt)
        return push(send_half.at[here], got_any.at[here], sends + k, across)

    def push_small(n):
        peer = ([core, across, beside] + along)[n]
        return push(vec.at[min(n, 3)], vecs.at[n], sends + pushed + n, peer)

    def total(cols):
        parts = [
            dot(stacked[s, :2 * w, cols], qk[s], TT) + dot(stacked[s, 2 * w:, cols], vo[s, :, :w], TT) for s in range(2)
        ]
        return parts[0] + parts[1]

    @pl.when(i == 0)
    def _():
        copies = loads()
        for c in copies[18:] + copies[:10]:
            c.start()
        gain_sum[...] = jnp.zeros_like(gain_sum)
        barrier = pltpu.get_barrier_semaphore()
        peers = [core, across, beside] + along
        for peer in peers:
            pl.semaphore_signal(barrier, inc=1, device_id=peer, device_id_type=MESH)
        pl.semaphore_wait(barrier, len(peers))
        for c in copies[18:]:
            c.wait()
        for j in range(outer):
            away[j] = (away[j].astype(F32) + came[0, j].astype(F32)).astype(BF16)
            push_near(j).start()
        for c in copies[:10]:
            c.wait()
        for c in copies[10:18]:
            c.start()

    run = 1 + pushed
    for k in range(far):
        @pl.when(i == k * run)
        def _():
            cols = pl.ds(pl.multiple_of(half + chunk_of(k) * ba, ba), ba)
            part[pl.ds(pl.multiple_of(chunk_of(k) * ba, ba), ba)] = total(cols).astype(BF16)
            push_part(k).start()

    place_in_run = lax.rem(i, run)
    at = jnp.where(place_in_run == 0, -1, i // run * pushed + place_in_run - 1)
    at = jnp.where(i == far + own_steps, own_steps, at)

    @pl.when(at == 0)
    def _():
        for c in loads()[10:18]:
            c.wait()

    for k in range(far):
        @pl.when(at == k * pushed)
        def _():
            push_part(k).wait()

    for j in range(outer - 1):
        @pl.when(at == j + 1)
        def _():
            push_near(j).wait_recv()
            keep[j] = (keep[j].astype(F32) + came[1, j].astype(F32) + near[j].astype(F32)).astype(BF16)
            push_hop(j).start()

    @pl.when((at >= 0) & (at < own_steps))
    def _():
        place = lax.rem(at + pushed * (1 - seq), own_steps)
        here = pl.ds(pl.multiple_of(place * bt, bt), bt)
        g_ha = total(here) + got[here].astype(F32)
        x = xs[here]
        inv = inverse_rms(x)
        normed = x * inv
        gain_sum[...] += eight(g_ha * normed)
        scaled = g_ha * gain_ref[...]
        gs[here] = gs[here] + inv * (scaled - normed * jnp.mean(scaled * normed, axis=-1, keepdims=True))

    @pl.when((at >= 0) & (at < pushed))
    def _():
        place = at + pushed * (1 - seq)
        send_half[pl.ds(pl.multiple_of(at * bt, bt), bt)] = gs[pl.ds(pl.multiple_of(place * bt, bt), bt)].astype(BF16)
        push_half(at).start()

    @pl.when(at == own_steps)
    def _():
        size = half // 2
        mine = pl.ds(pl.multiple_of(seq * size, size), size)
        out_own = pltpu.make_async_copy(gs.at[mine], own_any, store.at[0])
        out_own.start()
        first = lax.broadcasted_iota(jnp.int32, vec.shape[1:], 0) == 0
        vec[0] = small_ref[...] + jnp.where(first, jnp.sum(gain_sum[...], axis=0, keepdims=True), 0.0)
        for n in range(3):
            push_small(n).start()
            push_small(n).wait()
            vec[n + 1] = vec[n] + vecs[n]
        for n in range(3, 2 + outer):
            push_small(n).start()
        for n in range(3, 2 + outer):
            push_small(n).wait()
        sums = vec[3]
        for n in range(3, 2 + outer):
            sums = sums + vecs[n]
        sums_ref[...] = sums
        push_near(outer - 1).wait_recv()
        late = keep[outer - 1].astype(F32) + came[1, outer - 1].astype(F32) + near[outer - 1].astype(F32)
        for j in range(outer - 1):
            push_hop(j).wait()
            late = late + hops[j].astype(F32)
        late_ref[...] = late
        for j in range(outer):
            push_near(j).wait_send()
        for k in range(pushed):
            push_half(k).wait()
        out_own.wait()


def finish(grads, x, g, gain, small, piece, came, qk, vo, fsdp, ring, call):
    w, length = grads[0].shape
    rows, d = x.shape
    width = piece.shape[1]
    low = -(-w // 128) * 128
    outer, chunk = fsdp // 2, piece.shape[0] // fsdp
    far, own_steps = rows // 512, rows // 256
    weights = (*qk, *vo)
    slots = far + 2 * outer - 1 + own_steps // 2 + 2 + outer
    dma = pltpu.SemaphoreType.DMA
    return pl.pallas_call(
        functools.partial(finish_kernel, w, low, far, own_steps, outer, ring, stack_index(weights)),
        grid=(far + own_steps + 1,),
        in_specs=[fixed((1, d)), fixed(small.shape)] + [ANY] * 14,
        out_specs=[ANY, ANY, fixed((chunk, width)), fixed(small.shape)],
        out_shape=[shape_of((rows // 2, d), F32), shape_of((rows // 2, d)), shape_of((chunk, width), F32), shape_of(small.shape, F32)],
        scratch_shapes=[
            pltpu.VMEM((2, 3 * w, length), BF16), pltpu.VMEM((2, d, 2 * w), BF16), pltpu.VMEM((2, d, low), BF16),
            pltpu.VMEM((rows, d), BF16), pltpu.VMEM((rows, d), BF16),
            pltpu.VMEM((rows, d), F32), pltpu.VMEM((rows, d), F32),
            pltpu.VMEM((rows // 2, d), BF16),
            pltpu.VMEM((outer, chunk, width), BF16), pltpu.VMEM((outer, chunk, width), BF16),
            pltpu.VMEM((2, outer, chunk, width), BF16), pltpu.VMEM((outer, chunk, width), BF16),
            pltpu.VMEM((outer - 1, chunk, width), BF16),
            pltpu.VMEM((8, d), F32), pltpu.VMEM((4,) + small.shape, F32), pltpu.VMEM((2 + outer,) + small.shape, F32),
            dma((18 + 4 * outer,)), dma((1,)), dma((slots,)), dma((slots,)),
        ],
        compiler_params=pltpu.CompilerParams(vmem_limit_bytes=VMEM_LIMIT, collective_id=call, has_side_effects=True),
        cost_estimate=cost(6 * rows * d * 4 * w, 24 * rows * d),
        name="finish",
    )(gain, small, x, g, piece, came, *grads, *plain(weights))


def total_over_all(plan, a):
    n, f = plan.tp, plan.fsdp
    hop = 1
    while hop < n:
        a = a + lax.ppermute(a, "tp", [(t, t ^ hop) for t in range(n)])
        hop *= 2
    hop = 1
    while hop < f:
        a = a + lax.ppermute(a, "fsdp", [(t, t ^ hop) for t in range(f)])
        hop *= 2
    return a


def add_low(own, got):
    return (own.astype(F32) + got.astype(F32)).astype(BF16)


def scatter_rows(mine):
    return lax.psum_scatter(mine, "fsdp", scatter_dimension=0, tiled=True)


def after(*arrays):
    return lax.optimization_barrier(arrays)


def fast_body(plan, inputs, cotangent, w_qkv, w_out, w_up, w_down, norm_gain, query_scale, prefix_len):
    seqs, positions, d = inputs.shape
    layers, w = w_qkv.shape[0], w_qkv.shape[3]
    dh = query_scale.shape[1]
    unit = SOFT_ONE / math.sqrt(dh)
    factors = jax.nn.softplus(query_scale) * unit
    prefix = lax.dynamic_slice_in_dim(prefix_len, plan.seq, 1)
    order = plan.blocks(positions * plan.tp)
    out_shard, down_shard = jnp.swapaxes(w_out, 1, 2), jnp.swapaxes(w_down, 1, 2)
    pairs = jnp.concatenate(
        [
            jnp.concatenate([w_qkv[:, 0], w_qkv[:, 1]], axis=2)[:, None],
            jnp.concatenate([w_qkv[:, 2], out_shard], axis=2)[:, None],
            jnp.concatenate([w_up, down_shard], axis=2)[:, None],
        ],
        axis=1,
    )

    got, other = gather_call(pairs[0, :2], inputs, pieces_of(2, pairs.shape[2]), plan.fsdp, plan.ring)
    qk0, vo0 = got[0:2], got[2:4]

    def along(l, m):
        return lax.all_gather(pairs[l, m], "fsdp", axis=0, tiled=True)

    def both(rows):
        return rows, plan.across(rows)

    def stacked(rows):
        return (rows, 0), (rows, 1)

    un0_rows, qk1_rows = along(0, 2), along(1, 0)
    other, un0_rows, shards = after(other, un0_rows, pairs[1, 1:])
    shards_got, un0 = plan.across(shards), both(un0_rows)
    kept, weights = [], []
    for l in range(layers):
        qk, vo = (qk0, vo0) if l == 0 else (qk1, vo1)
        scale = jnp.tile(factors[l] * LOG2E, 2 * w // dh)[:, None]
        gain = norm_gain[l, 0][None]
        if l == 0:
            h, h_other, q, k, v, x = project((inputs, other), gain, qk, vo, scale, 3, plan.ring)
        else:
            h, h_other, q, k, v = project(x, gain, qk, vo, scale, 3 + l)
        if l == 0:
            q, shards_got, qk1_rows = after(q, shards_got, qk1_rows)
            shards = jnp.stack([shards, shards_got], axis=1)
            vo1_rows, un1_rows = (lax.all_gather(shards[m], "fsdp", axis=1, tiled=True) for m in range(2))
            qk1 = both(qk1_rows)
        att, lse = attention_forward(q, k, v, prefix, order, dh)
        if l == 0:
            att, un0_got = after(att, un0[1])
            un = un0[0], un0_got
        else:
            att, un1_rows, cot_got = after(att, un1_rows, cot_got)
            un = stacked(un1_rows)
        last = plan.ring if l == layers - 1 else 0
        mid, pre, res, *mats = middle_call(x, att, norm_gain[l, 1][None], vo, un, 5 + l, last)
        if last:
            *mats, out_send = mats
        if l == 0:
            res, cotangent = after(res, cotangent)
            cot_block = plan.pick(cotangent, 1 - plan.seq).astype(BF16)
            res, qk1_got, vo1_rows, cot_block = after(res, qk1[1], vo1_rows, cot_block)
            qk1, vo1 = (qk1[0], qk1_got), stacked(vo1_rows)
            cot_got = plan.across(cot_block)
        kept.append((x, h, h_other, q, k, v, att, lse, mid, pre))
        weights.append((qk, vo, mats))
        x = res
    g = cotangent, cot_got
    out_blocks = x.reshape(seqs, positions, d)
    cot_got, out_send = after(cot_got, out_send)
    g = cotangent, cot_got
    out_got = plan.across(out_send)
    outputs = None
    width = -(-3 * w // 128) * 128
    grads = [None] * layers
    for l in reversed(range(layers)):
        qk, vo, mats = weights[l]
        x, h, h_other, q, k, v, att, lse, mid, pre = kept[l]
        ring = plan.ring if l == layers - 1 else 0
        g_mid, gain_m, g_att, *early = mlp_back(g, mid, pre, norm_gain[l, 1][None], att, mats, width, 1 + l, ring)
        if l > 0:
            early = [scatter_rows(a) for a in early]
        else:
            early_got = plan.across(early[1])
        if l + 1 < layers:
            g_att, grads[l + 1][0][1] = after(g_att, grads[l + 1][0][1])
        dgrads, fgs, pieces = [None] * 6, [], [None] * 2
        for s in (1, 0):
            dq, dk, dv, fg = attention_backward(
                q, k, v, att, g_att, lse, factors[l], prefix, order, dh, s * w, w
            )
            if s == 1:
                pieces[1] = weight_grad(h, h_other, dq, dk, dv, width)
                if l > 0:
                    pieces[1], out_got = after(pieces[1], out_got)
                    g_att, pieces[1] = after(g_att, pieces[1])
                else:
                    g_att, pieces[1], out_got = after(g_att, pieces[1], out_got)
                    outputs = plan.order(plan.pick(out_blocks, plan.seq), out_got.astype(F32)).reshape(out_blocks.shape)
                    pieces[1], early_got, outputs = after(pieces[1], early_got, outputs)
                late_got = plan.across(pieces[1])
                if l + 1 < layers:
                    g_att, grads[l + 1][1] = after(g_att, grads[l + 1][1])
                if l == 0:
                    g_att, early_got = after(g_att, early_got)
                    mine, g_att = after(add_low(early[0], early_got), g_att)
                    early = scatter_rows(mine)
            elif l > 0:
                dq, early[0] = after(dq, early[0])
            dgrads[3 * s:3 * s + 3] = [dq, dk, dv]
            fgs.append(fg)
        fg = fgs[0] + fgs[1]
        if l > 0:
            g, gain_a, pieces[0] = input_back(
                dgrads, x, g_mid, norm_gain[l, 0][None], qk, vo, 7 + l, (h, h_other), width
            )
            pieces[0], late_got = after(pieces[0], late_got)
            mine, g = after(add_low(pieces[0], late_got), g)
        else:
            pieces[0] = weight_grad(h, h_other, *dgrads[:3], width)
        row = lambda a: jnp.pad(a, (0, d - a.shape[0]))[None]
        small = [row(jnp.sum(gain_m, axis=0)), row(jnp.sum(fg, axis=1) / (factors[l] * LOG2E))]
        if l > 0:
            late = scatter_rows(mine)
            small.append(row(jnp.sum(gain_a, axis=0)))
            grads[l] = [early, late, small]
    upper = grads[1][2]
    zero = jnp.zeros((1, d), F32)
    small = jnp.concatenate([zero, upper[2], small[0], upper[0], small[1], upper[1], zero, zero])
    own_half, got_half, late, small = finish(
        dgrads, x, g_mid, norm_gain[0, 0][None], small, pieces[0], late_got, qk, vo, plan.fsdp, plan.ring, 9
    )
    grads[0] = [early, late, small]
    input_grad = plan.order(own_half, got_half.astype(F32)).reshape(out_blocks.shape)
    early = []
    for entry, _, _ in grads:
        if isinstance(entry, list):
            early.append(entry[0].astype(F32) + plan.across(entry[1]).astype(F32))
        else:
            early.append(entry.astype(F32))
    early = jnp.stack(early)
    late = jnp.stack([entry[1].astype(F32) for entry in grads])
    qkv_g = jnp.stack([late[:, :, c * w:(c + 1) * w] for c in range(3)], axis=1)
    up_g, down_g, out_g = (early[:, :, c * w:(c + 1) * w] for c in range(3))
    scale_g = small[4:6, :dh] * jax.nn.sigmoid(query_scale) * unit
    return (
        outputs, input_grad, qkv_g, jnp.swapaxes(out_g, 1, 2), up_g, jnp.swapaxes(down_g, 1, 2),
        small[:2], small[2:4], scale_g,
    )


def body(inputs, cotangent, w_qkv, w_out, w_up, w_down, norm_gain, query_scale, prefix_len):
    seqs, positions, d = inputs.shape
    fsdp, tp = lax.axis_size("fsdp"), lax.axis_size("tp")
    layers = w_qkv.shape[0]
    plan = Plan(seqs, tp, fsdp, w_qkv.shape[2])
    if plan.fast:
        return fast_body(
            plan, inputs, cotangent, w_qkv, w_out, w_up, w_down, norm_gain, query_scale, prefix_len
        )
    dh = query_scale.shape[1]
    unit = SOFT_ONE / math.sqrt(dh)
    factors = jax.nn.softplus(query_scale) * unit
    prefix = lax.dynamic_slice_in_dim(prefix_len, plan.seq, 1)
    order = plan.blocks(positions * tp)
    out_shard, down_shard = jnp.swapaxes(w_out, 1, 2), jnp.swapaxes(w_down, 1, 2)

    weights = []
    for l in range(layers):
        qkv = plan.gather_heads(w_qkv[l])
        out_t = plan.gather_heads(out_shard[l][None])[:, 0]
        up, down_t = plan.gather_full(jnp.stack([w_up[l], down_shard[l]]))
        weights.append(([qkv[:, c] for c in range(3)], out_t, up, down_t))

    x = plan.swap(inputs)
    g = plan.swap(cotangent)
    kept = []
    for l in range(layers):
        x, saved = layer_forward(plan, x, prefix, order, *weights[l], norm_gain[l], factors[l])
        kept.append(saved)
    outputs = plan.unswap(x)
    grads = [None] * layers
    for l in reversed(range(layers)):
        g, grads[l] = layer_backward(
            plan, g, kept[l], prefix, order, *weights[l], norm_gain[l], factors[l]
        )
    input_grad = plan.unswap(g)
    qkv_g, out_g, up_g, down_g, gain_a, gain_m, f_g = (jnp.stack(a) for a in zip(*grads))
    scale_g = f_g * jax.nn.sigmoid(query_scale) * unit
    gain_a, gain_m, scale_g = lax.psum((gain_a, gain_m, scale_g), ("fsdp", "tp"))
    return outputs, input_grad, qkv_g, out_g, up_g, down_g, gain_a, gain_m, scale_g


def solution(mesh):
    placed = (
        P("fsdp", "tp", None),
        P("fsdp", "tp", None),
        P(None, None, "fsdp", "tp"),
        P(None, "tp", "fsdp"),
        P(None, "fsdp", "tp"),
        P(None, "tp", "fsdp"),
        P(),
        P(),
        P("fsdp"),
    )
    return jax.shard_map(
        body,
        mesh=mesh,
        in_specs=placed,
        out_specs=placed[:6] + (P(), P(), P()),
        check_vma=False,
    )
```

```python
import functools, math
import jax
import jax.numpy as jnp
from jax import lax
from jax.experimental import pallas as pl
from jax.experimental.pallas import tpu as pltpu
from jax.sharding import PartitionSpec as P

MASKED = -1e30
F32, BF16 = jnp.float32, jnp.bfloat16
EPSILON = 1e-06
SOFT_ONE = 1.442695041
LOG2E = math.log2(math.e)
MESH = pl.DeviceIdType.MESH
HINT = 1
VMEM_LIMIT = 60 * 2**20

def dot(a, b, dims=((1,), (0,))):
    return lax.dot_general(a, b, (dims, ((), ())), preferred_element_type=F32)

def key_range(row_start, rows, prefix, block):
    full = jnp.maximum(row_start + 1, prefix) // block
    stop = (jnp.maximum(row_start + rows, prefix) + block - 1) // block
    return full, stop

def forward_kernel(prefix_ref, order_ref, q_ref, k_ref, v_ref, o_ref, lse_ref, key_rows, value_ext, *, pair, dh, bq, bk):
    length = q_ref.shape[1]
    prefix = prefix_ref[0]
    ext = value_ext.shape[1]
    bound = 0.0
    for h in range(pair):
        rows = slice(h * dh, (h + 1) * dh)
        q, k = q_ref[rows, :].astype(F32), k_ref[rows, :].astype(F32)
        bound = jnp.maximum(bound, jnp.max(jnp.sum(q * q, axis=0)) * jnp.max(jnp.sum(k * k, axis=0)))
        key_rows[h] = k_ref[rows, :].T
        value_ext[h, :dh] = v_ref[rows, :]
        value_ext[h, dh:] = jnp.ones((ext - dh, length), BF16)

    def one_query(shifted, qi, carry):
        start = qi * bq
        here = pl.ds(pl.multiple_of(order_ref[qi] * bq, bq), bq)
        queries = [q_ref[h * dh:(h + 1) * dh, here] for h in range(pair)]
        full, stop = key_range(start, bq, prefix, bk)

        def step(masked, ki, state):
            first = ki * bk
            there = pl.ds(pl.multiple_of(order_ref[ki] * bk, bk), bk)
            if masked:
                rows = first + lax.broadcasted_iota(jnp.int32, (bk, bq), 0)
                cols = start + lax.broadcasted_iota(jnp.int32, (bk, bq), 1)
                allowed = rows <= jnp.maximum(cols, prefix - 1)
            scores = [dot(key_rows[h, there], queries[h]) for h in range(pair)]
            fresh = []
            for h in range(pair):
                s = jnp.where(allowed, scores[h], MASKED) if masked else scores[h]
                if shifted:
                    top, total = state[h]
                    new_top = jnp.maximum(top, jnp.max(s, axis=0, keepdims=True))
                    p = jnp.exp2(s - new_top).astype(BF16)
                    total = total * jnp.exp2(top - new_top) + dot(value_ext[h, :, there], p)
                    fresh.append((new_top, total))
                else:
                    fresh.append(state[h] + dot(value_ext[h, :, there], jnp.exp2(s).astype(BF16)))
            return tuple(fresh)

        zero = jnp.zeros((ext, bq), F32)
        state = tuple((jnp.full((1, bq), MASKED, F32), zero) if shifted else zero for _ in range(pair))
        state = lax.fori_loop(0, full, functools.partial(step, False), state)
        state = lax.fori_loop(full, stop, functools.partial(step, True), state)
        for h in range(pair):
            top, total = state[h] if shifted else (0.0, state[h])
            norm = total[dh:dh + 1]
            o_ref[h * dh:(h + 1) * dh, here] = (total[:dh] / norm).astype(BF16)
            lse_ref[h, :, here] = top + jnp.log2(norm)
        return carry

    small = bound <= 3600.0

    @pl.when(small)
    def _():
        lax.fori_loop(0, length // bq, functools.partial(one_query, False), 0)

    @pl.when(jnp.logical_not(small))
    def _():
        lax.fori_loop(0, length // bq, functools.partial(one_query, True), 0)


def attention_forward(q, k, v, prefix, order, dh, pair=4):
    width, length = q.shape
    heads = width // dh
    pair = min(pair, heads)
    bq = bk = length // order.shape[0]
    ext = dh + 16
    spec = pl.BlockSpec((pair * dh, length), lambda i, p, o: (i, 0))
    return pl.pallas_call(
        functools.partial(forward_kernel, pair=pair, dh=dh, bq=bq, bk=bk),
        grid_spec=pltpu.PrefetchScalarGridSpec(
            num_scalar_prefetch=2, grid=(heads // pair,),
            in_specs=[spec, spec, spec],
            out_specs=[spec, pl.BlockSpec((pair, 1, length), lambda i, p, o: (i, 0, 0))],
            scratch_shapes=[pltpu.VMEM((pair, length, dh), BF16), pltpu.VMEM((pair, ext, length), BF16)],
        ),
        out_shape=[jax.ShapeDtypeStruct((width, length), BF16), jax.ShapeDtypeStruct((heads, 1, length), F32)],
        compiler_params=pltpu.CompilerParams(vmem_limit_bytes=VMEM_LIMIT),
        cost_estimate=pl.CostEstimate(flops=int(HINT * 600 * length * length * heads), bytes_accessed=int(HINT * 8 * width * length), transcendentals=0),
        name="attention_forward",
    )(prefix, order, q, k, v)

def split3(x):
    a = x.astype(BF16)
    r = x - a.astype(F32)
    b = r.astype(BF16)
    c = (r - b.astype(F32)).astype(BF16)
    return a, b, c

def backward_kernel(prefix_ref, order_ref, q_ref, k_ref, v_ref, o_ref, g_ref, lse_ref, scale_ref, dq_ref, dk_ref, dv_ref, fg_ref,
                    key_ext, value_ext, query_ext, grad_ext, dk_acc, dv_acc, *, pair, dh, bq, bk):
    length = q_ref.shape[1]
    prefix = prefix_ref[0]
    pad = key_ext.shape[1] - dh
    index = lax.broadcasted_iota(jnp.int32, (pad, length), 0)
    ones = (index < 3).astype(F32).astype(BF16)

    @pl.when(pl.program_id(0) == 0)
    def _():
        fg_ref[...] = jnp.zeros_like(fg_ref)

    def tail(row):
        high, mid, low = (part.astype(F32) for part in split3(-row))
        rest = jnp.where(index == 1, mid, jnp.where(index == 2, low, 0.0))
        return jnp.where(index == 0, high, rest).astype(BF16)

    for h in range(pair):
        rows = slice(h * dh, (h + 1) * dh)
        g = g_ref[rows, :]
        key_ext[h, :dh] = k_ref[rows, :]
        key_ext[h, dh:] = ones
        value_ext[h, :dh] = v_ref[rows, :]
        value_ext[h, dh:] = ones
        delta = jnp.sum(o_ref[rows, :].astype(F32) * g.astype(F32), axis=0, keepdims=True)
        query_ext[h, :dh] = q_ref[rows, :]
        query_ext[h, dh:] = tail(lse_ref[h])
        grad_ext[h, :dh] = g
        grad_ext[h, dh:] = tail(delta)
        dk_acc[h] = jnp.zeros((dh, length), F32)
        dv_acc[h] = jnp.zeros((dh, length), F32)

    def one_query(qi, carry):
        start = qi * bq
        here = pl.ds(pl.multiple_of(order_ref[qi] * bq, bq), bq)
        full, stop = key_range(start, bq, prefix, bk)

        def step(masked, ki, state):
            first = ki * bk
            there = pl.ds(pl.multiple_of(order_ref[ki] * bk, bk), bk)
            if masked:
                rows = start + lax.broadcasted_iota(jnp.int32, (bq, bk), 0)
                cols = first + lax.broadcasted_iota(jnp.int32, (bq, bk), 1)
                allowed = cols <= jnp.maximum(rows, prefix - 1)
            fresh = []
            s = [dot(query_ext[h, :, here], key_ext[h, :, there], ((0,), (0,))) for h in range(pair)]
            gp = [dot(grad_ext[h, :, here], value_ext[h, :, there], ((0,), (0,))) for h in range(pair)]
            for h in range(pair):
                x = jnp.where(allowed, s[h], MASKED) if masked else s[h]
                p = jnp.exp2(x)
                ds = (p * gp[h]).astype(BF16)
                rows = slice(h * dh, (h + 1) * dh)
                dv_acc[h, :, there] += dot(g_ref[rows, here], p.astype(BF16))
                dk_acc[h, :, there] += dot(q_ref[rows, here], ds)
                fresh.append(state[h] + dot(ds, k_ref[rows, there], ((1,), (1,))))
            return tuple(fresh)

        def corner(_, state):
            cut, base = bk // 2, order_ref[qi] * bk
            fresh = []
            for low in (0, cut):
                size = bq - low
                keys = pl.ds(pl.multiple_of(base + low, cut), cut)
                queries = pl.ds(pl.multiple_of(base + low, cut), size)
                rows = low + lax.broadcasted_iota(jnp.int32, (size, cut), 0)
                cols = low + lax.broadcasted_iota(jnp.int32, (size, cut), 1)
                allowed = cols <= jnp.maximum(rows, prefix - 1 - start)
                s = [dot(query_ext[h, :, queries], key_ext[h, :, keys], ((0,), (0,))) for h in range(pair)]
                gp = [dot(grad_ext[h, :, queries], value_ext[h, :, keys], ((0,), (0,))) for h in range(pair)]
                parts = []
                for h in range(pair):
                    p = jnp.exp2(jnp.where(allowed, s[h], MASKED))
                    ds = (p * gp[h]).astype(BF16)
                    rows_h = slice(h * dh, (h + 1) * dh)
                    dv_acc[h, :, keys] += dot(g_ref[rows_h, queries], p.astype(BF16))
                    dk_acc[h, :, keys] += dot(q_ref[rows_h, queries], ds)
                    parts.append(dot(ds, k_ref[rows_h, keys], ((1,), (1,))))
                fresh.append(parts)
            upper = [state[h][:bk // 2] + fresh[0][h][:bk // 2] for h in range(pair)]
            lower = [state[h][bk // 2:] + fresh[0][h][bk // 2:] + fresh[1][h] for h in range(pair)]
            return tuple(jnp.concatenate([a, b], axis=0) for a, b in zip(upper, lower))

        state = tuple(jnp.zeros((bq, dh), F32) for _ in range(pair))
        state = lax.fori_loop(0, full, functools.partial(step, False), state)
        plain_corner = prefix <= start + bq // 2
        state = lax.fori_loop(full, jnp.where(plain_corner, full, stop), functools.partial(step, True), state)
        state = lax.fori_loop(0, plain_corner.astype(jnp.int32), corner, state)
        for h in range(pair):
            rows = slice(h * dh, (h + 1) * dh)
            dq = state[h].T
            prod = dq * q_ref[rows, here].astype(F32)
            part = prod[:, :128]
            for c in range(1, bq // 128):
                part = part + prod[:, c * 128:(c + 1) * 128]
            fg_ref[...] += part
            dq_ref[rows, here] = (dq * scale_ref[...]).astype(BF16)
        return carry

    lax.fori_loop(0, length // bq, one_query, 0)
    for h in range(pair):
        rows = slice(h * dh, (h + 1) * dh)
        dk_ref[rows, :] = (dk_acc[h] * math.log(2.0)).astype(BF16)
        dv_ref[rows, :] = dv_acc[h].astype(BF16)


def attention_backward(q, k, v, o, g, lse, factor, prefix, order, dh, base=0, width=None, pair=2):
    full, length = q.shape
    width = width or full
    heads = width // dh
    pair = min(pair, heads)
    bq = bk = length // order.shape[0]
    ext = dh + 16
    spec = pl.BlockSpec((pair * dh, length), lambda i, p, o: (i, 0))
    skip = base // (pair * dh)
    source = pl.BlockSpec((pair * dh, length), lambda i, p, o: (i + skip, 0))
    wide = jax.ShapeDtypeStruct((width, length), BF16)
    return pl.pallas_call(
        functools.partial(backward_kernel, pair=pair, dh=dh, bq=bq, bk=bk),
        grid_spec=pltpu.PrefetchScalarGridSpec(
            num_scalar_prefetch=2, grid=(heads // pair,),
            in_specs=[source] * 5 + [pl.BlockSpec((pair, 1, length), lambda i, p, o: (i + skip, 0, 0)), pl.BlockSpec((dh, 1), lambda i, p, o: (0, 0))],
            out_specs=[spec] * 3 + [pl.BlockSpec((dh, 128), lambda i, p, o: (0, 0))],
            scratch_shapes=[
                pltpu.VMEM((pair, ext, length), BF16),
                pltpu.VMEM((pair, ext, length), BF16),
                pltpu.VMEM((pair, ext, length), BF16),
                pltpu.VMEM((pair, ext, length), BF16),
                pltpu.VMEM((pair, dh, length), F32),
                pltpu.VMEM((pair, dh, length), F32)],
        ),
        out_shape=[wide] * 3 + [jax.ShapeDtypeStruct((dh, 128), F32)],
        compiler_params=pltpu.CompilerParams(vmem_limit_bytes=VMEM_LIMIT),
        cost_estimate=pl.CostEstimate(flops=int(HINT * 1600 * length * length * heads), bytes_accessed=int(HINT * 16 * width * length), transcendentals=0),
        name="attention_backward",
    )(prefix, order, q, k, v, o, g, lse, factor.reshape(dh, 1))


def rms(x):
    inv = lax.rsqrt(jnp.mean(x * x, axis=-1, keepdims=True) + EPSILON)
    return x * inv, inv


def rms_back(normed, inv, gain, grad):
    scaled = grad * gain
    out = inv * (scaled - normed * jnp.mean(scaled * normed, axis=-1, keepdims=True))
    return out, jnp.sum(grad * normed, axis=0)


def ein(spec, *args):
    return jnp.einsum(spec, *args, preferred_element_type=F32)


def gather_kernel(pieces, pairs, outer, ring, shard_ref, input_ref, *refs):
    outs = [refs[2 * m:2 * m + 2] for m in range(pairs)]
    got_ref = refs[2 * pairs]
    wide_ref, block_ref, send, recv, local = refs[2 * pairs + 1:]
    f, t = lax.axis_index("fsdp"), lax.axis_index("tp")
    zz, yy = f // 2, f % 2
    across = {"tp": lax.rem(t + ring, 2 * ring)}
    beside = {"fsdp": zz * 2 + 1 - yy}
    along = [{"fsdp": lax.rem(zz + k, outer) * 2 + yy} for k in range(1, outer)]
    peers = along + [across, beside]
    barrier = pltpu.get_barrier_semaphore()
    for peer in peers:
        pl.semaphore_signal(barrier, inc=1, device_id=peer, device_id_type=MESH)
    pl.semaphore_wait(barrier, len(peers))
    used = [0]
    wide = pltpu.make_async_copy(input_ref.at[1 - t // ring], wide_ref, local.at[len(pieces)])
    wide.start()

    def copy(src, dst, peer):
        slot = used[0]
        used[0] += 1
        return pltpu.make_async_remote_copy(
            src_ref=src, dst_ref=dst, send_sem=send.at[slot], recv_sem=recv.at[slot],
            device_id=peer, device_id_type=MESH,
        )

    count = len(pieces)
    chunks = 4
    step = block_ref.shape[0] // chunks
    blocks = [
        copy(block_ref.at[pl.ds(i * step, step)], got_ref.at[pl.ds(i * step, step)], across)
        for i in range(chunks)
    ]
    own, first, second, third = [], [], [], []
    for i, (m, low, rows, route) in enumerate(pieces):
        part = pl.ds(low, rows)
        w = [out.at[:, :, part] for out in outs[m]]
        src = shard_ref.at[m, part]
        own.append(pltpu.make_async_copy(src, w[0].at[zz, yy], local.at[i]))
        first.append([copy(src, w[0].at[zz, yy], peer) for peer in along])
        if route:
            second.append([copy(w[0].at[:, yy], w[0].at[:, yy], beside)])
            third.append([copy(w[0], w[1], across)])
        else:
            second.append([copy(w[0].at[:, yy], w[1].at[:, yy], across)])
            third.append([copy(w[s].at[:, yy], w[s].at[:, yy], beside) for s in range(2)])

    def begin(i):
        own[i].start()
        for c in first[i]:
            c.start()

    ahead = 3
    for i in range(min(ahead, count)):
        begin(i)
    wide.wait()
    block_ref[...] = wide_ref[...].astype(BF16)
    for b in blocks[:2]:
        b.start()
    started = 2
    for i in range(count + 2):
        if i < count:
            own[i].wait()
            for c in first[i]:
                c.wait_recv()
            for c in second[i]:
                c.start()
            if i + ahead < count:
                begin(i + ahead)
            if started < chunks:
                blocks[started].start()
                started += 1
        if 0 <= i - 1 < count:
            for c in second[i - 1]:
                c.wait_recv()
            for c in third[i - 1]:
                c.start()
        if 0 <= i - 2 < count:
            for c in third[i - 2]:
                c.wait_recv()
    for b in blocks[started:]:
        b.start()
    for i in range(count):
        for c in first[i] + second[i] + third[i]:
            c.wait_send()
    for b in blocks:
        b.wait()


def pieces_of(pairs, rows):
    half = rows // 32 * 16
    return tuple(
        (m, low, size, m_part) for m in range(pairs) for m_part, (low, size) in enumerate(((0, half), (half, rows - half)))
    )


def gather_call(shards, inputs, pieces, fsdp, ring):
    pairs, rows, w = shards.shape
    outer = fsdp // 2
    slots = 4 + len(pieces) * (outer + 2)
    any_spec = pl.BlockSpec(memory_space=pl.ANY)
    got = pl.pallas_call(
        functools.partial(gather_kernel, pieces, pairs, outer, ring),
        out_shape=[jax.ShapeDtypeStruct((outer, 2, rows, w), BF16)] * (2 * pairs)
        + [jax.ShapeDtypeStruct(inputs.shape[1:], BF16)],
        in_specs=[any_spec] * 2,
        out_specs=[any_spec] * (2 * pairs + 1),
        scratch_shapes=[
            pltpu.VMEM(inputs.shape[1:], F32),
            pltpu.VMEM(inputs.shape[1:], BF16),
            pltpu.SemaphoreType.DMA((slots,)),
            pltpu.SemaphoreType.DMA((slots,)),
            pltpu.SemaphoreType.DMA((len(pieces) + 1,)),
        ],
        compiler_params=pltpu.CompilerParams(vmem_limit_bytes=VMEM_LIMIT, collective_id=0, has_side_effects=True),
        name="gather_weights",
    )(shards, inputs)
    return [a.reshape(outer * 2 * rows, w) for a in got[:-1]], got[-1]


class Plan:
    def __init__(self, seqs, tp, fsdp, rows):
        self.seqs, self.tp, self.ring, self.fsdp = seqs, tp, tp // seqs, fsdp
        self.same_member = [[s * self.ring + r for s in range(seqs)] for r in range(self.ring)]
        self.same_seq = [[s * self.ring + r for r in range(self.ring)] for s in range(seqs)]
        self.fast = seqs == 2 and self.ring == 2 and fsdp % 2 == 0 and rows % 32 == 0
        t = lax.axis_index("tp")
        self.seq, self.member = t // self.ring, lax.rem(t, self.ring)

    def across(self, a):
        n = self.tp
        return lax.ppermute(a, "tp", [(t, (t + self.ring) % n) for t in range(n)])

    def core(self, a):
        return lax.ppermute(a, "tp", [(t, t ^ 1) for t in range(self.tp)])

    def pick(self, blocks, index):
        return lax.dynamic_index_in_dim(blocks, index, 0, keepdims=False)

    def order(self, own, other):
        first = self.seq == 0
        return jnp.concatenate([jnp.where(first, own, other), jnp.where(first, other, own)])

    def swap(self, blocks):
        if self.seqs == 2:
            other = self.across(self.pick(blocks, 1 - self.seq).astype(BF16))
            return self.order(self.pick(blocks, self.seq), other.astype(F32))
        got = lax.all_to_all(
            blocks.astype(BF16), "tp", 0, 0, tiled=True, axis_index_groups=self.same_member
        )
        return got.reshape(-1, got.shape[-1]).astype(F32)

    def unswap(self, rows):
        blocks = rows.reshape(self.seqs, -1, rows.shape[-1])
        return self.swap(blocks).reshape(blocks.shape)

    def whole(self, rows):
        if self.fast:
            return jnp.concatenate([rows, self.core(rows)])
        cut = rows.reshape(self.seqs, -1, rows.shape[-1])
        got = lax.all_gather(cut, "tp", axis=1, axis_index_groups=self.same_seq)
        return got.reshape(-1, rows.shape[-1])

    def share(self, full):
        if self.fast:
            own = full.shape[0] // 2
            return full[:own].astype(F32) + self.core(full[own:].astype(BF16)).astype(F32)
        cut = full.astype(BF16).reshape(self.seqs, self.ring, -1, full.shape[-1])
        got = lax.psum_scatter(cut, "tp", scatter_dimension=1, axis_index_groups=self.same_seq)
        return got.reshape(-1, full.shape[-1]).astype(F32)

    def blocks(self, length):
        if self.fast:
            j = jnp.arange(self.tp, dtype=jnp.int32)
            apart = (j % self.ring != self.member).astype(jnp.int32)
            return apart * self.seqs + j // self.ring
        return jnp.arange(max(1, length // 512), dtype=jnp.int32)

    def gather_heads(self, shards):
        rows = lax.all_gather(shards, "fsdp", axis=1, tiled=True)
        if self.fast:
            return jnp.stack([rows, self.across(rows)])
        return lax.all_gather(rows, "tp", axis_index_groups=self.same_member)

    def join(self, every):
        r, s, m, d, w = every.shape
        return every.transpose(2, 3, 0, 1, 4).reshape(m, d, r * s * w)

    def gather_full(self, shards):
        part = self.gather_heads(shards)
        if self.fast:
            return self.join(jnp.stack([part, self.core(part)]))
        return self.join(lax.all_gather(part, "tp", axis_index_groups=self.same_seq))

    def scatter_heads(self, grads):
        if self.fast:
            other = self.across(grads[1].astype(BF16))
            mine = (grads[0].astype(F32) + other.astype(F32)).astype(BF16)
        else:
            mine = lax.psum_scatter(
                grads.astype(BF16), "tp", scatter_dimension=0, axis_index_groups=self.same_member
            )
        return lax.psum_scatter(mine, "fsdp", scatter_dimension=1, tiled=True).astype(F32)

    def scatter_full(self, grads):
        m, d, cols = grads.shape
        if self.fast:
            half = cols // 2
            other = self.core(grads[:, :, half:].astype(BF16))
            mine = grads[:, :, :half].astype(F32) + other.astype(F32)
            mine = mine.astype(BF16).reshape(m, d, self.seqs, -1).transpose(2, 0, 1, 3)
        else:
            cut = grads.astype(BF16).reshape(m, d, self.ring, self.seqs, -1).transpose(2, 3, 0, 1, 4)
            mine = lax.psum_scatter(cut, "tp", scatter_dimension=0, axis_index_groups=self.same_seq)
        return self.scatter_heads(mine)


def layer_forward(plan, x, prefix, order, qkv, out_t, up, down_t, gains, factor):
    dh = factor.shape[0]
    normed, inv = rms(x)
    h = plan.whole((normed * gains[0]).astype(BF16))
    seqs, d, w = out_t.shape
    raw = [ein("sdc,td->sct", qkv[c], h).reshape(seqs * w, -1) for c in range(3)]
    scale = jnp.tile(factor * LOG2E, seqs * w // dh)[:, None]
    q, k, v = (raw[0] * scale).astype(BF16), raw[1].astype(BF16), raw[2].astype(BF16)
    att, lse = attention_forward(q, k, v, prefix, order, dh)
    middle = x + plan.share(ein("sct,sdc->td", att.reshape(seqs, w, -1), out_t))
    normed_m, inv_m = rms(middle)
    h_m = (normed_m * gains[1]).astype(BF16)
    pre = ein("td,df->tf", h_m, up)
    hidden = jax.nn.silu(pre).astype(BF16)
    result = middle + ein("tf,df->td", hidden, down_t)
    return result, (x, inv, h, q, k, v, att, lse, middle, inv_m, h_m, pre, hidden)


def layer_backward(plan, g, saved, prefix, order, qkv, out_t, up, down_t, gains, factor):
    x, inv, h, q, k, v, att, lse, middle, inv_m, h_m, pre, hidden = saved
    dh = factor.shape[0]
    seqs, d, w = out_t.shape
    length = h.shape[0]
    g_low = g.astype(BF16)
    down_grad = ein("td,tf->df", g_low, hidden)
    g_hidden = ein("td,df->tf", g_low, down_t)
    sig = jax.nn.sigmoid(pre)
    g_pre = (g_hidden * sig * (1.0 + pre * (1.0 - sig))).astype(BF16)
    up_grad = ein("td,tf->df", h_m, g_pre)
    mlp_grads = plan.scatter_full(jnp.stack([up_grad, down_grad]))
    g_hm = ein("tf,df->td", g_pre, up)
    back_m, gain_m = rms_back(middle * inv_m, inv_m, gains[1], g_hm)
    g_mid = g + back_m
    g_all = plan.whole(g_mid.astype(BF16))
    att3 = att.reshape(seqs, w, length)
    out_grad = plan.scatter_heads(ein("td,sct->sdc", g_all, att3)[:, None])[0]
    g_att = ein("td,sdc->sct", g_all, out_t).astype(BF16).reshape(seqs * w, length)
    dq, dk, dv, fg = attention_backward(q, k, v, att, g_att, lse, factor, prefix, order, dh)
    factor_grad = jnp.sum(fg, axis=1) / (factor * LOG2E)
    parts = [a.reshape(seqs, w, length) for a in (dq, dk, dv)]
    qkv_grad = plan.scatter_heads(jnp.stack([ein("td,sct->sdc", h, a) for a in parts], axis=1))
    g_ha = plan.share(sum(ein("sct,sdc->td", a, b) for a, b in zip(parts, qkv)))
    back_a, gain_a = rms_back(x * inv, inv, gains[0], g_ha)
    return g_mid + back_a, (qkv_grad, out_grad.T, mlp_grads[0], mlp_grads[1].T, gain_a, gain_m, factor_grad)


TN, NT, TT = ((0,), (0,)), ((1,), (1,)), ((0,), (1,))
ONE = pl.Buffered(1)


def cost(flops, nbytes):
    return pl.CostEstimate(flops=int(flops * HINT), bytes_accessed=int(nbytes * HINT), transcendentals=0)


def params(mib=60):
    return pltpu.CompilerParams(vmem_limit_bytes=mib * 2**20)


def fixed(shape):
    return pl.BlockSpec(shape, lambda *a: (0,) * len(shape), pipeline_mode=ONE)


def weight(w, lanes=None):
    stack, index = w if isinstance(w, tuple) else (w, None)
    shape = (stack.shape[-2], lanes or stack.shape[-1])
    if index is None:
        return fixed(shape)
    return pl.BlockSpec((None,) + shape, lambda *a: (index, 0, 0), pipeline_mode=ONE)


def plain(weights):
    return [w[0] if isinstance(w, tuple) else w for w in weights]


def shape_of(shape, dtype=BF16):
    return jax.ShapeDtypeStruct(shape, dtype)


def inverse_rms(x):
    return lax.rsqrt(jnp.mean(x * x, axis=-1, keepdims=True) + EPSILON)


def eight(x):
    return jnp.sum(x.reshape(-1, 8, x.shape[-1]), axis=0)


def join_lanes(dst, refs, low, high):
    width = high - low
    for i, ref in enumerate(refs):
        dst[:, i * width:(i + 1) * width] = ref[:, low:high]


def core_of():
    t = lax.axis_index("tp")
    return {"tp": t + 1 - 2 * lax.rem(t, 2)}


def pushes(send, recv, core):
    def push(src, dst, slot):
        return pltpu.make_async_remote_copy(
            src_ref=src, dst_ref=dst, send_sem=send.at[slot], recv_sem=recv.at[slot],
            device_id=core, device_id_type=MESH,
        )

    return push


def greet(core):
    barrier = pltpu.get_barrier_semaphore()
    pl.semaphore_signal(barrier, inc=1, device_id=core, device_id_type=MESH)
    pl.semaphore_wait(barrier, 1)


def stack_index(weights):
    return tuple(a[1] if isinstance(a, tuple) else None for a in weights)


def entry(ref, k):
    return ref if k is None else ref.at[k]


def stages(steps):
    starts = [sum(steps[:n]) for n in range(len(steps))]

    def at(n, make):
        return lambda i: make(jnp.clip(i - starts[n], 0, steps[n] - 1))

    return at


ANY = pl.BlockSpec(memory_space=pl.ANY)


class Halves:
    def __init__(self, own_any, got_any, own, got, load, ring):
        self.seq = lax.axis_index("tp") // ring
        self.own, self.got = own, got
        self.copies = [
            pltpu.make_async_copy(own_any.at[self.seq], own, load.at[0]),
            pltpu.make_async_copy(got_any, got, load.at[1]),
        ]

    def rows(self, k, size):
        per = self.own.shape[0] // size
        here = pl.ds(pl.multiple_of(lax.rem(k, per) * size, size), size)
        return jnp.where(k // per == self.seq, self.own[here], self.got[here].astype(F32))


def halves_scratch(rows, d):
    return [pltpu.VMEM((rows // 2, d), F32), pltpu.VMEM((rows // 2, d), BF16), pltpu.SemaphoreType.DMA((2,))]


def project_kernel(w, low, steps, index, bt, ring, gain_ref, scale_ref, *refs):
    weights, refs = refs[:4], refs[4:]
    if ring:
        own_any, got_any, own_ref, other_ref, q_ref, k_ref, v_ref, x_out = refs[:8]
        own, other, qk, vo, load, send, recv, *rest = refs[8:]
        halves = Halves(own_any, got_any, *rest, ring)
    else:
        x_ref, own_ref, other_ref, q_ref, k_ref, v_ref = refs[:6]
        own, other, qk, vo, load, send, recv = refs[6:]
    i = pl.program_id(0)
    rows_steps, half, _ = steps
    ba = q_ref.shape[1]
    core = core_of()
    push = pushes(send, recv, core)

    def loads():
        copies = [pltpu.make_async_copy(entry(weights[s], index[s]), qk.at[s], load.at[s]) for s in range(2)]
        for s in range(2):
            src = entry(weights[2 + s], index[2 + s]).at[:, pl.ds(0, low)]
            copies.append(pltpu.make_async_copy(src, vo.at[s], load.at[2 + s]))
        return copies

    def push_rows(k):
        part = pl.ds(pl.multiple_of(k * bt, bt), bt)
        return push(own.at[part], other.at[part], k)

    @pl.when(i == 0)
    def _():
        if ring:
            for c in halves.copies:
                c.start()
        for c in loads():
            c.start()
        greet(core)
        if ring:
            for c in halves.copies:
                c.wait()

    @pl.when(i < rows_steps)
    def _():
        if ring:
            x = halves.rows(i, bt)
            x_out[...] = x
        else:
            x = x_ref[...]
        h = (x * inverse_rms(x) * gain_ref[...]).astype(BF16)
        own[pl.ds(pl.multiple_of(i * bt, bt), bt)] = h
        own_ref[...] = h
        push_rows(i).start()

    at = i - rows_steps

    @pl.when(at == 0)
    def _():
        for c in loads():
            c.wait()

    @pl.when(at == half)
    def _():
        for k in range(rows_steps):
            push_rows(k).wait()

    def project(h):
        for s in range(2):
            rows = slice(s * w, (s + 1) * w)
            both = dot(qk[s], h, TT)
            q_ref[rows] = (both[:w] * scale_ref[rows]).astype(BF16)
            k_ref[rows] = both[w:].astype(BF16)
            v_ref[rows] = dot(vo[s, :, :w], h, TT).astype(BF16)

    @pl.when((at >= 0) & (at < half))
    def _():
        project(own[pl.ds(pl.multiple_of(at * ba, ba), ba)])

    @pl.when(at >= half)
    def _():
        h = other[pl.ds(pl.multiple_of((at - half) * ba, ba), ba)]
        other_ref[...] = h
        project(h)


def project(x, gain, qk, vo, scale, call, ring=0):
    xs = x if ring else (x,)
    d = xs[0].shape[-1]
    rows = 2 * xs[1].shape[0] if ring else x.shape[0]
    w2 = plain(qk)[0].shape[-1]
    w = w2 // 2
    low = -(-w // 128) * 128
    bt, ba = 256, 512
    half = rows // ba
    steps = (rows // bt, half, half)
    row = pl.BlockSpec((bt, d), lambda i: (jnp.minimum(i, steps[0] - 1), 0))
    wide = pl.BlockSpec((w2, ba), lambda i: (0, jnp.clip(i - steps[0], 0, 2 * half - 1)))
    tall = pl.BlockSpec((ba, d), lambda i: (jnp.clip(i - steps[0] - half, 0, half - 1), 0))
    weights = (*qk, *vo)
    return pl.pallas_call(
        functools.partial(project_kernel, w, low, steps, stack_index(weights), bt, ring),
        grid=(sum(steps),),
        in_specs=[fixed((1, d)), fixed((w2, 1))] + [ANY] * 4 + ([ANY] * 2 if ring else [row]),
        out_specs=[row, tall] + [wide] * 3 + ([row] if ring else []),
        out_shape=[shape_of((rows, d))] * 2 + [shape_of((w2, 2 * rows))] * 3 + ([shape_of((rows, d), F32)] if ring else []),
        scratch_shapes=[
            pltpu.VMEM((rows, d), BF16), pltpu.VMEM((rows, d), BF16),
            pltpu.VMEM((2, d, w2), BF16), pltpu.VMEM((2, d, low), BF16),
            pltpu.SemaphoreType.DMA((4,)), pltpu.SemaphoreType.DMA((steps[0],)), pltpu.SemaphoreType.DMA((steps[0],)),
        ]
        + (halves_scratch(rows, d) if ring else []),
        compiler_params=pltpu.CompilerParams(vmem_limit_bytes=VMEM_LIMIT, collective_id=call, has_side_effects=True),
        cost_estimate=cost(4 * rows * d * 3 * w2, 12 * rows * d),
        name="project",
    )(gain, scale, *plain(weights), *xs)


def middle_kernel(w, low, steps, index, ring, x_ref, gm_ref, att_any, *refs):
    weights, refs = refs[:4], refs[4:]
    mid_ref, pre_ref, res_ref, up_out, down_out, out_out = refs[:6]
    if ring:
        half_out, half = refs[6], refs[-1]
        refs = refs[:6] + refs[7:-1]
    (up_mat, down_mat, out_mat, blocks, vo_side, att, part, got, load, store, send, recv) = refs[6:]
    i = pl.program_id(0)
    far, rows_steps = steps
    bt = x_ref.shape[0]
    ba = part.shape[0] // far
    rows = part.shape[0]
    core = core_of()
    push = pushes(send, recv, core)

    def loads():
        copies = [pltpu.make_async_copy(att_any, att, load.at[0])]
        for s in range(2):
            src = entry(weights[s], index[s]).at[:, pl.ds(low, vo_side.shape[2])]
            copies.append(pltpu.make_async_copy(src, vo_side.at[s], load.at[1 + s]))
        for s in range(2):
            copies.append(pltpu.make_async_copy(entry(weights[2 + s], index[2 + s]), blocks.at[s], load.at[3 + s]))
        return copies

    def stores():
        pairs = [(up_mat, up_out), (down_mat, down_out), (out_mat, out_out)]
        return [pltpu.make_async_copy(src, dst, store.at[n]) for n, (src, dst) in enumerate(pairs)]

    def push_block(s):
        return push(blocks.at[s], blocks.at[2 + s], s)

    def push_part(k):
        here = pl.ds(pl.multiple_of(k * ba, ba), ba)
        return push(part.at[here], got.at[here], 2 + k)

    @pl.when(i == 0)
    def _():
        copies = loads()
        for c in copies:
            c.start()
        greet(core)
        for c in copies[:3]:
            c.wait()
        for s in range(2):
            out_mat[:, s * w:(s + 1) * w] = vo_side[s, :, 2 * w - low - w:2 * w - low]
        for s in range(2):
            copies[3 + s].wait()
            push_block(s).start()

    @pl.when(i < far)
    def _():
        here = pl.ds(pl.multiple_of(i * ba, ba), ba)
        cols = pl.ds(pl.multiple_of(rows + i * ba, ba), ba)
        part[here] = dot(att[:, cols], out_mat[...], TT).astype(BF16)
        push_part(i).start()

    at = i - far

    @pl.when(at == 0)
    def _():
        for s in range(2):
            push_block(s).wait()
        for b in range(4):
            up_mat[:, b * w:(b + 1) * w] = blocks[b, :, 0:w]
            down_mat[:, b * w:(b + 1) * w] = blocks[b, :, w:2 * w]
        for c in stores():
            c.start()

    for k in range(far):
        @pl.when(at == k * (ba // bt))
        def _():
            push_part(k).wait()

    @pl.when(at >= 0)
    def _():
        here = pl.ds(pl.multiple_of(at * bt, bt), bt)
        mid = x_ref[...] + got[here].astype(F32) + dot(att[:, here], out_mat[...], TT)
        mid_ref[...] = mid
        h_m = (mid * inverse_rms(mid) * gm_ref[...]).astype(BF16)
        pre = dot(h_m, up_mat[...])
        pre_ref[...] = pre
        hidden = (pre / (1.0 + jnp.exp(-pre))).astype(BF16)
        res = mid + dot(hidden, down_mat[...], NT)
        res_ref[...] = res
        if ring:
            per = rows_steps // 2

            @pl.when(at // per == 1 - lax.axis_index("tp") // ring)
            def _():
                half[pl.ds(pl.multiple_of(lax.rem(at, per) * bt, bt), bt)] = res.astype(BF16)

    @pl.when(at == rows_steps - 1)
    def _():
        if ring:
            leave = pltpu.make_async_copy(half, half_out, store.at[3])
            leave.start()
            leave.wait()
        for c in stores():
            c.wait()


def middle_call(x, att, gain_m, vo, un, call, ring=0):
    rows, d = x.shape
    w2 = plain(vo)[0].shape[-1]
    w, ff = w2 // 2, 2 * w2
    low = w // 128 * 128
    bt, ba = 256, 512
    steps = (rows // ba, rows // bt)
    row = pl.BlockSpec((bt, d), lambda i: (jnp.maximum(i - steps[0], 0), 0))
    wide = pl.BlockSpec((bt, ff), lambda i: (jnp.maximum(i - steps[0], 0), 0))
    weights = (*vo, *un)
    mats = [(d, ff), (d, ff), (d, w2)]
    slots = 2 + steps[0]
    return pl.pallas_call(
        functools.partial(middle_kernel, w, low, steps, stack_index(weights), ring),
        grid=(sum(steps),),
        in_specs=[row, fixed((1, d))] + [ANY] * 5,
        out_specs=[row, wide, row] + [ANY] * (4 if ring else 3),
        out_shape=[shape_of((rows, d), F32), shape_of((rows, ff), F32), shape_of((rows, d), F32)] + [shape_of(m) for m in mats]
        + ([shape_of((rows // 2, d))] if ring else []),
        scratch_shapes=[pltpu.VMEM(m, BF16) for m in mats]
        + [pltpu.VMEM((4, d, w2), BF16), pltpu.VMEM((2, d, w2 - low), BF16), pltpu.VMEM(att.shape, BF16)]
        + [pltpu.VMEM((rows, d), BF16)] * 2
        + [pltpu.SemaphoreType.DMA((5,)), pltpu.SemaphoreType.DMA((4,)), pltpu.SemaphoreType.DMA((slots,)), pltpu.SemaphoreType.DMA((slots,))]
        + ([pltpu.VMEM((rows // 2, d), BF16)] if ring else []),
        compiler_params=pltpu.CompilerParams(vmem_limit_bytes=VMEM_LIMIT, collective_id=call, has_side_effects=True),
        cost_estimate=cost(2 * rows * d * (2 * w2 + 2 * ff), 30 * rows * d),
        name="middle",
    )(x, gain_m, att, *plain(weights))


def mlp_back_kernel(w, steps, ring, mid_ref, pre_ref, gm_ref, att_any, *refs):
    mats, refs = refs[:3], refs[3:]
    if ring:
        own_any, got_any, refs = refs[0], refs[1], refs[2:]
        halves = Halves(own_any, got_any, *refs[-3:], ring)
        refs = refs[:-3]
    else:
        g_ref, refs = refs[0], refs[1:]
    g_mid_ref, gain_ref, g_att_ref, o0, o1 = refs[:5]
    (up_mat, down_mat, out_mat, g_all, hid_all, hm_all, gpre_all, low_own, low_other, blocks, got, att,
     load, send, recv) = refs[5:]
    i = pl.program_id(0)
    rows_steps, grad_steps, att_steps, _ = steps
    bt, bd, ba = mid_ref.shape[0], o0.shape[0], g_att_ref.shape[1]
    core = core_of()
    push = pushes(send, recv, core)

    def loads():
        pairs = (*zip(mats, (up_mat, down_mat, out_mat)), (att_any, att))
        return [pltpu.make_async_copy(src, dst, load.at[n]) for n, (src, dst) in enumerate(pairs)]

    def push_rows(k):
        part = pl.ds(pl.multiple_of(k * bt, bt), bt)
        return push(low_own.at[part], low_other.at[part], k)

    def push_block(c, s):
        part = pl.ds(pl.multiple_of(c * bd, bd), bd)
        return push(blocks.at[2 + s, part], got.at[s, part], rows_steps + 2 * c + s)

    @pl.when(i == 0)
    def _():
        copies = loads()
        for c in copies:
            c.start()
        gain_ref[...] = jnp.zeros_like(gain_ref)
        if ring:
            for c in halves.copies:
                c.start()
        greet(core)
        for c in copies[:2] + (halves.copies if ring else []):
            c.wait()

    @pl.when(i < rows_steps)
    def _():
        here = pl.ds(pl.multiple_of(i * bt, bt), bt)
        g = halves.rows(i, bt) if ring else g_ref[...]
        g_low = g.astype(BF16)
        g_all[here] = g_low
        pre = pre_ref[...]
        sig = 1.0 / (1.0 + jnp.exp(-pre))
        hid_all[here] = (pre * sig).astype(BF16)
        g_hidden = dot(g_low, down_mat[...])
        g_pre = (g_hidden * sig * (1.0 + pre * (1.0 - sig))).astype(BF16)
        gpre_all[here] = g_pre
        mid = mid_ref[...]
        inv = inverse_rms(mid)
        normed = mid * inv
        gain = gm_ref[...]
        hm_all[here] = (normed * gain).astype(BF16)
        g_hm = dot(g_pre, up_mat[...], NT)
        gain_ref[...] += eight(g_hm * normed)
        scaled = g_hm * gain
        g_mid = g + inv * (scaled - normed * jnp.mean(scaled * normed, axis=-1, keepdims=True))
        g_mid_ref[...] = g_mid
        low_own[here] = g_mid.astype(BF16)
        push_rows(i).start()

    at = i - rows_steps

    @pl.when((at >= 0) & (at < grad_steps))
    def _():
        cols = pl.ds(pl.multiple_of(at * bd, bd), bd)
        up = dot(hm_all[:, cols], gpre_all[...], TN).astype(BF16)
        down = dot(g_all[:, cols], hid_all[...], TN).astype(BF16)
        for b in range(4):
            blocks[b, cols, 0:w] = up[:, b * w:(b + 1) * w]
            blocks[b, cols, w:2 * w] = down[:, b * w:(b + 1) * w]
        for s in range(2):
            push_block(at, s).start()

    to = at - grad_steps

    @pl.when(to == 0)
    def _():
        loads()[2].wait()

    half = att_steps // 2

    @pl.when((to >= 0) & (to < half))
    def _():
        here = pl.ds(pl.multiple_of(to * ba, ba), ba)
        g_att_ref[...] = dot(out_mat[...], low_own[here], TT).astype(BF16)

    @pl.when(to == half)
    def _():
        for k in range(rows_steps):
            push_rows(k).wait()

    @pl.when((to >= half) & (to < att_steps))
    def _():
        here = pl.ds(pl.multiple_of((to - half) * ba, ba), ba)
        g_att_ref[...] = dot(out_mat[...], low_other[here], TT).astype(BF16)

    last = to - att_steps

    @pl.when(last == 0)
    def _():
        loads()[3].wait()

    @pl.when(last >= 0)
    def _():
        cols = pl.ds(pl.multiple_of(last * bd, bd), bd)
        rows = low_own.shape[0]
        grad = dot(low_own[:, cols], att[:, :rows], TT) + dot(low_other[:, cols], att[:, rows:], TT)
        grad = grad.astype(BF16)
        for s, out in enumerate((o0, o1)):
            push_block(last, s).wait()
            out[:, :2 * w] = (blocks[s, cols].astype(F32) + got[s, cols].astype(F32)).astype(BF16)
            out[:, 2 * w:3 * w] = grad[:, s * w:(s + 1) * w]
            out[:, 3 * w:] = jnp.zeros((bd, out.shape[1] - 3 * w), BF16)


def mlp_back(g, mid, pre, gain, att, mats, width, call, ring=0):
    rows, d = mid.shape
    gs = g if ring else (g,)
    ff = pre.shape[1]
    w2 = att.shape[0]
    w = w2 // 2
    bt, bd, ba = 256, 256, 512
    steps = (rows // bt, d // bd, 2 * rows // ba, d // bd)
    at = stages(steps)
    row = pl.BlockSpec((bt, d), at(0, lambda k: (k, 0)))
    wide = pl.BlockSpec((bt, ff), at(0, lambda k: (k, 0)))
    block = pl.BlockSpec((bd, width), at(3, lambda k: (k, 0)))
    slots = steps[0] + 2 * steps[1]
    return pl.pallas_call(
        functools.partial(mlp_back_kernel, w, steps, ring),
        grid=(sum(steps),),
        in_specs=[row, wide, fixed((1, d))] + [ANY] * 4 + ([ANY] * 2 if ring else [row]),
        out_specs=[row, fixed((8, d)), pl.BlockSpec((w2, ba), at(2, lambda k: (0, k))), block, block],
        out_shape=[shape_of((rows, d), F32), shape_of((8, d), F32), shape_of((w2, 2 * rows))] + [shape_of((d, width))] * 2,
        scratch_shapes=[pltpu.VMEM((d, ff), BF16)] * 2
        + [pltpu.VMEM((d, w2), BF16)]
        + [pltpu.VMEM((rows, d), BF16), pltpu.VMEM((rows, ff), BF16)] * 2
        + [pltpu.VMEM((rows, d), BF16)] * 2
        + [pltpu.VMEM((4, d, w2), BF16), pltpu.VMEM((2, d, w2), BF16)]
        + [pltpu.VMEM(att.shape, BF16)]
        + [pltpu.SemaphoreType.DMA((4,)), pltpu.SemaphoreType.DMA((slots,)), pltpu.SemaphoreType.DMA((slots,))]
        + (halves_scratch(rows, d) if ring else []),
        compiler_params=pltpu.CompilerParams(vmem_limit_bytes=62 * 2**20, collective_id=call, has_side_effects=True),
        cost_estimate=cost(8 * rows * d * ff + 8 * rows * d * w2, 40 * rows * d),
        name="mlp_back",
    )(mid, pre, gain, att, *mats, *gs)


def weight_grad_kernel(w, own_ref, other_ref, dq_ref, dk_ref, dv_ref, *refs):
    out, stacked = refs[-2:]
    half = own_ref.shape[0]

    @pl.when(pl.program_id(0) == 0)
    def _():
        for j, ref in enumerate((dq_ref, dk_ref, dv_ref)):
            stacked[j * w:(j + 1) * w, :] = ref[...]

    grad = dot(own_ref[...], stacked[:, :half], TT) + dot(other_ref[...], stacked[:, half:], TT)
    if len(refs) == 3:
        grad = grad + refs[0][:, :3 * w].astype(F32)
    out[:, :3 * w] = grad.astype(BF16)
    out[:, 3 * w:] = jnp.zeros((out.shape[0], out.shape[1] - 3 * w), BF16)


def weight_grad(own, other, dq, dk, dv, width, got=None):
    rows, d = own.shape
    w = dq.shape[0]
    bd = 256
    col = pl.BlockSpec((rows, bd), lambda i: (0, i))
    flat = pl.BlockSpec((bd, width), lambda i: (i, 0))
    extra = [] if got is None else [got]
    return pl.pallas_call(
        functools.partial(weight_grad_kernel, w),
        grid=(d // bd,),
        in_specs=[col, col] + [fixed(dq.shape)] * 3 + [flat] * len(extra),
        out_specs=flat,
        out_shape=shape_of((d, width)),
        scratch_shapes=[pltpu.VMEM((3 * w, 2 * rows), BF16)],
        compiler_params=params(),
        cost_estimate=cost(12 * rows * d * w, 12 * rows * d),
        name="weight_grad",
    )(own, other, dq, dk, dv, *extra)


def input_back_kernel(w, low, steps, index, x_ref, g_ref, gain_ref, *refs):
    grads, weights, refs = refs[:6], refs[6:10], refs[10:]
    stacked, qk, vo, part, got, load, send, recv = refs[-8:]
    i = pl.program_id(0)
    chunk_steps, far, _ = steps
    if chunk_steps:
        own_ref, other_ref, out_ref, sum_ref, piece_ref = refs[:-8]
    else:
        out_ref, sum_ref = refs[:-8]
    bt, half = x_ref.shape[0], part.shape[0]
    ba = half // far
    push = pushes(send, recv, core_of())

    def loads():
        copies = [
            pltpu.make_async_copy(grads[n], stacked.at[n // 3, pl.ds(n % 3 * w, w)], load.at[n]) for n in range(6)
        ]
        for s in range(2):
            copies.append(pltpu.make_async_copy(entry(weights[s], index[s]), qk.at[s], load.at[6 + s]))
        for s in range(2):
            src = entry(weights[2 + s], index[2 + s]).at[:, pl.ds(0, low)]
            copies.append(pltpu.make_async_copy(src, vo.at[s], load.at[8 + s]))
        return copies

    def push_part(k):
        here = pl.ds(pl.multiple_of(k * ba, ba), ba)
        return push(part.at[here], got.at[here], k)

    def total(cols):
        parts = [
            dot(stacked[s, :2 * w, cols], qk[s], TT) + dot(stacked[s, 2 * w:, cols], vo[s, :, :w], TT) for s in range(2)
        ]
        return parts[0] + parts[1]

    @pl.when(i == 0)
    def _():
        copies = loads()
        for c in copies:
            c.start()
        sum_ref[...] = jnp.zeros_like(sum_ref)
        greet(core_of())
        for c in copies[:3]:
            c.wait()

    if chunk_steps:
        @pl.when(i < chunk_steps)
        def _():
            grad = dot(own_ref[...], stacked[0, :, :half], TT) + dot(other_ref[...], stacked[0, :, half:], TT)
            piece_ref[:, :3 * w] = grad.astype(BF16)
            piece_ref[:, 3 * w:] = jnp.zeros((piece_ref.shape[0], piece_ref.shape[1] - 3 * w), BF16)

    to = i - chunk_steps

    @pl.when(to == 0)
    def _():
        for c in loads()[3:]:
            c.wait()

    @pl.when((to >= 0) & (to < far))
    def _():
        cols = pl.ds(pl.multiple_of(half + to * ba, ba), ba)
        part[pl.ds(pl.multiple_of(to * ba, ba), ba)] = total(cols).astype(BF16)
        push_part(to).start()

    at = to - far
    for k in range(far):
        @pl.when(at == k * (ba // bt))
        def _():
            push_part(k).wait()

    @pl.when(at >= 0)
    def _():
        here = pl.ds(pl.multiple_of(at * bt, bt), bt)
        g_ha = total(here) + got[here].astype(F32)
        x = x_ref[...]
        inv = inverse_rms(x)
        normed = x * inv
        sum_ref[...] += eight(g_ha * normed)
        scaled = g_ha * gain_ref[...]
        out_ref[...] = g_ref[...] + inv * (scaled - normed * jnp.mean(scaled * normed, axis=-1, keepdims=True))


def input_back(grads, x, g, gain, qk, vo, call, normed=(), width=0):
    w, length = grads[0].shape
    rows, d = x.shape
    low = -(-w // 128) * 128
    bt, bd, ba = 256, 256, 512
    chunks = d // bd if normed else 0
    steps = (chunks, rows // ba, rows // bt)
    row = pl.BlockSpec((bt, d), lambda i: (jnp.maximum(i - steps[0] - steps[1], 0), 0))

    def chunk(k):
        return jnp.minimum(k, chunks - 1)

    weights = (*qk, *vo)
    in_specs = [row, row, fixed((1, d))] + [ANY] * 10
    out_specs, out_shape = [row, fixed((8, d))], [shape_of((rows, d), F32), shape_of((8, d), F32)]
    if normed:
        in_specs += [pl.BlockSpec((rows, bd), lambda i: (0, chunk(i)))] * 2
        out_specs.append(pl.BlockSpec((bd, width), lambda i: (chunk(i), 0)))
        out_shape.append(shape_of((d, width)))
    return pl.pallas_call(
        functools.partial(input_back_kernel, w, low, steps, stack_index(weights)),
        grid=(sum(steps),),
        in_specs=in_specs,
        out_specs=out_specs,
        out_shape=out_shape,
        scratch_shapes=[
            pltpu.VMEM((2, 3 * w, length), BF16), pltpu.VMEM((2, d, 2 * w), BF16), pltpu.VMEM((2, d, low), BF16),
            pltpu.VMEM((rows, d), BF16), pltpu.VMEM((rows, d), BF16),
            pltpu.SemaphoreType.DMA((10,)), pltpu.SemaphoreType.DMA((steps[1],)), pltpu.SemaphoreType.DMA((steps[1],)),
        ],
        compiler_params=pltpu.CompilerParams(vmem_limit_bytes=VMEM_LIMIT, collective_id=call, has_side_effects=True),
        cost_estimate=cost(9 * rows * d * 4 * w, 24 * rows * d),
        name="input_back",
    )(x, g, gain, *grads, *plain(weights), *normed)


def finish_kernel(w, low, far, own_steps, outer, ring, index, gain_ref, small_ref, x_any, g_any, piece_any, came_any, *refs):
    grads, weights, refs = refs[:6], refs[6:10], refs[10:]
    own_any, got_any, late_ref, sums_ref = refs[:4]
    (stacked, qk, vo, part, got, xs, gs, send_half, keep, away, came, near, hops, gain_sum, vec, vecs,
     load, store, send, recv) = refs[4:]
    i = pl.program_id(0)
    half = part.shape[0]
    ba, bt = half // far, half // own_steps
    f, t = lax.axis_index("fsdp"), lax.axis_index("tp")
    zz, yy, seq = f // 2, lax.rem(f, 2), t // ring
    across = {"tp": lax.rem(t + ring, 2 * ring)}
    beside = {"fsdp": zz * 2 + 1 - yy}
    along = [{"fsdp": lax.rem(zz + k, outer) * 2 + yy} for k in range(1, outer)]
    core = core_of()
    chunk = keep.shape[1]
    sends = far + outer + outer - 1
    pushed = own_steps // 2

    def push(src, dst, slot, peer):
        return pltpu.make_async_remote_copy(
            src_ref=src, dst_ref=dst, send_sem=send.at[slot], recv_sem=recv.at[slot],
            device_id=peer, device_id_type=MESH,
        )

    def rows_of(j, side):
        z = lax.rem(zz + 1 + j, outer)
        return pl.ds(pl.multiple_of((z * 2 + side) * chunk, chunk), chunk)

    def loads():
        def columns(first):
            cols = pl.ds(first, half)
            return [(grads[n].at[:, cols], stacked.at[n // 3, pl.ds(n % 3 * w, w), cols]) for n in range(6)]

        pairs = columns(half)
        pairs += [(entry(weights[s], index[s]), qk.at[s]) for s in range(2)]
        pairs += [(entry(weights[2 + s], index[2 + s]).at[:, pl.ds(0, low)], vo.at[s]) for s in range(2)]
        pairs += columns(0)
        pairs += [(x_any, xs), (g_any, gs)]
        for j in range(outer):
            for n, (side, dst) in enumerate(((1 - yy, away), (yy, keep))):
                pairs += [(piece_any.at[rows_of(j, side)], dst.at[j]), (came_any.at[rows_of(j, side)], came.at[n, j])]
        return [pltpu.make_async_copy(src, dst, load.at[n]) for n, (src, dst) in enumerate(pairs)]

    def chunk_of(k):
        return 1 - seq if k == 0 else seq

    def push_part(k):
        here = pl.ds(pl.multiple_of(chunk_of(k) * ba, ba), ba)
        return push(part.at[here], got.at[here], k, core)

    def push_near(j):
        return push(away.at[j], near.at[j], far + j, beside)

    def push_hop(j):
        return push(keep.at[j], hops.at[j], far + outer + j, along[j])

    def push_half(k):
        here = pl.ds(pl.multiple_of(k * bt, bt), bt)
        return push(send_half.at[here], got_any.at[here], sends + k, across)

    def push_small(n):
        peer = ([core, across, beside] + along)[n]
        return push(vec.at[min(n, 3)], vecs.at[n], sends + pushed + n, peer)

    def total(cols):
        parts = [
            dot(stacked[s, :2 * w, cols], qk[s], TT) + dot(stacked[s, 2 * w:, cols], vo[s, :, :w], TT) for s in range(2)
        ]
        return parts[0] + parts[1]

    @pl.when(i == 0)
    def _():
        copies = loads()
        for c in copies[18:] + copies[:10]:
            c.start()
        gain_sum[...] = jnp.zeros_like(gain_sum)
        barrier = pltpu.get_barrier_semaphore()
        peers = [core, across, beside] + along
        for peer in peers:
            pl.semaphore_signal(barrier, inc=1, device_id=peer, device_id_type=MESH)
        pl.semaphore_wait(barrier, len(peers))
        for c in copies[18:]:
            c.wait()
        for j in range(outer):
            away[j] = (away[j].astype(F32) + came[0, j].astype(F32)).astype(BF16)
            push_near(j).start()
        for c in copies[:10]:
            c.wait()
        for c in copies[10:18]:
            c.start()

    run = 1 + pushed
    for k in range(far):
        @pl.when(i == k * run)
        def _():
            cols = pl.ds(pl.multiple_of(half + chunk_of(k) * ba, ba), ba)
            part[pl.ds(pl.multiple_of(chunk_of(k) * ba, ba), ba)] = total(cols).astype(BF16)
            push_part(k).start()

    place_in_run = lax.rem(i, run)
    at = jnp.where(place_in_run == 0, -1, i // run * pushed + place_in_run - 1)
    at = jnp.where(i == far + own_steps, own_steps, at)

    @pl.when(at == 0)
    def _():
        for c in loads()[10:18]:
            c.wait()

    for k in range(far):
        @pl.when(at == k * pushed)
        def _():
            push_part(k).wait()

    for j in range(outer - 1):
        @pl.when(at == j + 1)
        def _():
            push_near(j).wait_recv()
            keep[j] = (keep[j].astype(F32) + came[1, j].astype(F32) + near[j].astype(F32)).astype(BF16)
            push_hop(j).start()

    @pl.when((at >= 0) & (at < own_steps))
    def _():
        place = lax.rem(at + pushed * (1 - seq), own_steps)
        here = pl.ds(pl.multiple_of(place * bt, bt), bt)
        g_ha = total(here) + got[here].astype(F32)
        x = xs[here]
        inv = inverse_rms(x)
        normed = x * inv
        gain_sum[...] += eight(g_ha * normed)
        scaled = g_ha * gain_ref[...]
        gs[here] = gs[here] + inv * (scaled - normed * jnp.mean(scaled * normed, axis=-1, keepdims=True))

    @pl.when((at >= 0) & (at < pushed))
    def _():
        place = at + pushed * (1 - seq)
        send_half[pl.ds(pl.multiple_of(at * bt, bt), bt)] = gs[pl.ds(pl.multiple_of(place * bt, bt), bt)].astype(BF16)
        push_half(at).start()

    @pl.when(at == own_steps)
    def _():
        size = half // 2
        mine = pl.ds(pl.multiple_of(seq * size, size), size)
        out_own = pltpu.make_async_copy(gs.at[mine], own_any, store.at[0])
        out_own.start()
        first = lax.broadcasted_iota(jnp.int32, vec.shape[1:], 0) == 0
        vec[0] = small_ref[...] + jnp.where(first, jnp.sum(gain_sum[...], axis=0, keepdims=True), 0.0)
        for n in range(3):
            push_small(n).start()
            push_small(n).wait()
            vec[n + 1] = vec[n] + vecs[n]
        for n in range(3, 2 + outer):
            push_small(n).start()
        for n in range(3, 2 + outer):
            push_small(n).wait()
        sums = vec[3]
        for n in range(3, 2 + outer):
            sums = sums + vecs[n]
        sums_ref[...] = sums
        push_near(outer - 1).wait_recv()
        late = keep[outer - 1].astype(F32) + came[1, outer - 1].astype(F32) + near[outer - 1].astype(F32)
        for j in range(outer - 1):
            push_hop(j).wait()
            late = late + hops[j].astype(F32)
        late_ref[...] = late
        for j in range(outer):
            push_near(j).wait_send()
        for k in range(pushed):
            push_half(k).wait()
        out_own.wait()


def finish(grads, x, g, gain, small, piece, came, qk, vo, fsdp, ring, call):
    w, length = grads[0].shape
    rows, d = x.shape
    width = piece.shape[1]
    low = -(-w // 128) * 128
    outer, chunk = fsdp // 2, piece.shape[0] // fsdp
    far, own_steps = rows // 512, rows // 256
    weights = (*qk, *vo)
    slots = far + 2 * outer - 1 + own_steps // 2 + 2 + outer
    dma = pltpu.SemaphoreType.DMA
    return pl.pallas_call(
        functools.partial(finish_kernel, w, low, far, own_steps, outer, ring, stack_index(weights)),
        grid=(far + own_steps + 1,),
        in_specs=[fixed((1, d)), fixed(small.shape)] + [ANY] * 14,
        out_specs=[ANY, ANY, fixed((chunk, width)), fixed(small.shape)],
        out_shape=[shape_of((rows // 2, d), F32), shape_of((rows // 2, d)), shape_of((chunk, width), F32), shape_of(small.shape, F32)],
        scratch_shapes=[
            pltpu.VMEM((2, 3 * w, length), BF16), pltpu.VMEM((2, d, 2 * w), BF16), pltpu.VMEM((2, d, low), BF16),
            pltpu.VMEM((rows, d), BF16), pltpu.VMEM((rows, d), BF16),
            pltpu.VMEM((rows, d), F32), pltpu.VMEM((rows, d), F32),
            pltpu.VMEM((rows // 2, d), BF16),
            pltpu.VMEM((outer, chunk, width), BF16), pltpu.VMEM((outer, chunk, width), BF16),
            pltpu.VMEM((2, outer, chunk, width), BF16), pltpu.VMEM((outer, chunk, width), BF16),
            pltpu.VMEM((outer - 1, chunk, width), BF16),
            pltpu.VMEM((8, d), F32), pltpu.VMEM((4,) + small.shape, F32), pltpu.VMEM((2 + outer,) + small.shape, F32),
            dma((18 + 4 * outer,)), dma((1,)), dma((slots,)), dma((slots,)),
        ],
        compiler_params=pltpu.CompilerParams(vmem_limit_bytes=VMEM_LIMIT, collective_id=call, has_side_effects=True),
        cost_estimate=cost(6 * rows * d * 4 * w, 24 * rows * d),
        name="finish",
    )(gain, small, x, g, piece, came, *grads, *plain(weights))


def total_over_all(plan, a):
    n, f = plan.tp, plan.fsdp
    hop = 1
    while hop < n:
        a = a + lax.ppermute(a, "tp", [(t, t ^ hop) for t in range(n)])
        hop *= 2
    hop = 1
    while hop < f:
        a = a + lax.ppermute(a, "fsdp", [(t, t ^ hop) for t in range(f)])
        hop *= 2
    return a


def add_low(own, got):
    return (own.astype(F32) + got.astype(F32)).astype(BF16)


def scatter_rows(mine):
    return lax.psum_scatter(mine, "fsdp", scatter_dimension=0, tiled=True)


def after(*arrays):
    return lax.optimization_barrier(arrays)


def fast_body(plan, inputs, cotangent, w_qkv, w_out, w_up, w_down, norm_gain, query_scale, prefix_len):
    seqs, positions, d = inputs.shape
    layers, w = w_qkv.shape[0], w_qkv.shape[3]
    dh = query_scale.shape[1]
    unit = SOFT_ONE / math.sqrt(dh)
    factors = jax.nn.softplus(query_scale) * unit
    prefix = lax.dynamic_slice_in_dim(prefix_len, plan.seq, 1)
    order = plan.blocks(positions * plan.tp)
    out_shard, down_shard = jnp.swapaxes(w_out, 1, 2), jnp.swapaxes(w_down, 1, 2)
    pairs = jnp.concatenate(
        [
            jnp.concatenate([w_qkv[:, 0], w_qkv[:, 1]], axis=2)[:, None],
            jnp.concatenate([w_qkv[:, 2], out_shard], axis=2)[:, None],
            jnp.concatenate([w_up, down_shard], axis=2)[:, None],
        ],
        axis=1,
    )

    got, other = gather_call(pairs[0, :2], inputs, pieces_of(2, pairs.shape[2]), plan.fsdp, plan.ring)
    qk0, vo0 = got[0:2], got[2:4]

    def along(l, m):
        return lax.all_gather(pairs[l, m], "fsdp", axis=0, tiled=True)

    def both(rows):
        return rows, plan.across(rows)

    def stacked(rows):
        return (rows, 0), (rows, 1)

    un0_rows, qk1_rows = along(0, 2), along(1, 0)
    other, un0_rows, shards = after(other, un0_rows, pairs[1, 1:])
    shards_got, un0 = plan.across(shards), both(un0_rows)
    kept, weights = [], []
    for l in range(layers):
        qk, vo = (qk0, vo0) if l == 0 else (qk1, vo1)
        scale = jnp.tile(factors[l] * LOG2E, 2 * w // dh)[:, None]
        gain = norm_gain[l, 0][None]
        if l == 0:
            h, h_other, q, k, v, x = project((inputs, other), gain, qk, vo, scale, 3, plan.ring)
        else:
            h, h_other, q, k, v = project(x, gain, qk, vo, scale, 3 + l)
        if l == 0:
            q, shards_got, qk1_rows = after(q, shards_got, qk1_rows)
            shards = jnp.stack([shards, shards_got], axis=1)
            vo1_rows, un1_rows = (lax.all_gather(shards[m], "fsdp", axis=1, tiled=True) for m in range(2))
            qk1 = both(qk1_rows)
        att, lse = attention_forward(q, k, v, prefix, order, dh)
        if l == 0:
            att, un0_got = after(att, un0[1])
            un = un0[0], un0_got
        else:
            att, un1_rows, cot_got = after(att, un1_rows, cot_got)
            un = stacked(un1_rows)
        last = plan.ring if l == layers - 1 else 0
        mid, pre, res, *mats = middle_call(x, att, norm_gain[l, 1][None], vo, un, 5 + l, last)
        if last:
            *mats, out_send = mats
        if l == 0:
            res, cotangent = after(res, cotangent)
            cot_block = plan.pick(cotangent, 1 - plan.seq).astype(BF16)
            res, qk1_got, vo1_rows, cot_block = after(res, qk1[1], vo1_rows, cot_block)
            qk1, vo1 = (qk1[0], qk1_got), stacked(vo1_rows)
            cot_got = plan.across(cot_block)
        kept.append((x, h, h_other, q, k, v, att, lse, mid, pre))
        weights.append((qk, vo, mats))
        x = res
    g = cotangent, cot_got
    out_blocks = x.reshape(seqs, positions, d)
    cot_got, out_send = after(cot_got, out_send)
    g = cotangent, cot_got
    out_got = plan.across(out_send)
    outputs = None
    width = -(-3 * w // 128) * 128
    grads = [None] * layers
    for l in reversed(range(layers)):
        qk, vo, mats = weights[l]
        x, h, h_other, q, k, v, att, lse, mid, pre = kept[l]
        ring = plan.ring if l == layers - 1 else 0
        g_mid, gain_m, g_att, *early = mlp_back(g, mid, pre, norm_gain[l, 1][None], att, mats, width, 1 + l, ring)
        if l > 0:
            early = [scatter_rows(a) for a in early]
        else:
            early_got = plan.across(early[1])
        if l + 1 < layers:
            g_att, grads[l + 1][0][1] = after(g_att, grads[l + 1][0][1])
        dgrads, fgs, pieces = [None] * 6, [], [None] * 2
        for s in (1, 0):
            dq, dk, dv, fg = attention_backward(
                q, k, v, att, g_att, lse, factors[l], prefix, order, dh, s * w, w
            )
            if s == 1:
                pieces[1] = weight_grad(h, h_other, dq, dk, dv, width)
                if l > 0:
                    pieces[1], out_got = after(pieces[1], out_got)
                    g_att, pieces[1] = after(g_att, pieces[1])
                else:
                    g_att, pieces[1], out_got = after(g_att, pieces[1], out_got)
                    outputs = plan.order(plan.pick(out_blocks, plan.seq), out_got.astype(F32)).reshape(out_blocks.shape)
                    pieces[1], early_got, outputs = after(pieces[1], early_got, outputs)
                late_got = plan.across(pieces[1])
                if l + 1 < layers:
                    g_att, grads[l + 1][1] = after(g_att, grads[l + 1][1])
                if l == 0:
                    g_att, early_got = after(g_att, early_got)
                    mine, g_att = after(add_low(early[0], early_got), g_att)
                    early = scatter_rows(mine)
            elif l > 0:
                dq, early[0] = after(dq, early[0])
            dgrads[3 * s:3 * s + 3] = [dq, dk, dv]
            fgs.append(fg)
        fg = fgs[0] + fgs[1]
        if l > 0:
            g, gain_a, pieces[0] = input_back(
                dgrads, x, g_mid, norm_gain[l, 0][None], qk, vo, 7 + l, (h, h_other), width
            )
            pieces[0], late_got = after(pieces[0], late_got)
            mine, g = after(add_low(pieces[0], late_got), g)
        else:
            pieces[0] = weight_grad(h, h_other, *dgrads[:3], width)
        row = lambda a: jnp.pad(a, (0, d - a.shape[0]))[None]
        small = [row(jnp.sum(gain_m, axis=0)), row(jnp.sum(fg, axis=1) / (factors[l] * LOG2E))]
        if l > 0:
            late = scatter_rows(mine)
            small.append(row(jnp.sum(gain_a, axis=0)))
            grads[l] = [early, late, small]
    upper = grads[1][2]
    zero = jnp.zeros((1, d), F32)
    small = jnp.concatenate([zero, upper[2], small[0], upper[0], small[1], upper[1], zero, zero])
    own_half, got_half, late, small = finish(
        dgrads, x, g_mid, norm_gain[0, 0][None], small, pieces[0], late_got, qk, vo, plan.fsdp, plan.ring, 9
    )
    grads[0] = [early, late, small]
    input_grad = plan.order(own_half, got_half.astype(F32)).reshape(out_blocks.shape)
    early = []
    for entry, _, _ in grads:
        if isinstance(entry, list):
            early.append(entry[0].astype(F32) + plan.across(entry[1]).astype(F32))
        else:
            early.append(entry.astype(F32))
    early = jnp.stack(early)
    late = jnp.stack([entry[1].astype(F32) for entry in grads])
    qkv_g = jnp.stack([late[:, :, c * w:(c + 1) * w] for c in range(3)], axis=1)
    up_g, down_g, out_g = (early[:, :, c * w:(c + 1) * w] for c in range(3))
    scale_g = small[4:6, :dh] * jax.nn.sigmoid(query_scale) * unit
    return (
        outputs, input_grad, qkv_g, jnp.swapaxes(out_g, 1, 2), up_g, jnp.swapaxes(down_g, 1, 2),
        small[:2], small[2:4], scale_g,
    )


def body(inputs, cotangent, w_qkv, w_out, w_up, w_down, norm_gain, query_scale, prefix_len):
    seqs, positions, d = inputs.shape
    fsdp, tp = lax.axis_size("fsdp"), lax.axis_size("tp")
    layers = w_qkv.shape[0]
    plan = Plan(seqs, tp, fsdp, w_qkv.shape[2])
    if plan.fast:
        return fast_body(
            plan, inputs, cotangent, w_qkv, w_out, w_up, w_down, norm_gain, query_scale, prefix_len
        )
    dh = query_scale.shape[1]
    unit = SOFT_ONE / math.sqrt(dh)
    factors = jax.nn.softplus(query_scale) * unit
    prefix = lax.dynamic_slice_in_dim(prefix_len, plan.seq, 1)
    order = plan.blocks(positions * tp)
    out_shard, down_shard = jnp.swapaxes(w_out, 1, 2), jnp.swapaxes(w_down, 1, 2)

    weights = []
    for l in range(layers):
        qkv = plan.gather_heads(w_qkv[l])
        out_t = plan.gather_heads(out_shard[l][None])[:, 0]
        up, down_t = plan.gather_full(jnp.stack([w_up[l], down_shard[l]]))
        weights.append(([qkv[:, c] for c in range(3)], out_t, up, down_t))

    x = plan.swap(inputs)
    g = plan.swap(cotangent)
    kept = []
    for l in range(layers):
        x, saved = layer_forward(plan, x, prefix, order, *weights[l], norm_gain[l], factors[l])
        kept.append(saved)
    outputs = plan.unswap(x)
    grads = [None] * layers
    for l in reversed(range(layers)):
        g, grads[l] = layer_backward(
            plan, g, kept[l], prefix, order, *weights[l], norm_gain[l], factors[l]
        )
    input_grad = plan.unswap(g)
    qkv_g, out_g, up_g, down_g, gain_a, gain_m, f_g = (jnp.stack(a) for a in zip(*grads))
    scale_g = f_g * jax.nn.sigmoid(query_scale) * unit
    gain_a, gain_m, scale_g = lax.psum((gain_a, gain_m, scale_g), ("fsdp", "tp"))
    return outputs, input_grad, qkv_g, out_g, up_g, down_g, gain_a, gain_m, scale_g


def solution(mesh):
    placed = (
        P("fsdp", "tp", None),
        P("fsdp", "tp", None),
        P(None, None, "fsdp", "tp"),
        P(None, "tp", "fsdp"),
        P(None, "fsdp", "tp"),
        P(None, "tp", "fsdp"),
        P(),
        P(),
        P("fsdp"),
    )
    return jax.shard_map(
        body,
        mesh=mesh,
        in_specs=placed,
        out_specs=placed[:6] + (P(), P(), P()),
        check_vma=False,
    )
```
